32 devices in a mesh: rep: 4 (over z), shard: 8 (over y, x, core).
Axes of the slice: x: 2, y: 2, z: 4, core: 2. Of those that a mesh axis runs over, the one named last changes fastest.
Arguments:
- query_tokens: bfloat16 [128, 32, 768], P(('rep', 'shard')), may hold values from -6 to 6
- passage_tokens: bfloat16 [32, 256, 768], P(('rep', 'shard')), may hold values from -6 to 6
- query_cot: bfloat16 [128, 32, 768], P(('rep', 'shard')), may hold values from -4 to 4
- passage_cot: bfloat16 [32, 256, 768], P(('rep', 'shard')), may hold values from -4 to 4
- bucket_counts: int32 [32], replicated, may hold values from 0 to 1, as said below
- positives: int32 [128], P(('rep', 'shard')), may hold values from 0 to 127, as said below
- qkv_weight: bfloat16 [2, 768, 2304], P(None, 'shard'), may hold values from -0.21875 to 0.21875
- qv_bias: bfloat16 [2, 1536], P(None, 'shard'), may hold values from -3 to 3
- out_weight: bfloat16 [2, 768, 768], P(None, 'shard'), may hold values from -1.75 to 1.75
- out_bias: bfloat16 [2, 768], P(None, 'shard'), may hold values from -2 to 2
- up_weight: bfloat16 [2, 768, 3072], P(None, 'shard'), may hold values from -0.21875 to 0.21875
- up_bias: bfloat16 [2, 3072], P(None, 'shard'), may hold values from -2 to 2
- down_weight: bfloat16 [2, 3072, 768], P(None, 'shard'), may hold values from -0.109375 to 0.109375
- down_bias: bfloat16 [2, 768], P(None, 'shard'), may hold values from -2 to 2
- norm_gains: bfloat16 [2, 2, 768], P(None, None, 'shard'), may hold values from 0.5 to 1.5
- norm_shifts: bfloat16 [2, 2, 768], P(None, None, 'shard'), may hold values from -2 to 2
Outputs:
- loss: float32 [], replicated
- query_out: bfloat16 [128, 32, 768], P(('rep', 'shard'))
- passage_out: bfloat16 [32, 256, 768], P(('rep', 'shard'))
- query_grad: bfloat16 [128, 32, 768], P(('rep', 'shard'))
- passage_grad: bfloat16 [32, 256, 768], P(('rep', 'shard'))
- qkv_weight_grad: float32 [2, 768, 2304], P(None, 'shard')
- qv_bias_grad: float32 [2, 1536], P(None, 'shard')
- out_weight_grad: float32 [2, 768, 768], P(None, 'shard')
- out_bias_grad: float32 [2, 768], P(None, 'shard')
- up_weight_grad: float32 [2, 768, 3072], P(None, 'shard')
- up_bias_grad: float32 [2, 3072], P(None, 'shard')
- down_weight_grad: float32 [2, 3072, 768], P(None, 'shard')
- down_bias_grad: float32 [2, 768], P(None, 'shard')
- norm_gains_grad: float32 [2, 2, 768], P(None, None, 'shard')
- norm_shifts_grad: float32 [2, 2, 768], P(None, None, 'shard')
The draws below stay inside these ranges and needn't reach their ends.
Inputs may be any that keep to these rules, and one draw needn't show every extreme that they name: `bucket_counts`: each device's number of long-passage blocks (its first blocks); some device has 1 and some has 0; the last device has fewer than 1. `positives`: a valid slot d * 4 + b * 4 + s: s is 0 where block b of device d holds one long passage; the last query's positive is the last slot.
All inputs are finite; a program needn't handle non-finite values.
Results may differ from the reference program's by a relative error of at most 0.015.
Values may be sent and summed in bfloat16 or wider, within the bound.
A program may use at most 192 MiB of HBM per device.

```python
import math
import jax
import jax.numpy as jnp
from jax import lax

D = 768
HD = 64
FF = 3072
QLEN = 32
LONG = 256
SHORT = 64
NBLK = 1
TOWERS = 2
SUBS = 4
SLOTS = 4
NQ = 128
PBLOCKS = 32
NCAND = 128


def bucket_draw(key):
    devices_all = NCAND // SLOTS
    counts = jax.random.randint(jax.random.fold_in(key, 11), (devices_all,), 0, NBLK + 1)
    counts = counts.at[devices_all - 1].set(jnp.minimum(counts[devices_all - 1], NBLK - 1))
    chosen_spots = jax.random.permutation(jax.random.fold_in(key, 12), devices_all - 1)
    counts = counts.at[chosen_spots[0]].set(NBLK)
    counts = counts.at[chosen_spots[1]].set(0)
    return counts.astype(jnp.int32)


def draw_bucket_counts(key, part):
    return bucket_draw(key)


def draw_positives(key, part):
    counts = bucket_draw(key)
    key = jax.random.fold_in(key, 5)
    slot_ids = jax.random.randint(key, (NQ,), 0, NCAND)
    owner_dev = slot_ids // SLOTS
    block_ids = slot_ids % SLOTS // SUBS
    sub_ids = slot_ids % SUBS
    long_one = block_ids < counts[owner_dev]
    chosen = jnp.where(long_one, slot_ids - sub_ids, slot_ids)
    chosen = chosen.at[NQ - 1].set(NCAND - 1)
    return chosen.astype(jnp.int32)


def levels(own_key, shape, shards, smallest, high):
    gain, own = 1.0, jax.random.fold_in(own_key, 6)
    for dim, shards_of in shards:
        draws = jnp.exp(jax.random.uniform(jax.random.fold_in(own, dim), (shards_of,), jnp.float32, smallest / len(shards), high / len(shards)))
        gain = gain * jnp.repeat(draws, shape[dim] // shards_of).reshape([-1 if axis == dim else 1 for axis in range(len(shape))])
    return gain


def scatter_about(own_key, shape, spread, bound, shards=(), kind=jnp.bfloat16):
    drawn = spread * jax.random.normal(own_key, shape, jnp.float32)
    if shards:
        drawn = drawn * levels(own_key, shape, shards, -0.22, 0.18)
    return jnp.clip(drawn, -bound, bound).astype(kind)


def setup_inputs(seed: int = 0) -> dict:
    key_of = jax.random.split(jax.random.key(seed), 17)
    return {
        "query_tokens": scatter_about(key_of[0], (NQ, QLEN, D), 1.0, 6.0, ((0, 32),)),
        "passage_tokens": scatter_about(key_of[1], (PBLOCKS, LONG, D), 1.0, 6.0, ((0, 32),)),
        "query_cot": scatter_about(key_of[2], (NQ, QLEN, D), 0.5, 4.0, ((0, 32),)),
        "passage_cot": scatter_about(key_of[3], (PBLOCKS, LONG, D), 0.5, 4.0, ((0, 32),)),
        "bucket_counts": draw_bucket_counts(jax.random.fold_in(key_of[16], 71), 0),
        "positives": draw_positives(jax.random.fold_in(key_of[16], 71), 0),
        "qkv_weight": scatter_about(key_of[6], (TOWERS, D, 3 * D), D ** -0.5, 0.21875, ((1, 8),)),
        "qv_bias": scatter_about(key_of[7], (TOWERS, 2 * D), 0.5, 3.0, ((1, 8),)),
        "out_weight": scatter_about(key_of[8], (TOWERS, D, D), (D // 64) ** -0.5, 1.75, ((1, 8),)),
        "out_bias": scatter_about(key_of[9], (TOWERS, D), 0.3, 2.0, ((1, 8),)),
        "up_weight": scatter_about(key_of[10], (TOWERS, D, FF), D ** -0.5, 0.21875, ((1, 8),)),
        "up_bias": scatter_about(key_of[11], (TOWERS, FF), 0.3, 2.0, ((1, 8),)),
        "down_weight": scatter_about(key_of[12], (TOWERS, FF, D), FF ** -0.5, 0.109375, ((1, 8),)),
        "down_bias": scatter_about(key_of[13], (TOWERS, D), 0.3, 2.0, ((1, 8),)),
        "norm_gains": jnp.clip(1.0 + 0.1 * jax.random.normal(key_of[14], (TOWERS, 2, D), jnp.float32), 0.5, 1.5).astype(jnp.bfloat16),
        "norm_shifts": scatter_about(key_of[15], (TOWERS, 2, D), 0.3, 2.0, ((2, 8),)),
    }


@jax.custom_vjp
def low(v):
    return lax.optimization_barrier(v.astype(jnp.bfloat16)).astype(jnp.float32)

@jax.custom_vjp
def low_back(v):
    return v

def low_keep(v):
    return (low(v), None)

def low_pass(kept, grad):
    return (grad,)

def back_keep(v):
    return (v, None)

def back_low(kept, grad):
    return (low(grad),)
low.defvjp(low_keep, low_pass)
low_back.defvjp(back_keep, back_low)
HIGH = lax.Precision.HIGHEST
LN_EPS = 1e-05
NEG_FILL = -1e+30

def product(left, right):
    return jnp.dot(left, right, precision=HIGH, preferred_element_type=jnp.float32)

def normalize(hidden):
    row_mean = lax.optimization_barrier(jnp.mean(hidden, axis=-1, keepdims=True))
    centred = hidden - row_mean
    return centred * lax.rsqrt(lax.optimization_barrier(jnp.mean(centred * centred, axis=-1, keepdims=True)) + LN_EPS)

def layer(tokens, long_flags, layer_params, short_len):
    qkv_w, qv_b, out_w, out_b, up_w, up_b, down_w, down_b, gains, shifts = layer_params
    seq_count, length, model_width = tokens.shape
    head_count = model_width // HD
    token_rows = low(tokens.reshape(seq_count * length, model_width))
    qkv_bias = jnp.concatenate([qv_b[:model_width], jnp.zeros((model_width,), jnp.float32), qv_b[model_width:]])
    qkv_all = low(low_back(product(token_rows, qkv_w) + qkv_bias))
    head_split = qkv_all.reshape(seq_count, length, 3, head_count, HD)
    head_query = head_split[:, :, 0]
    head_key = head_split[:, :, 1]
    head_value = head_split[:, :, 2]
    raw_scores = low_back(jnp.einsum('slhd,smhd->shlm', head_query, head_key, precision=HIGH) * (1.0 / math.sqrt(HD)))
    positions = jnp.arange(length, dtype=jnp.int32) // short_len
    same_part = positions[:, None] == positions[None, :]
    attn_mask = long_flags[:, None, None] | same_part[None]
    scores = jnp.where(attn_mask[:, None], raw_scores, NEG_FILL)
    row_max = lax.optimization_barrier(jnp.max(scores, axis=-1, keepdims=True))
    exp_scores = jnp.exp(scores - row_max)
    attn_probs = low(exp_scores / lax.optimization_barrier(jnp.sum(exp_scores, axis=-1, keepdims=True)))
    attn_mixed = jnp.einsum('shlm,smhd->slhd', attn_probs, head_value, precision=HIGH)
    attn_low = low(low_back(attn_mixed.reshape(seq_count * length, model_width)))
    first_sum = token_rows + low_back(product(attn_low, out_w) + out_b)
    middle = normalize(first_sum) * gains[0] + shifts[0]
    pre_act = low_back(product(low(middle), up_w) + up_b)
    act_low = low(jax.nn.gelu(pre_act, approximate=False))
    second = middle + low_back(product(act_low, down_w) + down_b)
    result = normalize(second) * gains[1] + shifts[1]
    return result.reshape(seq_count, length, model_width)

def group_count(seq_count, length):
    group_len = max(1, min(seq_count, 4096 // length))
    while seq_count % group_len:
        group_len = group_len - 1
    return group_len

def run_tower(tokens, long_flags, layer_params, short_len):
    seq_count, length, model_width = tokens.shape
    group_len = group_count(seq_count, length)

    def scan_step(scan_carry, scan_item):
        return (scan_carry, layer(scan_item[0], scan_item[1], layer_params, short_len))
    checked = jax.checkpoint(scan_step)
    grouped = tokens.reshape(seq_count // group_len, group_len, length, model_width)
    flag_groups = long_flags.reshape(seq_count // group_len, group_len)
    unused, outputs = lax.scan(checked, jnp.zeros((), jnp.float32), (grouped, flag_groups))
    return outputs.reshape(seq_count, length, model_width)

def objective(query_x, passage_x, query_params, passage_params, query_cot, passage_cot, long_flags, slot_valid, positives):
    query_flags = jnp.ones((query_x.shape[0],), dtype=bool)
    query_out = run_tower(query_x, query_flags, query_params, QLEN)
    passage_out = run_tower(passage_x, long_flags, passage_params, SHORT)
    query_cls = low(query_out[:, 0])
    passage_cls = low(passage_out.reshape(PBLOCKS, SUBS, SHORT, D)[:, :, 0].reshape(NCAND, D))
    logits = low_back(product(query_cls, passage_cls.T) * (2.0 / math.sqrt(D)))
    masked = jnp.where(slot_valid[None], logits, NEG_FILL)
    row_max = lax.optimization_barrier(jnp.max(masked, axis=1, keepdims=True))
    log_total = row_max[:, 0] + jnp.log(lax.optimization_barrier(jnp.sum(jnp.exp(masked - row_max), axis=1)))
    picked = jnp.take_along_axis(masked, positives[:, None], axis=1)[:, 0]
    losses = log_total - picked
    objective_total = jnp.sum(losses) + jnp.sum(query_out * query_cot) + jnp.sum(passage_out * passage_cot)
    return (objective_total, (query_out, passage_out, jnp.mean(losses)))

def reference(query_tokens, passage_tokens, query_cot, passage_cot, bucket_counts, positives, qkv_weight, qv_bias, out_weight, out_bias, up_weight, up_bias, down_weight, down_bias, norm_gains, norm_shifts):
    stacks = (qkv_weight, qv_bias, out_weight, out_bias, up_weight, up_bias, down_weight, down_bias, norm_gains, norm_shifts)
    query_params = tuple((stack_arr[0].astype(jnp.float32) for stack_arr in stacks))
    passage_params = tuple((stack_arr[1].astype(jnp.float32) for stack_arr in stacks))
    block_ids = jnp.arange(PBLOCKS, dtype=jnp.int32)
    long_flags = block_ids % NBLK < bucket_counts[block_ids // NBLK]
    slot_ids = jnp.arange(NCAND, dtype=jnp.int32)
    slot_valid = (slot_ids % SLOTS // SUBS >= bucket_counts[slot_ids // SLOTS]) | (slot_ids % SUBS == 0)
    query_x = query_tokens.astype(jnp.float32)
    passage_x = passage_tokens.astype(jnp.float32)
    query_dout = query_cot.astype(jnp.float32)
    passage_dout = passage_cot.astype(jnp.float32)

    def wrapped(qx, px, qp, pp):
        return objective(qx, px, qp, pp, query_dout, passage_dout, long_flags, slot_valid, positives)
    objective_total, pullback, extras = jax.vjp(wrapped, query_x, passage_x, query_params, passage_params, has_aux=True)
    query_grad, passage_grad, query_pgrad, passage_pgrad = pullback(jnp.ones_like(objective_total))
    query_out, passage_out, loss = extras
    weight_grads = tuple((jnp.stack([first_g, second_g]) for first_g, second_g in zip(query_pgrad, passage_pgrad)))
    return (loss, query_out.astype(jnp.bfloat16), passage_out.astype(jnp.bfloat16), query_grad.astype(jnp.bfloat16), passage_grad.astype(jnp.bfloat16), weight_grads[0], weight_grads[1], weight_grads[2], weight_grads[3], weight_grads[4], weight_grads[5], weight_grads[6], weight_grads[7], weight_grads[8], weight_grads[9])
```

```python
import functools
import math

import jax
import jax.numpy as jnp
from jax import lax
from jax.experimental import pallas as pl
from jax.experimental.pallas import tpu as pltpu
from jax.sharding import PartitionSpec as P

HD = 64
SHORT = 64


LN_EPS = 1e-05
NEG_FILL = -1e30
INV_ROOT_TWO = 0.7071067811865476
INV_ROOT_TWO_PI = 0.3989422804014327
VMEM_LIMIT = 66 * 1000 * 1000


def for_sending(array):
    return jax.tree.map(lambda a: a.astype(jnp.bfloat16) if a.dtype == jnp.float32 else a, array)


def pick_tower(stacks, tower_index):
    qkv_w, qv_b, out_w, out_b, up_w, up_b, down_w, down_b, gains, shifts = stacks
    return (
        qkv_w[tower_index],
        qv_b[tower_index],
        out_w[tower_index],
        out_b[tower_index],
        up_w[tower_index],
        up_b[tower_index],
        down_w[tower_index],
        down_b[tower_index],
        gains[tower_index].T,
        shifts[tower_index].T,
    )


def fetch_layer(stacks, tower_index):
    return lax.all_gather(for_sending(pick_tower(stacks, tower_index)), "shard", axis=0, tiled=True)


def fetch_again(stacks, tower_index):
    return lax.all_gather(for_sending(pick_tower(stacks, tower_index)), "shard", axis=0, tiled=True)


def normalize(hidden):
    row_mean = jnp.mean(hidden, axis=-1, keepdims=True)
    centred = hidden - row_mean
    inv_std = lax.rsqrt(jnp.mean(centred * centred, axis=-1, keepdims=True) + LN_EPS)
    return (centred * inv_std, inv_std)


def norm_back(grad_in, normed, inv_std):
    return inv_std * (
        grad_in
        - jnp.mean(grad_in, axis=-1, keepdims=True)
        - normed * jnp.mean(grad_in * normed, axis=-1, keepdims=True)
    )


def block_mask(long_flags, length, short_len):
    row_part = lax.broadcasted_iota(jnp.int32, (length, length), 0) // short_len
    col_part = lax.broadcasted_iota(jnp.int32, (length, length), 1) // short_len
    return long_flags[:, None, None] | (row_part == col_part)[None]


def head_scores(head_query, head_key, attn_mask):
    raw_scores = jnp.einsum(
        "slhd,smhd->shlm", head_query, head_key, preferred_element_type=jnp.float32
    ) * (1.0 / math.sqrt(HD))
    return jnp.where(attn_mask[:, None], raw_scores, NEG_FILL)


def layer_forward(tokens, weights, attn_mask):
    qkv_w, qv_b, out_w, out_b, up_w, up_b, down_w, down_b, gains, shifts = weights
    seq_count, length, model_width = tokens.shape
    head_count = model_width // HD
    token_rows = tokens.reshape(seq_count * length, model_width)
    qv_float = qv_b.astype(jnp.float32)
    qkv_bias = jnp.concatenate(
        [qv_float[:model_width], jnp.zeros((model_width,), jnp.float32), qv_float[model_width:]]
    )
    qkv_low = (jnp.dot(token_rows, qkv_w, preferred_element_type=jnp.float32) + qkv_bias).astype(
        jnp.bfloat16
    )
    head_split = qkv_low.reshape(seq_count, length, 3, head_count, HD)
    scores = head_scores(head_split[:, :, 0], head_split[:, :, 1], attn_mask)
    row_max = jnp.max(scores, axis=-1, keepdims=True)
    exp_scores = jnp.exp(scores - row_max)
    row_total = jnp.sum(exp_scores, axis=-1, keepdims=True)
    attn_probs = (exp_scores / row_total).astype(jnp.bfloat16)
    log_total = row_max + jnp.log(row_total)
    attn_mixed = jnp.einsum(
        "shlm,smhd->slhd", attn_probs, head_split[:, :, 2], preferred_element_type=jnp.float32
    )
    attn_low = attn_mixed.reshape(seq_count * length, model_width).astype(jnp.bfloat16)
    first_sum = (
        token_rows.astype(jnp.float32)
        + jnp.dot(attn_low, out_w, preferred_element_type=jnp.float32)
        + out_b.astype(jnp.float32)
    )
    normed_one, inv_one = normalize(first_sum)
    gain_float = gains.astype(jnp.float32)
    shift_float = shifts.astype(jnp.float32)
    middle = normed_one * gain_float[:, 0] + shift_float[:, 0]
    middle_low = middle.astype(jnp.bfloat16)
    pre_act = jnp.dot(middle_low, up_w, preferred_element_type=jnp.float32) + up_b.astype(
        jnp.float32
    )
    act_low = jax.nn.gelu(pre_act, approximate=False).astype(jnp.bfloat16)
    second = (
        middle
        + jnp.dot(act_low, down_w, preferred_element_type=jnp.float32)
        + down_b.astype(jnp.float32)
    )
    normed_two, inv_two = normalize(second)
    result = normed_two * gain_float[:, 1] + shift_float[:, 1]
    kept = (
        token_rows,
        qkv_low,
        log_total,
        attn_low,
        normed_one,
        inv_one,
        middle_low,
        pre_act,
        act_low,
        normed_two,
        inv_two,
    )
    return (result, kept)


def layer_backward(grad_out, weights, kept, attn_mask):
    qkv_w, qv_b, out_w, out_b, up_w, up_b, down_w, down_b, gains, shifts = weights
    (
        token_rows,
        qkv_low,
        log_total,
        attn_low,
        normed_one,
        inv_one,
        middle_low,
        pre_act,
        act_low,
        normed_two,
        inv_two,
    ) = kept
    seq_count = attn_mask.shape[0]
    model_width = token_rows.shape[1]
    length = token_rows.shape[0] // seq_count
    head_count = model_width // HD
    gain_float = gains.astype(jnp.float32)
    gain_two = jnp.sum(grad_out * normed_two, axis=0)
    shift_two = jnp.sum(grad_out, axis=0)
    d_second = norm_back(grad_out * gain_float[:, 1], normed_two, inv_two)
    d_ffn = d_second.astype(jnp.bfloat16)
    d_down_w = jnp.dot(act_low.T, d_ffn, preferred_element_type=jnp.float32)
    d_down_b = jnp.sum(d_ffn.astype(jnp.float32), axis=0)
    d_act = jnp.dot(d_ffn, down_w.T, preferred_element_type=jnp.float32)
    gelu_slope = (
        0.5 * (1.0 + lax.erf(pre_act * INV_ROOT_TWO))
        + pre_act * jnp.exp(-0.5 * pre_act * pre_act) * INV_ROOT_TWO_PI
    )
    d_pre = (d_act * gelu_slope).astype(jnp.bfloat16)
    d_up_w = jnp.dot(middle_low.T, d_pre, preferred_element_type=jnp.float32)
    d_up_b = jnp.sum(d_pre.astype(jnp.float32), axis=0)
    d_middle = d_second + jnp.dot(d_pre, up_w.T, preferred_element_type=jnp.float32)
    gain_one = jnp.sum(d_middle * normed_one, axis=0)
    shift_one = jnp.sum(d_middle, axis=0)
    d_first = norm_back(d_middle * gain_float[:, 0], normed_one, inv_one)
    d_attn_out = d_first.astype(jnp.bfloat16)
    d_out_w = jnp.dot(attn_low.T, d_attn_out, preferred_element_type=jnp.float32)
    d_out_b = jnp.sum(d_attn_out.astype(jnp.float32), axis=0)
    d_mixed = (
        jnp.dot(d_attn_out, out_w.T, preferred_element_type=jnp.float32)
        .astype(jnp.bfloat16)
        .reshape(seq_count, length, head_count, HD)
    )
    head_split = qkv_low.reshape(seq_count, length, 3, head_count, HD)
    head_query = head_split[:, :, 0]
    head_key = head_split[:, :, 1]
    head_value = head_split[:, :, 2]
    attn_probs = jnp.exp(head_scores(head_query, head_key, attn_mask) - log_total)
    d_probs = jnp.einsum("slhd,smhd->shlm", d_mixed, head_value, preferred_element_type=jnp.float32)
    d_value = jnp.einsum(
        "shlm,slhd->smhd",
        attn_probs.astype(jnp.bfloat16),
        d_mixed,
        preferred_element_type=jnp.float32,
    )
    d_scores = (
        attn_probs * (d_probs - jnp.sum(d_probs * attn_probs, axis=-1, keepdims=True))
    ).astype(jnp.bfloat16)
    d_query = jnp.einsum(
        "shlm,smhd->slhd", d_scores, head_key, preferred_element_type=jnp.float32
    ) * (1.0 / math.sqrt(HD))
    d_key = jnp.einsum(
        "shlm,slhd->smhd", d_scores, head_query, preferred_element_type=jnp.float32
    ) * (1.0 / math.sqrt(HD))
    d_qkv = (
        jnp.stack([d_query, d_key, d_value], axis=2)
        .reshape(seq_count * length, 3 * model_width)
        .astype(jnp.bfloat16)
    )
    d_qkv_w = jnp.dot(token_rows.T, d_qkv, preferred_element_type=jnp.float32)
    column_sums = jnp.sum(d_qkv.astype(jnp.float32), axis=0)
    d_qv_b = jnp.concatenate([column_sums[:model_width], column_sums[2 * model_width :]])
    d_tokens = d_first + jnp.dot(d_qkv, qkv_w.T, preferred_element_type=jnp.float32)
    layer_grads = (
        d_qkv_w,
        d_qv_b,
        d_out_w,
        d_out_b,
        d_up_w,
        d_up_b,
        d_down_w,
        d_down_b,
        jnp.stack([gain_one, gain_two], axis=1),
        jnp.stack([shift_one, shift_two], axis=1),
    )
    return (d_tokens, layer_grads)


def reduce_layer(layer_grads):
    owned_grads = (
        lax.psum_scatter(layer_grads[0], "shard", scatter_dimension=0, tiled=True),
        lax.psum_scatter(layer_grads[1], "shard", scatter_dimension=0, tiled=True),
        lax.psum_scatter(layer_grads[2], "shard", scatter_dimension=0, tiled=True),
        lax.psum_scatter(layer_grads[3], "shard", scatter_dimension=0, tiled=True),
        lax.psum_scatter(layer_grads[4], "shard", scatter_dimension=0, tiled=True),
        lax.psum_scatter(layer_grads[5], "shard", scatter_dimension=0, tiled=True),
        lax.psum_scatter(layer_grads[6], "shard", scatter_dimension=0, tiled=True),
        lax.psum_scatter(layer_grads[7], "shard", scatter_dimension=0, tiled=True),
        lax.psum_scatter(layer_grads[8], "shard", scatter_dimension=0, tiled=True),
        lax.psum_scatter(layer_grads[9], "shard", scatter_dimension=0, tiled=True),
    )
    quarter = (
        lax.psum_scatter(
            owned_grads[0].astype(jnp.bfloat16), "rep", scatter_dimension=0, tiled=True
        ).astype(jnp.float32),
        lax.psum_scatter(
            owned_grads[1].astype(jnp.bfloat16), "rep", scatter_dimension=0, tiled=True
        ).astype(jnp.float32),
        lax.psum_scatter(
            owned_grads[2].astype(jnp.bfloat16), "rep", scatter_dimension=0, tiled=True
        ).astype(jnp.float32),
        lax.psum_scatter(
            owned_grads[3].astype(jnp.bfloat16), "rep", scatter_dimension=0, tiled=True
        ).astype(jnp.float32),
        lax.psum_scatter(
            owned_grads[4].astype(jnp.bfloat16), "rep", scatter_dimension=0, tiled=True
        ).astype(jnp.float32),
        lax.psum_scatter(
            owned_grads[5].astype(jnp.bfloat16), "rep", scatter_dimension=0, tiled=True
        ).astype(jnp.float32),
        lax.psum_scatter(
            owned_grads[6].astype(jnp.bfloat16), "rep", scatter_dimension=0, tiled=True
        ).astype(jnp.float32),
        lax.psum_scatter(
            owned_grads[7].astype(jnp.bfloat16), "rep", scatter_dimension=0, tiled=True
        ).astype(jnp.float32),
        lax.psum_scatter(
            owned_grads[8].astype(jnp.bfloat16), "rep", scatter_dimension=0, tiled=True
        ).astype(jnp.float32),
        lax.psum_scatter(
            owned_grads[9].astype(jnp.bfloat16), "rep", scatter_dimension=0, tiled=True
        ).astype(jnp.float32),
    )
    return (
        lax.all_gather(quarter[0].astype(jnp.bfloat16), "rep", axis=0, tiled=True).astype(
            jnp.float32
        ),
        lax.all_gather(quarter[1].astype(jnp.bfloat16), "rep", axis=0, tiled=True).astype(
            jnp.float32
        ),
        lax.all_gather(quarter[2].astype(jnp.bfloat16), "rep", axis=0, tiled=True).astype(
            jnp.float32
        ),
        lax.all_gather(quarter[3].astype(jnp.bfloat16), "rep", axis=0, tiled=True).astype(
            jnp.float32
        ),
        lax.all_gather(quarter[4].astype(jnp.bfloat16), "rep", axis=0, tiled=True).astype(
            jnp.float32
        ),
        lax.all_gather(quarter[5].astype(jnp.bfloat16), "rep", axis=0, tiled=True).astype(
            jnp.float32
        ),
        lax.all_gather(quarter[6].astype(jnp.bfloat16), "rep", axis=0, tiled=True).astype(
            jnp.float32
        ),
        lax.all_gather(quarter[7].astype(jnp.bfloat16), "rep", axis=0, tiled=True).astype(
            jnp.float32
        ),
        lax.all_gather(quarter[8].astype(jnp.bfloat16), "rep", axis=0, tiled=True).astype(
            jnp.float32
        ),
        lax.all_gather(quarter[9].astype(jnp.bfloat16), "rep", axis=0, tiled=True).astype(
            jnp.float32
        ),
    )


def local(
    query_tokens,
    passage_tokens,
    query_cot,
    passage_cot,
    bucket_counts,
    positives,
    qkv_weight,
    qv_bias,
    out_weight,
    out_bias,
    up_weight,
    up_bias,
    down_weight,
    down_bias,
    norm_gains,
    norm_shifts,
):
    stacks = (
        qkv_weight,
        qv_bias,
        out_weight,
        out_bias,
        up_weight,
        up_bias,
        down_weight,
        down_bias,
        norm_gains,
        norm_shifts,
    )
    blocks, long_len, model_width = passage_tokens.shape
    query_count, query_len, unused_width = query_tokens.shape
    subs_count = long_len // SHORT
    slot_count = blocks * subs_count
    my_index = lax.axis_index(("rep", "shard"))
    own_count = lax.dynamic_index_in_dim(bucket_counts, my_index, 0, keepdims=False)
    passage_mask = block_mask(lax.iota(jnp.int32, blocks) < own_count, long_len, SHORT)
    query_mask = block_mask(jnp.ones((query_count,), dtype=bool), query_len, query_len)
    query_weights = fetch_layer(stacks, 0)
    query_result, query_kept = layer_forward(query_tokens, query_weights, query_mask)
    passage_weights = fetch_layer(stacks, 1)
    passage_result, passage_kept = layer_forward(passage_tokens, passage_weights, passage_mask)
    query_cls = query_result.reshape(query_count, query_len, model_width)[:, 0].astype(jnp.bfloat16)
    passage_cls = (
        passage_result.reshape(blocks, subs_count, SHORT, model_width)[:, :, 0]
        .reshape(slot_count, model_width)
        .astype(jnp.bfloat16)
    )
    every_cls = lax.all_gather(passage_cls, ("rep", "shard"), axis=0, tiled=True)
    cand_count = every_cls.shape[0]
    device_count = bucket_counts.shape[0]
    score_scale = 2.0 / math.sqrt(model_width)
    logits = jnp.dot(query_cls, every_cls.T, preferred_element_type=jnp.float32) * score_scale
    slot_ids = lax.iota(jnp.int32, cand_count)
    owner_index = slot_ids // slot_count
    owner_counts = jnp.sum(
        jnp.where(
            owner_index[:, None] == lax.iota(jnp.int32, device_count)[None], bucket_counts[None], 0
        ),
        axis=1,
    )
    slot_valid = (slot_ids % slot_count // subs_count >= owner_counts) | (
        slot_ids % subs_count == 0
    )
    masked = jnp.where(slot_valid[None], logits, NEG_FILL)
    row_max = jnp.max(masked, axis=1, keepdims=True)
    exp_scores = jnp.exp(masked - row_max)
    row_total = jnp.sum(exp_scores, axis=1, keepdims=True)
    log_total = row_max[:, 0] + jnp.log(row_total[:, 0])
    hit_mask = slot_ids[None] == positives[:, None]
    picked = jnp.sum(jnp.where(hit_mask, masked, 0.0), axis=1)
    local_loss = jnp.sum(log_total - picked)
    d_logits = (exp_scores / row_total - hit_mask.astype(jnp.float32)).astype(jnp.bfloat16)
    d_query_cls = jnp.dot(d_logits, every_cls, preferred_element_type=jnp.float32) * score_scale
    d_cands = (
        lax.dot_general(
            d_logits, query_cls, (((0,), (0,)), ((), ())), preferred_element_type=jnp.float32
        )
        * score_scale
    )
    d_passage_cls = lax.psum_scatter(d_cands, ("rep", "shard"), scatter_dimension=0, tiled=True)
    loss_sum = lax.psum(local_loss, ("rep", "shard"))
    loss = loss_sum / (query_count * lax.axis_size(("rep", "shard")))
    query_dout = (
        query_cot.astype(jnp.float32)
        .at[:, 0]
        .add(d_query_cls)
        .reshape(query_count * query_len, model_width)
    )
    passage_dout = (
        passage_cot.astype(jnp.float32)
        .reshape(blocks, subs_count, SHORT, model_width)
        .at[:, :, 0]
        .add(d_passage_cls.reshape(blocks, subs_count, model_width))
        .reshape(blocks * long_len, model_width)
    )
    passage_back = fetch_again(stacks, 1)
    passage_dx, passage_grads = layer_backward(
        passage_dout, passage_back, passage_kept, passage_mask
    )
    passage_owned = reduce_layer(passage_grads)
    query_back = fetch_again(stacks, 0)
    query_dx, query_grads = layer_backward(query_dout, query_back, query_kept, query_mask)
    query_owned = reduce_layer(query_grads)
    stacked = [
        jnp.stack([first_g, second_g]) for first_g, second_g in zip(query_owned, passage_owned)
    ]
    gains_grad = jnp.swapaxes(stacked[8], 1, 2)
    shifts_grad = jnp.swapaxes(stacked[9], 1, 2)
    return (
        loss,
        query_result.reshape(query_count, query_len, model_width).astype(jnp.bfloat16),
        passage_result.reshape(blocks, long_len, model_width).astype(jnp.bfloat16),
        query_dx.reshape(query_count, query_len, model_width).astype(jnp.bfloat16),
        passage_dx.reshape(blocks, long_len, model_width).astype(jnp.bfloat16),
        stacked[0],
        stacked[1],
        stacked[2],
        stacked[3],
        stacked[4],
        stacked[5],
        stacked[6],
        stacked[7],
        gains_grad,
        shifts_grad,
    )


BF = jnp.bfloat16
F32 = jnp.float32
MESH = pl.DeviceIdType.MESH
ROWS = (128, 256)
D = 768
HALF = 384
FFN = 768
NEIGH = tuple((dy, dx, dc) for dy in (0, 1) for dx in (0, 1) for dc in (0, 1) if dy + dx + dc)

(S_X, S_QKV, S_OUT, S_UP, S_DN, S_OP, S_MY, S_MC,
 S_MF, S_F1A, S_F1B, S_F2, S_DY, S_DC, S_DF, S_D1A,
 S_D1B, S_D2, S_DA, S_DX, S_GD, S_GU, S_GO, S_GQ,
 S_ZAD, S_ZAU, S_ZAO, S_ZAQ, S_ZBD, S_ZBU, S_ZBO, S_ZBQ,
 S_ZOD, S_ZOU, S_ZOO, S_ZOQ) = range(36)
(S_SMALL, S_CZ, S_CP, S_BG, S_ZAS, S_ZBS, S_ZOS, S_COT, S_FIN, S_FIN2) = range(36, 46)
N_SEMS = 184


def nn(a, b):
    return jnp.dot(a, b, preferred_element_type=F32)


def nt(a, b):
    return lax.dot_general(a, b, (((1,), (1,)), ((), ())), preferred_element_type=F32)


def tn(a, b):
    return lax.dot_general(a, b, (((0,), (0,)), ((), ())), preferred_element_type=F32)


def flip(v, d):
    return 1 - v if d else v


def mo(v, m):
    return pl.multiple_of(v, m)


(B_X, B_COT, B_WQ, B_WO, B_WU, B_WD, B_QB, B_UB, B_QKV, B_P,
 B_ATT, B_OS, B_OR, B_N1, B_N2, B_R1, B_R2, B_MID, B_ACT, B_SL,
 B_S1, B_V1, B_S2, B_V2, B_KP, B_Y, B_DF, B_DA, B_GD, B_GU,
 B_GO, B_GQ, B_ZSD, B_ZSU, B_ZSO, B_ZSQ, B_ZAD, B_ZAU, B_ZAO, B_ZAQ,
 B_ZBD, B_ZBU, B_ZBO, B_ZBQ, B_SP, B_PV, B_BG, B_BGS, B_BGR, B_BGA,
 B_BGB, B_CM, B_GA, B_CG) = range(54)


def scratch_list():
    s = []

    def add(name, t, shape, dtype):
        s.append(((name, t), pltpu.VMEM(shape, dtype)))

    for t, T in enumerate(ROWS):
        add(B_X, t, (2 * T, D), BF)
        add(B_COT, t, (T, D), BF)
        add(B_WQ, t, (D, 3 * HALF), BF)
        add(B_WO, t, (HALF, D), BF)
        add(B_WU, t, (D, FFN), BF)
        add(B_WD, t, (FFN, D), BF)
        add(B_QB, t, (8, 3 * HALF), F32)
        add(B_UB, t, (8, FFN), F32)
        add(B_QKV, t, (2 * T, 3 * HALF), BF)
        add(B_P, t, (12, T, T), F32)
        add(B_ATT, t, (2 * T, HALF), BF)
        add(B_OS, t, (T, D), BF)
        add(B_OR, t, (T, D), BF)
        add(B_N1, t, (T, D), F32)
        add(B_N2, t, (T, D), F32)
        add(B_R1, t, (T, 128), F32)
        add(B_R2, t, (T, 128), F32)
        add(B_MID, t, (4 * T, D), BF)
        add(B_ACT, t, (4 * T, FFN), BF)
        add(B_SL, t, (4 * T, FFN), BF)
        add(B_S1, t, (2, T, D), BF)
        add(B_V1, t, (2, T, D), BF)
        add(B_S2, t, (T, D), BF)
        add(B_V2, t, (T, D), BF)
        add(B_KP, t, (2, T, D), F32)
        add(B_Y, t, (T, D), BF)
        add(B_DF, t, (4 * T, D), BF)
        add(B_DA, t, (2 * T, D), BF)
        add(B_GD, t, (HALF, D), BF)
        add(B_GU, t, (8, 96, FFN), BF)
        add(B_GO, t, (4, 96, D), BF)
        add(B_GQ, t, (8, 96, 3 * HALF), BF)
        for first in (B_ZSD, B_ZAD, B_ZBD):
            add(first, t, (HALF, D), BF)
            add(first + 1, t, (96, 4 * D), BF)
            add(first + 2, t, (96, D), BF)
            add(first + 3, t, (96, 3 * D), BF)
    add(B_SP, 0, (8, 32, D), BF)
    add(B_PV, 0, (32, D), F32)
    add(B_BG, 0, (32, D), F32)
    add(B_BGS, 0, (32, D), F32)
    add(B_BGR, 0, (8, 32, D), F32)
    add(B_BGA, 0, (32, D), F32)
    add(B_BGB, 0, (32, D), F32)
    add(B_CM, 0, (16, 512), BF)
    add(B_GA, 0, (32, 16, 512), BF)
    add(B_CG, 0, (2, 16, D), F32)
    return s


def fused_kernel(stop, *refs):
    (i_x0, i_x1, i_cot0, i_cot1, i_qkvw, i_outw, i_upw, i_dnw, i_small, i_pos, i_flags, i_valid,
     o_loss, o_y0, o_y1, o_gx0, o_gx1, o_oq, o_oo, o_ou, o_od, o_obg) = refs[:22]
    held = {key: ref for (key, _), ref in zip(scratch_list(), refs[22:])}
    sems = refs[-1]

    def g(name, t):
        return held[(name, t)]

    rep = lax.axis_index("rep")
    s = lax.axis_index("shard")
    y = s // 4
    x = (s // 2) % 2
    c = s % 2
    x_in = (i_x0, i_x1)
    cot_in = (i_cot0, i_cot1)

    def sem(name, t, side):
        return sems.at[4 * name + 2 * t + side]

    def sh(yy, xx, cc):
        return yy * 4 + xx * 2 + cc

    def send(src, dst, name, t, dev):
        pltpu.make_async_remote_copy(src, dst, send_sem=sem(name, t, 1), recv_sem=sem(name, t, 0),
                                     device_id=dev, device_id_type=MESH).start()

    def local(src, dst, name, t, side=0):
        pltpu.make_async_copy(src, dst, sem(name, t, side)).start()

    def wait(ref, name, t, side=0):
        pltpu.make_async_copy(ref, ref, sem(name, t, side)).wait()

    def peer(d):
        return flip(y, d[0]), flip(x, d[1]), flip(c, d[2])

    sib = (rep, sh(y, x, 1 - c))
    ypeer = (rep, sh(1 - y, x, c))
    xpeer = (rep, sh(y, 1 - x, c))

    bar = pltpu.get_barrier_semaphore()
    for d in NEIGH:
        pl.semaphore_signal(bar, 1, device_id=(rep, sh(*peer(d))), device_id_type=MESH)
    for k in (1, 2, 3):
        pl.semaphore_signal(bar, 1, device_id=((rep + k) % 4, s), device_id_type=MESH)
    pl.semaphore_wait(bar, 10)

    for t, T in enumerate(ROWS):
        own = g(B_X, t).at[pl.ds(mo(c * T, 128), T)]
        send(x_in[t], own, S_X, t, sib)
        local(x_in[t], own, S_X, t)
    for d in NEIGH:
        send(i_small, g(B_SP, 0).at[s], S_SMALL, 0, (rep, sh(*peer(d))))
    local(i_small, g(B_SP, 0).at[s], S_SMALL, 0)
    rows96 = pl.ds(mo(s * 96, 32), 96)

    def send_qkv(t):
        for part in range(3):
            for d in NEIGH:
                p = peer(d)
                send(i_qkvw.at[t, :, pl.ds(mo(part * D + p[2] * HALF, 128), HALF)],
                     g(B_WQ, t).at[rows96, pl.ds(part * HALF, HALF)], S_QKV, t, (rep, sh(*p)))
            local(i_qkvw.at[t, :, pl.ds(mo(part * D + c * HALF, 128), HALF)],
                  g(B_WQ, t).at[rows96, pl.ds(part * HALF, HALF)], S_QKV, t)

    def send_out(t):
        dst = g(B_WO, t).at[pl.ds(mo((x * 2 + c) * 96, 32), 96)]
        for dy in (0, 1):
            for dx in (0, 1):
                dev = (rep, sh(flip(y, dy), flip(x, dx), y))
                if dy + dx:
                    send(i_outw.at[t], dst, S_OUT, t, dev)
                else:
                    @pl.when(c == y)
                    def _():
                        local(i_outw.at[t], dst, S_OUT, t)

                    @pl.when(c != y)
                    def _():
                        send(i_outw.at[t], dst, S_OUT, t, dev)

    def send_up(t):
        for d in NEIGH + ((0, 0, 0),):
            p = peer(d)
            for xx in (0, 1):
                src = i_upw.at[t, :, pl.ds(mo(HALF * (4 * p[0] + 2 * xx + p[2]), 128), HALF)]
                dst = g(B_WU, t).at[rows96, pl.ds(xx * HALF, HALF)]
                if sum(d):
                    send(src, dst, S_UP, t, (rep, sh(*p)))
                else:
                    local(src, dst, S_UP, t)

    def send_dn(t):
        dst = g(B_WD, t).at[pl.ds(mo(x * HALF, 128), HALF)]
        send(i_dnw.at[t], dst, S_DN, t, xpeer)
        local(i_dnw.at[t], dst, S_DN, t)

    for t in (1, 0):
        send_qkv(t)
        send_out(t)
    for t in (1, 0):
        send_up(t)
        send_dn(t)
    for t in (0, 1):
        local(cot_in[t], g(B_COT, t), S_COT, 0, t)

    wait(g(B_SP, 0), S_SMALL, 0)
    tot = g(B_SP, 0)[0].astype(F32)
    for k in range(1, 8):
        tot = tot + g(B_SP, 0)[k].astype(F32)
    g(B_PV, 0)[...] = tot

    def prow(t, k):
        return g(B_PV, 0)[t * 16 + k:t * 16 + k + 1, :]

    lane_half = pl.ds(mo(c * HALF, 128), HALF)
    for t in (0, 1):
        g(B_QB, t)[...] = jnp.zeros((8, 3 * HALF), F32)
        g(B_QB, t)[0:1, 0:HALF] = g(B_PV, 0)[t * 16:t * 16 + 1, lane_half]
        g(B_QB, t)[0:1, 2 * HALF:] = g(B_PV, 0)[t * 16 + 1:t * 16 + 2, lane_half]
        for xx in (0, 1):
            lo = g(B_PV, 0)[t * 16 + 8 + xx:t * 16 + 9 + xx, lane_half]
            hi = g(B_PV, 0)[t * 16 + 10 + xx:t * 16 + 11 + xx, lane_half]
            g(B_UB, t)[0:1, xx * HALF:(xx + 1) * HALF] = jnp.where(jnp.full((1, HALF), y) == 0, lo, hi)

    def same_part(t, grp):
        T = ROWS[t]
        shift = 5 if t == 0 else 6
        ri = lax.broadcasted_iota(jnp.int32, (T, T), 0) >> shift
        ci = lax.broadcasted_iota(jnp.int32, (T, T), 1) >> shift
        m = ri == ci
        if t == 1:
            flag = i_flags[pl.ds(grp * 8, 1), 0:1]
            m = m | (flag > 0.0)
        return m

    lane_lo = lax.broadcasted_iota(jnp.int32, (1, 128), 1) < 64
    mask_a = lane_lo.astype(F32).astype(BF)
    mask_b = (1.0 - lane_lo.astype(F32)).astype(BF)

    def lnfwd(first, gain, shift):
        mean = jnp.mean(first, axis=-1, keepdims=True)
        cen = first - mean
        inv = lax.rsqrt(jnp.mean(cen * cen, axis=-1, keepdims=True) + LN_EPS)
        n = cen * inv
        return n, inv, n * gain + shift

    CH = 64

    def attention(t):
        T = ROWS[t]
        X, WQ, QKV, P, ATT = g(B_X, t), g(B_WQ, t), g(B_QKV, t), g(B_P, t), g(B_ATT, t)
        wait(X, S_X, t)
        wait(WQ, S_QKV, t)

        @pl.loop(0, 3)
        def _(j):
            cols = pl.ds(mo(j * HALF, 128), HALF)
            QKV[:, cols] = (nn(X[...], WQ[:, cols]) + g(B_QB, t)[0:1, cols]).astype(BF)

        @pl.loop(0, 2)
        def _(grp):
            rows = pl.ds(mo(grp * T, 128), T)
            m = same_part(t, grp)

            @pl.loop(0, 3)
            def _(hp):
                q = QKV[rows, pl.ds(mo(hp * 128, 128), 128)]
                k = QKV[rows, pl.ds(mo(HALF + hp * 128, 128), 128)]
                val = QKV[rows, pl.ds(mo(2 * HALF + hp * 128, 128), 128)]
                outs = []
                for h, msk in ((0, mask_a), (1, mask_b)):
                    sc = jnp.where(m, nt(q * msk, k) * (1.0 / math.sqrt(HD)), NEG_FILL)
                    mx = jnp.max(sc, axis=-1, keepdims=True)
                    e = jnp.exp(sc - mx)
                    p = e * (1.0 / jnp.sum(e, axis=-1, keepdims=True))
                    P[grp * 6 + hp * 2 + h] = p
                    outs.append(nn(p.astype(BF), val))
                ATT[rows, pl.ds(mo(hp * 128, 128), 128)] = jnp.where(lane_lo, outs[0], outs[1]).astype(BF)

        wait(g(B_WO, t), S_OUT, t)
        g(B_OS, t)[...] = nn(ATT[pl.ds(mo((1 - c) * T, 128), T), :], g(B_WO, t)[...]).astype(BF)
        send(g(B_OS, t), g(B_OR, t), S_OP, t, sib)
        g(B_KP, t)[0] = nn(ATT[pl.ds(mo(c * T, 128), T), :], g(B_WO, t)[...])
        wait(g(B_OR, t), S_OP, t)
        me4 = (2 * y + c) * T
        ob, gain, shift = prow(t, 2), prow(t, 4), prow(t, 6)

        @pl.loop(0, T // CH)
        def _(i):
            r = pl.ds(mo(i * CH, CH), CH)
            first = (X[pl.ds(mo(c * T + i * CH, CH), CH), :].astype(F32) + g(B_KP, t)[0, r, :]
                     + g(B_OR, t)[r, :].astype(F32) + ob)
            n, inv, mid = lnfwd(first, gain, shift)
            g(B_N1, t)[r, :] = n
            g(B_R1, t)[r, :] = jnp.broadcast_to(inv, (CH, 128))
            g(B_MID, t)[pl.ds(mo(me4 + i * CH, CH), CH), :] = mid.astype(BF)

        gather_rows(t, B_MID, S_MY, S_MC, S_MF)

    def slot_rows(t, yy, cc):
        T = ROWS[t]
        return pl.ds(mo((2 * yy + cc) * T, 128), T)

    def gather_rows(t, buf, ny, nc, nf):
        own = g(buf, t).at[slot_rows(t, y, c)]
        send(own, own, ny, t, ypeer)
        send(own, own, nc, t, sib)

    def gather_near(t, buf, nc):
        wait(g(buf, t).at[slot_rows(t, y, 1 - c)], nc, t)

    def gather_forward(t, buf, ny, nf):
        got = g(buf, t).at[slot_rows(t, 1 - y, c)]
        wait(got, ny, t)
        send(got, got, nf, t, sib)

    def gather_far(t, buf, nf):
        wait(g(buf, t).at[slot_rows(t, 1 - y, 1 - c)], nf, t)

    def gather_sent(t, buf, ny, nc, nf):
        own = g(buf, t).at[slot_rows(t, y, c)]
        wait(own, ny, t, 1)
        wait(own, nc, t, 1)
        wait(own, nf, t, 1)

    def up_pair(t, yy):
        T = ROWS[t]
        rows = pl.ds(mo(2 * yy * T, 128), 2 * T)

        @pl.loop(0, 3)
        def _(j):
            cols = pl.ds(mo(j * 256, 128), 256)
            pre = nn(g(B_MID, t)[rows, :], g(B_WU, t)[:, cols]) + g(B_UB, t)[0:1, cols]
            cdf = 0.5 * (1.0 + lax.erf(pre * INV_ROOT_TWO))
            g(B_ACT, t)[rows, cols] = (pre * cdf).astype(BF)
            g(B_SL, t)[rows, cols] = (cdf + pre * jnp.exp(-0.5 * pre * pre) * INV_ROOT_TWO_PI).astype(BF)

    def scatter_partial(t, part, n1a, n1b, n2):
        S1, V1, S2, V2, KP = g(B_S1, t), g(B_V1, t), g(B_S2, t), g(B_V2, t), g(B_KP, t)
        S1[0] = part(slot_rows(t, 1 - y, 1 - c)).astype(BF)
        send(S1.at[0], V1.at[0], n1a, t, sib)
        KP[0] = part(slot_rows(t, 1 - y, c))
        S1[1] = part(slot_rows(t, y, 1 - c)).astype(BF)
        send(S1.at[1], V1.at[1], n1b, t, sib)
        wait(V1.at[0], n1a, t)
        S2[...] = (KP[0] + V1[0].astype(F32)).astype(BF)
        send(S2, V2, n2, t, ypeer)
        KP[1] = part(slot_rows(t, y, c))

    def scatter_finish(t, n1b, n2):
        wait(g(B_V1, t).at[1], n1b, t)
        wait(g(B_V2, t), n2, t)

    def scatter_sent(t, n1a, n1b, n2):
        wait(g(B_S1, t).at[0], n1a, t, 1)
        wait(g(B_S1, t).at[1], n1b, t, 1)
        wait(g(B_S2, t), n2, t, 1)

    def summed(t, r):
        return g(B_KP, t)[1, r, :] + g(B_V1, t)[1, r, :].astype(F32) + g(B_V2, t)[r, :].astype(F32)

    def ffn(t):
        gather_near(t, B_MID, S_MC)
        gather_forward(t, B_MID, S_MY, S_MF)
        wait(g(B_WU, t), S_UP, t)
        up_pair(t, y)
        gather_far(t, B_MID, S_MF)
        up_pair(t, 1 - y)
        wait(g(B_WD, t), S_DN, t)
        scatter_partial(t, lambda rows: nn(g(B_ACT, t)[rows, :], g(B_WD, t)[...]), S_F1A, S_F1B, S_F2)

    def ffn_end(t):
        T = ROWS[t]
        scatter_finish(t, S_F1B, S_F2)
        db, g0, s0, g1, s1 = prow(t, 3), prow(t, 4), prow(t, 6), prow(t, 5), prow(t, 7)

        @pl.loop(0, T // CH)
        def _(i):
            r = pl.ds(mo(i * CH, CH), CH)
            second = g(B_N1, t)[r, :] * g0 + s0 + summed(t, r) + db
            n, inv, res = lnfwd(second, g1, s1)
            g(B_N2, t)[r, :] = n
            g(B_R2, t)[r, :] = jnp.broadcast_to(inv, (CH, 128))
            g(B_Y, t)[r, :] = res.astype(BF)

        local(g(B_Y, t), (o_y0, o_y1)[t], S_FIN, 0, t)

    attention(1)
    attention(0)
    ffn(1)
    ffn(0)
    ffn_end(1)
    ffn_end(0)

    def pick(T, lo, step):
        ri = lax.broadcasted_iota(jnp.int32, (16, T), 0) & 7
        ci = lax.broadcasted_iota(jnp.int32, (16, T), 1)
        return (((ri & 4) == lo) & (ci == (ri & 3) * step)).astype(F32).astype(BF)

    both = nn(pick(128, 0, 32), g(B_Y, 0)[...]) + nn(pick(256, 4, 64), g(B_Y, 1)[...])
    top = lax.broadcasted_iota(jnp.int32, (16, HALF), 0) < 8
    g(B_CM, 0)[:, :HALF] = jnp.where(top, both[:, :HALF], both[:, HALF:]).astype(BF)
    g(B_CM, 0)[:, HALF:] = i_pos[...]
    mine = g(B_GA, 0).at[s * 4 + rep]
    for k in (1, 2, 3):
        send(g(B_CM, 0), mine, S_CZ, 0, ((rep + k) % 4, s))
    g(B_GA, 0)[s * 4 + rep] = g(B_CM, 0)[...]
    wait(g(B_GA, 0).at[pl.ds(0, 3)], S_CZ, 0)
    four = g(B_GA, 0).at[pl.ds(s * 4, 4)]
    for d in NEIGH:
        send(four, four, S_CP, 0, (rep, sh(*peer(d))))

    for t in (0, 1):
        own = g(B_X, t).at[pl.ds(mo(c * ROWS[t], 128), ROWS[t])]
        wait(own, S_X, t, 1)
        wait(g(B_WQ, t).at[pl.ds(0, 672)], S_QKV, t, 1)

        @pl.when(c == y)
        def _():
            wait(g(B_WO, t).at[pl.ds(0, 288)], S_OUT, t, 1)

        @pl.when(c != y)
        def _():
            wait(g(B_WO, t), S_OUT, t, 1)

        wait(g(B_WU, t).at[pl.ds(0, 672)], S_UP, t, 1)
        wait(g(B_WD, t).at[pl.ds(0, HALF)], S_DN, t, 1)
        wait(g(B_OS, t), S_OP, t, 1)
        gather_sent(t, B_MID, S_MY, S_MC, S_MF)
        scatter_sent(t, S_F1A, S_F1B, S_F2)
        wait(g(B_COT, t), S_COT, 0, t)
    wait(g(B_SP, 0).at[pl.ds(0, 7)], S_SMALL, 0, 1)
    wait(g(B_GA, 0).at[pl.ds(0, 3)], S_CZ, 0, 1)
    g(B_BG, 0)[...] = jnp.zeros((32, D), F32)

    wait(g(B_GA, 0).at[pl.ds(0, 28)], S_CP, 0)
    wait(g(B_GA, 0).at[pl.ds(0, 28)], S_CP, 0, 1)

    def pick_all(base):
        ri = lax.broadcasted_iota(jnp.int32, (128, 512), 0)
        ci = lax.broadcasted_iota(jnp.int32, (128, 512), 1)
        blk = ci >> 4
        within = (ci & 15) - base
        row = ((blk & 3) * 8 + (blk >> 2)) * 4 + within
        return ((within >= 0) & (within < 4) & (ri == row)).astype(F32).astype(BF)

    ga = g(B_GA, 0)[...].reshape(512, 512)
    qa_f = nn(pick_all(0), ga)
    qa = qa_f[:, :HALF].astype(BF)
    pa = nn(pick_all(4), ga)[:, :HALF].astype(BF)
    qb = nn(pick_all(8), ga)[:, :HALF].astype(BF)
    pb = nn(pick_all(12), ga)[:, :HALF].astype(BF)
    scale = 2.0 / math.sqrt(D)
    logits = (nt(qa, pa) + nt(qb, pb)) * scale
    masked = jnp.where(i_valid[0:1, :] > 0.0, logits, NEG_FILL)
    mx = jnp.max(masked, axis=1, keepdims=True)
    ex = jnp.exp(masked - mx)
    sm = jnp.sum(ex, axis=1, keepdims=True)
    hit = lax.broadcasted_iota(jnp.int32, (128, 128), 1).astype(F32) == qa_f[:, HALF:]
    ce = mx + jnp.log(sm) - jnp.sum(jnp.where(hit, masked, 0.0), axis=1, keepdims=True)
    o_loss[...] = jnp.broadcast_to(jnp.sum(ce, axis=0, keepdims=True) * (1.0 / 128.0), (8, 128))
    dl = (ex / sm - hit.astype(F32)).astype(BF)
    ri = lax.broadcasted_iota(jnp.int32, (16, 128), 0)
    ci = lax.broadcasted_iota(jnp.int32, (16, 128), 1)
    sel = ((ri < 4) & (ci == ri + 4 * (rep * 8 + s))).astype(F32).astype(BF)
    dlq = nn(sel, dl).astype(BF)
    dlp = nt(sel, dl.T).astype(BF) if False else lax.dot_general(
        sel, dl, (((1,), (1,)), ((), ())), preferred_element_type=F32).astype(BF)
    g(B_CG, 0)[0, :, :HALF] = nn(dlq, pa) * scale
    g(B_CG, 0)[0, :, HALF:] = nn(dlq, pb) * scale
    g(B_CG, 0)[1, :, :HALF] = nn(dlp, qa) * scale
    g(B_CG, 0)[1, :, HALF:] = nn(dlp, qb) * scale

    def fold(a):
        return jnp.sum(a.reshape(CH // 8, 8, D), axis=0)

    def put_bias(t, k, row):
        g(B_BG, 0)[t * 16 + k:t * 16 + k + 1, :] = row

    def ln_back(t, din, nrm, inv, gain):
        gg = din * gain
        m1 = jnp.mean(gg, axis=-1, keepdims=True)
        m2 = jnp.mean(gg * nrm, axis=-1, keepdims=True)
        return inv * (gg - m1 - nrm * m2)

    def out_back(t):
        T = ROWS[t]
        step = 32 if t == 0 else 64
        KP = g(B_KP, t)
        KP[0] = g(B_COT, t)[...].astype(F32)
        for i in range(4):
            KP[0, i * step:i * step + 1, :] = KP[0, i * step:i * step + 1, :] + g(B_CG, 0)[t, i:i + 1, :]
        gain = prow(t, 5)
        me4 = (2 * y + c) * T
        zero = jnp.zeros((8, D), F32)

        def body(i, acc):
            r = pl.ds(mo(i * CH, CH), CH)
            dout = KP[0, r, :]
            nrm = g(B_N2, t)[r, :]
            dsec = ln_back(t, dout, nrm, g(B_R2, t)[r, 0:1], gain)
            low = dsec.astype(BF)
            g(B_N2, t)[r, :] = dsec
            g(B_DF, t)[pl.ds(mo(me4 + i * CH, CH), CH), :] = low
            return (acc[0] + fold(dout * nrm), acc[1] + fold(dout), acc[2] + fold(low.astype(F32)))

        acc = lax.fori_loop(0, T // CH, body, (zero, zero, zero))
        gather_rows(t, B_DF, S_DY, S_DC, S_DF)
        for k, a in zip((5, 7, 3), acc):
            put_bias(t, k, jnp.sum(a, axis=0, keepdims=True))

    def down_pair(t, yy):
        T = ROWS[t]
        rows = pl.ds(mo(2 * yy * T, 128), 2 * T)

        @pl.loop(0, 3)
        def _(j):
            cols = pl.ds(mo(j * 256, 128), 256)
            da = nt(g(B_DF, t)[rows, :], g(B_WD, t)[cols, :])
            g(B_SL, t)[rows, cols] = (da * g(B_SL, t)[rows, cols].astype(F32)).astype(BF)

    def ffn_back(t):
        gather_near(t, B_DF, S_DC)
        gather_forward(t, B_DF, S_DY, S_DF)
        down_pair(t, y)
        gather_far(t, B_DF, S_DF)
        down_pair(t, 1 - y)
        scatter_partial(t, lambda rows: nt(g(B_SL, t)[rows, :], g(B_WU, t)[...]), S_D1A, S_D1B, S_D2)
        ones = jnp.ones((8, 4 * ROWS[t]), F32).astype(BF)
        sums = nn(ones, g(B_SL, t)[...])[0:1, :]
        for xx in (0, 1):
            part = sums[:, xx * HALF:(xx + 1) * HALF]

            @pl.when(y == 0)
            def _():
                g(B_BG, 0)[t * 16 + 8 + xx:t * 16 + 9 + xx, lane_half] = part

            @pl.when(y == 1)
            def _():
                g(B_BG, 0)[t * 16 + 10 + xx:t * 16 + 11 + xx, lane_half] = part

        @pl.loop(0, 3)
        def _(j):
            cols = pl.ds(mo(j * 256, 128), 256)
            g(B_WD, t)[cols, :] = tn(g(B_ACT, t)[:, cols], g(B_DF, t)[...]).astype(BF)

        send(g(B_WD, t).at[pl.ds(mo((1 - x) * HALF, 128), HALF)], g(B_GD, t), S_GD, t, xpeer)

        @pl.loop(0, 3)
        def _(j):
            cols = pl.ds(mo(j * 256, 128), 256)
            g(B_WU, t)[cols, :] = tn(g(B_MID, t)[:, cols], g(B_SL, t)[...]).astype(BF)

        for d in NEIGH:
            p = peer(d)
            send(g(B_WU, t).at[pl.ds(mo(96 * sh(*p), 32), 96)], g(B_GU, t).at[s], S_GU, t, (rep, sh(*p)))
        local(g(B_WU, t).at[rows96], g(B_GU, t).at[s], S_GU, t)

    def mid_back(t):
        T = ROWS[t]
        scatter_finish(t, S_D1B, S_D2)
        gain = prow(t, 4)
        zero = jnp.zeros((8, D), F32)

        def body(i, acc):
            r = pl.ds(mo(i * CH, CH), CH)
            dmid = g(B_N2, t)[r, :] + summed(t, r)
            nrm = g(B_N1, t)[r, :]
            dfirst = ln_back(t, dmid, nrm, g(B_R1, t)[r, 0:1], gain)
            low = dfirst.astype(BF)
            g(B_N1, t)[r, :] = dfirst
            g(B_DA, t)[pl.ds(mo(c * T + i * CH, CH), CH), :] = low
            return (acc[0] + fold(dmid * nrm), acc[1] + fold(dmid), acc[2] + fold(low.astype(F32)))

        acc = lax.fori_loop(0, T // CH, body, (zero, zero, zero))
        own = g(B_DA, t).at[pl.ds(mo(c * T, 128), T)]
        send(own, own, S_DA, t, sib)
        for k, a in zip((4, 6, 2), acc):
            put_bias(t, k, jnp.sum(a, axis=0, keepdims=True))

    def attention_back(t):
        T = ROWS[t]
        QKV, P, ATT, DA, WO, WQ = g(B_QKV, t), g(B_P, t), g(B_ATT, t), g(B_DA, t), g(B_WO, t), g(B_WQ, t)
        wait(DA.at[pl.ds(mo((1 - c) * T, 128), T)], S_DA, t)

        @pl.loop(0, 2)
        def _(grp):
            rows = pl.ds(mo(grp * T, 128), T)

            @pl.loop(0, 3)
            def _(hp):
                lanes = pl.ds(mo(hp * 128, 128), 128)
                dat = nt(DA[rows, :], WO[lanes, :]).astype(BF)
                qs, ks = lanes, pl.ds(mo(HALF + hp * 128, 128), 128)
                vs = pl.ds(mo(2 * HALF + hp * 128, 128), 128)
                q, k, val = QKV[rows, qs], QKV[rows, ks], QKV[rows, vs]
                dq, dk, dv = [], [], []
                for h, msk in ((0, mask_a), (1, mask_b)):
                    p = P[grp * 6 + hp * 2 + h]
                    dp = nt(dat * msk, val)
                    ds = (p * (dp - jnp.sum(dp * p, axis=-1, keepdims=True))).astype(BF)
                    dv.append(tn(p.astype(BF), dat))
                    dq.append(nn(ds, k))
                    dk.append(tn(ds, q))
                root = 1.0 / math.sqrt(HD)
                QKV[rows, qs] = (jnp.where(lane_lo, dq[0], dq[1]) * root).astype(BF)
                QKV[rows, ks] = (jnp.where(lane_lo, dk[0], dk[1]) * root).astype(BF)
                QKV[rows, vs] = jnp.where(lane_lo, dv[0], dv[1]).astype(BF)

        g(B_OS, t)[...] = nt(QKV[pl.ds(mo((1 - c) * T, 128), T), :], WQ[...]).astype(BF)
        send(g(B_OS, t), g(B_OR, t), S_DX, t, sib)
        g(B_KP, t)[0] = nt(QKV[pl.ds(mo(c * T, 128), T), :], WQ[...])

        ones = jnp.ones((8, 2 * T), F32).astype(BF)
        sums = nn(ones, QKV[...])[0:1, :]
        g(B_BG, 0)[t * 16:t * 16 + 1, lane_half] = sums[:, :HALF]
        g(B_BG, 0)[t * 16 + 1:t * 16 + 2, lane_half] = sums[:, 2 * HALF:]

        @pl.loop(0, 3)
        def _(j):
            cols = pl.ds(mo(j * 128, 128), 128)
            WO[cols, :] = tn(ATT[:, cols], DA[...]).astype(BF)

        dst = g(B_GO, t).at[y * 2 + x]
        for dy in (0, 1):
            for dx in (0, 1):
                for dc in (0, 1):
                    pass
        for xx in (0, 1):
            for cc in (0, 1):
                src = WO.at[pl.ds((2 * xx + cc) * 96, 96)]
                dev = sh(c, xx, cc)

                @pl.when(dev == s)
                def _():
                    local(src, dst, S_GO, t)

                @pl.when(dev != s)
                def _():
                    send(src, dst, S_GO, t, (rep, dev))

        @pl.loop(0, 3)
        def _(j):
            cols = pl.ds(mo(j * 256, 128), 256)
            WQ[cols, :] = tn(g(B_X, t)[:, cols], QKV[...]).astype(BF)

        for d in NEIGH:
            p = peer(d)
            send(WQ.at[pl.ds(mo(96 * sh(*p), 32), 96)], g(B_GQ, t).at[s], S_GQ, t, (rep, sh(*p)))
        local(WQ.at[rows96], g(B_GQ, t).at[s], S_GQ, t)

    def input_back(t):
        T = ROWS[t]
        wait(g(B_OR, t), S_DX, t)

        @pl.loop(0, T // CH)
        def _(i):
            r = pl.ds(mo(i * CH, CH), CH)
            g(B_Y, t)[r, :] = (g(B_N1, t)[r, :] + g(B_KP, t)[0, r, :] + g(B_OR, t)[r, :].astype(F32)).astype(BF)

        local(g(B_Y, t), (o_gx0, o_gx1)[t], S_FIN2, 0, t)

    out_back(0)
    out_back(1)
    for t in (0, 1):
        wait(g(B_Y, t), S_FIN, 0, t)
    ffn_back(0)
    ffn_back(1)
    mid_back(0)
    mid_back(1)
    attention_back(0)
    attention_back(1)
    input_back(0)
    input_back(1)

    for d in NEIGH:
        send(g(B_BG, 0), g(B_BGR, 0).at[s], S_BG, 0, (rep, sh(*peer(d))))
    local(g(B_BG, 0), g(B_BGR, 0).at[s], S_BG, 0)

    def sum_dn(t, r0, n):
        return g(B_WD, t)[pl.ds(mo(x * HALF + r0, 32), n), :].astype(F32) + g(B_GD, t)[pl.ds(r0, n), :].astype(F32)

    def each_dn(t, use):
        wait(g(B_GD, t), S_GD, t)
        for r0 in range(0, HALF, 96):
            use(pl.ds(r0, 96), pl.ds(0, D), sum_dn(t, r0, 96))

    def each_up(t, use):
        wait(g(B_GU, t), S_GU, t)
        for yy in (0, 1):
            for cc in (0, 1):
                both = g(B_GU, t)[sh(yy, 0, cc)].astype(F32) + g(B_GU, t)[sh(yy, 1, cc)].astype(F32)
                for xx in (0, 1):
                    j = 4 * yy + 2 * xx + cc
                    use(pl.ds(0, 96), pl.ds(j * HALF, HALF), both[:, xx * HALF:(xx + 1) * HALF])

    def each_out(t, use):
        wait(g(B_GO, t), S_GO, t)
        tot = g(B_GO, t)[0].astype(F32)
        for k in range(1, 4):
            tot = tot + g(B_GO, t)[k].astype(F32)
        use(pl.ds(0, 96), pl.ds(0, D), tot)

    def each_qkv(t, use):
        wait(g(B_GQ, t), S_GQ, t)
        for cc in (0, 1):
            tot = g(B_GQ, t)[cc].astype(F32)
            for k in range(1, 4):
                tot = tot + g(B_GQ, t)[2 * k + cc].astype(F32)
            for part in range(3):
                use(pl.ds(0, 96), pl.ds(part * D + cc * HALF, HALF), tot[:, part * HALF:(part + 1) * HALF])

    def each_small(t, use):
        wait(g(B_BGR, 0), S_BG, 0)
        tot = g(B_BGR, 0)[0]
        for k in range(1, 8):
            tot = tot + g(B_BGR, 0)[k]
        use(pl.ds(0, 32), pl.ds(0, D), tot)

    is_end = (rep == 0) | (rep == 3)
    chunks = []
    for t in (0, 1):
        chunks.append((0, t, each_dn, o_od.at[t]))
        chunks.append((1, t, each_up, o_ou.at[t]))
    for t in (0, 1):
        chunks.append((2, t, each_out, o_oo.at[t]))
        chunks.append((3, t, each_qkv, o_oq.at[t]))
    chunks.append((4, 0, each_small, o_obg))

    def zbuf(kind, which, t):
        if kind == 4:
            return g((B_BGS, B_BGA, B_BGB)[which], 0)
        return g((B_ZSD, B_ZAD, B_ZBD)[which] + kind, t)

    def zsem(hop, kind):
        return (S_ZAS, S_ZBS, S_ZOS)[hop] if kind == 4 else (S_ZAD, S_ZBD, S_ZOD)[hop] + kind

    def stage_a(k):
        kind, t, each, out = chunks[k]
        ZS, ZA, ZB = zbuf(kind, 0, t), zbuf(kind, 1, t), zbuf(kind, 2, t)

        def put(r, cl, val):
            ZS[r, cl] = val.astype(ZS.dtype)

        def put_add(r, cl, val):
            ZS[r, cl] = (val + ZA[r, cl].astype(F32)).astype(ZS.dtype)

        for end, mid in ((0, 1), (3, 2)):
            @pl.when(rep == end)
            def _():
                each(t, put)
                send(ZS, ZA, zsem(0, kind), t, (mid, s))

            @pl.when(rep == mid)
            def _():
                wait(ZA, zsem(0, kind), t)
                each(t, put_add)
                send(ZS, ZB, zsem(1, kind), t, (3 - mid, s))

    def stage_b(k):
        kind, t, each, out = chunks[k]
        ZS, ZB = zbuf(kind, 0, t), zbuf(kind, 2, t)
        for end, mid in ((0, 1), (3, 2)):
            @pl.when(rep == mid)
            def _():
                wait(ZB, zsem(1, kind), t)
                wait(ZB, zsem(1, kind), t, 1)
                n = ZS.shape[0]
                for r0 in range(0, n, 32):
                    r = pl.ds(r0, 32)
                    ZS[r, :] = (ZS[r, :].astype(F32) + ZB[r, :].astype(F32)).astype(ZS.dtype)
                send(ZS, out, zsem(2, kind), t, (end, s))
                local(ZS, out, zsem(2, kind), t)

    for k in range(len(chunks)):
        stage_a(k)
        if k:
            stage_b(k - 1)
    stage_b(len(chunks) - 1)

    for k in range(len(chunks)):
        kind, t, each, out = chunks[k]
        ZS = zbuf(kind, 0, t)
        wait(ZS, zsem(2, kind), t)

        @pl.when(is_end)
        def _():
            wait(ZS, zsem(0, kind), t, 1)

        @pl.when(jnp.logical_not(is_end))
        def _():
            wait(ZS, zsem(2, kind), t, 1)

    for t in (0, 1):
        gather_sent(t, B_DF, S_DY, S_DC, S_DF)
        scatter_sent(t, S_D1A, S_D1B, S_D2)
        wait(g(B_OS, t), S_DA, t, 1)
        wait(g(B_OS, t), S_DX, t, 1)
        wait(g(B_GD, t), S_GD, t, 1)
        wait(g(B_GU, t).at[pl.ds(0, 7)], S_GU, t, 1)

        @pl.when(c == y)
        def _():
            wait(g(B_GO, t).at[pl.ds(0, 3)], S_GO, t, 1)

        @pl.when(c != y)
        def _():
            wait(g(B_GO, t), S_GO, t, 1)

        wait(g(B_GQ, t).at[pl.ds(0, 7)], S_GQ, t, 1)
        wait(g(B_Y, t), S_FIN2, 0, t)
    wait(g(B_BGR, 0).at[pl.ds(0, 7)], S_BG, 0, 1)


def fused_call(x0, x1, cot0, cot1, qkvw, outw, upw, dnw, small, pos, flags, valid):
    hbm = pl.BlockSpec(memory_space=pl.ANY)
    vm = pl.BlockSpec(memory_space=pltpu.VMEM)
    out_shape = [
        jax.ShapeDtypeStruct((8, 128), F32),
        jax.ShapeDtypeStruct((128, D), BF),
        jax.ShapeDtypeStruct((256, D), BF),
        jax.ShapeDtypeStruct((128, D), BF),
        jax.ShapeDtypeStruct((256, D), BF),
        jax.ShapeDtypeStruct((2, 96, 3 * D), BF),
        jax.ShapeDtypeStruct((2, 96, D), BF),
        jax.ShapeDtypeStruct((2, 96, 4 * D), BF),
        jax.ShapeDtypeStruct((2, HALF, D), BF),
        jax.ShapeDtypeStruct((32, D), F32),
    ]
    return pl.pallas_call(
        functools.partial(fused_kernel, None),
        out_shape=out_shape,
        in_specs=[hbm] * 8 + [hbm] + [vm] * 3,
        out_specs=[vm] + [hbm] * 9,
        scratch_shapes=[shape for _, shape in scratch_list()] + [pltpu.SemaphoreType.DMA((N_SEMS,))],
        compiler_params=pltpu.CompilerParams(collective_id=0, has_side_effects=True, vmem_limit_bytes=VMEM_LIMIT),
        cost_estimate=pl.CostEstimate(flops=18 * 10**9, bytes_accessed=40 * 10**6, transcendentals=4 * 10**6),
    )(x0, x1, cot0, cot1, qkvw, outw, upw, dnw, small, pos, flags, valid)


def spread(shard, s, n):
    w = shard.shape[1]
    place = lax.broadcasted_iota(jnp.int32, (1, n * w), 1) // w == s
    return jnp.where(place, jnp.tile(shard, (1, n)), jnp.zeros((), BF))


def local_fast(query_tokens, passage_tokens, query_cot, passage_cot, bucket_counts, positives, qkv_weight, qv_bias,
               out_weight, out_bias, up_weight, up_bias, down_weight, down_bias, norm_gains, norm_shifts):
    rep = lax.axis_index("rep")
    s = lax.axis_index("shard")
    rows = [
        spread(qv_bias, s, 8).reshape(2, 2, D),
        spread(out_bias, s, 8)[:, None],
        spread(down_bias, s, 8)[:, None],
        spread(norm_gains[:, 0], s, 8)[:, None],
        spread(norm_gains[:, 1], s, 8)[:, None],
        spread(norm_shifts[:, 0], s, 8)[:, None],
        spread(norm_shifts[:, 1], s, 8)[:, None],
        spread(up_bias, s, 8).reshape(2, 4, D),
        jnp.zeros((2, 4, D), BF),
    ]
    small = jnp.concatenate(rows, axis=1).reshape(32, D)
    pos = jnp.concatenate([jnp.broadcast_to(positives.astype(BF)[:, None], (4, 128)), jnp.zeros((12, 128), BF)], axis=0)
    chip = lax.dynamic_slice(bucket_counts, ((rep * 8 + s) // 2 * 2,), (2,))
    flags = jnp.broadcast_to((chip > 0).astype(F32)[:, None, None], (2, 8, 128)).reshape(16, 128)
    slot = lax.iota(jnp.int32, 128)
    counts = jnp.broadcast_to(bucket_counts[:, None], (32, 4)).reshape(128)
    valid = jnp.broadcast_to(((counts <= 0) | (slot % 4 == 0)).astype(F32)[None], (8, 128))
    loss, y0, y1, gx0, gx1, oq, oo, ou, od, bg = fused_call(
        query_tokens.reshape(128, D), passage_tokens.reshape(256, D),
        query_cot.reshape(128, D), passage_cot.reshape(256, D),
        qkv_weight, out_weight, up_weight, down_weight, small, pos, flags, valid)
    bg = bg.reshape(2, 16, D)

    def own(a, w):
        return lax.dynamic_slice(a, (0, s * w), (2, w))

    def own_pair(a):
        return lax.dynamic_slice(a, (0, 0, s * 96), (2, 2, 96))

    return (
        loss[0, 0],
        y0.reshape(query_tokens.shape), y1.reshape(passage_tokens.shape),
        gx0.reshape(query_tokens.shape), gx1.reshape(passage_tokens.shape),
        oq.astype(F32),
        own(bg[:, 0:2].reshape(2, 2 * D), 192),
        oo.astype(F32),
        own(bg[:, 2], 96),
        ou.astype(F32),
        own(bg[:, 8:12].reshape(2, 4 * D), HALF),
        od.astype(F32),
        own(bg[:, 3], 96),
        own_pair(bg[:, 4:6]),
        own_pair(bg[:, 6:8]),
    )


def solution(mesh):
    in_specs = (
        P(("rep", "shard"), None, None),
        P(("rep", "shard"), None, None),
        P(("rep", "shard"), None, None),
        P(("rep", "shard"), None, None),
        P(),
        P(("rep", "shard")),
        P(None, "shard", None),
        P(None, "shard"),
        P(None, "shard", None),
        P(None, "shard"),
        P(None, "shard", None),
        P(None, "shard"),
        P(None, "shard", None),
        P(None, "shard"),
        P(None, None, "shard"),
        P(None, None, "shard"),
    )
    out_specs = (
        P(),
        P(("rep", "shard"), None, None),
        P(("rep", "shard"), None, None),
        P(("rep", "shard"), None, None),
        P(("rep", "shard"), None, None),
        P(None, "shard", None),
        P(None, "shard"),
        P(None, "shard", None),
        P(None, "shard"),
        P(None, "shard", None),
        P(None, "shard"),
        P(None, "shard", None),
        P(None, "shard"),
        P(None, None, "shard"),
        P(None, None, "shard"),
    )
    small_mesh = (mesh.shape["rep"], mesh.shape["shard"]) == (4, 8)
    step = local_fast if small_mesh else local
    return jax.shard_map(step, mesh=mesh, in_specs=in_specs, out_specs=out_specs, check_vma=False)
```

```python
import functools
import math

import jax
import jax.numpy as jnp
from jax import lax
from jax.experimental import pallas as pl
from jax.experimental.pallas import tpu as pltpu
from jax.sharding import PartitionSpec as P

HD = 64
SHORT = 64


LN_EPS = 1e-05
NEG_FILL = -1e30
INV_ROOT_TWO = 0.7071067811865476
INV_ROOT_TWO_PI = 0.3989422804014327
VMEM_LIMIT = 66 * 1000 * 1000


def for_sending(array):
    return jax.tree.map(lambda a: a.astype(jnp.bfloat16) if a.dtype == jnp.float32 else a, array)


def pick_tower(stacks, tower_index):
    qkv_w, qv_b, out_w, out_b, up_w, up_b, down_w, down_b, gains, shifts = stacks
    return (
        qkv_w[tower_index],
        qv_b[tower_index],
        out_w[tower_index],
        out_b[tower_index],
        up_w[tower_index],
        up_b[tower_index],
        down_w[tower_index],
        down_b[tower_index],
        gains[tower_index].T,
        shifts[tower_index].T,
    )


def fetch_layer(stacks, tower_index):
    return lax.all_gather(for_sending(pick_tower(stacks, tower_index)), "shard", axis=0, tiled=True)


def fetch_again(stacks, tower_index):
    return lax.all_gather(for_sending(pick_tower(stacks, tower_index)), "shard", axis=0, tiled=True)


def normalize(hidden):
    row_mean = jnp.mean(hidden, axis=-1, keepdims=True)
    centred = hidden - row_mean
    inv_std = lax.rsqrt(jnp.mean(centred * centred, axis=-1, keepdims=True) + LN_EPS)
    return (centred * inv_std, inv_std)


def norm_back(grad_in, normed, inv_std):
    return inv_std * (
        grad_in
        - jnp.mean(grad_in, axis=-1, keepdims=True)
        - normed * jnp.mean(grad_in * normed, axis=-1, keepdims=True)
    )


def block_mask(long_flags, length, short_len):
    row_part = lax.broadcasted_iota(jnp.int32, (length, length), 0) // short_len
    col_part = lax.broadcasted_iota(jnp.int32, (length, length), 1) // short_len
    return long_flags[:, None, None] | (row_part == col_part)[None]


def head_scores(head_query, head_key, attn_mask):
    raw_scores = jnp.einsum(
        "slhd,smhd->shlm", head_query, head_key, preferred_element_type=jnp.float32
    ) * (1.0 / math.sqrt(HD))
    return jnp.where(attn_mask[:, None], raw_scores, NEG_FILL)


def layer_forward(tokens, weights, attn_mask):
    qkv_w, qv_b, out_w, out_b, up_w, up_b, down_w, down_b, gains, shifts = weights
    seq_count, length, model_width = tokens.shape
    head_count = model_width // HD
    token_rows = tokens.reshape(seq_count * length, model_width)
    qv_float = qv_b.astype(jnp.float32)
    qkv_bias = jnp.concatenate(
        [qv_float[:model_width], jnp.zeros((model_width,), jnp.float32), qv_float[model_width:]]
    )
    qkv_low = (jnp.dot(token_rows, qkv_w, preferred_element_type=jnp.float32) + qkv_bias).astype(
        jnp.bfloat16
    )
    head_split = qkv_low.reshape(seq_count, length, 3, head_count, HD)
    scores = head_scores(head_split[:, :, 0], head_split[:, :, 1], attn_mask)
    row_max = jnp.max(scores, axis=-1, keepdims=True)
    exp_scores = jnp.exp(scores - row_max)
    row_total = jnp.sum(exp_scores, axis=-1, keepdims=True)
    attn_probs = (exp_scores / row_total).astype(jnp.bfloat16)
    log_total = row_max + jnp.log(row_total)
    attn_mixed = jnp.einsum(
        "shlm,smhd->slhd", attn_probs, head_split[:, :, 2], preferred_element_type=jnp.float32
    )
    attn_low = attn_mixed.reshape(seq_count * length, model_width).astype(jnp.bfloat16)
    first_sum = (
        token_rows.astype(jnp.float32)
        + jnp.dot(attn_low, out_w, preferred_element_type=jnp.float32)
        + out_b.astype(jnp.float32)
    )
    normed_one, inv_one = normalize(first_sum)
    gain_float = gains.astype(jnp.float32)
    shift_float = shifts.astype(jnp.float32)
    middle = normed_one * gain_float[:, 0] + shift_float[:, 0]
    middle_low = middle.astype(jnp.bfloat16)
    pre_act = jnp.dot(middle_low, up_w, preferred_element_type=jnp.float32) + up_b.astype(
        jnp.float32
    )
    act_low = jax.nn.gelu(pre_act, approximate=False).astype(jnp.bfloat16)
    second = (
        middle
        + jnp.dot(act_low, down_w, preferred_element_type=jnp.float32)
        + down_b.astype(jnp.float32)
    )
    normed_two, inv_two = normalize(second)
    result = normed_two * gain_float[:, 1] + shift_float[:, 1]
    kept = (
        token_rows,
        qkv_low,
        log_total,
        attn_low,
        normed_one,
        inv_one,
        middle_low,
        pre_act,
        act_low,
        normed_two,
        inv_two,
    )
    return (result, kept)


def layer_backward(grad_out, weights, kept, attn_mask):
    qkv_w, qv_b, out_w, out_b, up_w, up_b, down_w, down_b, gains, shifts = weights
    (
        token_rows,
        qkv_low,
        log_total,
        attn_low,
        normed_one,
        inv_one,
        middle_low,
        pre_act,
        act_low,
        normed_two,
        inv_two,
    ) = kept
    seq_count = attn_mask.shape[0]
    model_width = token_rows.shape[1]
    length = token_rows.shape[0] // seq_count
    head_count = model_width // HD
    gain_float = gains.astype(jnp.float32)
    gain_two = jnp.sum(grad_out * normed_two, axis=0)
    shift_two = jnp.sum(grad_out, axis=0)
    d_second = norm_back(grad_out * gain_float[:, 1], normed_two, inv_two)
    d_ffn = d_second.astype(jnp.bfloat16)
    d_down_w = jnp.dot(act_low.T, d_ffn, preferred_element_type=jnp.float32)
    d_down_b = jnp.sum(d_ffn.astype(jnp.float32), axis=0)
    d_act = jnp.dot(d_ffn, down_w.T, preferred_element_type=jnp.float32)
    gelu_slope = (
        0.5 * (1.0 + lax.erf(pre_act * INV_ROOT_TWO))
        + pre_act * jnp.exp(-0.5 * pre_act * pre_act) * INV_ROOT_TWO_PI
    )
    d_pre = (d_act * gelu_slope).astype(jnp.bfloat16)
    d_up_w = jnp.dot(middle_low.T, d_pre, preferred_element_type=jnp.float32)
    d_up_b = jnp.sum(d_pre.astype(jnp.float32), axis=0)
    d_middle = d_second + jnp.dot(d_pre, up_w.T, preferred_element_type=jnp.float32)
    gain_one = jnp.sum(d_middle * normed_one, axis=0)
    shift_one = jnp.sum(d_middle, axis=0)
    d_first = norm_back(d_middle * gain_float[:, 0], normed_one, inv_one)
    d_attn_out = d_first.astype(jnp.bfloat16)
    d_out_w = jnp.dot(attn_low.T, d_attn_out, preferred_element_type=jnp.float32)
    d_out_b = jnp.sum(d_attn_out.astype(jnp.float32), axis=0)
    d_mixed = (
        jnp.dot(d_attn_out, out_w.T, preferred_element_type=jnp.float32)
        .astype(jnp.bfloat16)
        .reshape(seq_count, length, head_count, HD)
    )
    head_split = qkv_low.reshape(seq_count, length, 3, head_count, HD)
    head_query = head_split[:, :, 0]
    head_key = head_split[:, :, 1]
    head_value = head_split[:, :, 2]
    attn_probs = jnp.exp(head_scores(head_query, head_key, attn_mask) - log_total)
    d_probs = jnp.einsum("slhd,smhd->shlm", d_mixed, head_value, preferred_element_type=jnp.float32)
    d_value = jnp.einsum(
        "shlm,slhd->smhd",
        attn_probs.astype(jnp.bfloat16),
        d_mixed,
        preferred_element_type=jnp.float32,
    )
    d_scores = (
        attn_probs * (d_probs - jnp.sum(d_probs * attn_probs, axis=-1, keepdims=True))
    ).astype(jnp.bfloat16)
    d_query = jnp.einsum(
        "shlm,smhd->slhd", d_scores, head_key, preferred_element_type=jnp.float32
    ) * (1.0 / math.sqrt(HD))
    d_key = jnp.einsum(
        "shlm,slhd->smhd", d_scores, head_query, preferred_element_type=jnp.float32
    ) * (1.0 / math.sqrt(HD))
    d_qkv = (
        jnp.stack([d_query, d_key, d_value], axis=2)
        .reshape(seq_count * length, 3 * model_width)
        .astype(jnp.bfloat16)
    )
    d_qkv_w = jnp.dot(token_rows.T, d_qkv, preferred_element_type=jnp.float32)
    column_sums = jnp.sum(d_qkv.astype(jnp.float32), axis=0)
    d_qv_b = jnp.concatenate([column_sums[:model_width], column_sums[2 * model_width :]])
    d_tokens = d_first + jnp.dot(d_qkv, qkv_w.T, preferred_element_type=jnp.float32)
    layer_grads = (
        d_qkv_w,
        d_qv_b,
        d_out_w,
        d_out_b,
        d_up_w,
        d_up_b,
        d_down_w,
        d_down_b,
        jnp.stack([gain_one, gain_two], axis=1),
        jnp.stack([shift_one, shift_two], axis=1),
    )
    return (d_tokens, layer_grads)


def reduce_layer(layer_grads):
    owned_grads = (
        lax.psum_scatter(layer_grads[0], "shard", scatter_dimension=0, tiled=True),
        lax.psum_scatter(layer_grads[1], "shard", scatter_dimension=0, tiled=True),
        lax.psum_scatter(layer_grads[2], "shard", scatter_dimension=0, tiled=True),
        lax.psum_scatter(layer_grads[3], "shard", scatter_dimension=0, tiled=True),
        lax.psum_scatter(layer_grads[4], "shard", scatter_dimension=0, tiled=True),
        lax.psum_scatter(layer_grads[5], "shard", scatter_dimension=0, tiled=True),
        lax.psum_scatter(layer_grads[6], "shard", scatter_dimension=0, tiled=True),
        lax.psum_scatter(layer_grads[7], "shard", scatter_dimension=0, tiled=True),
        lax.psum_scatter(layer_grads[8], "shard", scatter_dimension=0, tiled=True),
        lax.psum_scatter(layer_grads[9], "shard", scatter_dimension=0, tiled=True),
    )
    quarter = (
        lax.psum_scatter(
            owned_grads[0].astype(jnp.bfloat16), "rep", scatter_dimension=0, tiled=True
        ).astype(jnp.float32),
        lax.psum_scatter(
            owned_grads[1].astype(jnp.bfloat16), "rep", scatter_dimension=0, tiled=True
        ).astype(jnp.float32),
        lax.psum_scatter(
            owned_grads[2].astype(jnp.bfloat16), "rep", scatter_dimension=0, tiled=True
        ).astype(jnp.float32),
        lax.psum_scatter(
            owned_grads[3].astype(jnp.bfloat16), "rep", scatter_dimension=0, tiled=True
        ).astype(jnp.float32),
        lax.psum_scatter(
            owned_grads[4].astype(jnp.bfloat16), "rep", scatter_dimension=0, tiled=True
        ).astype(jnp.float32),
        lax.psum_scatter(
            owned_grads[5].astype(jnp.bfloat16), "rep", scatter_dimension=0, tiled=True
        ).astype(jnp.float32),
        lax.psum_scatter(
            owned_grads[6].astype(jnp.bfloat16), "rep", scatter_dimension=0, tiled=True
        ).astype(jnp.float32),
        lax.psum_scatter(
            owned_grads[7].astype(jnp.bfloat16), "rep", scatter_dimension=0, tiled=True
        ).astype(jnp.float32),
        lax.psum_scatter(
            owned_grads[8].astype(jnp.bfloat16), "rep", scatter_dimension=0, tiled=True
        ).astype(jnp.float32),
        lax.psum_scatter(
            owned_grads[9].astype(jnp.bfloat16), "rep", scatter_dimension=0, tiled=True
        ).astype(jnp.float32),
    )
    return (
        lax.all_gather(quarter[0].astype(jnp.bfloat16), "rep", axis=0, tiled=True).astype(
            jnp.float32
        ),
        lax.all_gather(quarter[1].astype(jnp.bfloat16), "rep", axis=0, tiled=True).astype(
            jnp.float32
        ),
        lax.all_gather(quarter[2].astype(jnp.bfloat16), "rep", axis=0, tiled=True).astype(
            jnp.float32
        ),
        lax.all_gather(quarter[3].astype(jnp.bfloat16), "rep", axis=0, tiled=True).astype(
            jnp.float32
        ),
        lax.all_gather(quarter[4].astype(jnp.bfloat16), "rep", axis=0, tiled=True).astype(
            jnp.float32
        ),
        lax.all_gather(quarter[5].astype(jnp.bfloat16), "rep", axis=0, tiled=True).astype(
            jnp.float32
        ),
        lax.all_gather(quarter[6].astype(jnp.bfloat16), "rep", axis=0, tiled=True).astype(
            jnp.float32
        ),
        lax.all_gather(quarter[7].astype(jnp.bfloat16), "rep", axis=0, tiled=True).astype(
            jnp.float32
        ),
        lax.all_gather(quarter[8].astype(jnp.bfloat16), "rep", axis=0, tiled=True).astype(
            jnp.float32
        ),
        lax.all_gather(quarter[9].astype(jnp.bfloat16), "rep", axis=0, tiled=True).astype(
            jnp.float32
        ),
    )


def local(
    query_tokens,
    passage_tokens,
    query_cot,
    passage_cot,
    bucket_counts,
    positives,
    qkv_weight,
    qv_bias,
    out_weight,
    out_bias,
    up_weight,
    up_bias,
    down_weight,
    down_bias,
    norm_gains,
    norm_shifts,
):
    stacks = (
        qkv_weight,
        qv_bias,
        out_weight,
        out_bias,
        up_weight,
        up_bias,
        down_weight,
        down_bias,
        norm_gains,
        norm_shifts,
    )
    blocks, long_len, model_width = passage_tokens.shape
    query_count, query_len, unused_width = query_tokens.shape
    subs_count = long_len // SHORT
    slot_count = blocks * subs_count
    my_index = lax.axis_index(("rep", "shard"))
    own_count = lax.dynamic_index_in_dim(bucket_counts, my_index, 0, keepdims=False)
    passage_mask = block_mask(lax.iota(jnp.int32, blocks) < own_count, long_len, SHORT)
    query_mask = block_mask(jnp.ones((query_count,), dtype=bool), query_len, query_len)
    query_weights = fetch_layer(stacks, 0)
    query_result, query_kept = layer_forward(query_tokens, query_weights, query_mask)
    passage_weights = fetch_layer(stacks, 1)
    passage_result, passage_kept = layer_forward(passage_tokens, passage_weights, passage_mask)
    query_cls = query_result.reshape(query_count, query_len, model_width)[:, 0].astype(jnp.bfloat16)
    passage_cls = (
        passage_result.reshape(blocks, subs_count, SHORT, model_width)[:, :, 0]
        .reshape(slot_count, model_width)
        .astype(jnp.bfloat16)
    )
    every_cls = lax.all_gather(passage_cls, ("rep", "shard"), axis=0, tiled=True)
    cand_count = every_cls.shape[0]
    device_count = bucket_counts.shape[0]
    score_scale = 2.0 / math.sqrt(model_width)
    logits = jnp.dot(query_cls, every_cls.T, preferred_element_type=jnp.float32) * score_scale
    slot_ids = lax.iota(jnp.int32, cand_count)
    owner_index = slot_ids // slot_count
    owner_counts = jnp.sum(
        jnp.where(
            owner_index[:, None] == lax.iota(jnp.int32, device_count)[None], bucket_counts[None], 0
        ),
        axis=1,
    )
    slot_valid = (slot_ids % slot_count // subs_count >= owner_counts) | (
        slot_ids % subs_count == 0
    )
    masked = jnp.where(slot_valid[None], logits, NEG_FILL)
    row_max = jnp.max(masked, axis=1, keepdims=True)
    exp_scores = jnp.exp(masked - row_max)
    row_total = jnp.sum(exp_scores, axis=1, keepdims=True)
    log_total = row_max[:, 0] + jnp.log(row_total[:, 0])
    hit_mask = slot_ids[None] == positives[:, None]
    picked = jnp.sum(jnp.where(hit_mask, masked, 0.0), axis=1)
    local_loss = jnp.sum(log_total - picked)
    d_logits = (exp_scores / row_total - hit_mask.astype(jnp.float32)).astype(jnp.bfloat16)
    d_query_cls = jnp.dot(d_logits, every_cls, preferred_element_type=jnp.float32) * score_scale
    d_cands = (
        lax.dot_general(
            d_logits, query_cls, (((0,), (0,)), ((), ())), preferred_element_type=jnp.float32
        )
        * score_scale
    )
    d_passage_cls = lax.psum_scatter(d_cands, ("rep", "shard"), scatter_dimension=0, tiled=True)
    loss_sum = lax.psum(local_loss, ("rep", "shard"))
    loss = loss_sum / (query_count * lax.axis_size(("rep", "shard")))
    query_dout = (
        query_cot.astype(jnp.float32)
        .at[:, 0]
        .add(d_query_cls)
        .reshape(query_count * query_len, model_width)
    )
    passage_dout = (
        passage_cot.astype(jnp.float32)
        .reshape(blocks, subs_count, SHORT, model_width)
        .at[:, :, 0]
        .add(d_passage_cls.reshape(blocks, subs_count, model_width))
        .reshape(blocks * long_len, model_width)
    )
    passage_back = fetch_again(stacks, 1)
    passage_dx, passage_grads = layer_backward(
        passage_dout, passage_back, passage_kept, passage_mask
    )
    passage_owned = reduce_layer(passage_grads)
    query_back = fetch_again(stacks, 0)
    query_dx, query_grads = layer_backward(query_dout, query_back, query_kept, query_mask)
    query_owned = reduce_layer(query_grads)
    stacked = [
        jnp.stack([first_g, second_g]) for first_g, second_g in zip(query_owned, passage_owned)
    ]
    gains_grad = jnp.swapaxes(stacked[8], 1, 2)
    shifts_grad = jnp.swapaxes(stacked[9], 1, 2)
    return (
        loss,
        query_result.reshape(query_count, query_len, model_width).astype(jnp.bfloat16),
        passage_result.reshape(blocks, long_len, model_width).astype(jnp.bfloat16),
        query_dx.reshape(query_count, query_len, model_width).astype(jnp.bfloat16),
        passage_dx.reshape(blocks, long_len, model_width).astype(jnp.bfloat16),
        stacked[0],
        stacked[1],
        stacked[2],
        stacked[3],
        stacked[4],
        stacked[5],
        stacked[6],
        stacked[7],
        gains_grad,
        shifts_grad,
    )


BF = jnp.bfloat16
F32 = jnp.float32
MESH = pl.DeviceIdType.MESH
ROWS = (128, 256)
D = 768
HALF = 384
FFN = 768
NEIGH = tuple((dy, dx, dc) for dy in (0, 1) for dx in (0, 1) for dc in (0, 1) if dy + dx + dc)

(S_X, S_QKV, S_QKVC, S_QKVZ, S_OUT, S_OUTC, S_OUTZ, S_UP, S_UPC, S_UPZ,
 S_DN, S_OP, S_MY, S_MC, S_MF, S_F1A, S_F1B, S_F2, S_DY, S_DC, S_DF, S_D1A, S_D1B, S_D2,
 S_DA, S_DX, S_GD, S_GU, S_GO, S_GQ, S_SMALL, S_CZ, S_CP, S_BG, S_COT, S_FIN, S_FIN2, S_Z) = range(38)
N_UNITS = 17
N_SEMS = 4 * S_Z + 6 * N_UNITS + 2


def nn(a, b):
    return jnp.dot(a, b, preferred_element_type=F32)


def nt(a, b):
    return lax.dot_general(a, b, (((1,), (1,)), ((), ())), preferred_element_type=F32)


def tn(a, b):
    return lax.dot_general(a, b, (((0,), (0,)), ((), ())), preferred_element_type=F32)


def flip(v, d):
    return 1 - v if d else v


def mo(v, m):
    return pl.multiple_of(v, m)


(B_X, B_COT, B_WQ, B_WO, B_WU, B_WD, B_QB, B_UB, B_QKV, B_P,
 B_ATT, B_OS, B_OR, B_N1, B_N2, B_R1, B_R2, B_MID, B_ACT, B_SL,
 B_S1, B_V1, B_S2, B_V2, B_KP, B_Y, B_DF, B_DA, B_GD, B_GU,
 B_GO, B_GQ, B_ZSD, B_ZSU, B_ZSO, B_ZSQ, B_ZAD, B_ZAU, B_ZAO, B_ZAQ,
 B_ZBD, B_ZBU, B_ZBO, B_ZBQ, B_T96, B_T192, B_LP, B_SP, B_PV, B_BG, B_BGS, B_BGR, B_BGA,
 B_BGB, B_CM, B_GA, B_CG) = range(57)


def scratch_list():
    s = []

    def add(name, t, shape, dtype):
        s.append(((name, t), pltpu.VMEM(shape, dtype)))

    for t, T in enumerate(ROWS):
        add(B_X, t, (2 * T, D), BF)
        add(B_COT, t, (T, D), BF)
        add(B_WQ, t, (D, 3 * HALF), BF)
        add(B_WO, t, (HALF, D), BF)
        add(B_WU, t, (D, FFN), BF)
        add(B_WD, t, (FFN, D), BF)
        add(B_QB, t, (8, 3 * HALF), F32)
        add(B_UB, t, (8, FFN), F32)
        add(B_QKV, t, (2 * T, 3 * HALF), BF)
        add(B_P, t, (12, T, T), F32)
        add(B_ATT, t, (2 * T, HALF), BF)
        add(B_OS, t, (T, D), BF)
        add(B_OR, t, (T, D), BF)
        add(B_N1, t, (T, D), F32)
        add(B_N2, t, (T, D), F32)
        add(B_R1, t, (T, 128), F32)
        add(B_R2, t, (T, 128), F32)
        add(B_MID, t, (4 * T, D), BF)
        add(B_ACT, t, (4 * T, FFN), BF)
        add(B_SL, t, (4 * T, FFN), BF)
        add(B_S1, t, (2, T, D), BF)
        add(B_V1, t, (2, T, D), BF)
        add(B_S2, t, (T, D), BF)
        add(B_V2, t, (T, D), BF)
        add(B_KP, t, (2, T, D), F32)
        add(B_Y, t, (T, D), BF)
        add(B_DF, t, (4 * T, D), BF)
        add(B_DA, t, (2 * T, D), BF)
        add(B_GD, t, (HALF, D), BF)
        add(B_GU, t, (8, 96, FFN), BF)
        add(B_GO, t, (4, 96, D), BF)
        add(B_GQ, t, (8, 96, 3 * HALF), BF)
        for first in (B_ZSD, B_ZAD, B_ZBD):
            add(first, t, (HALF, D), BF)
            add(first + 1, t, (96, 4 * D), BF)
            add(first + 2, t, (96, D), BF)
            add(first + 3, t, (96, 3 * D), BF)
    add(B_T96, 0, (16, 128), F32)
    add(B_T192, 0, (8, 256), F32)
    add(B_LP, 0, (32, D), F32)
    add(B_SP, 0, (8, 32, D), BF)
    add(B_PV, 0, (32, D), F32)
    add(B_BG, 0, (32, D), F32)
    add(B_BGS, 0, (32, D), F32)
    add(B_BGR, 0, (8, 32, D), F32)
    add(B_BGA, 0, (32, D), F32)
    add(B_BGB, 0, (32, D), F32)
    add(B_CM, 0, (16, 512), BF)
    add(B_GA, 0, (32, 16, 512), BF)
    add(B_CG, 0, (2, 16, D), F32)
    return s


def fused_kernel(*refs):
    (i_x0, i_x1, i_cot0, i_cot1, i_qkvw, i_outw, i_upw, i_dnw, i_qvb, i_ob, i_ub, i_db, i_gn, i_sf, i_cnt, i_pos,
     o_loss, o_y0, o_y1, o_gx0, o_gx1, o_oq, o_oo, o_ou, o_od, o_obg) = refs[:26]
    held = {key: ref for (key, _), ref in zip(scratch_list(), refs[26:])}
    sems = refs[-1]

    def g(name, t):
        return held[(name, t)]

    rep = lax.axis_index("rep")
    s = lax.axis_index("shard")
    y = s // 4
    x = (s // 2) % 2
    c = s % 2
    x_in = (i_x0, i_x1)
    cot_in = (i_cot0, i_cot1)

    def sem(name, t, side):
        return sems.at[4 * name + 2 * t + side]

    def sh(yy, xx, cc):
        return yy * 4 + xx * 2 + cc

    def send(src, dst, name, t, dev):
        pltpu.make_async_remote_copy(src, dst, send_sem=sem(name, t, 1), recv_sem=sem(name, t, 0),
                                     device_id=dev, device_id_type=MESH).start()

    def local(src, dst, name, t, side=0):
        pltpu.make_async_copy(src, dst, sem(name, t, side)).start()

    def wait(ref, name, t, side=0):
        pltpu.make_async_copy(ref, ref, sem(name, t, side)).wait()

    def peer(d):
        return flip(y, d[0]), flip(x, d[1]), flip(c, d[2])

    sib = (rep, sh(y, x, 1 - c))
    ypeer = (rep, sh(1 - y, x, c))
    xpeer = (rep, sh(y, 1 - x, c))

    bar = pltpu.get_barrier_semaphore()
    for d in NEIGH:
        pl.semaphore_signal(bar, 1, device_id=(rep, sh(*peer(d))), device_id_type=MESH)
    for k in (1, 2, 3):
        pl.semaphore_signal(bar, 1, device_id=((rep + k) % 4, s), device_id_type=MESH)

    T96, T192, LP, SP, PV = (g(b, 0) for b in (B_T96, B_T192, B_LP, B_SP, B_PV))
    T96[...] = jnp.zeros((16, 128), F32)
    T192[...] = jnp.zeros((8, 256), F32)
    LP[...] = jnp.zeros((32, D), F32)
    T96[0:2, 0:96] = i_ob[...].astype(F32)
    T96[2:4, 0:96] = i_db[...].astype(F32)
    for t in (0, 1):
        for k in (0, 1):
            T96[4 + 2 * t + k:5 + 2 * t + k, 0:96] = i_gn[t, k:k + 1, :].astype(F32)
            T96[8 + 2 * t + k:9 + 2 * t + k, 0:96] = i_sf[t, k:k + 1, :].astype(F32)
    T192[0:2, 0:192] = i_qvb[...].astype(F32)

    def place(n, w, at):
        i = lax.broadcasted_iota(jnp.int32, (n, D), 0)
        j = lax.broadcasted_iota(jnp.int32, (n, D), 1)
        return ((j == i + at) & (i < w)).astype(F32).astype(BF)

    LP[0:16, :] = nn(T96[...].astype(BF), place(128, 96, s * 96))
    qv = nn(T192[...].astype(BF), place(256, 192, (s % 4) * 192))[0:2, :]
    in_q = jnp.full((2, D), y) == 0
    LP[12:14, :] = jnp.where(in_q, qv, 0.0)
    LP[14:16, :] = jnp.where(in_q, 0.0, qv)
    for t in (0, 1):
        LP[pl.ds(16 + 4 * t + s // 2, 1), pl.ds(mo((s % 2) * HALF, 128), HALF)] = i_ub[t:t + 1, :].astype(F32)
    SP[s] = LP[...].astype(BF)

    pl.semaphore_wait(bar, 10)

    half = rep % 2
    zpair = (rep + 1 - 2 * half, s)
    for d in NEIGH:
        send(SP.at[s], SP.at[s], S_SMALL, 0, (rep, sh(*peer(d))))
    rows96 = pl.ds(mo(s * 96, 32), 96)
    half48 = pl.ds(mo(half * 48, 16), 48)

    def send_x(t):
        T = ROWS[t]
        own = g(B_X, t).at[pl.ds(mo(c * T, 128), T)]
        send(x_in[t], own, S_X, t, sib)
        local(x_in[t], own, S_X, t)

    def rows48(owner):
        return pl.ds(mo(owner * 96 + half * 48, 16), 48)

    def send_cols(t, src, dst, pieces, far, near):
        for d in NEIGH + ((0, 0, 0),):
            p = peer(d)
            for k, at in enumerate(pieces(p)):
                cols, to = pl.ds(mo(at, 128), HALF), pl.ds(k * HALF, HALF)
                if d[0] + d[1]:
                    send(src.at[t, half48, cols], dst.at[rows48(s), to], far, t, (rep, sh(*p)))
                elif d[2]:
                    send(src.at[t, :, cols], dst.at[rows96, to], near, t, sib)
                else:
                    local(src.at[t, :, cols], dst.at[rows96, to], near, t)

    def send_qkv(t):
        send_cols(t, i_qkvw, g(B_WQ, t), lambda p: [part * D + p[2] * HALF for part in range(3)], S_QKV, S_QKVC)

    def send_up(t):
        send_cols(t, i_upw, g(B_WU, t), lambda p: [HALF * (4 * p[0] + 2 * xx + p[2]) for xx in (0, 1)], S_UP, S_UPC)

    def forward_cols(t, buf, far, pair):
        wait(buf.at[pl.ds(0, 288)], far, t)
        for d in NEIGH:
            if d[0] + d[1]:
                piece = buf.at[rows48(sh(*peer(d)))]
                send(piece, piece, pair, t, zpair)

    def whole_cols(t, buf, near, pair):
        wait(buf.at[pl.ds(0, 192)], near, t)
        wait(buf.at[pl.ds(0, 288)], pair, t)

    def send_out(t):
        WO = g(B_WO, t)
        for dy in (0, 1):
            for dx in (0, 1):
                dev = (rep, sh(flip(y, dy), flip(x, dx), y))
                if dy + dx:
                    send(i_outw.at[t, half48], WO.at[rows48(x * 2 + c)], S_OUT, t, dev)
                else:
                    dst = WO.at[pl.ds(mo((x * 2 + c) * 96, 32), 96)]

                    @pl.when(c == y)
                    def _():
                        local(i_outw.at[t], dst, S_OUTC, t)

                    @pl.when(c != y)
                    def _():
                        send(i_outw.at[t], dst, S_OUTC, t, dev)

    def forward_out(t):
        WO = g(B_WO, t)

        def go(xs):
            for xx in xs:
                for cc in (0, 1):
                    piece = WO.at[rows48(xx * 2 + cc)]
                    send(piece, piece, S_OUTZ, t, zpair)

        @pl.when(c == y)
        def _():
            wait(WO.at[pl.ds(0, 96)], S_OUT, t)
            go((1 - x,))

        @pl.when(c != y)
        def _():
            wait(WO.at[pl.ds(0, 192)], S_OUT, t)
            go((0, 1))

    def whole_out(t):
        WO = g(B_WO, t)

        @pl.when(c == y)
        def _():
            wait(WO.at[pl.ds(0, 192)], S_OUTC, t)
            wait(WO.at[pl.ds(0, 96)], S_OUTZ, t)

        @pl.when(c != y)
        def _():
            wait(WO.at[pl.ds(0, 192)], S_OUTZ, t)

    def send_dn(t):
        dst = g(B_WD, t).at[pl.ds(mo(x * HALF, 128), HALF)]
        send(i_dnw.at[t], dst, S_DN, t, xpeer)
        local(i_dnw.at[t], dst, S_DN, t)

    for t in (1, 0):
        send_x(t)
        send_qkv(t)
        send_out(t)
    send_up(1)
    send_dn(1)
    for t in (0, 1):
        local(cot_in[t], g(B_COT, t), S_COT, 0, t)

    wait(SP.at[pl.ds(0, 7)], S_SMALL, 0)
    tot = SP[0].astype(F32)
    for k in range(1, 8):
        tot = tot + SP[k].astype(F32)
    PV[...] = tot
    R_OB, R_DB, R_GN, R_SF, R_QB, R_VB, R_UB = 0, 2, 4, 8, 12, 14, 16

    def prow(k):
        return PV[k:k + 1, :]

    lane_half = pl.ds(mo(c * HALF, 128), HALF)
    for t in (0, 1):
        g(B_QB, t)[...] = jnp.zeros((8, 3 * HALF), F32)
        g(B_QB, t)[0:1, 0:HALF] = PV[R_QB + t:R_QB + t + 1, lane_half]
        g(B_QB, t)[0:1, 2 * HALF:] = PV[R_VB + t:R_VB + t + 1, lane_half]
        for xx in (0, 1):
            at = R_UB + 4 * t + xx
            lo, hi = PV[at:at + 1, lane_half], PV[at + 2:at + 3, lane_half]
            g(B_UB, t)[0:1, xx * HALF:(xx + 1) * HALF] = jnp.where(jnp.full((1, HALF), y) == 0, lo, hi)

    def same_part(t, grp):
        T = ROWS[t]
        shift = 5 if t == 0 else 6
        ri = lax.broadcasted_iota(jnp.int32, (T, T), 0) >> shift
        ci = lax.broadcasted_iota(jnp.int32, (T, T), 1) >> shift
        m = ri == ci
        if t == 1:
            m = m | (jnp.full((T, T), i_cnt[rep * 8 + (s // 2) * 2 + grp]) > 0)
        return m

    lane_lo = lax.broadcasted_iota(jnp.int32, (1, 128), 1) < 64
    mask_a = lane_lo.astype(F32).astype(BF)
    mask_b = (1.0 - lane_lo.astype(F32)).astype(BF)

    def lnfwd(first, gain, shift):
        mean = jnp.mean(first, axis=-1, keepdims=True)
        cen = first - mean
        inv = lax.rsqrt(jnp.mean(cen * cen, axis=-1, keepdims=True) + LN_EPS)
        n = cen * inv
        return n, inv, n * gain + shift

    CH = 64

    def attention(t):
        T = ROWS[t]
        X, WQ, QKV, P, ATT = g(B_X, t), g(B_WQ, t), g(B_QKV, t), g(B_P, t), g(B_ATT, t)
        wait(X, S_X, t)
        whole_cols(t, WQ, S_QKVC, S_QKVZ)

        @pl.loop(0, 3)
        def _(j):
            cols = pl.ds(mo(j * HALF, 128), HALF)
            QKV[:, cols] = (nn(X[...], WQ[:, cols]) + g(B_QB, t)[0:1, cols]).astype(BF)

        @pl.loop(0, 2)
        def _(grp):
            rows = pl.ds(mo(grp * T, 128), T)
            m = same_part(t, grp)

            @pl.loop(0, 3)
            def _(hp):
                q = QKV[rows, pl.ds(mo(hp * 128, 128), 128)]
                k = QKV[rows, pl.ds(mo(HALF + hp * 128, 128), 128)]
                val = QKV[rows, pl.ds(mo(2 * HALF + hp * 128, 128), 128)]
                outs = []
                for h, msk in ((0, mask_a), (1, mask_b)):
                    sc = jnp.where(m, nt(q * msk, k) * (1.0 / math.sqrt(HD)), NEG_FILL)
                    mx = jnp.max(sc, axis=-1, keepdims=True)
                    e = jnp.exp(sc - mx)
                    p = e * (1.0 / jnp.sum(e, axis=-1, keepdims=True))
                    P[grp * 6 + hp * 2 + h] = p
                    outs.append(nn(p.astype(BF), val))
                ATT[rows, pl.ds(mo(hp * 128, 128), 128)] = jnp.where(lane_lo, outs[0], outs[1]).astype(BF)

        whole_out(t)
        g(B_OS, t)[...] = nn(ATT[pl.ds(mo((1 - c) * T, 128), T), :], g(B_WO, t)[...]).astype(BF)
        send(g(B_OS, t), g(B_OR, t), S_OP, t, sib)
        g(B_KP, t)[0] = nn(ATT[pl.ds(mo(c * T, 128), T), :], g(B_WO, t)[...])
        wait(g(B_OR, t), S_OP, t)
        me4 = (2 * y + c) * T
        ob, gain, shift = prow(R_OB + t), prow(R_GN + 2 * t), prow(R_SF + 2 * t)

        @pl.loop(0, T // CH)
        def _(i):
            r = pl.ds(mo(i * CH, CH), CH)
            first = (X[pl.ds(mo(c * T + i * CH, CH), CH), :].astype(F32) + g(B_KP, t)[0, r, :]
                     + g(B_OR, t)[r, :].astype(F32) + ob)
            n, inv, mid = lnfwd(first, gain, shift)
            g(B_N1, t)[r, :] = n
            g(B_R1, t)[r, :] = jnp.broadcast_to(inv, (CH, 128))
            g(B_MID, t)[pl.ds(mo(me4 + i * CH, CH), CH), :] = mid.astype(BF)

        gather_rows(t, B_MID, S_MY, S_MC, S_MF)

    def slot_rows(t, yy, cc):
        T = ROWS[t]
        return pl.ds(mo((2 * yy + cc) * T, 128), T)

    def gather_rows(t, buf, ny, nc, nf):
        own = g(buf, t).at[slot_rows(t, y, c)]
        send(own, own, ny, t, ypeer)
        send(own, own, nc, t, sib)

    def gather_near(t, buf, nc):
        wait(g(buf, t).at[slot_rows(t, y, 1 - c)], nc, t)

    def gather_forward(t, buf, ny, nf):
        got = g(buf, t).at[slot_rows(t, 1 - y, c)]
        wait(got, ny, t)
        send(got, got, nf, t, sib)

    def gather_far(t, buf, nf):
        wait(g(buf, t).at[slot_rows(t, 1 - y, 1 - c)], nf, t)

    def gather_sent(t, buf, ny, nc, nf):
        own = g(buf, t).at[slot_rows(t, y, c)]
        wait(own, ny, t, 1)
        wait(own, nc, t, 1)
        wait(own, nf, t, 1)

    def up_pair(t, yy):
        T = ROWS[t]
        rows = pl.ds(mo(2 * yy * T, 128), 2 * T)

        @pl.loop(0, 3)
        def _(j):
            cols = pl.ds(mo(j * 256, 128), 256)
            pre = nn(g(B_MID, t)[rows, :], g(B_WU, t)[:, cols]) + g(B_UB, t)[0:1, cols]
            cdf = 0.5 * (1.0 + lax.erf(pre * INV_ROOT_TWO))
            g(B_ACT, t)[rows, cols] = (pre * cdf).astype(BF)
            g(B_SL, t)[rows, cols] = (cdf + pre * jnp.exp(-0.5 * pre * pre) * INV_ROOT_TWO_PI).astype(BF)

    def scatter_partial(t, part, n1a, n1b, n2):
        S1, V1, S2, V2, KP = g(B_S1, t), g(B_V1, t), g(B_S2, t), g(B_V2, t), g(B_KP, t)
        S1[0] = part(slot_rows(t, 1 - y, 1 - c)).astype(BF)
        send(S1.at[0], V1.at[0], n1a, t, sib)
        KP[0] = part(slot_rows(t, 1 - y, c))
        S1[1] = part(slot_rows(t, y, 1 - c)).astype(BF)
        send(S1.at[1], V1.at[1], n1b, t, sib)
        wait(V1.at[0], n1a, t)
        S2[...] = (KP[0] + V1[0].astype(F32)).astype(BF)
        send(S2, V2, n2, t, ypeer)
        KP[1] = part(slot_rows(t, y, c))

    def scatter_finish(t, n1b, n2):
        wait(g(B_V1, t).at[1], n1b, t)
        wait(g(B_V2, t), n2, t)

    def scatter_sent(t, n1a, n1b, n2):
        wait(g(B_S1, t).at[0], n1a, t, 1)
        wait(g(B_S1, t).at[1], n1b, t, 1)
        wait(g(B_S2, t), n2, t, 1)

    def summed(t, r):
        return g(B_KP, t)[1, r, :] + g(B_V1, t)[1, r, :].astype(F32) + g(B_V2, t)[r, :].astype(F32)

    def ffn(t):
        gather_near(t, B_MID, S_MC)
        gather_forward(t, B_MID, S_MY, S_MF)
        whole_cols(t, g(B_WU, t), S_UPC, S_UPZ)
        up_pair(t, y)
        gather_far(t, B_MID, S_MF)
        up_pair(t, 1 - y)
        wait(g(B_WD, t), S_DN, t)
        scatter_partial(t, lambda rows: nn(g(B_ACT, t)[rows, :], g(B_WD, t)[...]), S_F1A, S_F1B, S_F2)

    def ffn_end(t):
        T = ROWS[t]
        scatter_finish(t, S_F1B, S_F2)
        db = prow(R_DB + t)
        g0, g1, s0, s1 = (prow(base + 2 * t + k) for base in (R_GN, R_SF) for k in (0, 1))

        @pl.loop(0, T // CH)
        def _(i):
            r = pl.ds(mo(i * CH, CH), CH)
            second = g(B_N1, t)[r, :] * g0 + s0 + summed(t, r) + db
            n, inv, res = lnfwd(second, g1, s1)
            g(B_N2, t)[r, :] = n
            g(B_R2, t)[r, :] = jnp.broadcast_to(inv, (CH, 128))
            g(B_Y, t)[r, :] = res.astype(BF)

        local(g(B_Y, t), (o_y0, o_y1)[t], S_FIN, 0, t)

    forward_cols(1, g(B_WQ, 1), S_QKV, S_QKVZ)
    forward_out(1)
    forward_cols(0, g(B_WQ, 0), S_QKV, S_QKVZ)
    attention(1)
    send_up(0)
    send_dn(0)
    forward_out(0)
    forward_cols(1, g(B_WU, 1), S_UP, S_UPZ)
    attention(0)
    forward_cols(0, g(B_WU, 0), S_UP, S_UPZ)
    ffn(1)
    ffn(0)
    ffn_end(1)
    ffn_end(0)

    def pick(T, lo, step):
        ri = lax.broadcasted_iota(jnp.int32, (16, T), 0) & 7
        ci = lax.broadcasted_iota(jnp.int32, (16, T), 1)
        return (((ri & 4) == lo) & (ci == (ri & 3) * step)).astype(F32).astype(BF)

    both = nn(pick(128, 0, 32), g(B_Y, 0)[...]) + nn(pick(256, 4, 64), g(B_Y, 1)[...])
    top = lax.broadcasted_iota(jnp.int32, (16, HALF), 0) < 8
    g(B_CM, 0)[:, :HALF] = jnp.where(top, both[:, :HALF], both[:, HALF:]).astype(BF)
    ri = lax.broadcasted_iota(jnp.int32, (16, 128), 0)
    pos = jnp.zeros((16, 128), jnp.int32)
    for i in range(4):
        pos = jnp.where(ri == i, i_pos[i], pos)
    g(B_CM, 0)[:, HALF:] = pos.astype(F32).astype(BF)
    mine = g(B_GA, 0).at[s * 4 + rep]
    for k in (1, 2, 3):
        send(g(B_CM, 0), mine, S_CZ, 0, ((rep + k) % 4, s))
    g(B_GA, 0)[s * 4 + rep] = g(B_CM, 0)[...]
    wait(g(B_GA, 0).at[pl.ds(0, 3)], S_CZ, 0)
    four = g(B_GA, 0).at[pl.ds(s * 4, 4)]
    for d in NEIGH:
        send(four, four, S_CP, 0, (rep, sh(*peer(d))))

    for t in (0, 1):
        own = g(B_X, t).at[pl.ds(mo(c * ROWS[t], 128), ROWS[t])]
        wait(own, S_X, t, 1)
        for buf, far, near, pair in ((g(B_WQ, t), S_QKV, S_QKVC, S_QKVZ), (g(B_WU, t), S_UP, S_UPC, S_UPZ)):
            wait(buf.at[pl.ds(0, 288)], far, t, 1)
            wait(buf.at[pl.ds(0, 96)], near, t, 1)
            wait(buf.at[pl.ds(0, 288)], pair, t, 1)
        wait(g(B_WO, t).at[pl.ds(0, 144)], S_OUT, t, 1)

        @pl.when(c == y)
        def _():
            wait(g(B_WO, t).at[pl.ds(0, 96)], S_OUTZ, t, 1)

        @pl.when(c != y)
        def _():
            wait(g(B_WO, t).at[pl.ds(0, 96)], S_OUTC, t, 1)
            wait(g(B_WO, t).at[pl.ds(0, 192)], S_OUTZ, t, 1)

        wait(g(B_WD, t).at[pl.ds(0, HALF)], S_DN, t, 1)
        wait(g(B_OS, t), S_OP, t, 1)
        gather_sent(t, B_MID, S_MY, S_MC, S_MF)
        scatter_sent(t, S_F1A, S_F1B, S_F2)
        wait(g(B_COT, t), S_COT, 0, t)
    wait(g(B_SP, 0).at[pl.ds(0, 7)], S_SMALL, 0, 1)
    wait(g(B_GA, 0).at[pl.ds(0, 3)], S_CZ, 0, 1)
    g(B_BG, 0)[...] = jnp.zeros((32, D), F32)

    wait(g(B_GA, 0).at[pl.ds(0, 28)], S_CP, 0)
    wait(g(B_GA, 0).at[pl.ds(0, 28)], S_CP, 0, 1)

    def pick_all(base):
        ri = lax.broadcasted_iota(jnp.int32, (128, 512), 0)
        ci = lax.broadcasted_iota(jnp.int32, (128, 512), 1)
        blk = ci >> 4
        within = (ci & 15) - base
        row = ((blk & 3) * 8 + (blk >> 2)) * 4 + within
        return ((within >= 0) & (within < 4) & (ri == row)).astype(F32).astype(BF)

    ga = g(B_GA, 0)[...].reshape(512, 512)
    qa_f = nn(pick_all(0), ga)
    qa = qa_f[:, :HALF].astype(BF)
    pa = nn(pick_all(4), ga)[:, :HALF].astype(BF)
    qb = nn(pick_all(8), ga)[:, :HALF].astype(BF)
    pb = nn(pick_all(12), ga)[:, :HALF].astype(BF)
    scale = 2.0 / math.sqrt(D)
    logits = (nt(qa, pa) + nt(qb, pb)) * scale
    lane = lax.broadcasted_iota(jnp.int32, (1, 128), 1)
    cnt = jnp.zeros((1, 128), jnp.int32)
    for k in range(32):
        cnt = jnp.where(lane >> 2 == k, i_cnt[k], cnt)
    masked = jnp.where((cnt <= 0) | (lane & 3 == 0), logits, NEG_FILL)
    mx = jnp.max(masked, axis=1, keepdims=True)
    ex = jnp.exp(masked - mx)
    sm = jnp.sum(ex, axis=1, keepdims=True)
    hit = lax.broadcasted_iota(jnp.int32, (128, 128), 1).astype(F32) == qa_f[:, HALF:]
    ce = mx + jnp.log(sm) - jnp.sum(jnp.where(hit, masked, 0.0), axis=1, keepdims=True)
    o_loss[...] = jnp.broadcast_to(jnp.sum(ce, axis=0, keepdims=True) * (1.0 / 128.0), (8, 128))
    dl = (ex / sm - hit.astype(F32)).astype(BF)
    ri = lax.broadcasted_iota(jnp.int32, (16, 128), 0)
    ci = lax.broadcasted_iota(jnp.int32, (16, 128), 1)
    sel = ((ri < 4) & (ci == ri + 4 * (rep * 8 + s))).astype(F32).astype(BF)
    dlq = nn(sel, dl).astype(BF)
    dlp = nt(sel, dl.T).astype(BF) if False else lax.dot_general(
        sel, dl, (((1,), (1,)), ((), ())), preferred_element_type=F32).astype(BF)
    g(B_CG, 0)[0, :, :HALF] = nn(dlq, pa) * scale
    g(B_CG, 0)[0, :, HALF:] = nn(dlq, pb) * scale
    g(B_CG, 0)[1, :, :HALF] = nn(dlp, qa) * scale
    g(B_CG, 0)[1, :, HALF:] = nn(dlp, qb) * scale

    def fold(a):
        return jnp.sum(a.reshape(CH // 8, 8, D), axis=0)

    def put_bias(k, row):
        g(B_BG, 0)[k:k + 1, :] = row

    def ln_back(t, din, nrm, inv, gain):
        gg = din * gain
        m1 = jnp.mean(gg, axis=-1, keepdims=True)
        m2 = jnp.mean(gg * nrm, axis=-1, keepdims=True)
        return inv * (gg - m1 - nrm * m2)

    def out_back(t):
        T = ROWS[t]
        step = 32 if t == 0 else 64
        KP = g(B_KP, t)
        KP[0] = g(B_COT, t)[...].astype(F32)
        for i in range(4):
            KP[0, i * step:i * step + 1, :] = KP[0, i * step:i * step + 1, :] + g(B_CG, 0)[t, i:i + 1, :]
        gain = prow(R_GN + 2 * t + 1)
        me4 = (2 * y + c) * T
        zero = jnp.zeros((8, D), F32)

        def body(i, acc):
            r = pl.ds(mo(i * CH, CH), CH)
            dout = KP[0, r, :]
            nrm = g(B_N2, t)[r, :]
            dsec = ln_back(t, dout, nrm, g(B_R2, t)[r, 0:1], gain)
            low = dsec.astype(BF)
            g(B_N2, t)[r, :] = dsec
            g(B_DF, t)[pl.ds(mo(me4 + i * CH, CH), CH), :] = low
            return (acc[0] + fold(dout * nrm), acc[1] + fold(dout), acc[2] + fold(low.astype(F32)))

        acc = lax.fori_loop(0, T // CH, body, (zero, zero, zero))
        gather_rows(t, B_DF, S_DY, S_DC, S_DF)
        for k, a in zip((R_GN + 2 * t + 1, R_SF + 2 * t + 1, R_DB + t), acc):
            put_bias(k, jnp.sum(a, axis=0, keepdims=True))

    def down_pair(t, yy):
        T = ROWS[t]
        rows = pl.ds(mo(2 * yy * T, 128), 2 * T)

        @pl.loop(0, 3)
        def _(j):
            cols = pl.ds(mo(j * 256, 128), 256)
            da = nt(g(B_DF, t)[rows, :], g(B_WD, t)[cols, :])
            g(B_SL, t)[rows, cols] = (da * g(B_SL, t)[rows, cols].astype(F32)).astype(BF)

    def ffn_back(t):
        gather_near(t, B_DF, S_DC)
        gather_forward(t, B_DF, S_DY, S_DF)
        down_pair(t, y)
        gather_far(t, B_DF, S_DF)
        down_pair(t, 1 - y)
        scatter_partial(t, lambda rows: nt(g(B_SL, t)[rows, :], g(B_WU, t)[...]), S_D1A, S_D1B, S_D2)
        ones = jnp.ones((8, 4 * ROWS[t]), F32).astype(BF)
        sums = nn(ones, g(B_SL, t)[...])[0:1, :]
        for xx in (0, 1):
            part = sums[:, xx * HALF:(xx + 1) * HALF]
            at = R_UB + 4 * t + xx

            @pl.when(y == 0)
            def _():
                g(B_BG, 0)[at:at + 1, lane_half] = part

            @pl.when(y == 1)
            def _():
                g(B_BG, 0)[at + 2:at + 3, lane_half] = part

        @pl.loop(0, 3)
        def _(j):
            cols = pl.ds(mo(j * 256, 128), 256)
            g(B_WD, t)[cols, :] = tn(g(B_ACT, t)[:, cols], g(B_DF, t)[...]).astype(BF)

        send(g(B_WD, t).at[pl.ds(mo((1 - x) * HALF, 128), HALF)], g(B_GD, t), S_GD, t, xpeer)

        @pl.loop(0, 3)
        def _(j):
            cols = pl.ds(mo(j * 256, 128), 256)
            g(B_WU, t)[cols, :] = tn(g(B_MID, t)[:, cols], g(B_SL, t)[...]).astype(BF)

        for d in NEIGH:
            p = peer(d)
            send(g(B_WU, t).at[pl.ds(mo(96 * sh(*p), 32), 96)], g(B_GU, t).at[s], S_GU, t, (rep, sh(*p)))
        local(g(B_WU, t).at[rows96], g(B_GU, t).at[s], S_GU, t)

    def mid_back(t):
        T = ROWS[t]
        scatter_finish(t, S_D1B, S_D2)
        gain = prow(R_GN + 2 * t)
        zero = jnp.zeros((8, D), F32)

        def body(i, acc):
            r = pl.ds(mo(i * CH, CH), CH)
            dmid = g(B_N2, t)[r, :] + summed(t, r)
            nrm = g(B_N1, t)[r, :]
            dfirst = ln_back(t, dmid, nrm, g(B_R1, t)[r, 0:1], gain)
            low = dfirst.astype(BF)
            g(B_N1, t)[r, :] = dfirst
            g(B_DA, t)[pl.ds(mo(c * T + i * CH, CH), CH), :] = low
            return (acc[0] + fold(dmid * nrm), acc[1] + fold(dmid), acc[2] + fold(low.astype(F32)))

        acc = lax.fori_loop(0, T // CH, body, (zero, zero, zero))
        own = g(B_DA, t).at[pl.ds(mo(c * T, 128), T)]
        send(own, own, S_DA, t, sib)
        for k, a in zip((R_GN + 2 * t, R_SF + 2 * t, R_OB + t), acc):
            put_bias(k, jnp.sum(a, axis=0, keepdims=True))

    def attention_back(t):
        T = ROWS[t]
        QKV, P, ATT, DA, WO, WQ = g(B_QKV, t), g(B_P, t), g(B_ATT, t), g(B_DA, t), g(B_WO, t), g(B_WQ, t)
        wait(DA.at[pl.ds(mo((1 - c) * T, 128), T)], S_DA, t)

        @pl.loop(0, 2)
        def _(grp):
            rows = pl.ds(mo(grp * T, 128), T)

            @pl.loop(0, 3)
            def _(hp):
                lanes = pl.ds(mo(hp * 128, 128), 128)
                dat = nt(DA[rows, :], WO[lanes, :]).astype(BF)
                qs, ks = lanes, pl.ds(mo(HALF + hp * 128, 128), 128)
                vs = pl.ds(mo(2 * HALF + hp * 128, 128), 128)
                q, k, val = QKV[rows, qs], QKV[rows, ks], QKV[rows, vs]
                dq, dk, dv = [], [], []
                for h, msk in ((0, mask_a), (1, mask_b)):
                    p = P[grp * 6 + hp * 2 + h]
                    dp = nt(dat * msk, val)
                    ds = (p * (dp - jnp.sum(dp * p, axis=-1, keepdims=True))).astype(BF)
                    dv.append(tn(p.astype(BF), dat))
                    dq.append(nn(ds, k))
                    dk.append(tn(ds, q))
                root = 1.0 / math.sqrt(HD)
                QKV[rows, qs] = (jnp.where(lane_lo, dq[0], dq[1]) * root).astype(BF)
                QKV[rows, ks] = (jnp.where(lane_lo, dk[0], dk[1]) * root).astype(BF)
                QKV[rows, vs] = jnp.where(lane_lo, dv[0], dv[1]).astype(BF)

        g(B_OS, t)[...] = nt(QKV[pl.ds(mo((1 - c) * T, 128), T), :], WQ[...]).astype(BF)
        send(g(B_OS, t), g(B_OR, t), S_DX, t, sib)
        g(B_KP, t)[0] = nt(QKV[pl.ds(mo(c * T, 128), T), :], WQ[...])

        ones = jnp.ones((8, 2 * T), F32).astype(BF)
        sums = nn(ones, QKV[...])[0:1, :]
        g(B_BG, 0)[R_QB + t:R_QB + t + 1, lane_half] = sums[:, :HALF]
        g(B_BG, 0)[R_VB + t:R_VB + t + 1, lane_half] = sums[:, 2 * HALF:]

        @pl.loop(0, 3)
        def _(j):
            cols = pl.ds(mo(j * 128, 128), 128)
            WO[cols, :] = tn(ATT[:, cols], DA[...]).astype(BF)

        dst = g(B_GO, t).at[y * 2 + x]
        for xx in (0, 1):
            for cc in (0, 1):
                src = WO.at[pl.ds((2 * xx + cc) * 96, 96)]
                dev = sh(c, xx, cc)

                @pl.when(dev == s)
                def _():
                    local(src, dst, S_GO, t)

                @pl.when(dev != s)
                def _():
                    send(src, dst, S_GO, t, (rep, dev))

        if t == 1:
            for d in NEIGH:
                send(g(B_BG, 0), g(B_BGR, 0).at[s], S_BG, 0, (rep, sh(*peer(d))))
            local(g(B_BG, 0), g(B_BGR, 0).at[s], S_BG, 0)

        @pl.loop(0, 3)
        def _(j):
            cols = pl.ds(mo(j * 256, 128), 256)
            WQ[cols, :] = tn(g(B_X, t)[:, cols], QKV[...]).astype(BF)

        for d in NEIGH:
            p = peer(d)
            send(WQ.at[pl.ds(mo(96 * sh(*p), 32), 96)], g(B_GQ, t).at[s], S_GQ, t, (rep, sh(*p)))
        local(WQ.at[rows96], g(B_GQ, t).at[s], S_GQ, t)

    def input_back(t):
        T = ROWS[t]
        wait(g(B_OR, t), S_DX, t)

        @pl.loop(0, T // CH)
        def _(i):
            r = pl.ds(mo(i * CH, CH), CH)
            g(B_Y, t)[r, :] = (g(B_N1, t)[r, :] + g(B_KP, t)[0, r, :] + g(B_OR, t)[r, :].astype(F32)).astype(BF)

        local(g(B_Y, t), (o_gx0, o_gx1)[t], S_FIN2, 0, t)

    out_back(0)
    out_back(1)
    for t in (0, 1):
        wait(g(B_Y, t), S_FIN, 0, t)
    ffn_back(0)
    ffn_back(1)
    mid_back(0)
    mid_back(1)
    attention_back(0)
    attention_back(1)
    input_back(0)
    input_back(1)

    def make_dn(t, k):
        def each(use):
            if k == 0:
                wait(g(B_GD, t), S_GD, t)
            for r0 in (k * 192, k * 192 + 96):
                own = g(B_WD, t)[pl.ds(mo(x * HALF + r0, 32), 96), :].astype(F32)
                use(pl.ds(r0, 96), pl.ds(0, D), own + g(B_GD, t)[pl.ds(r0, 96), :].astype(F32))
        return each

    def make_up(t, yy):
        GU = g(B_GU, t)

        def each(use):
            if yy == 0:
                wait(GU, S_GU, t)
            for cc in (0, 1):
                both = GU[sh(yy, 0, cc)].astype(F32) + GU[sh(yy, 1, cc)].astype(F32)
                for xx in (0, 1):
                    j = 4 * yy + 2 * xx + cc
                    use(pl.ds(0, 96), pl.ds(j * HALF, HALF), both[:, xx * HALF:(xx + 1) * HALF])
        return each

    def make_out(t):
        GO = g(B_GO, t)

        def each(use):
            wait(GO, S_GO, t)
            tot = GO[0].astype(F32)
            for k in range(1, 4):
                tot = tot + GO[k].astype(F32)
            use(pl.ds(0, 96), pl.ds(0, D), tot)
        return each

    def make_qkv(t, part):
        GQ = g(B_GQ, t)

        def each(use):
            if part == 0:
                wait(GQ, S_GQ, t)
            cols = slice(part * HALF, (part + 1) * HALF)
            for cc in (0, 1):
                tot = GQ[cc, :, cols].astype(F32)
                for k in range(1, 4):
                    tot = tot + GQ[2 * k + cc, :, cols].astype(F32)
                use(pl.ds(0, 96), pl.ds(part * D + cc * HALF, HALF), tot)
        return each

    def each_small(use):
        BGR = g(B_BGR, 0)
        wait(BGR, S_BG, 0)
        tot = BGR[0]
        for k in range(1, 8):
            tot = tot + BGR[k]
        use(pl.ds(0, 32), pl.ds(0, D), tot)

    is_end = (rep == 0) | (rep == 3)
    units = []

    def unit(kind, t, each, out, rows, cols):
        if kind == 4:
            bufs = (B_BGS, B_BGA, B_BGB)
        else:
            bufs = (B_ZSD + kind, B_ZAD + kind, B_ZBD + kind)
        units.append((len(units), tuple(g(b, t) for b in bufs), each, out, rows, cols))

    def add_ffn(t):
        for k in (0, 1):
            unit(0, t, make_dn(t, k), o_od.at[t], (192 * k, 192), (0, D))
        for yy in (0, 1):
            unit(1, t, make_up(t, yy), o_ou.at[t], (0, 96), (2 * D * yy, 2 * D))

    def add_qkv(t):
        for part in range(3):
            unit(3, t, make_qkv(t, part), o_oq.at[t], (0, 96), (part * D, D))

    add_ffn(0)
    add_ffn(1)
    for t in (0, 1):
        unit(2, t, make_out(t), o_oo.at[t], (0, 96), (0, D))
        if t == 1:
            unit(4, 0, each_small, o_obg, (0, 32), (0, D))
        add_qkv(t)
    assert len(units) == N_UNITS

    def hop(which, u):
        at = which * N_UNITS + u[0]
        return S_Z + at // 2, at % 2

    def view(ref, u):
        return ref.at[pl.ds(*u[4]), pl.ds(*u[5])]

    def stage_a(u):
        ZS, ZA, ZB = u[1]

        def put(r, cl, val):
            ZS[r, cl] = val.astype(ZS.dtype)

        def put_add(r, cl, val):
            ZS[r, cl] = (val + ZA[r, cl].astype(F32)).astype(ZS.dtype)

        for end, mid in ((0, 1), (3, 2)):
            @pl.when(rep == end)
            def _():
                u[2](put)
                send(view(ZS, u), view(ZA, u), *hop(0, u), (mid, s))

            @pl.when(rep == mid)
            def _():
                wait(view(ZA, u), *hop(0, u))
                u[2](put_add)
                send(view(ZS, u), view(ZB, u), *hop(1, u), (3 - mid, s))

    def stage_b(u):
        ZS, ZA, ZB = u[1]
        for end, mid in ((0, 1), (3, 2)):
            @pl.when(rep == mid)
            def _():
                wait(view(ZB, u), *hop(1, u))
                wait(view(ZB, u), *hop(1, u), 1)
                for r0 in range(u[4][0], u[4][0] + u[4][1], 32):
                    r, cl = pl.ds(r0, 32), pl.ds(*u[5])
                    ZS[r, cl] = (ZS[r, cl].astype(F32) + ZB[r, cl].astype(F32)).astype(ZS.dtype)
                send(view(ZS, u), view(u[3], u), *hop(2, u), (end, s))
                local(view(ZS, u), view(u[3], u), *hop(2, u))

    for k, u in enumerate(units):
        stage_a(u)
        if k:
            stage_b(units[k - 1])
    stage_b(units[-1])

    for u in units:
        ZS = view(u[1][0], u)
        wait(ZS, *hop(2, u))

        @pl.when(is_end)
        def _():
            wait(ZS, *hop(0, u), 1)

        @pl.when(jnp.logical_not(is_end))
        def _():
            wait(ZS, *hop(2, u), 1)

    for t in (0, 1):
        gather_sent(t, B_DF, S_DY, S_DC, S_DF)
        scatter_sent(t, S_D1A, S_D1B, S_D2)
        wait(g(B_OS, t), S_DA, t, 1)
        wait(g(B_OS, t), S_DX, t, 1)
        wait(g(B_GD, t), S_GD, t, 1)
        wait(g(B_GU, t).at[pl.ds(0, 7)], S_GU, t, 1)

        @pl.when(c == y)
        def _():
            wait(g(B_GO, t).at[pl.ds(0, 3)], S_GO, t, 1)

        @pl.when(c != y)
        def _():
            wait(g(B_GO, t), S_GO, t, 1)

        wait(g(B_GQ, t).at[pl.ds(0, 7)], S_GQ, t, 1)
        wait(g(B_Y, t), S_FIN2, 0, t)
    wait(g(B_BGR, 0).at[pl.ds(0, 7)], S_BG, 0, 1)


def fused_call(*args):
    hbm = pl.BlockSpec(memory_space=pl.ANY)
    vm = pl.BlockSpec(memory_space=pltpu.VMEM)
    sm = pl.BlockSpec(memory_space=pltpu.SMEM)
    out_shape = [
        jax.ShapeDtypeStruct((8, 128), F32),
        jax.ShapeDtypeStruct((128, D), BF),
        jax.ShapeDtypeStruct((256, D), BF),
        jax.ShapeDtypeStruct((128, D), BF),
        jax.ShapeDtypeStruct((256, D), BF),
        jax.ShapeDtypeStruct((2, 96, 3 * D), BF),
        jax.ShapeDtypeStruct((2, 96, D), BF),
        jax.ShapeDtypeStruct((2, 96, 4 * D), BF),
        jax.ShapeDtypeStruct((2, HALF, D), BF),
        jax.ShapeDtypeStruct((32, D), F32),
    ]
    return pl.pallas_call(
        fused_kernel,
        out_shape=out_shape,
        in_specs=[hbm] * 8 + [vm] * 6 + [sm] * 2,
        out_specs=[vm] + [hbm] * 9,
        scratch_shapes=[shape for _, shape in scratch_list()] + [pltpu.SemaphoreType.DMA((N_SEMS,))],
        compiler_params=pltpu.CompilerParams(collective_id=0, has_side_effects=True, vmem_limit_bytes=VMEM_LIMIT),
        cost_estimate=pl.CostEstimate(flops=18 * 10**9, bytes_accessed=40 * 10**6, transcendentals=4 * 10**6),
    )(*args)


def widen_kernel(*refs):
    loss, y0, y1, gx0, gx1, oq, oo, ou, od, bg = refs[:10]
    r_loss, r_y0, r_y1, r_gx0, r_gx1, r_q, r_qb, r_o, r_ob, r_u, r_ub, r_d, r_db, r_gn, r_sf = refs[10:25]
    low = refs[25:29]
    wide = refs[29:33]
    through = refs[33:37]
    sem_in, sem_out, sem_move, sem_move_out = refs[37:]
    s = lax.axis_index("shard")
    groups = list(zip((oq, ou, od, oo), low, wide, (r_q, r_u, r_d, r_o)))
    reads, writes, moves = [], [], []
    for k, (src, lo, hi, dst) in enumerate(groups):
        for t in (0, 1):
            reads.append(pltpu.make_async_copy(src.at[t], lo.at[t], sem_in.at[2 * k + t]))
            reads[-1].start()
    for k, (src, dst) in enumerate(((y0, r_y0), (y1, r_y1), (gx0, r_gx0), (gx1, r_gx1))):
        moves.append((pltpu.make_async_copy(src, through[k], sem_move.at[k]),
                      pltpu.make_async_copy(through[k], dst, sem_move_out.at[k])))
        moves[-1][0].start()
    r_loss[...] = loss[0:1, 0:1]
    first = pltpu.roll(bg[0:16, :], lax.rem(D - 96 * s, D), 1)[:, :96]
    r_ob[...] = first[0:2, :]
    r_db[...] = first[2:4, :]
    for t in (0, 1):
        r_gn[t] = first[4 + 2 * t:6 + 2 * t, :]
        r_sf[t] = first[8 + 2 * t:10 + 2 * t, :]
    second = pltpu.roll(bg[8:16, :], lax.rem(D - 192 * (s % 4), D), 1)[:, :192]
    r_qb[...] = jnp.where(jnp.full((2, 192), s) < 4, second[4:6, :], second[6:8, :])
    for t in (0, 1):
        r_ub[t:t + 1, :] = bg[pl.ds(16 + 4 * t + s // 2, 1), pl.ds(mo((s % 2) * HALF, 128), HALF)]
    for k, (src, lo, hi, dst) in enumerate(groups):
        for t in (0, 1):
            reads[2 * k + t].wait()
            hi[t] = lo[t].astype(F32)
            writes.append(pltpu.make_async_copy(hi.at[t], dst.at[t], sem_out.at[2 * k + t]))
            writes[-1].start()
    for there, onward in moves:
        there.wait()
        onward.start()
    for copy in writes + [onward for there, onward in moves]:
        copy.wait()


def widen_call(*args):
    hbm = pl.BlockSpec(memory_space=pl.ANY)
    vm = pl.BlockSpec(memory_space=pltpu.VMEM)

    def out(dtype, *shape):
        return jax.ShapeDtypeStruct(shape, dtype)

    shapes = [(2, 96, 3 * D), (2, 96, 4 * D), (2, HALF, D), (2, 96, D)]
    return pl.pallas_call(
        widen_kernel,
        out_shape=[out(F32, 1, 1), out(BF, 128, D), out(BF, 256, D), out(BF, 128, D), out(BF, 256, D),
                   out(F32, *shapes[0]), out(F32, 2, 192), out(F32, *shapes[3]), out(F32, 2, 96),
                   out(F32, *shapes[1]), out(F32, 2, HALF), out(F32, *shapes[2]), out(F32, 2, 96),
                   out(F32, 2, 2, 96), out(F32, 2, 2, 96)],
        in_specs=[vm] + [hbm] * 8 + [vm],
        out_specs=[vm, hbm, hbm, hbm, hbm, hbm, vm, hbm, vm, hbm, vm, hbm, vm, vm, vm],
        scratch_shapes=[pltpu.VMEM(shape, BF) for shape in shapes] + [pltpu.VMEM(shape, F32) for shape in shapes]
        + [pltpu.VMEM((rows, D), BF) for rows in ROWS * 2]
        + [pltpu.SemaphoreType.DMA((8,)), pltpu.SemaphoreType.DMA((8,)), pltpu.SemaphoreType.DMA((4,)),
           pltpu.SemaphoreType.DMA((4,))],
        compiler_params=pltpu.CompilerParams(vmem_limit_bytes=VMEM_LIMIT),
    )(*args)


def local_fast(query_tokens, passage_tokens, query_cot, passage_cot, bucket_counts, positives, qkv_weight, qv_bias,
               out_weight, out_bias, up_weight, up_bias, down_weight, down_bias, norm_gains, norm_shifts):
    results = widen_call(*fused_call(
        query_tokens.reshape(128, D), passage_tokens.reshape(256, D),
        query_cot.reshape(128, D), passage_cot.reshape(256, D),
        qkv_weight, out_weight, up_weight, down_weight,
        qv_bias, out_bias, up_bias, down_bias, norm_gains, norm_shifts, bucket_counts, positives))
    loss, y0, y1, gx0, gx1 = results[:5]
    return (loss.reshape(()), y0.reshape(query_tokens.shape), y1.reshape(passage_tokens.shape),
            gx0.reshape(query_tokens.shape), gx1.reshape(passage_tokens.shape), *results[5:])


def solution(mesh):
    in_specs = (
        P(("rep", "shard"), None, None),
        P(("rep", "shard"), None, None),
        P(("rep", "shard"), None, None),
        P(("rep", "shard"), None, None),
        P(),
        P(("rep", "shard")),
        P(None, "shard", None),
        P(None, "shard"),
        P(None, "shard", None),
        P(None, "shard"),
        P(None, "shard", None),
        P(None, "shard"),
        P(None, "shard", None),
        P(None, "shard"),
        P(None, None, "shard"),
        P(None, None, "shard"),
    )
    out_specs = (
        P(),
        P(("rep", "shard"), None, None),
        P(("rep", "shard"), None, None),
        P(("rep", "shard"), None, None),
        P(("rep", "shard"), None, None),
        P(None, "shard", None),
        P(None, "shard"),
        P(None, "shard", None),
        P(None, "shard"),
        P(None, "shard", None),
        P(None, "shard"),
        P(None, "shard", None),
        P(None, "shard"),
        P(None, None, "shard"),
        P(None, None, "shard"),
    )
    small_mesh = (mesh.shape["rep"], mesh.shape["shard"]) == (4, 8)
    step = local_fast if small_mesh else local
    return jax.shard_map(step, mesh=mesh, in_specs=in_specs, out_specs=out_specs, check_vma=False)
```

```python
import functools
import math

import jax
import jax.numpy as jnp
from jax import lax
from jax.experimental import pallas as pl
from jax.experimental.pallas import tpu as pltpu
from jax.sharding import PartitionSpec as P

HD = 64
SHORT = 64


LN_EPS = 1e-05
NEG_FILL = -1e30
INV_ROOT_TWO = 0.7071067811865476
INV_ROOT_TWO_PI = 0.3989422804014327
VMEM_LIMIT = 66 * 1000 * 1000


def for_sending(array):
    return jax.tree.map(lambda a: a.astype(jnp.bfloat16) if a.dtype == jnp.float32 else a, array)


def pick_tower(stacks, tower_index):
    qkv_w, qv_b, out_w, out_b, up_w, up_b, down_w, down_b, gains, shifts = stacks
    return (
        qkv_w[tower_index],
        qv_b[tower_index],
        out_w[tower_index],
        out_b[tower_index],
        up_w[tower_index],
        up_b[tower_index],
        down_w[tower_index],
        down_b[tower_index],
        gains[tower_index].T,
        shifts[tower_index].T,
    )


def fetch_layer(stacks, tower_index):
    return lax.all_gather(for_sending(pick_tower(stacks, tower_index)), "shard", axis=0, tiled=True)


def fetch_again(stacks, tower_index):
    return lax.all_gather(for_sending(pick_tower(stacks, tower_index)), "shard", axis=0, tiled=True)


def normalize(hidden):
    row_mean = jnp.mean(hidden, axis=-1, keepdims=True)
    centred = hidden - row_mean
    inv_std = lax.rsqrt(jnp.mean(centred * centred, axis=-1, keepdims=True) + LN_EPS)
    return (centred * inv_std, inv_std)


def norm_back(grad_in, normed, inv_std):
    return inv_std * (
        grad_in
        - jnp.mean(grad_in, axis=-1, keepdims=True)
        - normed * jnp.mean(grad_in * normed, axis=-1, keepdims=True)
    )


def block_mask(long_flags, length, short_len):
    row_part = lax.broadcasted_iota(jnp.int32, (length, length), 0) // short_len
    col_part = lax.broadcasted_iota(jnp.int32, (length, length), 1) // short_len
    return long_flags[:, None, None] | (row_part == col_part)[None]


def head_scores(head_query, head_key, attn_mask):
    raw_scores = jnp.einsum(
        "slhd,smhd->shlm", head_query, head_key, preferred_element_type=jnp.float32
    ) * (1.0 / math.sqrt(HD))
    return jnp.where(attn_mask[:, None], raw_scores, NEG_FILL)


def layer_forward(tokens, weights, attn_mask):
    qkv_w, qv_b, out_w, out_b, up_w, up_b, down_w, down_b, gains, shifts = weights
    seq_count, length, model_width = tokens.shape
    head_count = model_width // HD
    token_rows = tokens.reshape(seq_count * length, model_width)
    qv_float = qv_b.astype(jnp.float32)
    qkv_bias = jnp.concatenate(
        [qv_float[:model_width], jnp.zeros((model_width,), jnp.float32), qv_float[model_width:]]
    )
    qkv_low = (jnp.dot(token_rows, qkv_w, preferred_element_type=jnp.float32) + qkv_bias).astype(
        jnp.bfloat16
    )
    head_split = qkv_low.reshape(seq_count, length, 3, head_count, HD)
    scores = head_scores(head_split[:, :, 0], head_split[:, :, 1], attn_mask)
    row_max = jnp.max(scores, axis=-1, keepdims=True)
    exp_scores = jnp.exp(scores - row_max)
    row_total = jnp.sum(exp_scores, axis=-1, keepdims=True)
    attn_probs = (exp_scores / row_total).astype(jnp.bfloat16)
    log_total = row_max + jnp.log(row_total)
    attn_mixed = jnp.einsum(
        "shlm,smhd->slhd", attn_probs, head_split[:, :, 2], preferred_element_type=jnp.float32
    )
    attn_low = attn_mixed.reshape(seq_count * length, model_width).astype(jnp.bfloat16)
    first_sum = (
        token_rows.astype(jnp.float32)
        + jnp.dot(attn_low, out_w, preferred_element_type=jnp.float32)
        + out_b.astype(jnp.float32)
    )
    normed_one, inv_one = normalize(first_sum)
    gain_float = gains.astype(jnp.float32)
    shift_float = shifts.astype(jnp.float32)
    middle = normed_one * gain_float[:, 0] + shift_float[:, 0]
    middle_low = middle.astype(jnp.bfloat16)
    pre_act = jnp.dot(middle_low, up_w, preferred_element_type=jnp.float32) + up_b.astype(
        jnp.float32
    )
    act_low = jax.nn.gelu(pre_act, approximate=False).astype(jnp.bfloat16)
    second = (
        middle
        + jnp.dot(act_low, down_w, preferred_element_type=jnp.float32)
        + down_b.astype(jnp.float32)
    )
    normed_two, inv_two = normalize(second)
    result = normed_two * gain_float[:, 1] + shift_float[:, 1]
    kept = (
        token_rows,
        qkv_low,
        log_total,
        attn_low,
        normed_one,
        inv_one,
        middle_low,
        pre_act,
        act_low,
        normed_two,
        inv_two,
    )
    return (result, kept)


def layer_backward(grad_out, weights, kept, attn_mask):
    qkv_w, qv_b, out_w, out_b, up_w, up_b, down_w, down_b, gains, shifts = weights
    (
        token_rows,
        qkv_low,
        log_total,
        attn_low,
        normed_one,
        inv_one,
        middle_low,
        pre_act,
        act_low,
        normed_two,
        inv_two,
    ) = kept
    seq_count = attn_mask.shape[0]
    model_width = token_rows.shape[1]
    length = token_rows.shape[0] // seq_count
    head_count = model_width // HD
    gain_float = gains.astype(jnp.float32)
    gain_two = jnp.sum(grad_out * normed_two, axis=0)
    shift_two = jnp.sum(grad_out, axis=0)
    d_second = norm_back(grad_out * gain_float[:, 1], normed_two, inv_two)
    d_ffn = d_second.astype(jnp.bfloat16)
    d_down_w = jnp.dot(act_low.T, d_ffn, preferred_element_type=jnp.float32)
    d_down_b = jnp.sum(d_ffn.astype(jnp.float32), axis=0)
    d_act = jnp.dot(d_ffn, down_w.T, preferred_element_type=jnp.float32)
    gelu_slope = (
        0.5 * (1.0 + lax.erf(pre_act * INV_ROOT_TWO))
        + pre_act * jnp.exp(-0.5 * pre_act * pre_act) * INV_ROOT_TWO_PI
    )
    d_pre = (d_act * gelu_slope).astype(jnp.bfloat16)
    d_up_w = jnp.dot(middle_low.T, d_pre, preferred_element_type=jnp.float32)
    d_up_b = jnp.sum(d_pre.astype(jnp.float32), axis=0)
    d_middle = d_second + jnp.dot(d_pre, up_w.T, preferred_element_type=jnp.float32)
    gain_one = jnp.sum(d_middle * normed_one, axis=0)
    shift_one = jnp.sum(d_middle, axis=0)
    d_first = norm_back(d_middle * gain_float[:, 0], normed_one, inv_one)
    d_attn_out = d_first.astype(jnp.bfloat16)
    d_out_w = jnp.dot(attn_low.T, d_attn_out, preferred_element_type=jnp.float32)
    d_out_b = jnp.sum(d_attn_out.astype(jnp.float32), axis=0)
    d_mixed = (
        jnp.dot(d_attn_out, out_w.T, preferred_element_type=jnp.float32)
        .astype(jnp.bfloat16)
        .reshape(seq_count, length, head_count, HD)
    )
    head_split = qkv_low.reshape(seq_count, length, 3, head_count, HD)
    head_query = head_split[:, :, 0]
    head_key = head_split[:, :, 1]
    head_value = head_split[:, :, 2]
    attn_probs = jnp.exp(head_scores(head_query, head_key, attn_mask) - log_total)
    d_probs = jnp.einsum("slhd,smhd->shlm", d_mixed, head_value, preferred_element_type=jnp.float32)
    d_value = jnp.einsum(
        "shlm,slhd->smhd",
        attn_probs.astype(jnp.bfloat16),
        d_mixed,
        preferred_element_type=jnp.float32,
    )
    d_scores = (
        attn_probs * (d_probs - jnp.sum(d_probs * attn_probs, axis=-1, keepdims=True))
    ).astype(jnp.bfloat16)
    d_query = jnp.einsum(
        "shlm,smhd->slhd", d_scores, head_key, preferred_element_type=jnp.float32
    ) * (1.0 / math.sqrt(HD))
    d_key = jnp.einsum(
        "shlm,slhd->smhd", d_scores, head_query, preferred_element_type=jnp.float32
    ) * (1.0 / math.sqrt(HD))
    d_qkv = (
        jnp.stack([d_query, d_key, d_value], axis=2)
        .reshape(seq_count * length, 3 * model_width)
        .astype(jnp.bfloat16)
    )
    d_qkv_w = jnp.dot(token_rows.T, d_qkv, preferred_element_type=jnp.float32)
    column_sums = jnp.sum(d_qkv.astype(jnp.float32), axis=0)
    d_qv_b = jnp.concatenate([column_sums[:model_width], column_sums[2 * model_width :]])
    d_tokens = d_first + jnp.dot(d_qkv, qkv_w.T, preferred_element_type=jnp.float32)
    layer_grads = (
        d_qkv_w,
        d_qv_b,
        d_out_w,
        d_out_b,
        d_up_w,
        d_up_b,
        d_down_w,
        d_down_b,
        jnp.stack([gain_one, gain_two], axis=1),
        jnp.stack([shift_one, shift_two], axis=1),
    )
    return (d_tokens, layer_grads)


def reduce_layer(layer_grads):
    owned_grads = (
        lax.psum_scatter(layer_grads[0], "shard", scatter_dimension=0, tiled=True),
        lax.psum_scatter(layer_grads[1], "shard", scatter_dimension=0, tiled=True),
        lax.psum_scatter(layer_grads[2], "shard", scatter_dimension=0, tiled=True),
        lax.psum_scatter(layer_grads[3], "shard", scatter_dimension=0, tiled=True),
        lax.psum_scatter(layer_grads[4], "shard", scatter_dimension=0, tiled=True),
        lax.psum_scatter(layer_grads[5], "shard", scatter_dimension=0, tiled=True),
        lax.psum_scatter(layer_grads[6], "shard", scatter_dimension=0, tiled=True),
        lax.psum_scatter(layer_grads[7], "shard", scatter_dimension=0, tiled=True),
        lax.psum_scatter(layer_grads[8], "shard", scatter_dimension=0, tiled=True),
        lax.psum_scatter(layer_grads[9], "shard", scatter_dimension=0, tiled=True),
    )
    quarter = (
        lax.psum_scatter(
            owned_grads[0].astype(jnp.bfloat16), "rep", scatter_dimension=0, tiled=True
        ).astype(jnp.float32),
        lax.psum_scatter(
            owned_grads[1].astype(jnp.bfloat16), "rep", scatter_dimension=0, tiled=True
        ).astype(jnp.float32),
        lax.psum_scatter(
            owned_grads[2].astype(jnp.bfloat16), "rep", scatter_dimension=0, tiled=True
        ).astype(jnp.float32),
        lax.psum_scatter(
            owned_grads[3].astype(jnp.bfloat16), "rep", scatter_dimension=0, tiled=True
        ).astype(jnp.float32),
        lax.psum_scatter(
            owned_grads[4].astype(jnp.bfloat16), "rep", scatter_dimension=0, tiled=True
        ).astype(jnp.float32),
        lax.psum_scatter(
            owned_grads[5].astype(jnp.bfloat16), "rep", scatter_dimension=0, tiled=True
        ).astype(jnp.float32),
        lax.psum_scatter(
            owned_grads[6].astype(jnp.bfloat16), "rep", scatter_dimension=0, tiled=True
        ).astype(jnp.float32),
        lax.psum_scatter(
            owned_grads[7].astype(jnp.bfloat16), "rep", scatter_dimension=0, tiled=True
        ).astype(jnp.float32),
        lax.psum_scatter(
            owned_grads[8].astype(jnp.bfloat16), "rep", scatter_dimension=0, tiled=True
        ).astype(jnp.float32),
        lax.psum_scatter(
            owned_grads[9].astype(jnp.bfloat16), "rep", scatter_dimension=0, tiled=True
        ).astype(jnp.float32),
    )
    return (
        lax.all_gather(quarter[0].astype(jnp.bfloat16), "rep", axis=0, tiled=True).astype(
            jnp.float32
        ),
        lax.all_gather(quarter[1].astype(jnp.bfloat16), "rep", axis=0, tiled=True).astype(
            jnp.float32
        ),
        lax.all_gather(quarter[2].astype(jnp.bfloat16), "rep", axis=0, tiled=True).astype(
            jnp.float32
        ),
        lax.all_gather(quarter[3].astype(jnp.bfloat16), "rep", axis=0, tiled=True).astype(
            jnp.float32
        ),
        lax.all_gather(quarter[4].astype(jnp.bfloat16), "rep", axis=0, tiled=True).astype(
            jnp.float32
        ),
        lax.all_gather(quarter[5].astype(jnp.bfloat16), "rep", axis=0, tiled=True).astype(
            jnp.float32
        ),
        lax.all_gather(quarter[6].astype(jnp.bfloat16), "rep", axis=0, tiled=True).astype(
            jnp.float32
        ),
        lax.all_gather(quarter[7].astype(jnp.bfloat16), "rep", axis=0, tiled=True).astype(
            jnp.float32
        ),
        lax.all_gather(quarter[8].astype(jnp.bfloat16), "rep", axis=0, tiled=True).astype(
            jnp.float32
        ),
        lax.all_gather(quarter[9].astype(jnp.bfloat16), "rep", axis=0, tiled=True).astype(
            jnp.float32
        ),
    )


def local(
    query_tokens,
    passage_tokens,
    query_cot,
    passage_cot,
    bucket_counts,
    positives,
    qkv_weight,
    qv_bias,
    out_weight,
    out_bias,
    up_weight,
    up_bias,
    down_weight,
    down_bias,
    norm_gains,
    norm_shifts,
):
    stacks = (
        qkv_weight,
        qv_bias,
        out_weight,
        out_bias,
        up_weight,
        up_bias,
        down_weight,
        down_bias,
        norm_gains,
        norm_shifts,
    )
    blocks, long_len, model_width = passage_tokens.shape
    query_count, query_len, unused_width = query_tokens.shape
    subs_count = long_len // SHORT
    slot_count = blocks * subs_count
    my_index = lax.axis_index(("rep", "shard"))
    own_count = lax.dynamic_index_in_dim(bucket_counts, my_index, 0, keepdims=False)
    passage_mask = block_mask(lax.iota(jnp.int32, blocks) < own_count, long_len, SHORT)
    query_mask = block_mask(jnp.ones((query_count,), dtype=bool), query_len, query_len)
    query_weights = fetch_layer(stacks, 0)
    query_result, query_kept = layer_forward(query_tokens, query_weights, query_mask)
    passage_weights = fetch_layer(stacks, 1)
    passage_result, passage_kept = layer_forward(passage_tokens, passage_weights, passage_mask)
    query_cls = query_result.reshape(query_count, query_len, model_width)[:, 0].astype(jnp.bfloat16)
    passage_cls = (
        passage_result.reshape(blocks, subs_count, SHORT, model_width)[:, :, 0]
        .reshape(slot_count, model_width)
        .astype(jnp.bfloat16)
    )
    every_cls = lax.all_gather(passage_cls, ("rep", "shard"), axis=0, tiled=True)
    cand_count = every_cls.shape[0]
    device_count = bucket_counts.shape[0]
    score_scale = 2.0 / math.sqrt(model_width)
    logits = jnp.dot(query_cls, every_cls.T, preferred_element_type=jnp.float32) * score_scale
    slot_ids = lax.iota(jnp.int32, cand_count)
    owner_index = slot_ids // slot_count
    owner_counts = jnp.sum(
        jnp.where(
            owner_index[:, None] == lax.iota(jnp.int32, device_count)[None], bucket_counts[None], 0
        ),
        axis=1,
    )
    slot_valid = (slot_ids % slot_count // subs_count >= owner_counts) | (
        slot_ids % subs_count == 0
    )
    masked = jnp.where(slot_valid[None], logits, NEG_FILL)
    row_max = jnp.max(masked, axis=1, keepdims=True)
    exp_scores = jnp.exp(masked - row_max)
    row_total = jnp.sum(exp_scores, axis=1, keepdims=True)
    log_total = row_max[:, 0] + jnp.log(row_total[:, 0])
    hit_mask = slot_ids[None] == positives[:, None]
    picked = jnp.sum(jnp.where(hit_mask, masked, 0.0), axis=1)
    local_loss = jnp.sum(log_total - picked)
    d_logits = (exp_scores / row_total - hit_mask.astype(jnp.float32)).astype(jnp.bfloat16)
    d_query_cls = jnp.dot(d_logits, every_cls, preferred_element_type=jnp.float32) * score_scale
    d_cands = (
        lax.dot_general(
            d_logits, query_cls, (((0,), (0,)), ((), ())), preferred_element_type=jnp.float32
        )
        * score_scale
    )
    d_passage_cls = lax.psum_scatter(d_cands, ("rep", "shard"), scatter_dimension=0, tiled=True)
    loss_sum = lax.psum(local_loss, ("rep", "shard"))
    loss = loss_sum / (query_count * lax.axis_size(("rep", "shard")))
    query_dout = (
        query_cot.astype(jnp.float32)
        .at[:, 0]
        .add(d_query_cls)
        .reshape(query_count * query_len, model_width)
    )
    passage_dout = (
        passage_cot.astype(jnp.float32)
        .reshape(blocks, subs_count, SHORT, model_width)
        .at[:, :, 0]
        .add(d_passage_cls.reshape(blocks, subs_count, model_width))
        .reshape(blocks * long_len, model_width)
    )
    passage_back = fetch_again(stacks, 1)
    passage_dx, passage_grads = layer_backward(
        passage_dout, passage_back, passage_kept, passage_mask
    )
    passage_owned = reduce_layer(passage_grads)
    query_back = fetch_again(stacks, 0)
    query_dx, query_grads = layer_backward(query_dout, query_back, query_kept, query_mask)
    query_owned = reduce_layer(query_grads)
    stacked = [
        jnp.stack([first_g, second_g]) for first_g, second_g in zip(query_owned, passage_owned)
    ]
    gains_grad = jnp.swapaxes(stacked[8], 1, 2)
    shifts_grad = jnp.swapaxes(stacked[9], 1, 2)
    return (
        loss,
        query_result.reshape(query_count, query_len, model_width).astype(jnp.bfloat16),
        passage_result.reshape(blocks, long_len, model_width).astype(jnp.bfloat16),
        query_dx.reshape(query_count, query_len, model_width).astype(jnp.bfloat16),
        passage_dx.reshape(blocks, long_len, model_width).astype(jnp.bfloat16),
        stacked[0],
        stacked[1],
        stacked[2],
        stacked[3],
        stacked[4],
        stacked[5],
        stacked[6],
        stacked[7],
        gains_grad,
        shifts_grad,
    )


BF = jnp.bfloat16
F32 = jnp.float32
MESH = pl.DeviceIdType.MESH
ROWS = (128, 256)
D = 768
HALF = 384
FFN = 768
PLAN = [(2, 0, 0),
        (3, 1, 0), (4, 2, 1), (5, 3, 2), (6, 4, 3), (7, 5, 4), (7, 6, 5),
        (8, 7, 6), (9, 8, 7), (10, 9, 8), (11, 10, 9), (12, 11, 10), (13, 12, 11),
        (14, 13, 12),
        (14, 14, 13), (15, 14, 14), (16, 15, 14), (17, 16, 15), (18, 17, 16), (19, 18, 17)]
NEIGH = tuple((dy, dx, dc) for dy in (0, 1) for dx in (0, 1) for dc in (0, 1) if dy + dx + dc)

(S_X, S_QKV, S_QKV1, S_QKV2, S_QKVC, S_QKVZ, S_QKVZ1, S_QKVZ2, S_OUT, S_OUTC, S_OUTZ, S_UP, S_UP1, S_UPC, S_UPZ, S_UPZ1,
 S_DN, S_OP, S_MY, S_MC, S_MF, S_F1A, S_F1B, S_F2, S_DY, S_DC, S_DF, S_D1A, S_D1B, S_D2,
 S_DA, S_DX, S_GD, S_GD1, S_GD2, S_GU, S_GU1, S_GO, S_GQ, S_GQ1, S_GQ2, S_YQ, S_YQ1, S_YQ2, S_SMALL, S_CZ, S_CP, S_BG, S_COT, S_FIN, S_FIN2, S_CF, S_Z) = range(53)
N_UNITS = 23
N_SEMS = 4 * S_Z + 6 * N_UNITS + 2


def nn(a, b):
    return jnp.dot(a, b, preferred_element_type=F32)


def nt(a, b):
    return lax.dot_general(a, b, (((1,), (1,)), ((), ())), preferred_element_type=F32)


def tn(a, b):
    return lax.dot_general(a, b, (((0,), (0,)), ((), ())), preferred_element_type=F32)


def flip(v, d):
    return 1 - v if d else v


def mo(v, m):
    return pl.multiple_of(v, m)


(B_X, B_COT, B_WQ, B_WO, B_WU, B_WD, B_QB, B_UB, B_QKV, B_P, B_ATT, B_OS,
 B_OR, B_N1, B_N2, B_R1, B_R2, B_MID, B_ACT, B_SL, B_S1, B_V1, B_S2, B_V2,
 B_KP, B_Y, B_DF, B_DA, B_GD, B_GU, B_GO, B_GQ, B_ZSD, B_ZSU, B_ZSO, B_ZSQ,
 B_ZAD, B_ZAU, B_ZAO, B_ZAQ, B_ZBD, B_ZBU, B_ZBO, B_ZBQ, B_CLN, B_CLR, B_CLC, B_CLS,
 B_CLD, B_CLP, B_CFW, B_CF, B_YQ, B_T96, B_SP, B_BGC, B_PV, B_BG, B_BGS, B_BGR,
 B_BGA, B_BGB, B_CM, B_GA, B_CG, B_DAT) = range(66)


def scratch_list():
    s = []

    def add(name, t, shape, dtype):
        s.append(((name, t), pltpu.VMEM(shape, dtype)))

    for t, T in enumerate(ROWS):
        add(B_X, t, (2 * T, D), BF)
        add(B_COT, t, (T, D), BF)
        add(B_WQ, t, (D, 3 * HALF), BF)
        add(B_WO, t, (HALF, D), BF)
        add(B_WU, t, (D, FFN), BF)
        add(B_WD, t, (FFN, D), BF)
        add(B_QB, t, (8, 3 * HALF), F32)
        add(B_UB, t, (8, FFN), F32)
        add(B_QKV, t, (2 * T, 3 * HALF), BF)
        add(B_P, t, (12, T, T), F32)
        add(B_ATT, t, (2 * T, HALF), BF)
        add(B_OS, t, (T, D), BF)
        add(B_OR, t, (T, D), BF)
        add(B_N1, t, (T, D), F32)
        add(B_N2, t, (T, D), F32)
        add(B_R1, t, (T, 128), F32)
        add(B_R2, t, (T, 128), F32)
        add(B_MID, t, (4 * T, D), BF)
        add(B_ACT, t, (4 * T, FFN), BF)
        add(B_SL, t, (4 * T, FFN), BF)
        add(B_S1, t, (2, T, D), BF)
        add(B_V1, t, (2, T, D), BF)
        add(B_S2, t, (T, D), BF)
        add(B_V2, t, (T, D), BF)
        add(B_KP, t, (2, T, D), F32)
        add(B_Y, t, (T, D), BF)
        add(B_DF, t, (4 * T, D), BF)
        add(B_DA, t, (2 * T, D), BF)
        add(B_DAT, t, (2 * T, HALF), BF)
        add(B_GD, t, (HALF, D), BF)
        add(B_GU, t, (8, 96, FFN), BF)
        add(B_GO, t, (4, 96, D), BF)
        add(B_GQ, t, (4, 96, 3 * HALF), BF)
        add(B_YQ, t, (HALF, 3 * HALF), BF)
        for first in (B_ZSD, B_ZAD, B_ZBD):
            add(first, t, (HALF, D), BF)
            add(first + 1, t, (96, 4 * D), BF)
            add(first + 2, t, (96, D), BF)
            add(first + 3, t, (96, 3 * D), BF)
    for t in (0, 1):
        add(B_CLN, t, (8, D), F32)
        add(B_CLR, t, (8, 128), F32)
        add(B_CLC, t, (8, D), F32)
        add(B_CLS, t, (16, FFN), BF)
        add(B_CLD, t, (16, D), F32)
        add(B_CLP, t, (16, FFN), F32)
    add(B_CFW, 0, (16, D), F32)
    add(B_CF, 0, (4, 16, D), BF)
    add(B_T96, 0, (16, HALF), F32)
    add(B_SP, 0, (8, 16, HALF), BF)
    add(B_PV, 0, (32, D), F32)
    add(B_BG, 0, (32, D), F32)
    add(B_BGC, 0, (8, 16, HALF), BF)
    add(B_BGR, 0, (8, 16, HALF), BF)
    add(B_BGS, 0, (16, HALF), F32)
    add(B_BGA, 0, (16, HALF), F32)
    add(B_BGB, 0, (16, HALF), F32)
    add(B_CM, 0, (16, 512), BF)
    add(B_GA, 0, (32, 16, 512), BF)
    add(B_CG, 0, (2, 16, D), F32)
    return s


def fused_kernel(*refs):
    (i_x0, i_x1, i_cot0, i_cot1, i_qkvw, i_outw, i_upw, i_dnw, i_qvb, i_ob, i_ub, i_db, i_gn, i_sf, i_cnt, i_pos,
     o_loss, o_y0, o_y1, o_gx0, o_gx1, o_oq, o_oo, o_ou, o_od, o_obg) = refs[:26]
    held = {key: ref for (key, _), ref in zip(scratch_list(), refs[26:])}
    sems = refs[-1]

    def g(name, t):
        return held[(name, t)]

    rep = lax.axis_index("rep")
    s = lax.axis_index("shard")
    y = s // 4
    x = (s // 2) % 2
    c = s % 2
    x_in = (i_x0, i_x1)
    cot_in = (i_cot0, i_cot1)

    def sem(name, t, side):
        return sems.at[4 * name + 2 * t + side]

    def sh(yy, xx, cc):
        return yy * 4 + xx * 2 + cc

    def send(src, dst, name, t, dev):
        pltpu.make_async_remote_copy(src, dst, send_sem=sem(name, t, 1), recv_sem=sem(name, t, 0),
                                     device_id=dev, device_id_type=MESH).start()

    def local(src, dst, name, t, side=0):
        pltpu.make_async_copy(src, dst, sem(name, t, side)).start()

    def wait(ref, name, t, side=0):
        pltpu.make_async_copy(ref, ref, sem(name, t, side)).wait()

    def peer(d):
        return flip(y, d[0]), flip(x, d[1]), flip(c, d[2])

    sib = (rep, sh(y, x, 1 - c))
    ypeer = (rep, sh(1 - y, x, c))
    xpeer = (rep, sh(y, 1 - x, c))

    bar = pltpu.get_barrier_semaphore()
    for d in NEIGH:
        pl.semaphore_signal(bar, 1, device_id=(rep, sh(*peer(d))), device_id_type=MESH)
    for k in (1, 2, 3):
        pl.semaphore_signal(bar, 1, device_id=((rep + k) % 4, s), device_id_type=MESH)

    T96, SP, PV = (g(b, 0) for b in (B_T96, B_SP, B_PV))
    T96[...] = jnp.zeros((16, HALF), F32)
    T96[0:2, 0:96] = i_ob[...].astype(F32)
    T96[2:4, 0:96] = i_db[...].astype(F32)
    for t in (0, 1):
        for k in (0, 1):
            T96[4 + 2 * t + k:5 + 2 * t + k, 0:96] = i_gn[t, k:k + 1, :].astype(F32)
            T96[8 + 2 * t + k:9 + 2 * t + k, 0:96] = i_sf[t, k:k + 1, :].astype(F32)
    T96[0:2, 128:320] = i_qvb[...].astype(F32)
    T96[12:14, :] = i_ub[...].astype(F32)
    SP[s] = T96[...].astype(BF)

    def place(n, w, at):
        i = lax.broadcasted_iota(jnp.int32, (n, D), 0)
        j = lax.broadcasted_iota(jnp.int32, (n, D), 1)
        return ((j == i + at) & (i < w)).astype(F32).astype(BF)

    pl.semaphore_wait(bar, 10)

    half = rep % 2
    zpair = (rep + 1 - 2 * half, s)
    for d in NEIGH:
        send(SP.at[s], SP.at[s], S_SMALL, 0, (rep, sh(*peer(d))))
    rows96 = pl.ds(mo(s * 96, 32), 96)
    half48 = pl.ds(mo(half * 48, 16), 48)

    def send_x(t):
        T = ROWS[t]
        own = g(B_X, t).at[pl.ds(mo(c * T, 128), T)]
        send(x_in[t], own, S_X, t, sib)
        local(x_in[t], own, S_X, t)

    def rows48(owner):
        return pl.ds(mo(owner * 96 + half * 48, 16), 48)

    def send_cols(t, src, dst, pieces, far, near):
        for k in range(len(pieces((y, x, c)))):
            for d in NEIGH + ((0, 0, 0),):
                p = peer(d)
                cols, to = pl.ds(mo(pieces(p)[k], 128), HALF), pl.ds(k * HALF, HALF)
                if d[0] + d[1]:
                    send(src.at[t, half48, cols], dst.at[rows48(s), to], far + k, t, (rep, sh(*p)))
                elif d[2]:
                    send(src.at[t, :, cols], dst.at[rows96, to], near, t, sib)
                else:
                    local(src.at[t, :, cols], dst.at[rows96, to], near, t)

    def send_qkv(t):
        send_cols(t, i_qkvw, g(B_WQ, t), lambda p: [part * D + p[2] * HALF for part in range(3)], S_QKV, S_QKVC)

    def send_up(t):
        send_cols(t, i_upw, g(B_WU, t), lambda p: [HALF * (4 * p[0] + 2 * xx + p[2]) for xx in (0, 1)], S_UP, S_UPC)

    def part_of(buf, rows, k):
        return buf.at[pl.ds(0, rows), pl.ds(k * HALF, HALF)]

    def forward_cols(t, buf, k, far, pair):
        wait(part_of(buf, 288, k), far + k, t)
        for d in NEIGH:
            if d[0] + d[1]:
                piece = buf.at[rows48(sh(*peer(d))), pl.ds(k * HALF, HALF)]
                send(piece, piece, pair + k, t, zpair)

    def send_out(t):
        WO = g(B_WO, t)
        for dy in (0, 1):
            for dx in (0, 1):
                dev = (rep, sh(flip(y, dy), flip(x, dx), y))
                if dy + dx:
                    send(i_outw.at[t, half48], WO.at[rows48(x * 2 + c)], S_OUT, t, dev)
                else:
                    dst = WO.at[pl.ds(mo((x * 2 + c) * 96, 32), 96)]

                    @pl.when(c == y)
                    def _():
                        local(i_outw.at[t], dst, S_OUTC, t)

                    @pl.when(c != y)
                    def _():
                        send(i_outw.at[t], dst, S_OUTC, t, dev)

    def forward_out(t):
        WO = g(B_WO, t)

        def go(xs):
            for xx in xs:
                for cc in (0, 1):
                    piece = WO.at[rows48(xx * 2 + cc)]
                    send(piece, piece, S_OUTZ, t, zpair)

        @pl.when(c == y)
        def _():
            wait(WO.at[pl.ds(0, 96)], S_OUT, t)
            go((1 - x,))

        @pl.when(c != y)
        def _():
            wait(WO.at[pl.ds(0, 192)], S_OUT, t)
            go((0, 1))

    def whole_out(t):
        WO = g(B_WO, t)

        @pl.when(c == y)
        def _():
            wait(WO.at[pl.ds(0, 192)], S_OUTC, t)
            wait(WO.at[pl.ds(0, 96)], S_OUTZ, t)

        @pl.when(c != y)
        def _():
            wait(WO.at[pl.ds(0, 192)], S_OUTZ, t)

    def send_dn(t):
        dst = g(B_WD, t).at[pl.ds(mo(x * HALF, 128), HALF)]
        send(i_dnw.at[t], dst, S_DN, t, xpeer)
        local(i_dnw.at[t], dst, S_DN, t)

    for t in (1, 0):
        send_x(t)
        send_qkv(t)
        send_out(t)
    send_up(1)
    send_dn(1)
    for t in (0, 1):
        local(cot_in[t], g(B_COT, t), S_COT, 0, t)

    wait(SP.at[pl.ds(0, 7)], S_SMALL, 0)
    low96 = jnp.zeros((16, D), F32)
    low192 = [jnp.zeros((16, D), F32) for _ in (0, 1)]
    for k in range(8):
        low96 = low96 + nn(SP[k, :, 0:128], place(128, 96, 96 * k))
        low192[k // 4] = low192[k // 4] + nn(SP[k, :, 128:384], place(256, 192, 192 * (k % 4)))
    PV[0:16, :] = low96
    PV[12:14, :] = low192[0][0:2, :]
    PV[14:16, :] = low192[1][0:2, :]
    for k in range(8):
        for t in (0, 1):
            at, lanes = 16 + 4 * t + k // 2, slice(k % 2 * HALF, (k % 2 + 1) * HALF)
            PV[at:at + 1, lanes] = SP[k].astype(F32)[12 + t:13 + t, :]
    R_OB, R_DB, R_GN, R_SF, R_QB, R_VB, R_UB = 0, 2, 4, 8, 12, 14, 16

    def prow(k):
        return PV[k:k + 1, :]

    lane_half = pl.ds(mo(c * HALF, 128), HALF)
    for t in (0, 1):
        g(B_QB, t)[...] = jnp.zeros((8, 3 * HALF), F32)
        g(B_QB, t)[0:1, 0:HALF] = PV[R_QB + t:R_QB + t + 1, lane_half]
        g(B_QB, t)[0:1, 2 * HALF:] = PV[R_VB + t:R_VB + t + 1, lane_half]
        for xx in (0, 1):
            at = R_UB + 4 * t + xx
            lo, hi = PV[at:at + 1, lane_half], PV[at + 2:at + 3, lane_half]
            g(B_UB, t)[0:1, xx * HALF:(xx + 1) * HALF] = jnp.where(jnp.full((1, HALF), y) == 0, lo, hi)

    def same_part(t, grp):
        T = ROWS[t]
        shift = 5 if t == 0 else 6
        ri = lax.broadcasted_iota(jnp.int32, (T, T), 0) >> shift
        ci = lax.broadcasted_iota(jnp.int32, (T, T), 1) >> shift
        m = ri == ci
        if t == 1:
            m = m | (jnp.full((T, T), i_cnt[rep * 8 + (s // 2) * 2 + grp]) > 0)
        return m

    lane_lo = lax.broadcasted_iota(jnp.int32, (1, 128), 1) < 64
    mask_a = lane_lo.astype(F32).astype(BF)
    mask_b = (1.0 - lane_lo.astype(F32)).astype(BF)

    def lnfwd(first, gain, shift):
        mean = jnp.mean(first, axis=-1, keepdims=True)
        cen = first - mean
        inv = lax.rsqrt(jnp.mean(cen * cen, axis=-1, keepdims=True) + LN_EPS)
        n = cen * inv
        return n, inv, n * gain + shift

    CH = 64

    def project(t, k):
        X, WQ = g(B_X, t), g(B_WQ, t)
        if k == 0:
            wait(X, S_X, t)
            wait(WQ.at[pl.ds(0, 192)], S_QKVC, t)
        wait(part_of(WQ, 288, k), S_QKVZ + k, t)
        cols = slice(k * HALF, (k + 1) * HALF)
        g(B_QKV, t)[:, cols] = (nn(X[...], WQ[:, cols]) + g(B_QB, t)[0:1, cols]).astype(BF)

    def attention(t):
        T = ROWS[t]
        X, WQ, QKV, P, ATT = g(B_X, t), g(B_WQ, t), g(B_QKV, t), g(B_P, t), g(B_ATT, t)
        @pl.loop(0, 2)
        def _(grp):
            rows = pl.ds(mo(grp * T, 128), T)
            m = same_part(t, grp)

            @pl.loop(0, 3)
            def _(hp):
                q = QKV[rows, pl.ds(mo(hp * 128, 128), 128)]
                k = QKV[rows, pl.ds(mo(HALF + hp * 128, 128), 128)]
                val = QKV[rows, pl.ds(mo(2 * HALF + hp * 128, 128), 128)]
                outs = []
                for h, msk in ((0, mask_a), (1, mask_b)):
                    sc = jnp.where(m, nt(q * msk, k) * (1.0 / math.sqrt(HD)), NEG_FILL)
                    mx = jnp.max(sc, axis=-1, keepdims=True)
                    e = jnp.exp(sc - mx)
                    p = e * (1.0 / jnp.sum(e, axis=-1, keepdims=True))
                    P[grp * 6 + hp * 2 + h] = p
                    outs.append(nn(p.astype(BF), val))
                ATT[rows, pl.ds(mo(hp * 128, 128), 128)] = jnp.where(lane_lo, outs[0], outs[1]).astype(BF)

        whole_out(t)
        g(B_OS, t)[...] = nn(ATT[pl.ds(mo((1 - c) * T, 128), T), :], g(B_WO, t)[...]).astype(BF)
        send(g(B_OS, t), g(B_OR, t), S_OP, t, sib)
        g(B_KP, t)[0] = nn(ATT[pl.ds(mo(c * T, 128), T), :], g(B_WO, t)[...])
        wait(g(B_OR, t), S_OP, t)
        me4 = (2 * y + c) * T
        ob, gain, shift = prow(R_OB + t), prow(R_GN + 2 * t), prow(R_SF + 2 * t)

        @pl.loop(0, T // CH)
        def _(i):
            r = pl.ds(mo(i * CH, CH), CH)
            first = (X[pl.ds(mo(c * T + i * CH, CH), CH), :].astype(F32) + g(B_KP, t)[0, r, :]
                     + g(B_OR, t)[r, :].astype(F32) + ob)
            n, inv, mid = lnfwd(first, gain, shift)
            g(B_N1, t)[r, :] = n
            g(B_R1, t)[r, :] = jnp.broadcast_to(inv, (CH, 128))
            g(B_MID, t)[pl.ds(mo(me4 + i * CH, CH), CH), :] = mid.astype(BF)

        gather_rows(t, B_MID, S_MY, S_MC, S_MF)

    def slot_rows(t, yy, cc):
        T = ROWS[t]
        return pl.ds(mo((2 * yy + cc) * T, 128), T)

    def gather_rows(t, buf, ny, nc, nf):
        own = g(buf, t).at[slot_rows(t, y, c)]
        send(own, own, ny, t, ypeer)
        send(own, own, nc, t, sib)

    def gather_near(t, buf, nc):
        wait(g(buf, t).at[slot_rows(t, y, 1 - c)], nc, t)

    def gather_forward(t, buf, ny, nf):
        got = g(buf, t).at[slot_rows(t, 1 - y, c)]
        wait(got, ny, t)
        send(got, got, nf, t, sib)

    def gather_far(t, buf, nf):
        wait(g(buf, t).at[slot_rows(t, 1 - y, 1 - c)], nf, t)

    def gather_sent(t, buf, ny, nc, nf):
        own = g(buf, t).at[slot_rows(t, y, c)]
        wait(own, ny, t, 1)
        wait(own, nc, t, 1)
        wait(own, nf, t, 1)

    def up_pair(t, yy):
        T = ROWS[t]
        rows = pl.ds(mo(2 * yy * T, 128), 2 * T)

        @pl.loop(0, 3)
        def _(j):
            cols = pl.ds(mo(j * 256, 128), 256)
            pre = nn(g(B_MID, t)[rows, :], g(B_WU, t)[:, cols]) + g(B_UB, t)[0:1, cols]
            cdf = 0.5 * (1.0 + lax.erf(pre * INV_ROOT_TWO))
            g(B_ACT, t)[rows, cols] = (pre * cdf).astype(BF)
            g(B_SL, t)[rows, cols] = (cdf + pre * jnp.exp(-0.5 * pre * pre) * INV_ROOT_TWO_PI).astype(BF)

    def scatter_partial(t, part, n1a, n1b, n2):
        S1, V1, S2, V2, KP = g(B_S1, t), g(B_V1, t), g(B_S2, t), g(B_V2, t), g(B_KP, t)
        S1[0] = part(slot_rows(t, 1 - y, 1 - c)).astype(BF)
        send(S1.at[0], V1.at[0], n1a, t, sib)
        KP[0] = part(slot_rows(t, 1 - y, c))
        S1[1] = part(slot_rows(t, y, 1 - c)).astype(BF)
        send(S1.at[1], V1.at[1], n1b, t, sib)
        wait(V1.at[0], n1a, t)
        S2[...] = (KP[0] + V1[0].astype(F32)).astype(BF)
        send(S2, V2, n2, t, ypeer)
        KP[1] = part(slot_rows(t, y, c))

    def scatter_finish(t, n1b, n2):
        wait(g(B_V1, t).at[1], n1b, t)
        wait(g(B_V2, t), n2, t)

    def scatter_sent(t, n1a, n1b, n2):
        wait(g(B_S1, t).at[0], n1a, t, 1)
        wait(g(B_S1, t).at[1], n1b, t, 1)
        wait(g(B_S2, t), n2, t, 1)

    def summed(t, r):
        return g(B_KP, t)[1, r, :] + g(B_V1, t)[1, r, :].astype(F32) + g(B_V2, t)[r, :].astype(F32)

    def ffn(t):
        gather_near(t, B_MID, S_MC)
        gather_forward(t, B_MID, S_MY, S_MF)
        wait(g(B_WU, t).at[pl.ds(0, 192)], S_UPC, t)
        for k in (0, 1):
            wait(part_of(g(B_WU, t), 288, k), S_UPZ + k, t)
        up_pair(t, y)
        gather_far(t, B_MID, S_MF)
        up_pair(t, 1 - y)
        T = ROWS[t]
        r = lax.broadcasted_iota(jnp.int32, (16, 4 * T), 0)
        j = lax.broadcasted_iota(jnp.int32, (16, 4 * T), 1)
        at_cls = (j == (r >> 2) * T + (r & 3) * (32, 64)[t]).astype(F32).astype(BF)
        g(B_CLS, t)[...] = nn(at_cls, g(B_SL, t)[...]).astype(BF)
        wait(g(B_WD, t), S_DN, t)
        scatter_partial(t, lambda rows: nn(g(B_ACT, t)[rows, :], g(B_WD, t)[...]), S_F1A, S_F1B, S_F2)

    def ffn_end(t):
        T = ROWS[t]
        scatter_finish(t, S_F1B, S_F2)
        db = prow(R_DB + t)
        g0, g1, s0, s1 = (prow(base + 2 * t + k) for base in (R_GN, R_SF) for k in (0, 1))

        @pl.loop(0, T // CH)
        def _(i):
            r = pl.ds(mo(i * CH, CH), CH)
            second = g(B_N1, t)[r, :] * g0 + s0 + summed(t, r) + db
            n, inv, res = lnfwd(second, g1, s1)
            g(B_N2, t)[r, :] = n
            g(B_R2, t)[r, :] = jnp.broadcast_to(inv, (CH, 128))
            g(B_Y, t)[r, :] = res.astype(BF)

        local(g(B_Y, t), (o_y0, o_y1)[t], S_FIN, 0, t)

    def forward_qkv(t, k):
        forward_cols(t, g(B_WQ, t), k, S_QKV, S_QKVZ)

    def forward_up(t):
        for k in (0, 1):
            forward_cols(t, g(B_WU, t), k, S_UP, S_UPZ)

    for k in range(3):
        forward_qkv(1, k)
    forward_out(1)
    for k in range(3):
        project(1, k)
        forward_qkv(0, k)
    attention(1)
    send_up(0)
    send_dn(0)
    forward_out(0)
    forward_up(1)
    for k in range(3):
        project(0, k)
    attention(0)
    forward_up(0)
    def fold(a):
        return jnp.sum(a.reshape(CH // 8, 8, D), axis=0)

    def put_bias(k, row):
        g(B_BG, 0)[k:k + 1, :] = row

    def ln_back(t, din, nrm, inv, gain):
        gg = din * gain
        m1 = jnp.mean(gg, axis=-1, keepdims=True)
        m2 = jnp.mean(gg * nrm, axis=-1, keepdims=True)
        return inv * (gg - m1 - nrm * m2)

    steps = (32, 64)

    def out_back(t):
        T = ROWS[t]
        wait(g(B_COT, t), S_COT, 0, t)
        for i in range(4):
            row = slice(i * steps[t], i * steps[t] + 1)
            g(B_CLN, t)[i:i + 1, :] = g(B_N2, t)[row, :]
            g(B_CLR, t)[i:i + 1, :] = g(B_R2, t)[row, :]
            g(B_CLC, t)[i:i + 1, :] = g(B_COT, t)[row, :].astype(F32)
        gain = prow(R_GN + 2 * t + 1)
        me4 = (2 * y + c) * T
        zero = jnp.zeros((8, D), F32)

        def body(i, acc):
            r = pl.ds(mo(i * CH, CH), CH)
            dout = g(B_COT, t)[r, :].astype(F32)
            nrm = g(B_N2, t)[r, :]
            dsec = ln_back(t, dout, nrm, g(B_R2, t)[r, 0:1], gain)
            g(B_N2, t)[r, :] = dsec
            g(B_DF, t)[pl.ds(mo(me4 + i * CH, CH), CH), :] = dsec.astype(BF)
            return (acc[0] + fold(dout * nrm), acc[1] + fold(dout))

        acc = lax.fori_loop(0, T // CH, body, (zero, zero))
        for k, a in zip((R_GN + 2 * t + 1, R_SF + 2 * t + 1), acc):
            put_bias(k, jnp.sum(a, axis=0, keepdims=True))

    def cls_back(t):
        dcls = g(B_CG, 0)[t, 0:4, :]
        nrm = g(B_CLN, t)[0:4, :]
        dsec = ln_back(t, g(B_CLC, t)[0:4, :] + dcls, nrm, g(B_CLR, t)[0:4, 0:1], prow(R_GN + 2 * t + 1))
        for i in range(4):
            g(B_N2, t)[i * steps[t]:i * steps[t] + 1, :] = dsec[i:i + 1, :]
        g(B_CFW, 0)[4 * t:4 * t + 4, :] = dsec
        for k, a in ((R_GN + 2 * t + 1, dcls * nrm), (R_SF + 2 * t + 1, dcls)):
            put_bias(k, g(B_BG, 0)[k:k + 1, :] + jnp.sum(a, axis=0, keepdims=True))

    def cls_place(t):
        T = ROWS[t]
        r = lax.broadcasted_iota(jnp.int32, (16, 64), 0)
        j = lax.broadcasted_iota(jnp.int32, (16, 64), 1)
        which = (j == (r >> 2) * 16 + 4 * t + (r & 3)).astype(F32).astype(BF)
        rows = nn(which, g(B_CF, 0)[...].reshape(64, D))
        g(B_CLD, t)[...] = rows
        da = nt(rows.astype(BF), g(B_WD, t)[...])
        g(B_CLP, t)[...] = da * g(B_CLS, t)[...].astype(F32)
        top = lax.broadcasted_iota(jnp.int32, (16, 1), 0) == 0
        for slot in range(4):
            for i in range(4):
                tile = pl.ds(slot * T + i * steps[t], 16)
                k = slot * 4 + i
                for buf, new in ((g(B_DF, t), g(B_CLD, t)), (g(B_SL, t), g(B_CLP, t))):
                    buf[tile, :] = jnp.where(top, new[k:k + 1, :], buf[tile, :].astype(F32)).astype(BF)

    def down_pair(t, yy):
        T = ROWS[t]
        rows = pl.ds(mo(2 * yy * T, 128), 2 * T)

        @pl.loop(0, 3)
        def _(j):
            cols = pl.ds(mo(j * 256, 128), 256)
            da = nt(g(B_DF, t)[rows, :], g(B_WD, t)[cols, :])
            g(B_SL, t)[rows, cols] = (da * g(B_SL, t)[rows, cols].astype(F32)).astype(BF)

    def pre_back(t):
        gather_near(t, B_DF, S_DC)
        gather_forward(t, B_DF, S_DY, S_DF)
        down_pair(t, y)
        gather_far(t, B_DF, S_DF)
        down_pair(t, 1 - y)

    def ffn_back(t):
        gather_sent(t, B_DF, S_DY, S_DC, S_DF)
        cls_place(t)
        ACT, DF, WD, WU = g(B_ACT, t), g(B_DF, t), g(B_WD, t), g(B_WU, t)
        for k in range(3):
            cols = pl.ds(mo((1 - x) * HALF + 128 * k, 128), 128)
            WD[cols, :] = tn(ACT[:, cols], DF[...]).astype(BF)
            send(WD.at[cols], g(B_GD, t).at[pl.ds(128 * k, 128)], S_GD + k, t, xpeer)

        scatter_partial(t, lambda rows: nt(g(B_SL, t)[rows, :], g(B_WU, t)[...]), S_D1A, S_D1B, S_D2)
        own_sum = nn(jnp.ones((8, ROWS[t]), F32).astype(BF), g(B_DF, t)[slot_rows(t, y, c), :])
        put_bias(R_DB + t, own_sum[0:1, :])
        ones = jnp.ones((8, 4 * ROWS[t]), F32).astype(BF)
        sums = nn(ones, g(B_SL, t)[...])[0:1, :]
        for xx in (0, 1):
            part = sums[:, xx * HALF:(xx + 1) * HALF]
            at = R_UB + 4 * t + xx

            @pl.when(y == 0)
            def _():
                g(B_BG, 0)[at:at + 1, lane_half] = part

            @pl.when(y == 1)
            def _():
                g(B_BG, 0)[at + 2:at + 3, lane_half] = part

        cols = pl.ds(mo(x * HALF, 128), HALF)
        WD[cols, :] = tn(ACT[:, cols], DF[...]).astype(BF)
        for dy in (1, 0):
            @pl.loop(0, 3)
            def _(j):
                cols = pl.ds(mo(flip(y, dy) * HALF + j * 128, 128), 128)
                WU[cols, :] = tn(g(B_MID, t)[:, cols], g(B_SL, t)[...]).astype(BF)

            for d in NEIGH:
                if d[0] == dy:
                    dest = sh(*peer(d))
                    send(WU.at[pl.ds(mo(96 * dest, 32), 96)], g(B_GU, t).at[s], S_GU1 - dy, t, (rep, dest))
        local(WU.at[rows96], g(B_GU, t).at[s], S_GU1, t)

    g(B_BG, 0)[...] = jnp.zeros((32, D), F32)
    g(B_CFW, 0)[...] = jnp.zeros((16, D), F32)
    ffn(1)
    ffn(0)
    ffn_end(1)
    out_back(1)
    gather_rows(1, B_DF, S_DY, S_DC, S_DF)
    ffn_end(0)

    def pick(T, lo, step):
        ri = lax.broadcasted_iota(jnp.int32, (16, T), 0) & 7
        ci = lax.broadcasted_iota(jnp.int32, (16, T), 1)
        return (((ri & 4) == lo) & (ci == (ri & 3) * step)).astype(F32).astype(BF)

    both = nn(pick(128, 0, 32), g(B_Y, 0)[...]) + nn(pick(256, 4, 64), g(B_Y, 1)[...])
    top = lax.broadcasted_iota(jnp.int32, (16, HALF), 0) < 8
    g(B_CM, 0)[:, :HALF] = jnp.where(top, both[:, :HALF], both[:, HALF:]).astype(BF)
    ri = lax.broadcasted_iota(jnp.int32, (16, 128), 0)
    pos = jnp.zeros((16, 128), jnp.int32)
    for i in range(4):
        pos = jnp.where(ri == i, i_pos[i], pos)
    g(B_CM, 0)[:, HALF:] = pos.astype(F32).astype(BF)
    mine = g(B_GA, 0).at[s * 4 + rep]
    for k in (1, 2, 3):
        send(g(B_CM, 0), mine, S_CZ, 0, ((rep + k) % 4, s))
    g(B_GA, 0)[s * 4 + rep] = g(B_CM, 0)[...]
    out_back(0)
    wait(g(B_GA, 0).at[pl.ds(0, 3)], S_CZ, 0)
    four = g(B_GA, 0).at[pl.ds(s * 4, 4)]
    for d in NEIGH:
        send(four, four, S_CP, 0, (rep, sh(*peer(d))))
    gather_rows(0, B_DF, S_DY, S_DC, S_DF)

    for t in (0, 1):
        own = g(B_X, t).at[pl.ds(mo(c * ROWS[t], 128), ROWS[t])]
        wait(own, S_X, t, 1)
        for buf, n, far, near, pair in ((g(B_WQ, t), 3, S_QKV, S_QKVC, S_QKVZ), (g(B_WU, t), 2, S_UP, S_UPC, S_UPZ)):
            wait(buf.at[pl.ds(0, 96)], near, t, 1)
            for k in range(n):
                wait(part_of(buf, 288, k), far + k, t, 1)
                wait(part_of(buf, 288, k), pair + k, t, 1)
        wait(g(B_WO, t).at[pl.ds(0, 144)], S_OUT, t, 1)

        @pl.when(c == y)
        def _():
            wait(g(B_WO, t).at[pl.ds(0, 96)], S_OUTZ, t, 1)

        @pl.when(c != y)
        def _():
            wait(g(B_WO, t).at[pl.ds(0, 96)], S_OUTC, t, 1)
            wait(g(B_WO, t).at[pl.ds(0, 192)], S_OUTZ, t, 1)

        wait(g(B_WD, t).at[pl.ds(0, HALF)], S_DN, t, 1)
        wait(g(B_OS, t), S_OP, t, 1)
        gather_sent(t, B_MID, S_MY, S_MC, S_MF)
        scatter_sent(t, S_F1A, S_F1B, S_F2)
    wait(g(B_SP, 0).at[pl.ds(0, 7)], S_SMALL, 0, 1)
    wait(g(B_GA, 0).at[pl.ds(0, 3)], S_CZ, 0, 1)
    pre_back(1)

    wait(g(B_GA, 0).at[pl.ds(0, 28)], S_CP, 0)
    wait(g(B_GA, 0).at[pl.ds(0, 28)], S_CP, 0, 1)

    def pick_all(base):
        ri = lax.broadcasted_iota(jnp.int32, (128, 512), 0)
        ci = lax.broadcasted_iota(jnp.int32, (128, 512), 1)
        blk = ci >> 4
        within = (ci & 15) - base
        row = ((blk & 3) * 8 + (blk >> 2)) * 4 + within
        return ((within >= 0) & (within < 4) & (ri == row)).astype(F32).astype(BF)

    ga = g(B_GA, 0)[...].reshape(512, 512)
    qa_f = nn(pick_all(0), ga)
    qa = qa_f[:, :HALF].astype(BF)
    pa = nn(pick_all(4), ga)[:, :HALF].astype(BF)
    qb = nn(pick_all(8), ga)[:, :HALF].astype(BF)
    pb = nn(pick_all(12), ga)[:, :HALF].astype(BF)
    scale = 2.0 / math.sqrt(D)
    logits = (nt(qa, pa) + nt(qb, pb)) * scale
    lane = lax.broadcasted_iota(jnp.int32, (1, 128), 1)
    cnt = jnp.zeros((1, 128), jnp.int32)
    for k in range(32):
        cnt = jnp.where(lane >> 2 == k, i_cnt[k], cnt)
    masked = jnp.where((cnt <= 0) | (lane & 3 == 0), logits, NEG_FILL)
    mx = jnp.max(masked, axis=1, keepdims=True)
    ex = jnp.exp(masked - mx)
    sm = jnp.sum(ex, axis=1, keepdims=True)
    hit = lax.broadcasted_iota(jnp.int32, (128, 128), 1).astype(F32) == qa_f[:, HALF:]
    ce = mx + jnp.log(sm) - jnp.sum(jnp.where(hit, masked, 0.0), axis=1, keepdims=True)
    o_loss[...] = jnp.broadcast_to(jnp.sum(ce, axis=0, keepdims=True) * (1.0 / 128.0), (8, 128))
    dl = (ex / sm - hit.astype(F32)).astype(BF)
    ri = lax.broadcasted_iota(jnp.int32, (16, 128), 0)
    ci = lax.broadcasted_iota(jnp.int32, (16, 128), 1)
    sel = ((ri < 4) & (ci == ri + 4 * (rep * 8 + s))).astype(F32).astype(BF)
    dlq = nn(sel, dl).astype(BF)
    dlp = nt(sel, dl.T).astype(BF) if False else lax.dot_general(
        sel, dl, (((1,), (1,)), ((), ())), preferred_element_type=F32).astype(BF)
    g(B_CG, 0)[0, :, :HALF] = nn(dlq, pa) * scale
    g(B_CG, 0)[0, :, HALF:] = nn(dlq, pb) * scale
    g(B_CG, 0)[1, :, :HALF] = nn(dlp, qa) * scale
    g(B_CG, 0)[1, :, HALF:] = nn(dlp, qb) * scale

    def mid_back(t):
        T = ROWS[t]
        scatter_finish(t, S_D1B, S_D2)
        gain = prow(R_GN + 2 * t)
        zero = jnp.zeros((8, D), F32)

        def body(i, acc):
            r = pl.ds(mo(i * CH, CH), CH)
            dmid = g(B_N2, t)[r, :] + summed(t, r)
            nrm = g(B_N1, t)[r, :]
            dfirst = ln_back(t, dmid, nrm, g(B_R1, t)[r, 0:1], gain)
            low = dfirst.astype(BF)
            g(B_N1, t)[r, :] = dfirst
            g(B_DA, t)[pl.ds(mo(c * T + i * CH, CH), CH), :] = low
            return (acc[0] + fold(dmid * nrm), acc[1] + fold(dmid), acc[2] + fold(low.astype(F32)))

        acc = lax.fori_loop(0, T // CH, body, (zero, zero, zero))
        own = g(B_DA, t).at[pl.ds(mo(c * T, 128), T)]
        send(own, own, S_DA, t, sib)
        for k, a in zip((R_GN + 2 * t, R_SF + 2 * t, R_OB + t), acc):
            put_bias(k, jnp.sum(a, axis=0, keepdims=True))

    def attention_back(t, point):
        T = ROWS[t]
        QKV, P, ATT, DA, WO, WQ = g(B_QKV, t), g(B_P, t), g(B_ATT, t), g(B_DA, t), g(B_WO, t), g(B_WQ, t)
        wait(DA.at[pl.ds(mo((1 - c) * T, 128), T)], S_DA, t)

        DAT = g(B_DAT, t)
        DAT[...] = nt(DA[...], WO[...]).astype(BF)

        @pl.loop(0, 3)
        def _(j):
            cols = pl.ds(mo(j * 128, 128), 128)
            WO[cols, :] = tn(ATT[:, cols], DA[...]).astype(BF)

        dst = g(B_GO, t).at[y * 2 + x]
        for xx in (0, 1):
            for cc in (0, 1):
                src = WO.at[pl.ds((2 * xx + cc) * 96, 96)]
                dev = sh(c, xx, cc)

                @pl.when(dev == s)
                def _():
                    local(src, dst, S_GO, t)

                @pl.when(dev != s)
                def _():
                    send(src, dst, S_GO, t, (rep, dev))

        point()
        for grp in (0, 1):
            rows = pl.ds(grp * T, T)

            @pl.loop(0, 3)
            def _(hp):
                lanes = pl.ds(mo(hp * 128, 128), 128)
                dat = DAT[rows, lanes]
                qs, ks = lanes, pl.ds(mo(HALF + hp * 128, 128), 128)
                vs = pl.ds(mo(2 * HALF + hp * 128, 128), 128)
                q, k, val = QKV[rows, qs], QKV[rows, ks], QKV[rows, vs]
                dq, dk, dv = [], [], []
                for h, msk in ((0, mask_a), (1, mask_b)):
                    p = P[grp * 6 + hp * 2 + h]
                    dp = nt(dat * msk, val)
                    ds = (p * (dp - jnp.sum(dp * p, axis=-1, keepdims=True))).astype(BF)
                    dv.append(tn(p.astype(BF), dat))
                    dq.append(nn(ds, k))
                    dk.append(tn(ds, q))
                root = 1.0 / math.sqrt(HD)
                QKV[rows, qs] = (jnp.where(lane_lo, dq[0], dq[1]) * root).astype(BF)
                QKV[rows, ks] = (jnp.where(lane_lo, dk[0], dk[1]) * root).astype(BF)
                QKV[rows, vs] = jnp.where(lane_lo, dv[0], dv[1]).astype(BF)

            point()

        g(B_OS, t)[...] = nt(QKV[pl.ds(mo((1 - c) * T, 128), T), :], WQ[...]).astype(BF)
        send(g(B_OS, t), g(B_OR, t), S_DX, t, sib)
        g(B_KP, t)[0] = nt(QKV[pl.ds(mo(c * T, 128), T), :], WQ[...])

        ones = jnp.ones((8, 2 * T), F32).astype(BF)
        sums = nn(ones, QKV[...])[0:1, :]
        g(B_BG, 0)[R_QB + t:R_QB + t + 1, lane_half] = sums[:, :HALF]
        g(B_BG, 0)[R_VB + t:R_VB + t + 1, lane_half] = sums[:, 2 * HALF:]

        if t == 0:
            send_small()
        far_rows = pl.ds(mo((1 - y) * HALF, 128), HALF)
        for k in range(3):
            lanes = slice(k * HALF, (k + 1) * HALF)

            @pl.loop(0, 3)
            def _(j):
                cols = pl.ds(mo(j * 256, 128), 256)
                WQ[cols, lanes] = tn(g(B_X, t)[:, cols], QKV[:, lanes]).astype(BF)

            send(WQ.at[far_rows, pl.ds(k * HALF, HALF)], g(B_YQ, t).at[:, pl.ds(k * HALF, HALF)], S_YQ + k, t, ypeer)
            point()

    def send_small():
        BG, BGC, BGR = (g(b, 0) for b in (B_BG, B_BGC, B_BGR))
        low = BG[...].astype(BF)
        for k in range(8):
            T96[...] = jnp.zeros((16, HALF), F32)
            T96[:, 0:128] = nt(low[0:16, :], place(128, 96, 96 * k))
            at = 12 + 2 * (k // 4)
            T96[0:2, 128:384] = nt(low[0:16, :], place(256, 192, 192 * (k % 4)))[at:at + 2, :]
            for t in (0, 1):
                row = 16 + 4 * t + k // 2
                T96[12 + t:13 + t, :] = BG[row:row + 1, k % 2 * HALF:(k % 2 + 1) * HALF]
            BGC[k] = T96[...].astype(BF)
        for d in NEIGH:
            dest = sh(*peer(d))
            send(BGC.at[dest], BGR.at[s], S_BG, 0, (rep, dest))
        local(BGC.at[s], BGR.at[s], S_BG, 0)

    def relay_qkv(t, k):
        WQ, YQ, lanes = g(B_WQ, t), g(B_YQ, t), pl.ds(k * HALF, HALF)
        wait(YQ.at[:, lanes], S_YQ + k, t)
        for r0 in range(0, HALF, 128):
            r = pl.ds(mo(y * HALF + r0, 128), 128)
            WQ[r, lanes] = (WQ[r, lanes].astype(F32) + YQ[pl.ds(r0, 128), lanes].astype(F32)).astype(BF)
        dst = g(B_GQ, t).at[2 * x + c, :, lanes]
        for dx, dc in ((1, 0), (1, 1), (0, 1), (0, 0)):
            owner = sh(y, flip(x, dx), flip(c, dc))
            src = WQ.at[pl.ds(mo(96 * owner, 32), 96), lanes]
            if dx + dc:
                send(src, dst, S_GQ + k, t, (rep, owner))
            else:
                local(src, dst, S_GQ + k, t)

    def input_back(t):
        T = ROWS[t]
        wait(g(B_OR, t), S_DX, t)

        @pl.loop(0, T // CH)
        def _(i):
            r = pl.ds(mo(i * CH, CH), CH)
            g(B_Y, t)[r, :] = (g(B_N1, t)[r, :] + g(B_KP, t)[0, r, :] + g(B_OR, t)[r, :].astype(F32)).astype(BF)

        local(g(B_Y, t), (o_gx0, o_gx1)[t], S_FIN2, 0, t)

    def make_dn(t, k):
        def each(use):
            wait(g(B_GD, t).at[pl.ds(128 * k, 128)], S_GD + k, t)
            for r0 in (128 * k, 128 * k + 64):
                own = g(B_WD, t)[pl.ds(mo(x * HALF + r0, 64), 64), :].astype(F32)
                use(pl.ds(r0, 64), pl.ds(0, D), own + g(B_GD, t)[pl.ds(r0, 64), :].astype(F32))
        return each

    def make_up(t, dy, xx):
        GU = g(B_GU, t)
        yy = flip(y, dy)

        def each(use):
            if xx == 0:
                wait(GU.at[pl.ds(0, 4)], S_GU1 - dy, t)
            cols = slice(xx * HALF, (xx + 1) * HALF)
            for cc in (0, 1):
                both = GU[sh(yy, 0, cc), :, cols].astype(F32) + GU[sh(yy, 1, cc), :, cols].astype(F32)
                use(pl.ds(0, 96), pl.ds(mo((4 * yy + 2 * xx + cc) * HALF, 128), HALF), both)
        return each

    def make_out(t):
        GO = g(B_GO, t)

        def each(use):
            wait(GO, S_GO, t)
            tot = GO[0].astype(F32)
            for k in range(1, 4):
                tot = tot + GO[k].astype(F32)
            use(pl.ds(0, 96), pl.ds(0, D), tot)
        return each

    def make_qkv(t, part):
        GQ = g(B_GQ, t)

        def each(use):
            cols = slice(part * HALF, (part + 1) * HALF)
            wait(GQ.at[:, :, pl.ds(part * HALF, HALF)], S_GQ + part, t)
            for cc in (0, 1):
                tot = GQ[cc, :, cols].astype(F32) + GQ[2 + cc, :, cols].astype(F32)
                use(pl.ds(0, 96), pl.ds(part * D + cc * HALF, HALF), tot)
        return each

    def each_small(use):
        BGR = g(B_BGR, 0)
        wait(BGR, S_BG, 0)
        tot = BGR[0].astype(F32)
        for k in range(1, 8):
            tot = tot + BGR[k].astype(F32)
        use(pl.ds(0, 16), pl.ds(0, HALF), tot)

    is_end = (rep == 0) | (rep == 3)
    units = []

    def unit(kind, t, each, out, rows, cols):
        if kind == 4:
            bufs = (B_BGS, B_BGA, B_BGB)
        else:
            bufs = (B_ZSD + kind, B_ZAD + kind, B_ZBD + kind)
        units.append((len(units), tuple(g(b, t) for b in bufs), each, out, rows, cols))

    def add_ffn(t):
        for k in range(3):
            unit(0, t, make_dn(t, k), o_od.at[t], (128 * k, 128), (0, D))
        for dy in (1, 0):
            for xx in (0, 1):
                at = mo((2 * flip(y, dy) + xx) * D, 128)
                unit(1, t, make_up(t, dy, xx), o_ou.at[t], (0, 96), (at, D))

    def add_qkv(t):
        for part in range(3):
            unit(3, t, make_qkv(t, part), o_oq.at[t], (0, 96), (part * D, D))

    add_ffn(1)
    add_ffn(0)
    unit(2, 1, make_out(1), o_oo.at[1], (0, 96), (0, D))
    unit(2, 0, make_out(0), o_oo.at[0], (0, 96), (0, D))
    add_qkv(1)
    unit(4, 0, each_small, o_obg, (0, 16), (0, HALF))
    add_qkv(0)
    assert len(units) == N_UNITS

    def hop(which, u):
        at = which * N_UNITS + u[0]
        return S_Z + at // 2, at % 2

    def view(ref, u):
        return ref.at[pl.ds(*u[4]), pl.ds(*u[5])]

    def ends(u):
        ZS, ZA, ZB = u[1]

        def put(r, cl, val):
            ZS[r, cl] = val.astype(ZS.dtype)

        for end, mid in ((0, 1), (3, 2)):
            @pl.when(rep == end)
            def _():
                u[2](put)
                send(view(ZS, u), view(ZA, u), *hop(0, u), (mid, s))

    def stage_a(u):
        ZS, ZA, ZB = u[1]

        def put_add(r, cl, val):
            ZS[r, cl] = (val + ZA[r, cl].astype(F32)).astype(ZS.dtype)

        for end, mid in ((0, 1), (3, 2)):
            @pl.when(rep == mid)
            def _():
                wait(view(ZA, u), *hop(0, u))
                u[2](put_add)
                send(view(ZS, u), view(ZB, u), *hop(1, u), (3 - mid, s))

    def stage_b(u):
        ZS, ZA, ZB = u[1]
        for end, mid in ((0, 1), (3, 2)):
            @pl.when(rep == mid)
            def _():
                wait(view(ZB, u), *hop(1, u))
                wait(view(ZB, u), *hop(1, u), 1)
                for r0 in range(u[4][0], u[4][0] + u[4][1], 16):
                    r, cl = pl.ds(r0, 16), pl.ds(*u[5])
                    ZS[r, cl] = (ZS[r, cl].astype(F32) + ZB[r, cl].astype(F32)).astype(ZS.dtype)
                send(view(ZS, u), view(u[3], u), *hop(2, u), (end, s))
                local(view(ZS, u), view(u[3], u), *hop(2, u))

    done = [0, 0, 0]

    def advance(n0, n1, n2):
        while done[0] < n0 or done[1] < n1 or done[2] < n2:
            for k, (step, n) in enumerate(((ends, n0), (stage_a, n1), (stage_b, n2))):
                if done[k] < n:
                    step(units[done[k]])
                    done[k] += 1

    cls_back(1)
    cls_back(0)
    mine = g(B_CF, 0).at[2 * y + c]
    g(B_CF, 0)[2 * y + c] = g(B_CFW, 0)[...].astype(BF)
    fixers = (ypeer, sib, (rep, sh(1 - y, x, 1 - c)))
    for dev in fixers:
        send(mine, mine, S_CF, 0, dev)
    pre_back(0)
    wait(g(B_CF, 0).at[pl.ds(0, 3)], S_CF, 0)
    for t in (0, 1):
        wait(g(B_Y, t), S_FIN, 0, t)
    ffn_back(1)
    ffn_back(0)
    def point():
        advance(*plan.pop(0))

    plan = PLAN[:]
    point()
    mid_back(1)
    attention_back(1, point)
    mid_back(0)
    attention_back(0, point)
    input_back(1)
    input_back(0)
    point()
    for t in (1, 0):
        for k in range(3):
            relay_qkv(t, k)
            point()
    for k in range(done[0], N_UNITS + 1):
        advance(min(k + 1, N_UNITS), k, k - 1)
    advance(N_UNITS, N_UNITS, N_UNITS)

    for u in units:
        ZS = view(u[1][0], u)
        wait(ZS, *hop(2, u))

        @pl.when(is_end)
        def _():
            wait(ZS, *hop(0, u), 1)

        @pl.when(jnp.logical_not(is_end))
        def _():
            wait(ZS, *hop(2, u), 1)

    for t in (0, 1):
        scatter_sent(t, S_D1A, S_D1B, S_D2)
        wait(g(B_OS, t), S_DA, t, 1)
        wait(g(B_OS, t), S_DX, t, 1)
        for k in range(3):
            wait(g(B_GD, t).at[pl.ds(0, 128)], S_GD + k, t, 1)
        wait(g(B_GU, t).at[pl.ds(0, 4)], S_GU, t, 1)
        wait(g(B_GU, t).at[pl.ds(0, 3)], S_GU1, t, 1)

        @pl.when(c == y)
        def _():
            wait(g(B_GO, t).at[pl.ds(0, 3)], S_GO, t, 1)

        @pl.when(c != y)
        def _():
            wait(g(B_GO, t), S_GO, t, 1)

        for k in range(3):
            wait(g(B_YQ, t).at[:, pl.ds(k * HALF, HALF)], S_YQ + k, t, 1)
            wait(g(B_GQ, t).at[pl.ds(0, 3), :, pl.ds(k * HALF, HALF)], S_GQ + k, t, 1)
        wait(g(B_Y, t), S_FIN2, 0, t)
    wait(g(B_BGR, 0).at[pl.ds(0, 7)], S_BG, 0, 1)
    wait(g(B_CF, 0).at[pl.ds(0, 3)], S_CF, 0, 1)


def fused_call(*args):
    hbm = pl.BlockSpec(memory_space=pl.ANY)
    vm = pl.BlockSpec(memory_space=pltpu.VMEM)
    sm = pl.BlockSpec(memory_space=pltpu.SMEM)
    out_shape = [
        jax.ShapeDtypeStruct((8, 128), F32),
        jax.ShapeDtypeStruct((128, D), BF),
        jax.ShapeDtypeStruct((256, D), BF),
        jax.ShapeDtypeStruct((128, D), BF),
        jax.ShapeDtypeStruct((256, D), BF),
        jax.ShapeDtypeStruct((2, 96, 3 * D), BF),
        jax.ShapeDtypeStruct((2, 96, D), BF),
        jax.ShapeDtypeStruct((2, 96, 4 * D), BF),
        jax.ShapeDtypeStruct((2, HALF, D), BF),
        jax.ShapeDtypeStruct((16, HALF), F32),
    ]
    return pl.pallas_call(
        fused_kernel,
        out_shape=out_shape,
        in_specs=[hbm] * 8 + [vm] * 6 + [sm] * 2,
        out_specs=[vm] + [hbm] * 9,
        scratch_shapes=[shape for _, shape in scratch_list()] + [pltpu.SemaphoreType.DMA((N_SEMS,))],
        compiler_params=pltpu.CompilerParams(collective_id=0, has_side_effects=True, vmem_limit_bytes=VMEM_LIMIT),
        cost_estimate=pl.CostEstimate(flops=18 * 10**9, bytes_accessed=40 * 10**6, transcendentals=4 * 10**6),
    )(*args)


def widen_kernel(*refs):
    loss, y0, y1, gx0, gx1, oq, oo, ou, od, bg = refs[:10]
    r_loss, r_y0, r_y1, r_gx0, r_gx1, r_q, r_qb, r_o, r_ob, r_u, r_ub, r_d, r_db, r_gn, r_sf = refs[10:25]
    low = refs[25:29]
    wide = refs[29:33]
    through = refs[33:37]
    sem_in, sem_out, sem_move, sem_move_out = refs[37:]
    groups = list(zip((oq, ou, od, oo), low, wide, (r_q, r_u, r_d, r_o)))
    reads, writes, moves = [], [], []
    for k, (src, lo, hi, dst) in enumerate(groups):
        for t in (0, 1):
            reads.append(pltpu.make_async_copy(src.at[t], lo.at[t], sem_in.at[2 * k + t]))
            reads[-1].start()
    for k, (src, dst) in enumerate(((y0, r_y0), (y1, r_y1), (gx0, r_gx0), (gx1, r_gx1))):
        moves.append((pltpu.make_async_copy(src, through[k], sem_move.at[k]),
                      pltpu.make_async_copy(through[k], dst, sem_move_out.at[k])))
        moves[-1][0].start()
    r_loss[...] = loss[0:1, 0:1]
    r_ob[...] = bg[0:2, 0:96]
    r_db[...] = bg[2:4, 0:96]
    for t in (0, 1):
        r_gn[t] = bg[4 + 2 * t:6 + 2 * t, 0:96]
        r_sf[t] = bg[8 + 2 * t:10 + 2 * t, 0:96]
    r_qb[...] = bg[0:2, 128:320]
    r_ub[...] = bg[12:14, :]
    for k, (src, lo, hi, dst) in enumerate(groups):
        for t in (0, 1):
            reads[2 * k + t].wait()
            hi[t] = lo[t].astype(F32)
            writes.append(pltpu.make_async_copy(hi.at[t], dst.at[t], sem_out.at[2 * k + t]))
            writes[-1].start()
    for there, onward in moves:
        there.wait()
        onward.start()
    for copy in writes + [onward for there, onward in moves]:
        copy.wait()


def widen_call(*args):
    hbm = pl.BlockSpec(memory_space=pl.ANY)
    vm = pl.BlockSpec(memory_space=pltpu.VMEM)

    def out(dtype, *shape):
        return jax.ShapeDtypeStruct(shape, dtype)

    shapes = [(2, 96, 3 * D), (2, 96, 4 * D), (2, HALF, D), (2, 96, D)]
    return pl.pallas_call(
        widen_kernel,
        out_shape=[out(F32, 1, 1), out(BF, 128, D), out(BF, 256, D), out(BF, 128, D), out(BF, 256, D),
                   out(F32, *shapes[0]), out(F32, 2, 192), out(F32, *shapes[3]), out(F32, 2, 96),
                   out(F32, *shapes[1]), out(F32, 2, HALF), out(F32, *shapes[2]), out(F32, 2, 96),
                   out(F32, 2, 2, 96), out(F32, 2, 2, 96)],
        in_specs=[vm] + [hbm] * 8 + [vm],
        out_specs=[vm, hbm, hbm, hbm, hbm, hbm, vm, hbm, vm, hbm, vm, hbm, vm, vm, vm],
        scratch_shapes=[pltpu.VMEM(shape, BF) for shape in shapes] + [pltpu.VMEM(shape, F32) for shape in shapes]
        + [pltpu.VMEM((rows, D), BF) for rows in ROWS * 2]
        + [pltpu.SemaphoreType.DMA((8,)), pltpu.SemaphoreType.DMA((8,)), pltpu.SemaphoreType.DMA((4,)),
           pltpu.SemaphoreType.DMA((4,))],
        compiler_params=pltpu.CompilerParams(vmem_limit_bytes=VMEM_LIMIT),
    )(*args)


def local_fast(query_tokens, passage_tokens, query_cot, passage_cot, bucket_counts, positives, qkv_weight, qv_bias,
               out_weight, out_bias, up_weight, up_bias, down_weight, down_bias, norm_gains, norm_shifts):
    results = widen_call(*fused_call(
        query_tokens.reshape(128, D), passage_tokens.reshape(256, D),
        query_cot.reshape(128, D), passage_cot.reshape(256, D),
        qkv_weight, out_weight, up_weight, down_weight,
        qv_bias, out_bias, up_bias, down_bias, norm_gains, norm_shifts, bucket_counts, positives))
    loss, y0, y1, gx0, gx1 = results[:5]
    return (loss.reshape(()), y0.reshape(query_tokens.shape), y1.reshape(passage_tokens.shape),
            gx0.reshape(query_tokens.shape), gx1.reshape(passage_tokens.shape), *results[5:])


def solution(mesh):
    in_specs = (
        P(("rep", "shard"), None, None),
        P(("rep", "shard"), None, None),
        P(("rep", "shard"), None, None),
        P(("rep", "shard"), None, None),
        P(),
        P(("rep", "shard")),
        P(None, "shard", None),
        P(None, "shard"),
        P(None, "shard", None),
        P(None, "shard"),
        P(None, "shard", None),
        P(None, "shard"),
        P(None, "shard", None),
        P(None, "shard"),
        P(None, None, "shard"),
        P(None, None, "shard"),
    )
    out_specs = (
        P(),
        P(("rep", "shard"), None, None),
        P(("rep", "shard"), None, None),
        P(("rep", "shard"), None, None),
        P(("rep", "shard"), None, None),
        P(None, "shard", None),
        P(None, "shard"),
        P(None, "shard", None),
        P(None, "shard"),
        P(None, "shard", None),
        P(None, "shard"),
        P(None, "shard", None),
        P(None, "shard"),
        P(None, None, "shard"),
        P(None, None, "shard"),
    )
    small_mesh = (mesh.shape["rep"], mesh.shape["shard"]) == (4, 8)
    step = local_fast if small_mesh else local
    return jax.shard_map(step, mesh=mesh, in_specs=in_specs, out_specs=out_specs, check_vma=False)
```

```python
import functools
import math

import jax
import jax.numpy as jnp
from jax import lax
from jax.experimental import pallas as pl
from jax.experimental.pallas import tpu as pltpu
from jax.sharding import PartitionSpec as P

HD = 64
SHORT = 64


LN_EPS = 1e-05
NEG_FILL = -1e30
INV_ROOT_TWO = 0.7071067811865476
INV_ROOT_TWO_PI = 0.3989422804014327
VMEM_LIMIT = 66 * 1000 * 1000


def for_sending(array):
    return jax.tree.map(lambda a: a.astype(jnp.bfloat16) if a.dtype == jnp.float32 else a, array)


def pick_tower(stacks, tower_index):
    qkv_w, qv_b, out_w, out_b, up_w, up_b, down_w, down_b, gains, shifts = stacks
    return (
        qkv_w[tower_index],
        qv_b[tower_index],
        out_w[tower_index],
        out_b[tower_index],
        up_w[tower_index],
        up_b[tower_index],
        down_w[tower_index],
        down_b[tower_index],
        gains[tower_index].T,
        shifts[tower_index].T,
    )


def fetch_layer(stacks, tower_index):
    return lax.all_gather(for_sending(pick_tower(stacks, tower_index)), "shard", axis=0, tiled=True)


def fetch_again(stacks, tower_index):
    return lax.all_gather(for_sending(pick_tower(stacks, tower_index)), "shard", axis=0, tiled=True)


def normalize(hidden):
    row_mean = jnp.mean(hidden, axis=-1, keepdims=True)
    centred = hidden - row_mean
    inv_std = lax.rsqrt(jnp.mean(centred * centred, axis=-1, keepdims=True) + LN_EPS)
    return (centred * inv_std, inv_std)


def norm_back(grad_in, normed, inv_std):
    return inv_std * (
        grad_in
        - jnp.mean(grad_in, axis=-1, keepdims=True)
        - normed * jnp.mean(grad_in * normed, axis=-1, keepdims=True)
    )


def block_mask(long_flags, length, short_len):
    row_part = lax.broadcasted_iota(jnp.int32, (length, length), 0) // short_len
    col_part = lax.broadcasted_iota(jnp.int32, (length, length), 1) // short_len
    return long_flags[:, None, None] | (row_part == col_part)[None]


def head_scores(head_query, head_key, attn_mask):
    raw_scores = jnp.einsum(
        "slhd,smhd->shlm", head_query, head_key, preferred_element_type=jnp.float32
    ) * (1.0 / math.sqrt(HD))
    return jnp.where(attn_mask[:, None], raw_scores, NEG_FILL)


def layer_forward(tokens, weights, attn_mask):
    qkv_w, qv_b, out_w, out_b, up_w, up_b, down_w, down_b, gains, shifts = weights
    seq_count, length, model_width = tokens.shape
    head_count = model_width // HD
    token_rows = tokens.reshape(seq_count * length, model_width)
    qv_float = qv_b.astype(jnp.float32)
    qkv_bias = jnp.concatenate(
        [qv_float[:model_width], jnp.zeros((model_width,), jnp.float32), qv_float[model_width:]]
    )
    qkv_low = (jnp.dot(token_rows, qkv_w, preferred_element_type=jnp.float32) + qkv_bias).astype(
        jnp.bfloat16
    )
    head_split = qkv_low.reshape(seq_count, length, 3, head_count, HD)
    scores = head_scores(head_split[:, :, 0], head_split[:, :, 1], attn_mask)
    row_max = jnp.max(scores, axis=-1, keepdims=True)
    exp_scores = jnp.exp(scores - row_max)
    row_total = jnp.sum(exp_scores, axis=-1, keepdims=True)
    attn_probs = (exp_scores / row_total).astype(jnp.bfloat16)
    log_total = row_max + jnp.log(row_total)
    attn_mixed = jnp.einsum(
        "shlm,smhd->slhd", attn_probs, head_split[:, :, 2], preferred_element_type=jnp.float32
    )
    attn_low = attn_mixed.reshape(seq_count * length, model_width).astype(jnp.bfloat16)
    first_sum = (
        token_rows.astype(jnp.float32)
        + jnp.dot(attn_low, out_w, preferred_element_type=jnp.float32)
        + out_b.astype(jnp.float32)
    )
    normed_one, inv_one = normalize(first_sum)
    gain_float = gains.astype(jnp.float32)
    shift_float = shifts.astype(jnp.float32)
    middle = normed_one * gain_float[:, 0] + shift_float[:, 0]
    middle_low = middle.astype(jnp.bfloat16)
    pre_act = jnp.dot(middle_low, up_w, preferred_element_type=jnp.float32) + up_b.astype(
        jnp.float32
    )
    act_low = jax.nn.gelu(pre_act, approximate=False).astype(jnp.bfloat16)
    second = (
        middle
        + jnp.dot(act_low, down_w, preferred_element_type=jnp.float32)
        + down_b.astype(jnp.float32)
    )
    normed_two, inv_two = normalize(second)
    result = normed_two * gain_float[:, 1] + shift_float[:, 1]
    kept = (
        token_rows,
        qkv_low,
        log_total,
        attn_low,
        normed_one,
        inv_one,
        middle_low,
        pre_act,
        act_low,
        normed_two,
        inv_two,
    )
    return (result, kept)


def layer_backward(grad_out, weights, kept, attn_mask):
    qkv_w, qv_b, out_w, out_b, up_w, up_b, down_w, down_b, gains, shifts = weights
    (
        token_rows,
        qkv_low,
        log_total,
        attn_low,
        normed_one,
        inv_one,
        middle_low,
        pre_act,
        act_low,
        normed_two,
        inv_two,
    ) = kept
    seq_count = attn_mask.shape[0]
    model_width = token_rows.shape[1]
    length = token_rows.shape[0] // seq_count
    head_count = model_width // HD
    gain_float = gains.astype(jnp.float32)
    gain_two = jnp.sum(grad_out * normed_two, axis=0)
    shift_two = jnp.sum(grad_out, axis=0)
    d_second = norm_back(grad_out * gain_float[:, 1], normed_two, inv_two)
    d_ffn = d_second.astype(jnp.bfloat16)
    d_down_w = jnp.dot(act_low.T, d_ffn, preferred_element_type=jnp.float32)
    d_down_b = jnp.sum(d_ffn.astype(jnp.float32), axis=0)
    d_act = jnp.dot(d_ffn, down_w.T, preferred_element_type=jnp.float32)
    gelu_slope = (
        0.5 * (1.0 + lax.erf(pre_act * INV_ROOT_TWO))
        + pre_act * jnp.exp(-0.5 * pre_act * pre_act) * INV_ROOT_TWO_PI
    )
    d_pre = (d_act * gelu_slope).astype(jnp.bfloat16)
    d_up_w = jnp.dot(middle_low.T, d_pre, preferred_element_type=jnp.float32)
    d_up_b = jnp.sum(d_pre.astype(jnp.float32), axis=0)
    d_middle = d_second + jnp.dot(d_pre, up_w.T, preferred_element_type=jnp.float32)
    gain_one = jnp.sum(d_middle * normed_one, axis=0)
    shift_one = jnp.sum(d_middle, axis=0)
    d_first = norm_back(d_middle * gain_float[:, 0], normed_one, inv_one)
    d_attn_out = d_first.astype(jnp.bfloat16)
    d_out_w = jnp.dot(attn_low.T, d_attn_out, preferred_element_type=jnp.float32)
    d_out_b = jnp.sum(d_attn_out.astype(jnp.float32), axis=0)
    d_mixed = (
        jnp.dot(d_attn_out, out_w.T, preferred_element_type=jnp.float32)
        .astype(jnp.bfloat16)
        .reshape(seq_count, length, head_count, HD)
    )
    head_split = qkv_low.reshape(seq_count, length, 3, head_count, HD)
    head_query = head_split[:, :, 0]
    head_key = head_split[:, :, 1]
    head_value = head_split[:, :, 2]
    attn_probs = jnp.exp(head_scores(head_query, head_key, attn_mask) - log_total)
    d_probs = jnp.einsum("slhd,smhd->shlm", d_mixed, head_value, preferred_element_type=jnp.float32)
    d_value = jnp.einsum(
        "shlm,slhd->smhd",
        attn_probs.astype(jnp.bfloat16),
        d_mixed,
        preferred_element_type=jnp.float32,
    )
    d_scores = (
        attn_probs * (d_probs - jnp.sum(d_probs * attn_probs, axis=-1, keepdims=True))
    ).astype(jnp.bfloat16)
    d_query = jnp.einsum(
        "shlm,smhd->slhd", d_scores, head_key, preferred_element_type=jnp.float32
    ) * (1.0 / math.sqrt(HD))
    d_key = jnp.einsum(
        "shlm,slhd->smhd", d_scores, head_query, preferred_element_type=jnp.float32
    ) * (1.0 / math.sqrt(HD))
    d_qkv = (
        jnp.stack([d_query, d_key, d_value], axis=2)
        .reshape(seq_count * length, 3 * model_width)
        .astype(jnp.bfloat16)
    )
    d_qkv_w = jnp.dot(token_rows.T, d_qkv, preferred_element_type=jnp.float32)
    column_sums = jnp.sum(d_qkv.astype(jnp.float32), axis=0)
    d_qv_b = jnp.concatenate([column_sums[:model_width], column_sums[2 * model_width :]])
    d_tokens = d_first + jnp.dot(d_qkv, qkv_w.T, preferred_element_type=jnp.float32)
    layer_grads = (
        d_qkv_w,
        d_qv_b,
        d_out_w,
        d_out_b,
        d_up_w,
        d_up_b,
        d_down_w,
        d_down_b,
        jnp.stack([gain_one, gain_two], axis=1),
        jnp.stack([shift_one, shift_two], axis=1),
    )
    return (d_tokens, layer_grads)


def reduce_layer(layer_grads):
    owned_grads = (
        lax.psum_scatter(layer_grads[0], "shard", scatter_dimension=0, tiled=True),
        lax.psum_scatter(layer_grads[1], "shard", scatter_dimension=0, tiled=True),
        lax.psum_scatter(layer_grads[2], "shard", scatter_dimension=0, tiled=True),
        lax.psum_scatter(layer_grads[3], "shard", scatter_dimension=0, tiled=True),
        lax.psum_scatter(layer_grads[4], "shard", scatter_dimension=0, tiled=True),
        lax.psum_scatter(layer_grads[5], "shard", scatter_dimension=0, tiled=True),
        lax.psum_scatter(layer_grads[6], "shard", scatter_dimension=0, tiled=True),
        lax.psum_scatter(layer_grads[7], "shard", scatter_dimension=0, tiled=True),
        lax.psum_scatter(layer_grads[8], "shard", scatter_dimension=0, tiled=True),
        lax.psum_scatter(layer_grads[9], "shard", scatter_dimension=0, tiled=True),
    )
    quarter = (
        lax.psum_scatter(
            owned_grads[0].astype(jnp.bfloat16), "rep", scatter_dimension=0, tiled=True
        ).astype(jnp.float32),
        lax.psum_scatter(
            owned_grads[1].astype(jnp.bfloat16), "rep", scatter_dimension=0, tiled=True
        ).astype(jnp.float32),
        lax.psum_scatter(
            owned_grads[2].astype(jnp.bfloat16), "rep", scatter_dimension=0, tiled=True
        ).astype(jnp.float32),
        lax.psum_scatter(
            owned_grads[3].astype(jnp.bfloat16), "rep", scatter_dimension=0, tiled=True
        ).astype(jnp.float32),
        lax.psum_scatter(
            owned_grads[4].astype(jnp.bfloat16), "rep", scatter_dimension=0, tiled=True
        ).astype(jnp.float32),
        lax.psum_scatter(
            owned_grads[5].astype(jnp.bfloat16), "rep", scatter_dimension=0, tiled=True
        ).astype(jnp.float32),
        lax.psum_scatter(
            owned_grads[6].astype(jnp.bfloat16), "rep", scatter_dimension=0, tiled=True
        ).astype(jnp.float32),
        lax.psum_scatter(
            owned_grads[7].astype(jnp.bfloat16), "rep", scatter_dimension=0, tiled=True
        ).astype(jnp.float32),
        lax.psum_scatter(
            owned_grads[8].astype(jnp.bfloat16), "rep", scatter_dimension=0, tiled=True
        ).astype(jnp.float32),
        lax.psum_scatter(
            owned_grads[9].astype(jnp.bfloat16), "rep", scatter_dimension=0, tiled=True
        ).astype(jnp.float32),
    )
    return (
        lax.all_gather(quarter[0].astype(jnp.bfloat16), "rep", axis=0, tiled=True).astype(
            jnp.float32
        ),
        lax.all_gather(quarter[1].astype(jnp.bfloat16), "rep", axis=0, tiled=True).astype(
            jnp.float32
        ),
        lax.all_gather(quarter[2].astype(jnp.bfloat16), "rep", axis=0, tiled=True).astype(
            jnp.float32
        ),
        lax.all_gather(quarter[3].astype(jnp.bfloat16), "rep", axis=0, tiled=True).astype(
            jnp.float32
        ),
        lax.all_gather(quarter[4].astype(jnp.bfloat16), "rep", axis=0, tiled=True).astype(
            jnp.float32
        ),
        lax.all_gather(quarter[5].astype(jnp.bfloat16), "rep", axis=0, tiled=True).astype(
            jnp.float32
        ),
        lax.all_gather(quarter[6].astype(jnp.bfloat16), "rep", axis=0, tiled=True).astype(
            jnp.float32
        ),
        lax.all_gather(quarter[7].astype(jnp.bfloat16), "rep", axis=0, tiled=True).astype(
            jnp.float32
        ),
        lax.all_gather(quarter[8].astype(jnp.bfloat16), "rep", axis=0, tiled=True).astype(
            jnp.float32
        ),
        lax.all_gather(quarter[9].astype(jnp.bfloat16), "rep", axis=0, tiled=True).astype(
            jnp.float32
        ),
    )


def local(
    query_tokens,
    passage_tokens,
    query_cot,
    passage_cot,
    bucket_counts,
    positives,
    qkv_weight,
    qv_bias,
    out_weight,
    out_bias,
    up_weight,
    up_bias,
    down_weight,
    down_bias,
    norm_gains,
    norm_shifts,
):
    stacks = (
        qkv_weight,
        qv_bias,
        out_weight,
        out_bias,
        up_weight,
        up_bias,
        down_weight,
        down_bias,
        norm_gains,
        norm_shifts,
    )
    blocks, long_len, model_width = passage_tokens.shape
    query_count, query_len, unused_width = query_tokens.shape
    subs_count = long_len // SHORT
    slot_count = blocks * subs_count
    my_index = lax.axis_index(("rep", "shard"))
    own_count = lax.dynamic_index_in_dim(bucket_counts, my_index, 0, keepdims=False)
    passage_mask = block_mask(lax.iota(jnp.int32, blocks) < own_count, long_len, SHORT)
    query_mask = block_mask(jnp.ones((query_count,), dtype=bool), query_len, query_len)
    query_weights = fetch_layer(stacks, 0)
    query_result, query_kept = layer_forward(query_tokens, query_weights, query_mask)
    passage_weights = fetch_layer(stacks, 1)
    passage_result, passage_kept = layer_forward(passage_tokens, passage_weights, passage_mask)
    query_cls = query_result.reshape(query_count, query_len, model_width)[:, 0].astype(jnp.bfloat16)
    passage_cls = (
        passage_result.reshape(blocks, subs_count, SHORT, model_width)[:, :, 0]
        .reshape(slot_count, model_width)
        .astype(jnp.bfloat16)
    )
    every_cls = lax.all_gather(passage_cls, ("rep", "shard"), axis=0, tiled=True)
    cand_count = every_cls.shape[0]
    device_count = bucket_counts.shape[0]
    score_scale = 2.0 / math.sqrt(model_width)
    logits = jnp.dot(query_cls, every_cls.T, preferred_element_type=jnp.float32) * score_scale
    slot_ids = lax.iota(jnp.int32, cand_count)
    owner_index = slot_ids // slot_count
    owner_counts = jnp.sum(
        jnp.where(
            owner_index[:, None] == lax.iota(jnp.int32, device_count)[None], bucket_counts[None], 0
        ),
        axis=1,
    )
    slot_valid = (slot_ids % slot_count // subs_count >= owner_counts) | (
        slot_ids % subs_count == 0
    )
    masked = jnp.where(slot_valid[None], logits, NEG_FILL)
    row_max = jnp.max(masked, axis=1, keepdims=True)
    exp_scores = jnp.exp(masked - row_max)
    row_total = jnp.sum(exp_scores, axis=1, keepdims=True)
    log_total = row_max[:, 0] + jnp.log(row_total[:, 0])
    hit_mask = slot_ids[None] == positives[:, None]
    picked = jnp.sum(jnp.where(hit_mask, masked, 0.0), axis=1)
    local_loss = jnp.sum(log_total - picked)
    d_logits = (exp_scores / row_total - hit_mask.astype(jnp.float32)).astype(jnp.bfloat16)
    d_query_cls = jnp.dot(d_logits, every_cls, preferred_element_type=jnp.float32) * score_scale
    d_cands = (
        lax.dot_general(
            d_logits, query_cls, (((0,), (0,)), ((), ())), preferred_element_type=jnp.float32
        )
        * score_scale
    )
    d_passage_cls = lax.psum_scatter(d_cands, ("rep", "shard"), scatter_dimension=0, tiled=True)
    loss_sum = lax.psum(local_loss, ("rep", "shard"))
    loss = loss_sum / (query_count * lax.axis_size(("rep", "shard")))
    query_dout = (
        query_cot.astype(jnp.float32)
        .at[:, 0]
        .add(d_query_cls)
        .reshape(query_count * query_len, model_width)
    )
    passage_dout = (
        passage_cot.astype(jnp.float32)
        .reshape(blocks, subs_count, SHORT, model_width)
        .at[:, :, 0]
        .add(d_passage_cls.reshape(blocks, subs_count, model_width))
        .reshape(blocks * long_len, model_width)
    )
    passage_back = fetch_again(stacks, 1)
    passage_dx, passage_grads = layer_backward(
        passage_dout, passage_back, passage_kept, passage_mask
    )
    passage_owned = reduce_layer(passage_grads)
    query_back = fetch_again(stacks, 0)
    query_dx, query_grads = layer_backward(query_dout, query_back, query_kept, query_mask)
    query_owned = reduce_layer(query_grads)
    stacked = [
        jnp.stack([first_g, second_g]) for first_g, second_g in zip(query_owned, passage_owned)
    ]
    gains_grad = jnp.swapaxes(stacked[8], 1, 2)
    shifts_grad = jnp.swapaxes(stacked[9], 1, 2)
    return (
        loss,
        query_result.reshape(query_count, query_len, model_width).astype(jnp.bfloat16),
        passage_result.reshape(blocks, long_len, model_width).astype(jnp.bfloat16),
        query_dx.reshape(query_count, query_len, model_width).astype(jnp.bfloat16),
        passage_dx.reshape(blocks, long_len, model_width).astype(jnp.bfloat16),
        stacked[0],
        stacked[1],
        stacked[2],
        stacked[3],
        stacked[4],
        stacked[5],
        stacked[6],
        stacked[7],
        gains_grad,
        shifts_grad,
    )


BF = jnp.bfloat16
F32 = jnp.float32
MESH = pl.DeviceIdType.MESH
ROWS = (128, 256)
D = 768
HALF = 384
FFN = 768
PLAN = [(2, 2, 0, 0), (2, 2, 1, 0), (2, 2, 1, 0), (3, 3, 2, 1), (4, 3, 2, 2), (6, 4, 2, 2), (6, 5, 3, 2), (10, 8, 5, 2), (10, 8, 7, 3), (10, 10, 9, 3), (13, 10, 10, 5), (14, 11, 10, 5), (15, 12, 10, 6), (15, 15, 13, 6), (18, 17, 15, 7), (20, 18, 16, 7), (21, 21, 18, 9), (21, 21, 18, 9), (22, 21, 18, 10), (23, 21, 18, 10), (23, 21, 20, 10)]
NEIGH = tuple((dy, dx, dc) for dy in (0, 1) for dx in (0, 1) for dc in (0, 1) if dy + dx + dc)

(S_X, S_QKV, S_QKV1, S_QKV2, S_QKVC, S_QKVZ, S_QKVZ1, S_QKVZ2, S_OUT, S_OUTC, S_OUTZ, S_UP, S_UP1, S_UPC, S_UPZ, S_UPZ1,
 S_DN, S_OP, S_MY, S_MC, S_MF, S_F1A, S_F1B, S_F2, S_DY, S_DC, S_DF, S_D1A, S_D1B, S_D2,
 S_DA, S_DX, S_GD, S_GD1, S_GD2, S_GU, S_GU1, S_XU, S_XU1, S_GO, S_GQ, S_GQ1, S_GQ2, S_YQ, S_YQ1, S_YQ2, S_SMALL, S_CZ, S_CP, S_CPC, S_CPF, S_BG, S_COT, S_FIN, S_FIN2, S_CF, S_Z) = range(57)
N_UNITS = 23
N_SEMS = 4 * S_Z + 6 * N_UNITS + 2


def nn(a, b):
    return jnp.dot(a, b, preferred_element_type=F32)


def nt(a, b):
    return lax.dot_general(a, b, (((1,), (1,)), ((), ())), preferred_element_type=F32)


def tn(a, b):
    return lax.dot_general(a, b, (((0,), (0,)), ((), ())), preferred_element_type=F32)


def flip(v, d):
    return 1 - v if d else v


def mo(v, m):
    return pl.multiple_of(v, m)


(B_X, B_COT, B_WQ, B_WO, B_WU, B_WD, B_QB, B_UB, B_QKV, B_P, B_ATT, B_OS,
 B_OR, B_N1, B_N2, B_R1, B_R2, B_MID, B_ACT, B_SL, B_S1, B_V1, B_S2, B_V2,
 B_KP, B_Y, B_DF, B_DA, B_GD, B_GU, B_GO, B_GQ, B_ZSD, B_ZSU, B_ZSO, B_ZSQ,
 B_ZAD, B_ZAU, B_ZAO, B_ZAQ, B_ZBD, B_ZBU, B_ZBO, B_ZBQ, B_CLN, B_CLR, B_CLC, B_CLS,
 B_CLD, B_CLP, B_CFW, B_CF, B_YQ, B_T96, B_SP, B_BGC, B_PV, B_BG, B_BGS, B_BGR,
 B_BGA, B_BGB, B_CM, B_GA, B_CG, B_DAT, B_XU) = range(67)


def scratch_list():
    s = []

    def add(name, t, shape, dtype):
        s.append(((name, t), pltpu.VMEM(shape, dtype)))

    for t, T in enumerate(ROWS):
        add(B_X, t, (2 * T, D), BF)
        add(B_COT, t, (T, D), BF)
        add(B_WQ, t, (D, 3 * HALF), BF)
        add(B_WO, t, (HALF, D), BF)
        add(B_WU, t, (D, FFN), BF)
        add(B_WD, t, (FFN, D), BF)
        add(B_QB, t, (8, 3 * HALF), F32)
        add(B_UB, t, (8, FFN), F32)
        add(B_QKV, t, (2 * T, 3 * HALF), BF)
        add(B_P, t, (12, T, T), F32)
        add(B_ATT, t, (2 * T, HALF), BF)
        add(B_OS, t, (T, D), BF)
        add(B_OR, t, (T, D), BF)
        add(B_N1, t, (T, D), F32)
        add(B_N2, t, (T, D), F32)
        add(B_R1, t, (T, 128), F32)
        add(B_R2, t, (T, 128), F32)
        add(B_MID, t, (4 * T, D), BF)
        add(B_ACT, t, (4 * T, FFN), BF)
        add(B_SL, t, (4 * T, FFN), BF)
        add(B_S1, t, (2, T, D), BF)
        add(B_V1, t, (2, T, D), BF)
        add(B_S2, t, (T, D), BF)
        add(B_V2, t, (T, D), BF)
        add(B_KP, t, (2, T, D), F32)
        add(B_Y, t, (T, D), BF)
        add(B_DF, t, (4 * T, D), BF)
        add(B_DA, t, (2 * T, D), BF)
        add(B_DAT, t, (2 * T, HALF), BF)
        add(B_GD, t, (HALF, D), BF)
        add(B_GU, t, (4, 96, FFN), BF)
        add(B_XU, t, (HALF, FFN), BF)
        add(B_GO, t, (4, 96, D), BF)
        add(B_GQ, t, (4, 96, 3 * HALF), BF)
        add(B_YQ, t, (HALF, 3 * HALF), BF)
        for first in (B_ZSD, B_ZAD, B_ZBD):
            add(first, t, (HALF, D), BF)
            add(first + 1, t, (96, 4 * D), BF)
            add(first + 2, t, (96, D), BF)
            add(first + 3, t, (96, 3 * D), BF)
    for t in (0, 1):
        add(B_CLN, t, (8, D), F32)
        add(B_CLR, t, (8, 128), F32)
        add(B_CLC, t, (8, D), F32)
        add(B_CLS, t, (16, FFN), BF)
        add(B_CLD, t, (16, D), F32)
        add(B_CLP, t, (16, FFN), F32)
    add(B_CFW, 0, (16, D), F32)
    add(B_CF, 0, (4, 16, D), BF)
    add(B_T96, 0, (16, HALF), F32)
    add(B_SP, 0, (8, 16, HALF), BF)
    add(B_PV, 0, (32, D), F32)
    add(B_BG, 0, (32, D), F32)
    add(B_BGC, 0, (8, 16, HALF), BF)
    add(B_BGR, 0, (8, 16, HALF), BF)
    add(B_BGS, 0, (16, HALF), F32)
    add(B_BGA, 0, (16, HALF), F32)
    add(B_BGB, 0, (16, HALF), F32)
    add(B_CM, 0, (16, 512), BF)
    add(B_GA, 0, (32, 16, 512), BF)
    add(B_CG, 0, (2, 16, D), F32)
    return s


def fused_kernel(*refs):
    (i_x0, i_x1, i_cot0, i_cot1, i_qkvw, i_outw, i_upw, i_dnw, i_qvb, i_ob, i_ub, i_db, i_gn, i_sf, i_cnt, i_pos,
     o_loss, o_y0, o_y1, o_gx0, o_gx1, o_oq, o_oo, o_ou, o_od, o_obg) = refs[:26]
    held = {key: ref for (key, _), ref in zip(scratch_list(), refs[26:])}
    sems = refs[-1]

    def g(name, t):
        return held[(name, t)]

    rep = lax.axis_index("rep")
    s = lax.axis_index("shard")
    y = s // 4
    x = (s // 2) % 2
    c = s % 2
    x_in = (i_x0, i_x1)
    cot_in = (i_cot0, i_cot1)

    def sem(name, t, side):
        return sems.at[4 * name + 2 * t + side]

    def sh(yy, xx, cc):
        return yy * 4 + xx * 2 + cc

    def send(src, dst, name, t, dev):
        pltpu.make_async_remote_copy(src, dst, send_sem=sem(name, t, 1), recv_sem=sem(name, t, 0),
                                     device_id=dev, device_id_type=MESH).start()

    def local(src, dst, name, t, side=0):
        pltpu.make_async_copy(src, dst, sem(name, t, side)).start()

    def wait(ref, name, t, side=0):
        pltpu.make_async_copy(ref, ref, sem(name, t, side)).wait()

    def peer(d):
        return flip(y, d[0]), flip(x, d[1]), flip(c, d[2])

    sib = (rep, sh(y, x, 1 - c))
    ypeer = (rep, sh(1 - y, x, c))
    xpeer = (rep, sh(y, 1 - x, c))

    bar = pltpu.get_barrier_semaphore()
    for d in NEIGH:
        pl.semaphore_signal(bar, 1, device_id=(rep, sh(*peer(d))), device_id_type=MESH)
    for k in (1, 2, 3):
        pl.semaphore_signal(bar, 1, device_id=((rep + k) % 4, s), device_id_type=MESH)

    T96, SP, PV = (g(b, 0) for b in (B_T96, B_SP, B_PV))
    T96[...] = jnp.zeros((16, HALF), F32)
    T96[0:2, 0:96] = i_ob[...].astype(F32)
    T96[2:4, 0:96] = i_db[...].astype(F32)
    for t in (0, 1):
        for k in (0, 1):
            T96[4 + 2 * t + k:5 + 2 * t + k, 0:96] = i_gn[t, k:k + 1, :].astype(F32)
            T96[8 + 2 * t + k:9 + 2 * t + k, 0:96] = i_sf[t, k:k + 1, :].astype(F32)
    T96[0:2, 128:320] = i_qvb[...].astype(F32)
    T96[12:14, :] = i_ub[...].astype(F32)
    SP[s] = T96[...].astype(BF)

    def place(n, w, at):
        i = lax.broadcasted_iota(jnp.int32, (n, D), 0)
        j = lax.broadcasted_iota(jnp.int32, (n, D), 1)
        return ((j == i + at) & (i < w)).astype(F32).astype(BF)

    pl.semaphore_wait(bar, 10)

    half = rep % 2
    zpair = (rep + 1 - 2 * half, s)
    for d in NEIGH:
        send(SP.at[s], SP.at[s], S_SMALL, 0, (rep, sh(*peer(d))))
    rows96 = pl.ds(mo(s * 96, 32), 96)
    half48 = pl.ds(mo(half * 48, 16), 48)

    def send_x(t):
        T = ROWS[t]
        own = g(B_X, t).at[pl.ds(mo(c * T, 128), T)]
        send(x_in[t], own, S_X, t, sib)
        local(x_in[t], own, S_X, t)

    def rows48(owner):
        return pl.ds(mo(owner * 96 + half * 48, 16), 48)

    def send_cols(t, src, dst, pieces, far, near):
        for k in range(len(pieces((y, x, c)))):
            for d in NEIGH + ((0, 0, 0),):
                p = peer(d)
                cols, to = pl.ds(mo(pieces(p)[k], 128), HALF), pl.ds(k * HALF, HALF)
                if d[0] + d[1]:
                    send(src.at[t, half48, cols], dst.at[rows48(s), to], far + k, t, (rep, sh(*p)))
                elif d[2]:
                    send(src.at[t, :, cols], dst.at[rows96, to], near, t, sib)
                else:
                    local(src.at[t, :, cols], dst.at[rows96, to], near, t)

    def send_qkv(t):
        send_cols(t, i_qkvw, g(B_WQ, t), lambda p: [part * D + p[2] * HALF for part in range(3)], S_QKV, S_QKVC)

    def send_up(t):
        send_cols(t, i_upw, g(B_WU, t), lambda p: [HALF * (4 * p[0] + 2 * xx + p[2]) for xx in (0, 1)], S_UP, S_UPC)

    def part_of(buf, rows, k):
        return buf.at[pl.ds(0, rows), pl.ds(k * HALF, HALF)]

    def forward_cols(t, buf, k, far, pair):
        wait(part_of(buf, 288, k), far + k, t)
        for d in NEIGH:
            if d[0] + d[1]:
                piece = buf.at[rows48(sh(*peer(d))), pl.ds(k * HALF, HALF)]
                send(piece, piece, pair + k, t, zpair)

    def send_out(t):
        WO = g(B_WO, t)
        for dy in (0, 1):
            for dx in (0, 1):
                dev = (rep, sh(flip(y, dy), flip(x, dx), y))
                if dy + dx:
                    send(i_outw.at[t, half48], WO.at[rows48(x * 2 + c)], S_OUT, t, dev)
                else:
                    dst = WO.at[pl.ds(mo((x * 2 + c) * 96, 32), 96)]

                    @pl.when(c == y)
                    def _():
                        local(i_outw.at[t], dst, S_OUTC, t)

                    @pl.when(c != y)
                    def _():
                        send(i_outw.at[t], dst, S_OUTC, t, dev)

    def forward_out(t):
        WO = g(B_WO, t)

        def go(xs):
            for xx in xs:
                for cc in (0, 1):
                    piece = WO.at[rows48(xx * 2 + cc)]
                    send(piece, piece, S_OUTZ, t, zpair)

        @pl.when(c == y)
        def _():
            wait(WO.at[pl.ds(0, 96)], S_OUT, t)
            go((1 - x,))

        @pl.when(c != y)
        def _():
            wait(WO.at[pl.ds(0, 192)], S_OUT, t)
            go((0, 1))

    def whole_out(t):
        WO = g(B_WO, t)

        @pl.when(c == y)
        def _():
            wait(WO.at[pl.ds(0, 192)], S_OUTC, t)
            wait(WO.at[pl.ds(0, 96)], S_OUTZ, t)

        @pl.when(c != y)
        def _():
            wait(WO.at[pl.ds(0, 192)], S_OUTZ, t)

    def send_dn(t):
        dst = g(B_WD, t).at[pl.ds(mo(x * HALF, 128), HALF)]
        send(i_dnw.at[t], dst, S_DN, t, xpeer)
        local(i_dnw.at[t], dst, S_DN, t)

    for t in (1, 0):
        send_x(t)
        send_qkv(t)
        send_out(t)
    send_up(1)
    send_dn(1)
    for t in (0, 1):
        local(cot_in[t], g(B_COT, t), S_COT, 0, t)

    wait(SP.at[pl.ds(0, 7)], S_SMALL, 0)
    low96 = jnp.zeros((16, D), F32)
    low192 = [jnp.zeros((16, D), F32) for _ in (0, 1)]
    for k in range(8):
        low96 = low96 + nn(SP[k, :, 0:128], place(128, 96, 96 * k))
        low192[k // 4] = low192[k // 4] + nn(SP[k, :, 128:384], place(256, 192, 192 * (k % 4)))
    PV[0:16, :] = low96
    PV[12:14, :] = low192[0][0:2, :]
    PV[14:16, :] = low192[1][0:2, :]
    for k in range(8):
        for t in (0, 1):
            at, lanes = 16 + 4 * t + k // 2, slice(k % 2 * HALF, (k % 2 + 1) * HALF)
            PV[at:at + 1, lanes] = SP[k].astype(F32)[12 + t:13 + t, :]
    R_OB, R_DB, R_GN, R_SF, R_QB, R_VB, R_UB = 0, 2, 4, 8, 12, 14, 16

    def prow(k):
        return PV[k:k + 1, :]

    lane_half = pl.ds(mo(c * HALF, 128), HALF)
    for t in (0, 1):
        g(B_QB, t)[...] = jnp.zeros((8, 3 * HALF), F32)
        g(B_QB, t)[0:1, 0:HALF] = PV[R_QB + t:R_QB + t + 1, lane_half]
        g(B_QB, t)[0:1, 2 * HALF:] = PV[R_VB + t:R_VB + t + 1, lane_half]
        for xx in (0, 1):
            at = R_UB + 4 * t + xx
            lo, hi = PV[at:at + 1, lane_half], PV[at + 2:at + 3, lane_half]
            g(B_UB, t)[0:1, xx * HALF:(xx + 1) * HALF] = jnp.where(jnp.full((1, HALF), y) == 0, lo, hi)

    def same_part(t, grp):
        T = ROWS[t]
        shift = 5 if t == 0 else 6
        ri = lax.broadcasted_iota(jnp.int32, (T, T), 0) >> shift
        ci = lax.broadcasted_iota(jnp.int32, (T, T), 1) >> shift
        m = ri == ci
        if t == 1:
            m = m | (jnp.full((T, T), i_cnt[rep * 8 + (s // 2) * 2 + grp]) > 0)
        return m

    lane_lo = lax.broadcasted_iota(jnp.int32, (1, 128), 1) < 64
    mask_a = lane_lo.astype(F32).astype(BF)
    mask_b = (1.0 - lane_lo.astype(F32)).astype(BF)

    def lnfwd(first, gain, shift):
        mean = jnp.mean(first, axis=-1, keepdims=True)
        cen = first - mean
        inv = lax.rsqrt(jnp.mean(cen * cen, axis=-1, keepdims=True) + LN_EPS)
        n = cen * inv
        return n, inv, n * gain + shift

    CH = 64

    def project(t, k):
        X, WQ = g(B_X, t), g(B_WQ, t)
        if k == 0:
            wait(X, S_X, t)
            wait(WQ.at[pl.ds(0, 192)], S_QKVC, t)
        wait(part_of(WQ, 288, k), S_QKVZ + k, t)
        cols = slice(k * HALF, (k + 1) * HALF)
        g(B_QKV, t)[:, cols] = (nn(X[...], WQ[:, cols]) + g(B_QB, t)[0:1, cols]).astype(BF)

    def attention(t):
        T = ROWS[t]
        X, WQ, QKV, P, ATT = g(B_X, t), g(B_WQ, t), g(B_QKV, t), g(B_P, t), g(B_ATT, t)
        @pl.loop(0, 2)
        def _(grp):
            rows = pl.ds(mo(grp * T, 128), T)
            m = same_part(t, grp)

            @pl.loop(0, 3)
            def _(hp):
                q = QKV[rows, pl.ds(mo(hp * 128, 128), 128)]
                k = QKV[rows, pl.ds(mo(HALF + hp * 128, 128), 128)]
                val = QKV[rows, pl.ds(mo(2 * HALF + hp * 128, 128), 128)]
                outs = []
                for h, msk in ((0, mask_a), (1, mask_b)):
                    sc = jnp.where(m, nt(q * msk, k) * (1.0 / math.sqrt(HD)), NEG_FILL)
                    mx = jnp.max(sc, axis=-1, keepdims=True)
                    e = jnp.exp(sc - mx)
                    p = e * (1.0 / jnp.sum(e, axis=-1, keepdims=True))
                    P[grp * 6 + hp * 2 + h] = p
                    outs.append(nn(p.astype(BF), val))
                ATT[rows, pl.ds(mo(hp * 128, 128), 128)] = jnp.where(lane_lo, outs[0], outs[1]).astype(BF)

        whole_out(t)
        g(B_OS, t)[...] = nn(ATT[pl.ds(mo((1 - c) * T, 128), T), :], g(B_WO, t)[...]).astype(BF)
        send(g(B_OS, t), g(B_OR, t), S_OP, t, sib)
        g(B_KP, t)[0] = nn(ATT[pl.ds(mo(c * T, 128), T), :], g(B_WO, t)[...])
        wait(g(B_OR, t), S_OP, t)
        me4 = (2 * y + c) * T
        ob, gain, shift = prow(R_OB + t), prow(R_GN + 2 * t), prow(R_SF + 2 * t)

        @pl.loop(0, T // CH)
        def _(i):
            r = pl.ds(mo(i * CH, CH), CH)
            first = (X[pl.ds(mo(c * T + i * CH, CH), CH), :].astype(F32) + g(B_KP, t)[0, r, :]
                     + g(B_OR, t)[r, :].astype(F32) + ob)
            n, inv, mid = lnfwd(first, gain, shift)
            g(B_N1, t)[r, :] = n
            g(B_R1, t)[r, :] = jnp.broadcast_to(inv, (CH, 128))
            g(B_MID, t)[pl.ds(mo(me4 + i * CH, CH), CH), :] = mid.astype(BF)

        gather_rows(t, B_MID, S_MY, S_MC, S_MF)

    def slot_rows(t, yy, cc):
        T = ROWS[t]
        return pl.ds(mo((2 * yy + cc) * T, 128), T)

    def gather_rows(t, buf, ny, nc, nf):
        own = g(buf, t).at[slot_rows(t, y, c)]
        send(own, own, ny, t, ypeer)
        send(own, own, nc, t, sib)

    def gather_near(t, buf, nc):
        wait(g(buf, t).at[slot_rows(t, y, 1 - c)], nc, t)

    def gather_forward(t, buf, ny, nf):
        got = g(buf, t).at[slot_rows(t, 1 - y, c)]
        wait(got, ny, t)
        send(got, got, nf, t, sib)

    def gather_far(t, buf, nf):
        wait(g(buf, t).at[slot_rows(t, 1 - y, 1 - c)], nf, t)

    def gather_sent(t, buf, ny, nc, nf):
        own = g(buf, t).at[slot_rows(t, y, c)]
        wait(own, ny, t, 1)
        wait(own, nc, t, 1)
        wait(own, nf, t, 1)

    def up_pair(t, yy):
        T = ROWS[t]
        rows = pl.ds(mo(2 * yy * T, 128), 2 * T)

        @pl.loop(0, 3)
        def _(j):
            cols = pl.ds(mo(j * 256, 128), 256)
            pre = nn(g(B_MID, t)[rows, :], g(B_WU, t)[:, cols]) + g(B_UB, t)[0:1, cols]
            cdf = 0.5 * (1.0 + lax.erf(pre * INV_ROOT_TWO))
            g(B_ACT, t)[rows, cols] = (pre * cdf).astype(BF)
            g(B_SL, t)[rows, cols] = (cdf + pre * jnp.exp(-0.5 * pre * pre) * INV_ROOT_TWO_PI).astype(BF)

    def scatter_partial(t, part, n1a, n1b, n2):
        S1, V1, S2, V2, KP = g(B_S1, t), g(B_V1, t), g(B_S2, t), g(B_V2, t), g(B_KP, t)
        S1[0] = part(slot_rows(t, 1 - y, 1 - c)).astype(BF)
        send(S1.at[0], V1.at[0], n1a, t, sib)
        KP[0] = part(slot_rows(t, 1 - y, c))
        S1[1] = part(slot_rows(t, y, 1 - c)).astype(BF)
        send(S1.at[1], V1.at[1], n1b, t, sib)
        wait(V1.at[0], n1a, t)
        S2[...] = (KP[0] + V1[0].astype(F32)).astype(BF)
        send(S2, V2, n2, t, ypeer)
        KP[1] = part(slot_rows(t, y, c))

    def scatter_finish(t, n1b, n2):
        wait(g(B_V1, t).at[1], n1b, t)
        wait(g(B_V2, t), n2, t)

    def scatter_sent(t, n1a, n1b, n2):
        wait(g(B_S1, t).at[0], n1a, t, 1)
        wait(g(B_S1, t).at[1], n1b, t, 1)
        wait(g(B_S2, t), n2, t, 1)

    def summed(t, r):
        return g(B_KP, t)[1, r, :] + g(B_V1, t)[1, r, :].astype(F32) + g(B_V2, t)[r, :].astype(F32)

    def ffn(t):
        gather_near(t, B_MID, S_MC)
        gather_forward(t, B_MID, S_MY, S_MF)
        wait(g(B_WU, t).at[pl.ds(0, 192)], S_UPC, t)
        for k in (0, 1):
            wait(part_of(g(B_WU, t), 288, k), S_UPZ + k, t)
        up_pair(t, y)
        gather_far(t, B_MID, S_MF)
        up_pair(t, 1 - y)
        T = ROWS[t]
        r = lax.broadcasted_iota(jnp.int32, (16, 4 * T), 0)
        j = lax.broadcasted_iota(jnp.int32, (16, 4 * T), 1)
        at_cls = (j == (r >> 2) * T + (r & 3) * (32, 64)[t]).astype(F32).astype(BF)
        g(B_CLS, t)[...] = nn(at_cls, g(B_SL, t)[...]).astype(BF)
        wait(g(B_WD, t), S_DN, t)
        scatter_partial(t, lambda rows: nn(g(B_ACT, t)[rows, :], g(B_WD, t)[...]), S_F1A, S_F1B, S_F2)

    def ffn_end(t):
        T = ROWS[t]
        scatter_finish(t, S_F1B, S_F2)
        db = prow(R_DB + t)
        g0, g1, s0, s1 = (prow(base + 2 * t + k) for base in (R_GN, R_SF) for k in (0, 1))

        @pl.loop(0, T // CH)
        def _(i):
            r = pl.ds(mo(i * CH, CH), CH)
            second = g(B_N1, t)[r, :] * g0 + s0 + summed(t, r) + db
            n, inv, res = lnfwd(second, g1, s1)
            g(B_N2, t)[r, :] = n
            g(B_R2, t)[r, :] = jnp.broadcast_to(inv, (CH, 128))
            g(B_Y, t)[r, :] = res.astype(BF)

        local(g(B_Y, t), (o_y0, o_y1)[t], S_FIN, 0, t)

    def forward_qkv(t, k):
        forward_cols(t, g(B_WQ, t), k, S_QKV, S_QKVZ)

    def forward_up(t):
        for k in (0, 1):
            forward_cols(t, g(B_WU, t), k, S_UP, S_UPZ)

    for k in range(3):
        forward_qkv(1, k)
    forward_out(1)
    for k in range(3):
        project(1, k)
        forward_qkv(0, k)
    attention(1)
    send_up(0)
    send_dn(0)
    forward_out(0)
    forward_up(1)
    for k in range(3):
        project(0, k)
    attention(0)
    forward_up(0)
    def fold(a):
        return jnp.sum(a.reshape(CH // 8, 8, D), axis=0)

    def put_bias(k, row):
        g(B_BG, 0)[k:k + 1, :] = row

    def ln_back(t, din, nrm, inv, gain):
        gg = din * gain
        m1 = jnp.mean(gg, axis=-1, keepdims=True)
        m2 = jnp.mean(gg * nrm, axis=-1, keepdims=True)
        return inv * (gg - m1 - nrm * m2)

    steps = (32, 64)

    def out_back(t):
        T = ROWS[t]
        wait(g(B_COT, t), S_COT, 0, t)
        for i in range(4):
            row = slice(i * steps[t], i * steps[t] + 1)
            g(B_CLN, t)[i:i + 1, :] = g(B_N2, t)[row, :]
            g(B_CLR, t)[i:i + 1, :] = g(B_R2, t)[row, :]
            g(B_CLC, t)[i:i + 1, :] = g(B_COT, t)[row, :].astype(F32)
        gain = prow(R_GN + 2 * t + 1)
        me4 = (2 * y + c) * T
        zero = jnp.zeros((8, D), F32)

        def body(i, acc):
            r = pl.ds(mo(i * CH, CH), CH)
            dout = g(B_COT, t)[r, :].astype(F32)
            nrm = g(B_N2, t)[r, :]
            dsec = ln_back(t, dout, nrm, g(B_R2, t)[r, 0:1], gain)
            g(B_N2, t)[r, :] = dsec
            g(B_DF, t)[pl.ds(mo(me4 + i * CH, CH), CH), :] = dsec.astype(BF)
            return (acc[0] + fold(dout * nrm), acc[1] + fold(dout))

        acc = lax.fori_loop(0, T // CH, body, (zero, zero))
        for k, a in zip((R_GN + 2 * t + 1, R_SF + 2 * t + 1), acc):
            put_bias(k, jnp.sum(a, axis=0, keepdims=True))

    def cls_back(t):
        dcls = g(B_CG, 0)[t, 0:4, :]
        nrm = g(B_CLN, t)[0:4, :]
        dsec = ln_back(t, g(B_CLC, t)[0:4, :] + dcls, nrm, g(B_CLR, t)[0:4, 0:1], prow(R_GN + 2 * t + 1))
        for i in range(4):
            g(B_N2, t)[i * steps[t]:i * steps[t] + 1, :] = dsec[i:i + 1, :]
        g(B_CFW, 0)[4 * t:4 * t + 4, :] = dsec
        for k, a in ((R_GN + 2 * t + 1, dcls * nrm), (R_SF + 2 * t + 1, dcls)):
            put_bias(k, g(B_BG, 0)[k:k + 1, :] + jnp.sum(a, axis=0, keepdims=True))

    def cls_place(t):
        T = ROWS[t]
        r = lax.broadcasted_iota(jnp.int32, (16, 64), 0)
        j = lax.broadcasted_iota(jnp.int32, (16, 64), 1)
        which = (j == (r >> 2) * 16 + 4 * t + (r & 3)).astype(F32).astype(BF)
        rows = nn(which, g(B_CF, 0)[...].reshape(64, D))
        g(B_CLD, t)[...] = rows
        da = nt(rows.astype(BF), g(B_WD, t)[...])
        g(B_CLP, t)[...] = da * g(B_CLS, t)[...].astype(F32)
        top = lax.broadcasted_iota(jnp.int32, (16, 1), 0) == 0
        for slot in range(4):
            for i in range(4):
                tile = pl.ds(slot * T + i * steps[t], 16)
                k = slot * 4 + i
                for buf, new in ((g(B_DF, t), g(B_CLD, t)), (g(B_SL, t), g(B_CLP, t))):
                    buf[tile, :] = jnp.where(top, new[k:k + 1, :], buf[tile, :].astype(F32)).astype(BF)

    def down_pair(t, yy):
        T = ROWS[t]
        rows = pl.ds(mo(2 * yy * T, 128), 2 * T)

        @pl.loop(0, 3)
        def _(j):
            cols = pl.ds(mo(j * 256, 128), 256)
            da = nt(g(B_DF, t)[rows, :], g(B_WD, t)[cols, :])
            g(B_SL, t)[rows, cols] = (da * g(B_SL, t)[rows, cols].astype(F32)).astype(BF)

    def pre_back(t, between=lambda: None):
        gather_near(t, B_DF, S_DC)
        down_pair(t, y)
        between()
        gather_forward(t, B_DF, S_DY, S_DF)
        gather_far(t, B_DF, S_DF)
        down_pair(t, 1 - y)

    def ffn_back(t, point=lambda: None):
        gather_sent(t, B_DF, S_DY, S_DC, S_DF)
        cls_place(t)
        ACT, DF, WD, WU = g(B_ACT, t), g(B_DF, t), g(B_WD, t), g(B_WU, t)
        for k in range(3):
            cols = pl.ds(mo((1 - x) * HALF + 128 * k, 128), 128)
            WD[cols, :] = tn(ACT[:, cols], DF[...]).astype(BF)
            send(WD.at[cols], g(B_GD, t).at[pl.ds(128 * k, 128)], S_GD + k, t, xpeer)
        point()

        scatter_partial(t, lambda rows: nt(g(B_SL, t)[rows, :], g(B_WU, t)[...]), S_D1A, S_D1B, S_D2)
        point()
        own_sum = nn(jnp.ones((8, ROWS[t]), F32).astype(BF), g(B_DF, t)[slot_rows(t, y, c), :])
        put_bias(R_DB + t, own_sum[0:1, :])
        ones = jnp.ones((8, 4 * ROWS[t]), F32).astype(BF)
        sums = nn(ones, g(B_SL, t)[...])[0:1, :]
        for xx in (0, 1):
            part = sums[:, xx * HALF:(xx + 1) * HALF]
            at = R_UB + 4 * t + xx

            @pl.when(y == 0)
            def _():
                g(B_BG, 0)[at:at + 1, lane_half] = part

            @pl.when(y == 1)
            def _():
                g(B_BG, 0)[at + 2:at + 3, lane_half] = part

        cols = pl.ds(mo(x * HALF, 128), HALF)
        WD[cols, :] = tn(ACT[:, cols], DF[...]).astype(BF)
        for dy in (1, 0):
            far, near = (pl.ds(mo(flip(y, dy) * HALF + xx * 192, 64), 192) for xx in (1 - x, x))

            @pl.loop(0, 3)
            def _(j):
                cols = pl.ds(mo(flip(y, dy) * HALF + j * 128, 128), 128)
                WU[cols, :] = tn(g(B_MID, t)[:, cols], g(B_SL, t)[...]).astype(BF)

            send(WU.at[far], g(B_XU, t).at[pl.ds((1 - dy) * 192, 192)], S_XU1 - dy, t, xpeer)
            point()

    def relay_up(t, dy):
        WU, GU, mine = g(B_WU, t), g(B_GU, t), 2 * y + c
        got = g(B_XU, t).at[pl.ds((1 - dy) * 192, 192)]
        wait(got, S_XU1 - dy, t)
        yy = flip(y, dy)
        for r0 in (0, 96):
            r = pl.ds(mo(yy * HALF + x * 192 + r0, 32), 96)
            WU[r, :] = (WU[r, :].astype(F32) + got[pl.ds(r0, 96), :].astype(F32)).astype(BF)
        for dc in (1, 0):
            owner = sh(yy, x, flip(c, dc))
            rows = WU.at[pl.ds(mo(96 * owner, 32), 96)]
            if dy + dc:
                send(rows, GU.at[mine], S_GU1 - dy, t, (rep, owner))
            else:
                local(rows, GU.at[mine], S_GU1, t)

    g(B_BG, 0)[...] = jnp.zeros((32, D), F32)
    g(B_CFW, 0)[...] = jnp.zeros((16, D), F32)
    ffn(1)
    ffn(0)
    ffn_end(1)
    out_back(1)
    gather_rows(1, B_DF, S_DY, S_DC, S_DF)
    ffn_end(0)

    def pick(T, lo, step):
        ri = lax.broadcasted_iota(jnp.int32, (16, T), 0) & 7
        ci = lax.broadcasted_iota(jnp.int32, (16, T), 1)
        return (((ri & 4) == lo) & (ci == (ri & 3) * step)).astype(F32).astype(BF)

    both = nn(pick(128, 0, 32), g(B_Y, 0)[...]) + nn(pick(256, 4, 64), g(B_Y, 1)[...])
    top = lax.broadcasted_iota(jnp.int32, (16, HALF), 0) < 8
    g(B_CM, 0)[:, :HALF] = jnp.where(top, both[:, :HALF], both[:, HALF:]).astype(BF)
    ri = lax.broadcasted_iota(jnp.int32, (16, 128), 0)
    pos = jnp.zeros((16, 128), jnp.int32)
    for i in range(4):
        pos = jnp.where(ri == i, i_pos[i], pos)
    g(B_CM, 0)[:, HALF:] = pos.astype(F32).astype(BF)
    mine = g(B_GA, 0).at[s * 4 + rep]
    for k in (1, 2, 3):
        send(g(B_CM, 0), mine, S_CZ, 0, ((rep + k) % 4, s))
    g(B_GA, 0)[s * 4 + rep] = g(B_CM, 0)[...]
    out_back(0)
    wait(g(B_GA, 0).at[pl.ds(0, 3)], S_CZ, 0)
    four = g(B_GA, 0).at[pl.ds(s * 4, 4)]
    send(four, four, S_CPC, 0, sib)
    for d in NEIGH:
        if not d[2]:
            send(four, four, S_CP, 0, (rep, sh(*peer(d))))
    gather_rows(0, B_DF, S_DY, S_DC, S_DF)

    for t in (0, 1):
        own = g(B_X, t).at[pl.ds(mo(c * ROWS[t], 128), ROWS[t])]
        wait(own, S_X, t, 1)
        for buf, n, far, near, pair in ((g(B_WQ, t), 3, S_QKV, S_QKVC, S_QKVZ), (g(B_WU, t), 2, S_UP, S_UPC, S_UPZ)):
            wait(buf.at[pl.ds(0, 96)], near, t, 1)
            for k in range(n):
                wait(part_of(buf, 288, k), far + k, t, 1)
                wait(part_of(buf, 288, k), pair + k, t, 1)
        wait(g(B_WO, t).at[pl.ds(0, 144)], S_OUT, t, 1)

        @pl.when(c == y)
        def _():
            wait(g(B_WO, t).at[pl.ds(0, 96)], S_OUTZ, t, 1)

        @pl.when(c != y)
        def _():
            wait(g(B_WO, t).at[pl.ds(0, 96)], S_OUTC, t, 1)
            wait(g(B_WO, t).at[pl.ds(0, 192)], S_OUTZ, t, 1)

        wait(g(B_WD, t).at[pl.ds(0, HALF)], S_DN, t, 1)
        wait(g(B_OS, t), S_OP, t, 1)
        gather_sent(t, B_MID, S_MY, S_MC, S_MF)
        scatter_sent(t, S_F1A, S_F1B, S_F2)
    wait(g(B_SP, 0).at[pl.ds(0, 7)], S_SMALL, 0, 1)
    wait(g(B_GA, 0).at[pl.ds(0, 3)], S_CZ, 0, 1)
    def pass_cls():
        twelve = g(B_GA, 0).at[pl.ds(0, 12)]
        wait(twelve, S_CP, 0)
        for d in NEIGH:
            if not d[2]:
                got = g(B_GA, 0).at[pl.ds(sh(*peer(d)) * 4, 4)]
                send(got, got, S_CPF, 0, sib)

    pre_back(1, pass_cls)

    wait(g(B_GA, 0).at[pl.ds(0, 4)], S_CPC, 0)
    wait(g(B_GA, 0).at[pl.ds(0, 12)], S_CPF, 0)
    wait(g(B_GA, 0).at[pl.ds(0, 4)], S_CPC, 0, 1)
    for name in (S_CP, S_CPF):
        wait(g(B_GA, 0).at[pl.ds(0, 12)], name, 0, 1)

    def pick_all(base):
        ri = lax.broadcasted_iota(jnp.int32, (128, 512), 0)
        ci = lax.broadcasted_iota(jnp.int32, (128, 512), 1)
        blk = ci >> 4
        within = (ci & 15) - base
        row = ((blk & 3) * 8 + (blk >> 2)) * 4 + within
        return ((within >= 0) & (within < 4) & (ri == row)).astype(F32).astype(BF)

    ga = g(B_GA, 0)[...].reshape(512, 512)
    qa_f = nn(pick_all(0), ga)
    qa = qa_f[:, :HALF].astype(BF)
    pa = nn(pick_all(4), ga)[:, :HALF].astype(BF)
    qb = nn(pick_all(8), ga)[:, :HALF].astype(BF)
    pb = nn(pick_all(12), ga)[:, :HALF].astype(BF)
    scale = 2.0 / math.sqrt(D)
    logits = (nt(qa, pa) + nt(qb, pb)) * scale
    lane = lax.broadcasted_iota(jnp.int32, (1, 128), 1)
    cnt = jnp.zeros((1, 128), jnp.int32)
    for k in range(32):
        cnt = jnp.where(lane >> 2 == k, i_cnt[k], cnt)
    masked = jnp.where((cnt <= 0) | (lane & 3 == 0), logits, NEG_FILL)
    mx = jnp.max(masked, axis=1, keepdims=True)
    ex = jnp.exp(masked - mx)
    sm = jnp.sum(ex, axis=1, keepdims=True)
    hit = lax.broadcasted_iota(jnp.int32, (128, 128), 1).astype(F32) == qa_f[:, HALF:]
    ce = mx + jnp.log(sm) - jnp.sum(jnp.where(hit, masked, 0.0), axis=1, keepdims=True)
    o_loss[...] = jnp.broadcast_to(jnp.sum(ce, axis=0, keepdims=True) * (1.0 / 128.0), (8, 128))
    dl = (ex / sm - hit.astype(F32)).astype(BF)
    ri = lax.broadcasted_iota(jnp.int32, (16, 128), 0)
    ci = lax.broadcasted_iota(jnp.int32, (16, 128), 1)
    sel = ((ri < 4) & (ci == ri + 4 * (rep * 8 + s))).astype(F32).astype(BF)
    dlq = nn(sel, dl).astype(BF)
    dlp = nt(sel, dl.T).astype(BF) if False else lax.dot_general(
        sel, dl, (((1,), (1,)), ((), ())), preferred_element_type=F32).astype(BF)
    g(B_CG, 0)[0, :, :HALF] = nn(dlq, pa) * scale
    g(B_CG, 0)[0, :, HALF:] = nn(dlq, pb) * scale
    g(B_CG, 0)[1, :, :HALF] = nn(dlp, qa) * scale
    g(B_CG, 0)[1, :, HALF:] = nn(dlp, qb) * scale

    def mid_back(t):
        T = ROWS[t]
        scatter_finish(t, S_D1B, S_D2)
        gain = prow(R_GN + 2 * t)
        zero = jnp.zeros((8, D), F32)

        def body(i, acc):
            r = pl.ds(mo(i * CH, CH), CH)
            dmid = g(B_N2, t)[r, :] + summed(t, r)
            nrm = g(B_N1, t)[r, :]
            dfirst = ln_back(t, dmid, nrm, g(B_R1, t)[r, 0:1], gain)
            low = dfirst.astype(BF)
            g(B_N1, t)[r, :] = dfirst
            g(B_DA, t)[pl.ds(mo(c * T + i * CH, CH), CH), :] = low
            return (acc[0] + fold(dmid * nrm), acc[1] + fold(dmid), acc[2] + fold(low.astype(F32)))

        acc = lax.fori_loop(0, T // CH, body, (zero, zero, zero))
        own = g(B_DA, t).at[pl.ds(mo(c * T, 128), T)]
        send(own, own, S_DA, t, sib)
        for k, a in zip((R_GN + 2 * t, R_SF + 2 * t, R_OB + t), acc):
            put_bias(k, jnp.sum(a, axis=0, keepdims=True))

    def attention_back(t, point):
        T = ROWS[t]
        QKV, P, ATT, DA, WO, WQ = g(B_QKV, t), g(B_P, t), g(B_ATT, t), g(B_DA, t), g(B_WO, t), g(B_WQ, t)
        wait(DA.at[pl.ds(mo((1 - c) * T, 128), T)], S_DA, t)

        DAT = g(B_DAT, t)
        DAT[...] = nt(DA[...], WO[...]).astype(BF)

        @pl.loop(0, 3)
        def _(j):
            cols = pl.ds(mo(j * 128, 128), 128)
            WO[cols, :] = tn(ATT[:, cols], DA[...]).astype(BF)

        dst = g(B_GO, t).at[y * 2 + x]
        for xx in (0, 1):
            for cc in (0, 1):
                src = WO.at[pl.ds((2 * xx + cc) * 96, 96)]
                dev = sh(c, xx, cc)

                @pl.when(dev == s)
                def _():
                    local(src, dst, S_GO, t)

                @pl.when(dev != s)
                def _():
                    send(src, dst, S_GO, t, (rep, dev))

        point()
        for grp in (0, 1):
            rows = pl.ds(grp * T, T)

            @pl.loop(0, 3)
            def _(hp):
                lanes = pl.ds(mo(hp * 128, 128), 128)
                dat = DAT[rows, lanes]
                qs, ks = lanes, pl.ds(mo(HALF + hp * 128, 128), 128)
                vs = pl.ds(mo(2 * HALF + hp * 128, 128), 128)
                q, k, val = QKV[rows, qs], QKV[rows, ks], QKV[rows, vs]
                dq, dk, dv = [], [], []
                for h, msk in ((0, mask_a), (1, mask_b)):
                    p = P[grp * 6 + hp * 2 + h]
                    dp = nt(dat * msk, val)
                    ds = (p * (dp - jnp.sum(dp * p, axis=-1, keepdims=True))).astype(BF)
                    dv.append(tn(p.astype(BF), dat))
                    dq.append(nn(ds, k))
                    dk.append(tn(ds, q))
                root = 1.0 / math.sqrt(HD)
                QKV[rows, qs] = (jnp.where(lane_lo, dq[0], dq[1]) * root).astype(BF)
                QKV[rows, ks] = (jnp.where(lane_lo, dk[0], dk[1]) * root).astype(BF)
                QKV[rows, vs] = jnp.where(lane_lo, dv[0], dv[1]).astype(BF)

            point()

        g(B_OS, t)[...] = nt(QKV[pl.ds(mo((1 - c) * T, 128), T), :], WQ[...]).astype(BF)
        send(g(B_OS, t), g(B_OR, t), S_DX, t, sib)
        g(B_KP, t)[0] = nt(QKV[pl.ds(mo(c * T, 128), T), :], WQ[...])

        ones = jnp.ones((8, 2 * T), F32).astype(BF)
        sums = nn(ones, QKV[...])[0:1, :]
        g(B_BG, 0)[R_QB + t:R_QB + t + 1, lane_half] = sums[:, :HALF]
        g(B_BG, 0)[R_VB + t:R_VB + t + 1, lane_half] = sums[:, 2 * HALF:]

        if t == 0:
            send_small()
        far_rows = pl.ds(mo((1 - y) * HALF, 128), HALF)
        for k in range(3):
            lanes = slice(k * HALF, (k + 1) * HALF)

            @pl.loop(0, 3)
            def _(j):
                cols = pl.ds(mo(j * 256, 128), 256)
                WQ[cols, lanes] = tn(g(B_X, t)[:, cols], QKV[:, lanes]).astype(BF)

            send(WQ.at[far_rows, pl.ds(k * HALF, HALF)], g(B_YQ, t).at[:, pl.ds(k * HALF, HALF)], S_YQ + k, t, ypeer)
            point()

    def send_small():
        BG, BGC, BGR = (g(b, 0) for b in (B_BG, B_BGC, B_BGR))
        low = BG[...].astype(BF)
        for k in range(8):
            T96[...] = jnp.zeros((16, HALF), F32)
            T96[:, 0:128] = nt(low[0:16, :], place(128, 96, 96 * k))
            at = 12 + 2 * (k // 4)
            T96[0:2, 128:384] = nt(low[0:16, :], place(256, 192, 192 * (k % 4)))[at:at + 2, :]
            for t in (0, 1):
                row = 16 + 4 * t + k // 2
                T96[12 + t:13 + t, :] = BG[row:row + 1, k % 2 * HALF:(k % 2 + 1) * HALF]
            BGC[k] = T96[...].astype(BF)
        for d in NEIGH:
            dest = sh(*peer(d))
            send(BGC.at[dest], BGR.at[s], S_BG, 0, (rep, dest))
        local(BGC.at[s], BGR.at[s], S_BG, 0)

    def relay_qkv(t, k):
        WQ, YQ, lanes = g(B_WQ, t), g(B_YQ, t), pl.ds(k * HALF, HALF)
        wait(YQ.at[:, lanes], S_YQ + k, t)
        for r0 in range(0, HALF, 128):
            r = pl.ds(mo(y * HALF + r0, 128), 128)
            WQ[r, lanes] = (WQ[r, lanes].astype(F32) + YQ[pl.ds(r0, 128), lanes].astype(F32)).astype(BF)
        dst = g(B_GQ, t).at[2 * x + c, :, lanes]
        for dx, dc in ((1, 0), (1, 1), (0, 1), (0, 0)):
            owner = sh(y, flip(x, dx), flip(c, dc))
            src = WQ.at[pl.ds(mo(96 * owner, 32), 96), lanes]
            if dx + dc:
                send(src, dst, S_GQ + k, t, (rep, owner))
            else:
                local(src, dst, S_GQ + k, t)

    def input_back(t):
        T = ROWS[t]
        wait(g(B_OR, t), S_DX, t)

        @pl.loop(0, T // CH)
        def _(i):
            r = pl.ds(mo(i * CH, CH), CH)
            g(B_Y, t)[r, :] = (g(B_N1, t)[r, :] + g(B_KP, t)[0, r, :] + g(B_OR, t)[r, :].astype(F32)).astype(BF)

        local(g(B_Y, t), (o_gx0, o_gx1)[t], S_FIN2, 0, t)

    def make_dn(t, k):
        def each(use):
            wait(g(B_GD, t).at[pl.ds(128 * k, 128)], S_GD + k, t)
            for r0 in (128 * k, 128 * k + 64):
                own = g(B_WD, t)[pl.ds(mo(x * HALF + r0, 64), 64), :].astype(F32)
                use(pl.ds(r0, 64), pl.ds(0, D), own + g(B_GD, t)[pl.ds(r0, 64), :].astype(F32))
        return each

    def make_up(t, dy, xx):
        GU = g(B_GU, t)
        yy = flip(y, dy)

        def each(use):
            if xx == 0:
                wait(GU.at[pl.ds(0, 2)], S_GU1 - dy, t)
            cols = slice(xx * HALF, (xx + 1) * HALF)
            for cc in (0, 1):
                use(pl.ds(0, 96), pl.ds(mo((4 * yy + 2 * xx + cc) * HALF, 128), HALF), GU[2 * yy + cc, :, cols].astype(F32))
        return each

    def make_out(t):
        GO = g(B_GO, t)

        def each(use):
            wait(GO, S_GO, t)
            tot = GO[0].astype(F32)
            for k in range(1, 4):
                tot = tot + GO[k].astype(F32)
            use(pl.ds(0, 96), pl.ds(0, D), tot)
        return each

    def make_qkv(t, part):
        GQ = g(B_GQ, t)

        def each(use):
            cols = slice(part * HALF, (part + 1) * HALF)
            wait(GQ.at[:, :, pl.ds(part * HALF, HALF)], S_GQ + part, t)
            for cc in (0, 1):
                tot = GQ[cc, :, cols].astype(F32) + GQ[2 + cc, :, cols].astype(F32)
                use(pl.ds(0, 96), pl.ds(part * D + cc * HALF, HALF), tot)
        return each

    def each_small(use):
        BGR = g(B_BGR, 0)
        wait(BGR, S_BG, 0)
        tot = BGR[0].astype(F32)
        for k in range(1, 8):
            tot = tot + BGR[k].astype(F32)
        use(pl.ds(0, 16), pl.ds(0, HALF), tot)

    is_end = (rep == 0) | (rep == 3)
    units = []

    def unit(kind, t, each, out, rows, cols):
        if kind == 4:
            bufs = (B_BGS, B_BGA, B_BGB)
        else:
            bufs = (B_ZSD + kind, B_ZAD + kind, B_ZBD + kind)
        units.append((len(units), tuple(g(b, t) for b in bufs), each, out, rows, cols))

    def add_dn(t):
        for k in range(3):
            unit(0, t, make_dn(t, k), o_od.at[t], (128 * k, 128), (0, D))
    def add_up(t):
        for dy in (1, 0):
            for xx in (0, 1):
                at = mo((2 * flip(y, dy) + xx) * D, 128)
                unit(1, t, make_up(t, dy, xx), o_ou.at[t], (0, 96), (at, D))

    def add_qkv(t):
        for part in range(3):
            unit(3, t, make_qkv(t, part), o_oq.at[t], (0, 96), (part * D, D))

    add_dn(1)
    add_up(1)
    add_dn(0)
    unit(2, 1, make_out(1), o_oo.at[1], (0, 96), (0, D))
    add_up(0)
    unit(2, 0, make_out(0), o_oo.at[0], (0, 96), (0, D))
    add_qkv(1)
    unit(4, 0, each_small, o_obg, (0, 16), (0, HALF))
    add_qkv(0)
    assert len(units) == N_UNITS

    def hop(which, u):
        at = which * N_UNITS + u[0]
        return S_Z + at // 2, at % 2

    def view(ref, u):
        return ref.at[pl.ds(*u[4]), pl.ds(*u[5])]

    def ends(u):
        ZS, ZA, ZB = u[1]

        def put(r, cl, val):
            ZS[r, cl] = val.astype(ZS.dtype)

        for end, mid in ((0, 1), (3, 2)):
            @pl.when(rep == end)
            def _():
                u[2](put)
                send(view(ZS, u), view(ZA, u), *hop(0, u), (mid, s))

    def stage_a(u):
        ZS, ZA, ZB = u[1]

        def put_add(r, cl, val):
            ZS[r, cl] = (val + ZA[r, cl].astype(F32)).astype(ZS.dtype)

        for end, mid in ((0, 1), (3, 2)):
            @pl.when(rep == mid)
            def _():
                wait(view(ZA, u), *hop(0, u))
                u[2](put_add)
                send(view(ZS, u), view(ZB, u), *hop(1, u), (3 - mid, s))

    def stage_b(u):
        ZS, ZA, ZB = u[1]
        for end, mid in ((0, 1), (3, 2)):
            @pl.when(rep == mid)
            def _():
                wait(view(ZB, u), *hop(1, u))
                wait(view(ZB, u), *hop(1, u), 1)
                for r0 in range(u[4][0], u[4][0] + u[4][1], 16):
                    r, cl = pl.ds(r0, 16), pl.ds(*u[5])
                    ZS[r, cl] = (ZS[r, cl].astype(F32) + ZB[r, cl].astype(F32)).astype(ZS.dtype)
                send(view(ZS, u), view(u[3], u), *hop(2, u), (end, s))
                local(view(ZS, u), view(u[3], u), *hop(2, u))

    done = [0, 0, 0]

    def advance(n0, n1, n2):
        while done[0] < n0 or done[1] < n1 or done[2] < n2:
            for k, (step, n) in enumerate(((ends, n0), (stage_a, n1), (stage_b, n2))):
                if done[k] < n:
                    step(units[done[k]])
                    done[k] += 1

    relays = [functools.partial(relay_up, t, dy) for t in (1, 0) for dy in (1, 0)]
    relays += [functools.partial(relay_qkv, t, k) for t in (1, 0) for k in range(3)]

    def point():
        *steps, through = plan.pop(0)
        while len(relays) > 10 - through:
            relays.pop(0)()
        advance(*steps)

    plan = PLAN[:]
    cls_back(1)
    cls_back(0)
    mine = g(B_CF, 0).at[2 * y + c]
    g(B_CF, 0)[2 * y + c] = g(B_CFW, 0)[...].astype(BF)
    fixers = (ypeer, sib, (rep, sh(1 - y, x, 1 - c)))
    for dev in fixers:
        send(mine, mine, S_CF, 0, dev)
    pre_back(0)
    wait(g(B_CF, 0).at[pl.ds(0, 3)], S_CF, 0)
    for t in (0, 1):
        wait(g(B_Y, t), S_FIN, 0, t)
    ffn_back(1)
    ffn_back(0, point)
    mid_back(1)
    attention_back(1, point)
    mid_back(0)
    attention_back(0, point)
    input_back(1)
    input_back(0)
    while plan:
        point()
    for k in range(done[0], N_UNITS + 1):
        advance(min(k + 1, N_UNITS), k, k - 2)
    advance(N_UNITS, N_UNITS, N_UNITS)

    for u in units:
        ZS = view(u[1][0], u)
        wait(ZS, *hop(2, u))

        @pl.when(is_end)
        def _():
            wait(ZS, *hop(0, u), 1)

        @pl.when(jnp.logical_not(is_end))
        def _():
            wait(ZS, *hop(2, u), 1)

    for t in (0, 1):
        scatter_sent(t, S_D1A, S_D1B, S_D2)
        wait(g(B_OS, t), S_DA, t, 1)
        wait(g(B_OS, t), S_DX, t, 1)
        for k in range(3):
            wait(g(B_GD, t).at[pl.ds(0, 128)], S_GD + k, t, 1)
        wait(g(B_GU, t).at[pl.ds(0, 2)], S_GU, t, 1)
        wait(g(B_GU, t).at[pl.ds(0, 1)], S_GU1, t, 1)
        for dy in (0, 1):
            wait(g(B_XU, t).at[pl.ds(0, 192)], S_XU1 - dy, t, 1)

        @pl.when(c == y)
        def _():
            wait(g(B_GO, t).at[pl.ds(0, 3)], S_GO, t, 1)

        @pl.when(c != y)
        def _():
            wait(g(B_GO, t), S_GO, t, 1)

        for k in range(3):
            wait(g(B_YQ, t).at[:, pl.ds(k * HALF, HALF)], S_YQ + k, t, 1)
            wait(g(B_GQ, t).at[pl.ds(0, 3), :, pl.ds(k * HALF, HALF)], S_GQ + k, t, 1)
        wait(g(B_Y, t), S_FIN2, 0, t)
    wait(g(B_BGR, 0).at[pl.ds(0, 7)], S_BG, 0, 1)
    wait(g(B_CF, 0).at[pl.ds(0, 3)], S_CF, 0, 1)


def fused_call(*args):
    hbm = pl.BlockSpec(memory_space=pl.ANY)
    vm = pl.BlockSpec(memory_space=pltpu.VMEM)
    sm = pl.BlockSpec(memory_space=pltpu.SMEM)
    out_shape = [
        jax.ShapeDtypeStruct((8, 128), F32),
        jax.ShapeDtypeStruct((128, D), BF),
        jax.ShapeDtypeStruct((256, D), BF),
        jax.ShapeDtypeStruct((128, D), BF),
        jax.ShapeDtypeStruct((256, D), BF),
        jax.ShapeDtypeStruct((2, 96, 3 * D), BF),
        jax.ShapeDtypeStruct((2, 96, D), BF),
        jax.ShapeDtypeStruct((2, 96, 4 * D), BF),
        jax.ShapeDtypeStruct((2, HALF, D), BF),
        jax.ShapeDtypeStruct((16, HALF), F32),
    ]
    return pl.pallas_call(
        fused_kernel,
        out_shape=out_shape,
        in_specs=[hbm] * 8 + [vm] * 6 + [sm] * 2,
        out_specs=[vm] + [hbm] * 9,
        scratch_shapes=[shape for _, shape in scratch_list()] + [pltpu.SemaphoreType.DMA((N_SEMS,))],
        compiler_params=pltpu.CompilerParams(collective_id=0, has_side_effects=True, vmem_limit_bytes=VMEM_LIMIT),
        cost_estimate=pl.CostEstimate(flops=18 * 10**9, bytes_accessed=40 * 10**6, transcendentals=4 * 10**6),
    )(*args)


def widen_kernel(*refs):
    loss, y0, y1, gx0, gx1, oq, oo, ou, od, bg = refs[:10]
    r_loss, r_y0, r_y1, r_gx0, r_gx1, r_q, r_qb, r_o, r_ob, r_u, r_ub, r_d, r_db, r_gn, r_sf = refs[10:25]
    low = refs[25:29]
    wide = refs[29:33]
    through = refs[33:37]
    sem_in, sem_out, sem_move, sem_move_out = refs[37:]
    groups = list(zip((oq, ou, od, oo), low, wide, (r_q, r_u, r_d, r_o)))
    reads, writes, moves = [], [], []
    for k, (src, lo, hi, dst) in enumerate(groups):
        for t in (0, 1):
            reads.append(pltpu.make_async_copy(src.at[t], lo.at[t], sem_in.at[2 * k + t]))
            reads[-1].start()
    for k, (src, dst) in enumerate(((y0, r_y0), (y1, r_y1), (gx0, r_gx0), (gx1, r_gx1))):
        moves.append((pltpu.make_async_copy(src, through[k], sem_move.at[k]),
                      pltpu.make_async_copy(through[k], dst, sem_move_out.at[k])))
        moves[-1][0].start()
    r_loss[...] = loss[0:1, 0:1]
    r_ob[...] = bg[0:2, 0:96]
    r_db[...] = bg[2:4, 0:96]
    for t in (0, 1):
        r_gn[t] = bg[4 + 2 * t:6 + 2 * t, 0:96]
        r_sf[t] = bg[8 + 2 * t:10 + 2 * t, 0:96]
    r_qb[...] = bg[0:2, 128:320]
    r_ub[...] = bg[12:14, :]
    for k, (src, lo, hi, dst) in enumerate(groups):
        for t in (0, 1):
            reads[2 * k + t].wait()
            hi[t] = lo[t].astype(F32)
            writes.append(pltpu.make_async_copy(hi.at[t], dst.at[t], sem_out.at[2 * k + t]))
            writes[-1].start()
    for there, onward in moves:
        there.wait()
        onward.start()
    for copy in writes + [onward for there, onward in moves]:
        copy.wait()


def widen_call(*args):
    hbm = pl.BlockSpec(memory_space=pl.ANY)
    vm = pl.BlockSpec(memory_space=pltpu.VMEM)

    def out(dtype, *shape):
        return jax.ShapeDtypeStruct(shape, dtype)

    shapes = [(2, 96, 3 * D), (2, 96, 4 * D), (2, HALF, D), (2, 96, D)]
    return pl.pallas_call(
        widen_kernel,
        out_shape=[out(F32, 1, 1), out(BF, 128, D), out(BF, 256, D), out(BF, 128, D), out(BF, 256, D),
                   out(F32, *shapes[0]), out(F32, 2, 192), out(F32, *shapes[3]), out(F32, 2, 96),
                   out(F32, *shapes[1]), out(F32, 2, HALF), out(F32, *shapes[2]), out(F32, 2, 96),
                   out(F32, 2, 2, 96), out(F32, 2, 2, 96)],
        in_specs=[vm] + [hbm] * 8 + [vm],
        out_specs=[vm, hbm, hbm, hbm, hbm, hbm, vm, hbm, vm, hbm, vm, hbm, vm, vm, vm],
        scratch_shapes=[pltpu.VMEM(shape, BF) for shape in shapes] + [pltpu.VMEM(shape, F32) for shape in shapes]
        + [pltpu.VMEM((rows, D), BF) for rows in ROWS * 2]
        + [pltpu.SemaphoreType.DMA((8,)), pltpu.SemaphoreType.DMA((8,)), pltpu.SemaphoreType.DMA((4,)),
           pltpu.SemaphoreType.DMA((4,))],
        compiler_params=pltpu.CompilerParams(vmem_limit_bytes=VMEM_LIMIT),
    )(*args)


def local_fast(query_tokens, passage_tokens, query_cot, passage_cot, bucket_counts, positives, qkv_weight, qv_bias,
               out_weight, out_bias, up_weight, up_bias, down_weight, down_bias, norm_gains, norm_shifts):
    results = widen_call(*fused_call(
        query_tokens.reshape(128, D), passage_tokens.reshape(256, D),
        query_cot.reshape(128, D), passage_cot.reshape(256, D),
        qkv_weight, out_weight, up_weight, down_weight,
        qv_bias, out_bias, up_bias, down_bias, norm_gains, norm_shifts, bucket_counts, positives))
    loss, y0, y1, gx0, gx1 = results[:5]
    return (loss.reshape(()), y0.reshape(query_tokens.shape), y1.reshape(passage_tokens.shape),
            gx0.reshape(query_tokens.shape), gx1.reshape(passage_tokens.shape), *results[5:])


def solution(mesh):
    in_specs = (
        P(("rep", "shard"), None, None),
        P(("rep", "shard"), None, None),
        P(("rep", "shard"), None, None),
        P(("rep", "shard"), None, None),
        P(),
        P(("rep", "shard")),
        P(None, "shard", None),
        P(None, "shard"),
        P(None, "shard", None),
        P(None, "shard"),
        P(None, "shard", None),
        P(None, "shard"),
        P(None, "shard", None),
        P(None, "shard"),
        P(None, None, "shard"),
        P(None, None, "shard"),
    )
    out_specs = (
        P(),
        P(("rep", "shard"), None, None),
        P(("rep", "shard"), None, None),
        P(("rep", "shard"), None, None),
        P(("rep", "shard"), None, None),
        P(None, "shard", None),
        P(None, "shard"),
        P(None, "shard", None),
        P(None, "shard"),
        P(None, "shard", None),
        P(None, "shard"),
        P(None, "shard", None),
        P(None, "shard"),
        P(None, None, "shard"),
        P(None, None, "shard"),
    )
    small_mesh = (mesh.shape["rep"], mesh.shape["shard"]) == (4, 8)
    step = local_fast if small_mesh else local
    return jax.shard_map(step, mesh=mesh, in_specs=in_specs, out_specs=out_specs, check_vma=False)
```

```python
import functools
import math

import jax
import jax.numpy as jnp
from jax import lax
from jax.experimental import pallas as pl
from jax.experimental.pallas import tpu as pltpu
from jax.sharding import PartitionSpec as P

HD = 64
SHORT = 64


LN_EPS = 1e-05
NEG_FILL = -1e30
INV_ROOT_TWO = 0.7071067811865476
INV_ROOT_TWO_PI = 0.3989422804014327
VMEM_LIMIT = 66 * 1000 * 1000


def for_sending(array):
    return jax.tree.map(lambda a: a.astype(jnp.bfloat16) if a.dtype == jnp.float32 else a, array)


def pick_tower(stacks, tower_index):
    qkv_w, qv_b, out_w, out_b, up_w, up_b, down_w, down_b, gains, shifts = stacks
    return (
        qkv_w[tower_index],
        qv_b[tower_index],
        out_w[tower_index],
        out_b[tower_index],
        up_w[tower_index],
        up_b[tower_index],
        down_w[tower_index],
        down_b[tower_index],
        gains[tower_index].T,
        shifts[tower_index].T,
    )


def fetch_layer(stacks, tower_index):
    return lax.all_gather(for_sending(pick_tower(stacks, tower_index)), "shard", axis=0, tiled=True)


def fetch_again(stacks, tower_index):
    return lax.all_gather(for_sending(pick_tower(stacks, tower_index)), "shard", axis=0, tiled=True)


def normalize(hidden):
    row_mean = jnp.mean(hidden, axis=-1, keepdims=True)
    centred = hidden - row_mean
    inv_std = lax.rsqrt(jnp.mean(centred * centred, axis=-1, keepdims=True) + LN_EPS)
    return (centred * inv_std, inv_std)


def norm_back(grad_in, normed, inv_std):
    return inv_std * (
        grad_in
        - jnp.mean(grad_in, axis=-1, keepdims=True)
        - normed * jnp.mean(grad_in * normed, axis=-1, keepdims=True)
    )


def block_mask(long_flags, length, short_len):
    row_part = lax.broadcasted_iota(jnp.int32, (length, length), 0) // short_len
    col_part = lax.broadcasted_iota(jnp.int32, (length, length), 1) // short_len
    return long_flags[:, None, None] | (row_part == col_part)[None]


def head_scores(head_query, head_key, attn_mask):
    raw_scores = jnp.einsum(
        "slhd,smhd->shlm", head_query, head_key, preferred_element_type=jnp.float32
    ) * (1.0 / math.sqrt(HD))
    return jnp.where(attn_mask[:, None], raw_scores, NEG_FILL)


def layer_forward(tokens, weights, attn_mask):
    qkv_w, qv_b, out_w, out_b, up_w, up_b, down_w, down_b, gains, shifts = weights
    seq_count, length, model_width = tokens.shape
    head_count = model_width // HD
    token_rows = tokens.reshape(seq_count * length, model_width)
    qv_float = qv_b.astype(jnp.float32)
    qkv_bias = jnp.concatenate(
        [qv_float[:model_width], jnp.zeros((model_width,), jnp.float32), qv_float[model_width:]]
    )
    qkv_low = (jnp.dot(token_rows, qkv_w, preferred_element_type=jnp.float32) + qkv_bias).astype(
        jnp.bfloat16
    )
    head_split = qkv_low.reshape(seq_count, length, 3, head_count, HD)
    scores = head_scores(head_split[:, :, 0], head_split[:, :, 1], attn_mask)
    row_max = jnp.max(scores, axis=-1, keepdims=True)
    exp_scores = jnp.exp(scores - row_max)
    row_total = jnp.sum(exp_scores, axis=-1, keepdims=True)
    attn_probs = (exp_scores / row_total).astype(jnp.bfloat16)
    log_total = row_max + jnp.log(row_total)
    attn_mixed = jnp.einsum(
        "shlm,smhd->slhd", attn_probs, head_split[:, :, 2], preferred_element_type=jnp.float32
    )
    attn_low = attn_mixed.reshape(seq_count * length, model_width).astype(jnp.bfloat16)
    first_sum = (
        token_rows.astype(jnp.float32)
        + jnp.dot(attn_low, out_w, preferred_element_type=jnp.float32)
        + out_b.astype(jnp.float32)
    )
    normed_one, inv_one = normalize(first_sum)
    gain_float = gains.astype(jnp.float32)
    shift_float = shifts.astype(jnp.float32)
    middle = normed_one * gain_float[:, 0] + shift_float[:, 0]
    middle_low = middle.astype(jnp.bfloat16)
    pre_act = jnp.dot(middle_low, up_w, preferred_element_type=jnp.float32) + up_b.astype(
        jnp.float32
    )
    act_low = jax.nn.gelu(pre_act, approximate=False).astype(jnp.bfloat16)
    second = (
        middle
        + jnp.dot(act_low, down_w, preferred_element_type=jnp.float32)
        + down_b.astype(jnp.float32)
    )
    normed_two, inv_two = normalize(second)
    result = normed_two * gain_float[:, 1] + shift_float[:, 1]
    kept = (
        token_rows,
        qkv_low,
        log_total,
        attn_low,
        normed_one,
        inv_one,
        middle_low,
        pre_act,
        act_low,
        normed_two,
        inv_two,
    )
    return (result, kept)


def layer_backward(grad_out, weights, kept, attn_mask):
    qkv_w, qv_b, out_w, out_b, up_w, up_b, down_w, down_b, gains, shifts = weights
    (
        token_rows,
        qkv_low,
        log_total,
        attn_low,
        normed_one,
        inv_one,
        middle_low,
        pre_act,
        act_low,
        normed_two,
        inv_two,
    ) = kept
    seq_count = attn_mask.shape[0]
    model_width = token_rows.shape[1]
    length = token_rows.shape[0] // seq_count
    head_count = model_width // HD
    gain_float = gains.astype(jnp.float32)
    gain_two = jnp.sum(grad_out * normed_two, axis=0)
    shift_two = jnp.sum(grad_out, axis=0)
    d_second = norm_back(grad_out * gain_float[:, 1], normed_two, inv_two)
    d_ffn = d_second.astype(jnp.bfloat16)
    d_down_w = jnp.dot(act_low.T, d_ffn, preferred_element_type=jnp.float32)
    d_down_b = jnp.sum(d_ffn.astype(jnp.float32), axis=0)
    d_act = jnp.dot(d_ffn, down_w.T, preferred_element_type=jnp.float32)
    gelu_slope = (
        0.5 * (1.0 + lax.erf(pre_act * INV_ROOT_TWO))
        + pre_act * jnp.exp(-0.5 * pre_act * pre_act) * INV_ROOT_TWO_PI
    )
    d_pre = (d_act * gelu_slope).astype(jnp.bfloat16)
    d_up_w = jnp.dot(middle_low.T, d_pre, preferred_element_type=jnp.float32)
    d_up_b = jnp.sum(d_pre.astype(jnp.float32), axis=0)
    d_middle = d_second + jnp.dot(d_pre, up_w.T, preferred_element_type=jnp.float32)
    gain_one = jnp.sum(d_middle * normed_one, axis=0)
    shift_one = jnp.sum(d_middle, axis=0)
    d_first = norm_back(d_middle * gain_float[:, 0], normed_one, inv_one)
    d_attn_out = d_first.astype(jnp.bfloat16)
    d_out_w = jnp.dot(attn_low.T, d_attn_out, preferred_element_type=jnp.float32)
    d_out_b = jnp.sum(d_attn_out.astype(jnp.float32), axis=0)
    d_mixed = (
        jnp.dot(d_attn_out, out_w.T, preferred_element_type=jnp.float32)
        .astype(jnp.bfloat16)
        .reshape(seq_count, length, head_count, HD)
    )
    head_split = qkv_low.reshape(seq_count, length, 3, head_count, HD)
    head_query = head_split[:, :, 0]
    head_key = head_split[:, :, 1]
    head_value = head_split[:, :, 2]
    attn_probs = jnp.exp(head_scores(head_query, head_key, attn_mask) - log_total)
    d_probs = jnp.einsum("slhd,smhd->shlm", d_mixed, head_value, preferred_element_type=jnp.float32)
    d_value = jnp.einsum(
        "shlm,slhd->smhd",
        attn_probs.astype(jnp.bfloat16),
        d_mixed,
        preferred_element_type=jnp.float32,
    )
    d_scores = (
        attn_probs * (d_probs - jnp.sum(d_probs * attn_probs, axis=-1, keepdims=True))
    ).astype(jnp.bfloat16)
    d_query = jnp.einsum(
        "shlm,smhd->slhd", d_scores, head_key, preferred_element_type=jnp.float32
    ) * (1.0 / math.sqrt(HD))
    d_key = jnp.einsum(
        "shlm,slhd->smhd", d_scores, head_query, preferred_element_type=jnp.float32
    ) * (1.0 / math.sqrt(HD))
    d_qkv = (
        jnp.stack([d_query, d_key, d_value], axis=2)
        .reshape(seq_count * length, 3 * model_width)
        .astype(jnp.bfloat16)
    )
    d_qkv_w = jnp.dot(token_rows.T, d_qkv, preferred_element_type=jnp.float32)
    column_sums = jnp.sum(d_qkv.astype(jnp.float32), axis=0)
    d_qv_b = jnp.concatenate([column_sums[:model_width], column_sums[2 * model_width :]])
    d_tokens = d_first + jnp.dot(d_qkv, qkv_w.T, preferred_element_type=jnp.float32)
    layer_grads = (
        d_qkv_w,
        d_qv_b,
        d_out_w,
        d_out_b,
        d_up_w,
        d_up_b,
        d_down_w,
        d_down_b,
        jnp.stack([gain_one, gain_two], axis=1),
        jnp.stack([shift_one, shift_two], axis=1),
    )
    return (d_tokens, layer_grads)


def reduce_layer(layer_grads):
    owned_grads = (
        lax.psum_scatter(layer_grads[0], "shard", scatter_dimension=0, tiled=True),
        lax.psum_scatter(layer_grads[1], "shard", scatter_dimension=0, tiled=True),
        lax.psum_scatter(layer_grads[2], "shard", scatter_dimension=0, tiled=True),
        lax.psum_scatter(layer_grads[3], "shard", scatter_dimension=0, tiled=True),
        lax.psum_scatter(layer_grads[4], "shard", scatter_dimension=0, tiled=True),
        lax.psum_scatter(layer_grads[5], "shard", scatter_dimension=0, tiled=True),
        lax.psum_scatter(layer_grads[6], "shard", scatter_dimension=0, tiled=True),
        lax.psum_scatter(layer_grads[7], "shard", scatter_dimension=0, tiled=True),
        lax.psum_scatter(layer_grads[8], "shard", scatter_dimension=0, tiled=True),
        lax.psum_scatter(layer_grads[9], "shard", scatter_dimension=0, tiled=True),
    )
    quarter = (
        lax.psum_scatter(
            owned_grads[0].astype(jnp.bfloat16), "rep", scatter_dimension=0, tiled=True
        ).astype(jnp.float32),
        lax.psum_scatter(
            owned_grads[1].astype(jnp.bfloat16), "rep", scatter_dimension=0, tiled=True
        ).astype(jnp.float32),
        lax.psum_scatter(
            owned_grads[2].astype(jnp.bfloat16), "rep", scatter_dimension=0, tiled=True
        ).astype(jnp.float32),
        lax.psum_scatter(
            owned_grads[3].astype(jnp.bfloat16), "rep", scatter_dimension=0, tiled=True
        ).astype(jnp.float32),
        lax.psum_scatter(
            owned_grads[4].astype(jnp.bfloat16), "rep", scatter_dimension=0, tiled=True
        ).astype(jnp.float32),
        lax.psum_scatter(
            owned_grads[5].astype(jnp.bfloat16), "rep", scatter_dimension=0, tiled=True
        ).astype(jnp.float32),
        lax.psum_scatter(
            owned_grads[6].astype(jnp.bfloat16), "rep", scatter_dimension=0, tiled=True
        ).astype(jnp.float32),
        lax.psum_scatter(
            owned_grads[7].astype(jnp.bfloat16), "rep", scatter_dimension=0, tiled=True
        ).astype(jnp.float32),
        lax.psum_scatter(
            owned_grads[8].astype(jnp.bfloat16), "rep", scatter_dimension=0, tiled=True
        ).astype(jnp.float32),
        lax.psum_scatter(
            owned_grads[9].astype(jnp.bfloat16), "rep", scatter_dimension=0, tiled=True
        ).astype(jnp.float32),
    )
    return (
        lax.all_gather(quarter[0].astype(jnp.bfloat16), "rep", axis=0, tiled=True).astype(
            jnp.float32
        ),
        lax.all_gather(quarter[1].astype(jnp.bfloat16), "rep", axis=0, tiled=True).astype(
            jnp.float32
        ),
        lax.all_gather(quarter[2].astype(jnp.bfloat16), "rep", axis=0, tiled=True).astype(
            jnp.float32
        ),
        lax.all_gather(quarter[3].astype(jnp.bfloat16), "rep", axis=0, tiled=True).astype(
            jnp.float32
        ),
        lax.all_gather(quarter[4].astype(jnp.bfloat16), "rep", axis=0, tiled=True).astype(
            jnp.float32
        ),
        lax.all_gather(quarter[5].astype(jnp.bfloat16), "rep", axis=0, tiled=True).astype(
            jnp.float32
        ),
        lax.all_gather(quarter[6].astype(jnp.bfloat16), "rep", axis=0, tiled=True).astype(
            jnp.float32
        ),
        lax.all_gather(quarter[7].astype(jnp.bfloat16), "rep", axis=0, tiled=True).astype(
            jnp.float32
        ),
        lax.all_gather(quarter[8].astype(jnp.bfloat16), "rep", axis=0, tiled=True).astype(
            jnp.float32
        ),
        lax.all_gather(quarter[9].astype(jnp.bfloat16), "rep", axis=0, tiled=True).astype(
            jnp.float32
        ),
    )


def local(
    query_tokens,
    passage_tokens,
    query_cot,
    passage_cot,
    bucket_counts,
    positives,
    qkv_weight,
    qv_bias,
    out_weight,
    out_bias,
    up_weight,
    up_bias,
    down_weight,
    down_bias,
    norm_gains,
    norm_shifts,
):
    stacks = (
        qkv_weight,
        qv_bias,
        out_weight,
        out_bias,
        up_weight,
        up_bias,
        down_weight,
        down_bias,
        norm_gains,
        norm_shifts,
    )
    blocks, long_len, model_width = passage_tokens.shape
    query_count, query_len, unused_width = query_tokens.shape
    subs_count = long_len // SHORT
    slot_count = blocks * subs_count
    my_index = lax.axis_index(("rep", "shard"))
    own_count = lax.dynamic_index_in_dim(bucket_counts, my_index, 0, keepdims=False)
    passage_mask = block_mask(lax.iota(jnp.int32, blocks) < own_count, long_len, SHORT)
    query_mask = block_mask(jnp.ones((query_count,), dtype=bool), query_len, query_len)
    query_weights = fetch_layer(stacks, 0)
    query_result, query_kept = layer_forward(query_tokens, query_weights, query_mask)
    passage_weights = fetch_layer(stacks, 1)
    passage_result, passage_kept = layer_forward(passage_tokens, passage_weights, passage_mask)
    query_cls = query_result.reshape(query_count, query_len, model_width)[:, 0].astype(jnp.bfloat16)
    passage_cls = (
        passage_result.reshape(blocks, subs_count, SHORT, model_width)[:, :, 0]
        .reshape(slot_count, model_width)
        .astype(jnp.bfloat16)
    )
    every_cls = lax.all_gather(passage_cls, ("rep", "shard"), axis=0, tiled=True)
    cand_count = every_cls.shape[0]
    device_count = bucket_counts.shape[0]
    score_scale = 2.0 / math.sqrt(model_width)
    logits = jnp.dot(query_cls, every_cls.T, preferred_element_type=jnp.float32) * score_scale
    slot_ids = lax.iota(jnp.int32, cand_count)
    owner_index = slot_ids // slot_count
    owner_counts = jnp.sum(
        jnp.where(
            owner_index[:, None] == lax.iota(jnp.int32, device_count)[None], bucket_counts[None], 0
        ),
        axis=1,
    )
    slot_valid = (slot_ids % slot_count // subs_count >= owner_counts) | (
        slot_ids % subs_count == 0
    )
    masked = jnp.where(slot_valid[None], logits, NEG_FILL)
    row_max = jnp.max(masked, axis=1, keepdims=True)
    exp_scores = jnp.exp(masked - row_max)
    row_total = jnp.sum(exp_scores, axis=1, keepdims=True)
    log_total = row_max[:, 0] + jnp.log(row_total[:, 0])
    hit_mask = slot_ids[None] == positives[:, None]
    picked = jnp.sum(jnp.where(hit_mask, masked, 0.0), axis=1)
    local_loss = jnp.sum(log_total - picked)
    d_logits = (exp_scores / row_total - hit_mask.astype(jnp.float32)).astype(jnp.bfloat16)
    d_query_cls = jnp.dot(d_logits, every_cls, preferred_element_type=jnp.float32) * score_scale
    d_cands = (
        lax.dot_general(
            d_logits, query_cls, (((0,), (0,)), ((), ())), preferred_element_type=jnp.float32
        )
        * score_scale
    )
    d_passage_cls = lax.psum_scatter(d_cands, ("rep", "shard"), scatter_dimension=0, tiled=True)
    loss_sum = lax.psum(local_loss, ("rep", "shard"))
    loss = loss_sum / (query_count * lax.axis_size(("rep", "shard")))
    query_dout = (
        query_cot.astype(jnp.float32)
        .at[:, 0]
        .add(d_query_cls)
        .reshape(query_count * query_len, model_width)
    )
    passage_dout = (
        passage_cot.astype(jnp.float32)
        .reshape(blocks, subs_count, SHORT, model_width)
        .at[:, :, 0]
        .add(d_passage_cls.reshape(blocks, subs_count, model_width))
        .reshape(blocks * long_len, model_width)
    )
    passage_back = fetch_again(stacks, 1)
    passage_dx, passage_grads = layer_backward(
        passage_dout, passage_back, passage_kept, passage_mask
    )
    passage_owned = reduce_layer(passage_grads)
    query_back = fetch_again(stacks, 0)
    query_dx, query_grads = layer_backward(query_dout, query_back, query_kept, query_mask)
    query_owned = reduce_layer(query_grads)
    stacked = [
        jnp.stack([first_g, second_g]) for first_g, second_g in zip(query_owned, passage_owned)
    ]
    gains_grad = jnp.swapaxes(stacked[8], 1, 2)
    shifts_grad = jnp.swapaxes(stacked[9], 1, 2)
    return (
        loss,
        query_result.reshape(query_count, query_len, model_width).astype(jnp.bfloat16),
        passage_result.reshape(blocks, long_len, model_width).astype(jnp.bfloat16),
        query_dx.reshape(query_count, query_len, model_width).astype(jnp.bfloat16),
        passage_dx.reshape(blocks, long_len, model_width).astype(jnp.bfloat16),
        stacked[0],
        stacked[1],
        stacked[2],
        stacked[3],
        stacked[4],
        stacked[5],
        stacked[6],
        stacked[7],
        gains_grad,
        shifts_grad,
    )


BF = jnp.bfloat16
F32 = jnp.float32
MESH = pl.DeviceIdType.MESH
ROWS = (128, 256)
D = 768
HALF = 384
FFN = 768
PLAN = [(2, 2, 0, 0), (2, 2, 1, 0), (2, 2, 1, 0), (3, 3, 2, 1), (4, 3, 2, 2), (6, 4, 2, 2), (6, 5, 3, 2), (10, 8, 5, 2), (10, 8, 7, 3), (10, 10, 9, 3), (13, 10, 10, 5), (14, 11, 10, 5), (15, 12, 10, 6), (15, 15, 13, 6), (18, 17, 15, 7), (20, 18, 16, 7), (21, 21, 18, 9), (21, 21, 18, 9), (22, 21, 18, 10), (23, 21, 18, 10), (23, 21, 20, 10)]
NEIGH = tuple((dy, dx, dc) for dy in (0, 1) for dx in (0, 1) for dc in (0, 1) if dy + dx + dc)

(S_X, S_QKV, S_QKV1, S_QKV2, S_QKVC, S_QKVZ, S_QKVZ1, S_QKVZ2, S_OUT, S_OUTC, S_OUTZ, S_UP, S_UP1, S_UPC, S_UPZ, S_UPZ1,
 S_DN, S_OP, S_MY, S_MC, S_MF, S_F1A, S_F1B, S_F2, S_DY, S_DC, S_DF, S_D1A, S_D1B, S_D2,
 S_DA, S_DX, S_GD, S_GD1, S_GD2, S_GU, S_GU1, S_XU, S_XU1, S_GO, S_GQ, S_GQ1, S_GQ2, S_YQ, S_YQ1, S_YQ2, S_SMALL, S_CZ, S_CP, S_CPC, S_CPF, S_BG, S_COT, S_FIN, S_FIN2, S_CF, S_Z) = range(57)
N_UNITS = 23
N_SEMS = 4 * S_Z + 6 * N_UNITS + 2


def nn(a, b):
    return jnp.dot(a, b, preferred_element_type=F32)


def nt(a, b):
    return lax.dot_general(a, b, (((1,), (1,)), ((), ())), preferred_element_type=F32)


def tn(a, b):
    return lax.dot_general(a, b, (((0,), (0,)), ((), ())), preferred_element_type=F32)


def flip(v, d):
    return 1 - v if d else v


def mo(v, m):
    return pl.multiple_of(v, m)


(B_X, B_COT, B_WQ, B_WO, B_WU, B_WD, B_QB, B_UB, B_QKV, B_P, B_ATT, B_OS,
 B_OR, B_N1, B_N2, B_R1, B_R2, B_MID, B_ACT, B_SL, B_S1, B_V1, B_S2, B_V2,
 B_KP, B_Y, B_DF, B_DA, B_GD, B_GU, B_GO, B_GQ, B_ZSD, B_ZSU, B_ZSO, B_ZSQ,
 B_ZAD, B_ZAU, B_ZAO, B_ZAQ, B_ZBD, B_ZBU, B_ZBO, B_ZBQ, B_CLN, B_CLR, B_CLC, B_CLS,
 B_CLD, B_CLP, B_CFW, B_CF, B_YQ, B_T96, B_SP, B_BGC, B_PV, B_BG, B_BGS, B_BGR,
 B_BGA, B_BGB, B_CM, B_GA, B_CG, B_DAT, B_XU) = range(67)


def scratch_list():
    s = []

    def add(name, t, shape, dtype):
        s.append(((name, t), pltpu.VMEM(shape, dtype)))

    for t, T in enumerate(ROWS):
        add(B_X, t, (2 * T, D), BF)
        add(B_COT, t, (T, D), BF)
        add(B_WQ, t, (D, 3 * HALF), BF)
        add(B_WO, t, (HALF, D), BF)
        add(B_WU, t, (D, FFN), BF)
        add(B_WD, t, (FFN, D), BF)
        add(B_QB, t, (8, 3 * HALF), F32)
        add(B_UB, t, (8, FFN), F32)
        add(B_QKV, t, (2 * T, 3 * HALF), BF)
        add(B_P, t, (12, T, T), F32)
        add(B_ATT, t, (2 * T, HALF), BF)
        add(B_OS, t, (T, D), BF)
        add(B_OR, t, (T, D), BF)
        add(B_N1, t, (T, D), F32)
        add(B_N2, t, (T, D), F32)
        add(B_R1, t, (T, 128), F32)
        add(B_R2, t, (T, 128), F32)
        add(B_MID, t, (4 * T, D), BF)
        add(B_ACT, t, (4 * T, FFN), BF)
        add(B_SL, t, (4 * T, FFN), BF)
        add(B_S1, t, (2, T, D), BF)
        add(B_V1, t, (2, T, D), BF)
        add(B_S2, t, (T, D), BF)
        add(B_V2, t, (T, D), BF)
        add(B_KP, t, (2, T, D), F32)
        add(B_Y, t, (T, D), BF)
        add(B_DF, t, (4 * T, D), BF)
        add(B_DA, t, (2 * T, D), BF)
        add(B_DAT, t, (2 * T, HALF), BF)
        add(B_GD, t, (HALF, D), BF)
        add(B_GU, t, (4, 96, FFN), BF)
        add(B_XU, t, (HALF, FFN), BF)
        add(B_GO, t, (4, 96, D), BF)
        add(B_GQ, t, (4, 96, 3 * HALF), BF)
        add(B_YQ, t, (HALF, 3 * HALF), BF)
        for first in (B_ZSD, B_ZAD, B_ZBD):
            add(first, t, (HALF, D), BF)
            add(first + 1, t, (96, 4 * D), BF)
            add(first + 2, t, (96, D), BF)
            add(first + 3, t, (96, 3 * D), BF)
    for t in (0, 1):
        add(B_CLN, t, (8, D), F32)
        add(B_CLR, t, (8, 128), F32)
        add(B_CLC, t, (8, D), F32)
        add(B_CLS, t, (16, FFN), BF)
        add(B_CLD, t, (16, D), F32)
        add(B_CLP, t, (16, FFN), F32)
    add(B_CFW, 0, (16, D), F32)
    add(B_CF, 0, (4, 16, D), BF)
    add(B_T96, 0, (16, HALF), F32)
    add(B_SP, 0, (8, 16, HALF), BF)
    add(B_PV, 0, (32, D), F32)
    add(B_BG, 0, (32, D), F32)
    add(B_BGC, 0, (8, 16, HALF), BF)
    add(B_BGR, 0, (8, 16, HALF), BF)
    add(B_BGS, 0, (16, HALF), F32)
    add(B_BGA, 0, (16, HALF), F32)
    add(B_BGB, 0, (16, HALF), F32)
    add(B_CM, 0, (16, 512), BF)
    add(B_GA, 0, (32, 16, 512), BF)
    add(B_CG, 0, (2, 16, D), F32)
    return s


def fused_kernel(*refs):
    (i_x0, i_x1, i_cot0, i_cot1, i_qkvw, i_outw, i_upw, i_dnw, i_qvb, i_ob, i_ub, i_db, i_gn, i_sf, i_cnt, i_pos,
     o_loss, o_y0, o_y1, o_gx0, o_gx1, o_oq, o_oo, o_ou, o_od, o_obg) = refs[:26]
    held = {key: ref for (key, _), ref in zip(scratch_list(), refs[26:])}
    sems = refs[-1]

    def g(name, t):
        return held[(name, t)]

    rep = lax.axis_index("rep")
    s = lax.axis_index("shard")
    y = s // 4
    x = (s // 2) % 2
    c = s % 2
    x_in = (i_x0, i_x1)
    cot_in = (i_cot0, i_cot1)

    def sem(name, t, side):
        return sems.at[4 * name + 2 * t + side]

    def sh(yy, xx, cc):
        return yy * 4 + xx * 2 + cc

    def send(src, dst, name, t, dev):
        pltpu.make_async_remote_copy(src, dst, send_sem=sem(name, t, 1), recv_sem=sem(name, t, 0),
                                     device_id=dev, device_id_type=MESH).start()

    def local(src, dst, name, t, side=0):
        pltpu.make_async_copy(src, dst, sem(name, t, side)).start()

    def wait(ref, name, t, side=0):
        pltpu.make_async_copy(ref, ref, sem(name, t, side)).wait()

    def peer(d):
        return flip(y, d[0]), flip(x, d[1]), flip(c, d[2])

    sib = (rep, sh(y, x, 1 - c))
    ypeer = (rep, sh(1 - y, x, c))
    xpeer = (rep, sh(y, 1 - x, c))

    bar = pltpu.get_barrier_semaphore()
    for d in NEIGH:
        pl.semaphore_signal(bar, 1, device_id=(rep, sh(*peer(d))), device_id_type=MESH)
    for k in (1, 2, 3):
        pl.semaphore_signal(bar, 1, device_id=((rep + k) % 4, s), device_id_type=MESH)

    T96, SP, PV = (g(b, 0) for b in (B_T96, B_SP, B_PV))
    T96[...] = jnp.zeros((16, HALF), F32)
    T96[0:2, 0:96] = i_ob[...].astype(F32)
    T96[2:4, 0:96] = i_db[...].astype(F32)
    for t in (0, 1):
        for k in (0, 1):
            T96[4 + 2 * t + k:5 + 2 * t + k, 0:96] = i_gn[t, k:k + 1, :].astype(F32)
            T96[8 + 2 * t + k:9 + 2 * t + k, 0:96] = i_sf[t, k:k + 1, :].astype(F32)
    T96[0:2, 128:320] = i_qvb[...].astype(F32)
    T96[12:14, :] = i_ub[...].astype(F32)
    SP[s] = T96[...].astype(BF)

    def place(n, w, at):
        i = lax.broadcasted_iota(jnp.int32, (n, D), 0)
        j = lax.broadcasted_iota(jnp.int32, (n, D), 1)
        return ((j == i + at) & (i < w)).astype(F32).astype(BF)

    pl.semaphore_wait(bar, 10)

    half = rep % 2
    zpair = (rep + 1 - 2 * half, s)
    for d in NEIGH:
        send(SP.at[s], SP.at[s], S_SMALL, 0, (rep, sh(*peer(d))))
    rows96 = pl.ds(mo(s * 96, 32), 96)
    half48 = pl.ds(mo(half * 48, 16), 48)

    def send_x(t):
        T = ROWS[t]
        own = g(B_X, t).at[pl.ds(mo(c * T, 128), T)]
        send(x_in[t], own, S_X, t, sib)
        local(x_in[t], own, S_X, t)

    def rows48(owner):
        return pl.ds(mo(owner * 96 + half * 48, 16), 48)

    def send_cols(t, src, dst, pieces, far, near):
        for k in range(len(pieces((y, x, c)))):
            for d in NEIGH + ((0, 0, 0),):
                p = peer(d)
                cols, to = pl.ds(mo(pieces(p)[k], 128), HALF), pl.ds(k * HALF, HALF)
                if d[0] + d[1]:
                    send(src.at[t, half48, cols], dst.at[rows48(s), to], far + k, t, (rep, sh(*p)))
                elif d[2]:
                    send(src.at[t, :, cols], dst.at[rows96, to], near, t, sib)
                else:
                    local(src.at[t, :, cols], dst.at[rows96, to], near, t)

    def send_qkv(t):
        send_cols(t, i_qkvw, g(B_WQ, t), lambda p: [part * D + p[2] * HALF for part in range(3)], S_QKV, S_QKVC)

    def send_up(t):
        send_cols(t, i_upw, g(B_WU, t), lambda p: [HALF * (4 * p[0] + 2 * xx + p[2]) for xx in (0, 1)], S_UP, S_UPC)

    def part_of(buf, rows, k):
        return buf.at[pl.ds(0, rows), pl.ds(k * HALF, HALF)]

    def forward_cols(t, buf, k, far, pair):
        wait(part_of(buf, 288, k), far + k, t)
        for d in NEIGH:
            if d[0] + d[1]:
                piece = buf.at[rows48(sh(*peer(d))), pl.ds(k * HALF, HALF)]
                send(piece, piece, pair + k, t, zpair)

    def send_out(t):
        WO = g(B_WO, t)
        for dy in (0, 1):
            for dx in (0, 1):
                dev = (rep, sh(flip(y, dy), flip(x, dx), y))
                if dy + dx:
                    send(i_outw.at[t, half48], WO.at[rows48(x * 2 + c)], S_OUT, t, dev)
                else:
                    dst = WO.at[pl.ds(mo((x * 2 + c) * 96, 32), 96)]

                    @pl.when(c == y)
                    def _():
                        local(i_outw.at[t], dst, S_OUTC, t)

                    @pl.when(c != y)
                    def _():
                        send(i_outw.at[t], dst, S_OUTC, t, dev)

    def forward_out(t):
        WO = g(B_WO, t)

        def go(xs):
            for xx in xs:
                for cc in (0, 1):
                    piece = WO.at[rows48(xx * 2 + cc)]
                    send(piece, piece, S_OUTZ, t, zpair)

        @pl.when(c == y)
        def _():
            wait(WO.at[pl.ds(0, 96)], S_OUT, t)
            go((1 - x,))

        @pl.when(c != y)
        def _():
            wait(WO.at[pl.ds(0, 192)], S_OUT, t)
            go((0, 1))

    def whole_out(t):
        WO = g(B_WO, t)

        @pl.when(c == y)
        def _():
            wait(WO.at[pl.ds(0, 192)], S_OUTC, t)
            wait(WO.at[pl.ds(0, 96)], S_OUTZ, t)

        @pl.when(c != y)
        def _():
            wait(WO.at[pl.ds(0, 192)], S_OUTZ, t)

    def send_dn(t):
        dst = g(B_WD, t).at[pl.ds(mo(x * HALF, 128), HALF)]
        send(i_dnw.at[t], dst, S_DN, t, xpeer)
        local(i_dnw.at[t], dst, S_DN, t)

    for t in (1, 0):
        send_x(t)
        send_qkv(t)
        send_out(t)
    send_up(1)
    send_dn(1)
    for t in (0, 1):
        local(cot_in[t], g(B_COT, t), S_COT, 0, t)

    wait(SP.at[pl.ds(0, 7)], S_SMALL, 0)
    low96 = jnp.zeros((16, D), F32)
    low192 = [jnp.zeros((16, D), F32) for _ in (0, 1)]
    for k in range(8):
        low96 = low96 + nn(SP[k, :, 0:128], place(128, 96, 96 * k))
        low192[k // 4] = low192[k // 4] + nn(SP[k, :, 128:384], place(256, 192, 192 * (k % 4)))
    PV[0:16, :] = low96
    PV[12:14, :] = low192[0][0:2, :]
    PV[14:16, :] = low192[1][0:2, :]
    for k in range(8):
        for t in (0, 1):
            at, lanes = 16 + 4 * t + k // 2, slice(k % 2 * HALF, (k % 2 + 1) * HALF)
            PV[at:at + 1, lanes] = SP[k].astype(F32)[12 + t:13 + t, :]
    R_OB, R_DB, R_GN, R_SF, R_QB, R_VB, R_UB = 0, 2, 4, 8, 12, 14, 16

    def prow(k):
        return PV[k:k + 1, :]

    lane_half = pl.ds(mo(c * HALF, 128), HALF)
    for t in (0, 1):
        g(B_QB, t)[...] = jnp.zeros((8, 3 * HALF), F32)
        g(B_QB, t)[0:1, 0:HALF] = PV[R_QB + t:R_QB + t + 1, lane_half]
        g(B_QB, t)[0:1, 2 * HALF:] = PV[R_VB + t:R_VB + t + 1, lane_half]
        for xx in (0, 1):
            at = R_UB + 4 * t + xx
            lo, hi = PV[at:at + 1, lane_half], PV[at + 2:at + 3, lane_half]
            g(B_UB, t)[0:1, xx * HALF:(xx + 1) * HALF] = jnp.where(jnp.full((1, HALF), y) == 0, lo, hi)

    def same_part(t, grp):
        T = ROWS[t]
        shift = 5 if t == 0 else 6
        ri = lax.broadcasted_iota(jnp.int32, (T, T), 0) >> shift
        ci = lax.broadcasted_iota(jnp.int32, (T, T), 1) >> shift
        m = ri == ci
        if t == 1:
            m = m | (jnp.full((T, T), i_cnt[rep * 8 + (s // 2) * 2 + grp]) > 0)
        return m

    lane_lo = lax.broadcasted_iota(jnp.int32, (1, 128), 1) < 64
    mask_a = lane_lo.astype(F32).astype(BF)
    mask_b = (1.0 - lane_lo.astype(F32)).astype(BF)

    def lnfwd(first, gain, shift):
        mean = jnp.mean(first, axis=-1, keepdims=True)
        cen = first - mean
        inv = lax.rsqrt(jnp.mean(cen * cen, axis=-1, keepdims=True) + LN_EPS)
        n = cen * inv
        return n, inv, n * gain + shift

    CH = 64

    def project(t, k):
        X, WQ = g(B_X, t), g(B_WQ, t)
        if k == 0:
            wait(X, S_X, t)
            wait(WQ.at[pl.ds(0, 192)], S_QKVC, t)
        wait(part_of(WQ, 288, k), S_QKVZ + k, t)
        cols = slice(k * HALF, (k + 1) * HALF)
        g(B_QKV, t)[:, cols] = (nn(X[...], WQ[:, cols]) + g(B_QB, t)[0:1, cols]).astype(BF)

    def attention(t):
        T = ROWS[t]
        X, WQ, QKV, P, ATT = g(B_X, t), g(B_WQ, t), g(B_QKV, t), g(B_P, t), g(B_ATT, t)
        @pl.loop(0, 2)
        def _(grp):
            rows = pl.ds(mo(grp * T, 128), T)
            m = same_part(t, grp)

            @pl.loop(0, 3)
            def _(hp):
                q = QKV[rows, pl.ds(mo(hp * 128, 128), 128)]
                k = QKV[rows, pl.ds(mo(HALF + hp * 128, 128), 128)]
                val = QKV[rows, pl.ds(mo(2 * HALF + hp * 128, 128), 128)]
                outs = []
                for h, msk in ((0, mask_a), (1, mask_b)):
                    sc = jnp.where(m, nt(q * msk, k) * (1.0 / math.sqrt(HD)), NEG_FILL)
                    mx = jnp.max(sc, axis=-1, keepdims=True)
                    e = jnp.exp(sc - mx)
                    p = e * (1.0 / jnp.sum(e, axis=-1, keepdims=True))
                    P[grp * 6 + hp * 2 + h] = p
                    outs.append(nn(p.astype(BF), val))
                ATT[rows, pl.ds(mo(hp * 128, 128), 128)] = jnp.where(lane_lo, outs[0], outs[1]).astype(BF)

        whole_out(t)
        g(B_OS, t)[...] = nn(ATT[pl.ds(mo((1 - c) * T, 128), T), :], g(B_WO, t)[...]).astype(BF)
        send(g(B_OS, t), g(B_OR, t), S_OP, t, sib)
        g(B_KP, t)[0] = nn(ATT[pl.ds(mo(c * T, 128), T), :], g(B_WO, t)[...])
        wait(g(B_OR, t), S_OP, t)
        me4 = (2 * y + c) * T
        ob, gain, shift = prow(R_OB + t), prow(R_GN + 2 * t), prow(R_SF + 2 * t)

        @pl.loop(0, T // CH)
        def _(i):
            r = pl.ds(mo(i * CH, CH), CH)
            first = (X[pl.ds(mo(c * T + i * CH, CH), CH), :].astype(F32) + g(B_KP, t)[0, r, :]
                     + g(B_OR, t)[r, :].astype(F32) + ob)
            n, inv, mid = lnfwd(first, gain, shift)
            g(B_N1, t)[r, :] = n
            g(B_R1, t)[r, :] = jnp.broadcast_to(inv, (CH, 128))
            g(B_MID, t)[pl.ds(mo(me4 + i * CH, CH), CH), :] = mid.astype(BF)

        gather_rows(t, B_MID, S_MY, S_MC, S_MF)

    def slot_rows(t, yy, cc):
        T = ROWS[t]
        return pl.ds(mo((2 * yy + cc) * T, 128), T)

    def gather_rows(t, buf, ny, nc, nf):
        own = g(buf, t).at[slot_rows(t, y, c)]
        send(own, own, ny, t, ypeer)
        send(own, own, nc, t, sib)

    def gather_near(t, buf, nc):
        wait(g(buf, t).at[slot_rows(t, y, 1 - c)], nc, t)

    def gather_forward(t, buf, ny, nf):
        got = g(buf, t).at[slot_rows(t, 1 - y, c)]
        wait(got, ny, t)
        send(got, got, nf, t, sib)

    def gather_far(t, buf, nf):
        wait(g(buf, t).at[slot_rows(t, 1 - y, 1 - c)], nf, t)

    def gather_sent(t, buf, ny, nc, nf):
        own = g(buf, t).at[slot_rows(t, y, c)]
        wait(own, ny, t, 1)
        wait(own, nc, t, 1)
        wait(own, nf, t, 1)

    def up_pair(t, yy):
        T = ROWS[t]
        rows = pl.ds(mo(2 * yy * T, 128), 2 * T)

        @pl.loop(0, 3)
        def _(j):
            cols = pl.ds(mo(j * 256, 128), 256)
            pre = nn(g(B_MID, t)[rows, :], g(B_WU, t)[:, cols]) + g(B_UB, t)[0:1, cols]
            cdf = 0.5 * (1.0 + lax.erf(pre * INV_ROOT_TWO))
            g(B_ACT, t)[rows, cols] = (pre * cdf).astype(BF)
            g(B_SL, t)[rows, cols] = (cdf + pre * jnp.exp(-0.5 * pre * pre) * INV_ROOT_TWO_PI).astype(BF)

    def scatter_partial(t, part, n1a, n1b, n2):
        S1, V1, S2, V2, KP = g(B_S1, t), g(B_V1, t), g(B_S2, t), g(B_V2, t), g(B_KP, t)
        S1[0] = part(slot_rows(t, 1 - y, 1 - c)).astype(BF)
        send(S1.at[0], V1.at[0], n1a, t, sib)
        KP[0] = part(slot_rows(t, 1 - y, c))
        S1[1] = part(slot_rows(t, y, 1 - c)).astype(BF)
        send(S1.at[1], V1.at[1], n1b, t, sib)
        wait(V1.at[0], n1a, t)
        S2[...] = (KP[0] + V1[0].astype(F32)).astype(BF)
        send(S2, V2, n2, t, ypeer)
        KP[1] = part(slot_rows(t, y, c))

    def scatter_finish(t, n1b, n2):
        wait(g(B_V1, t).at[1], n1b, t)
        wait(g(B_V2, t), n2, t)

    def scatter_sent(t, n1a, n1b, n2):
        wait(g(B_S1, t).at[0], n1a, t, 1)
        wait(g(B_S1, t).at[1], n1b, t, 1)
        wait(g(B_S2, t), n2, t, 1)

    def summed(t, r):
        return g(B_KP, t)[1, r, :] + g(B_V1, t)[1, r, :].astype(F32) + g(B_V2, t)[r, :].astype(F32)

    def ffn(t):
        gather_near(t, B_MID, S_MC)
        gather_forward(t, B_MID, S_MY, S_MF)
        wait(g(B_WU, t).at[pl.ds(0, 192)], S_UPC, t)
        for k in (0, 1):
            wait(part_of(g(B_WU, t), 288, k), S_UPZ + k, t)
        up_pair(t, y)
        gather_far(t, B_MID, S_MF)
        up_pair(t, 1 - y)
        wait(g(B_WD, t), S_DN, t)
        scatter_partial(t, lambda rows: nn(g(B_ACT, t)[rows, :], g(B_WD, t)[...]), S_F1A, S_F1B, S_F2)
        T = ROWS[t]
        r = lax.broadcasted_iota(jnp.int32, (16, 4 * T), 0)
        j = lax.broadcasted_iota(jnp.int32, (16, 4 * T), 1)
        at_cls = (j == (r >> 2) * T + (r & 3) * (32, 64)[t]).astype(F32).astype(BF)
        g(B_CLS, t)[...] = nn(at_cls, g(B_SL, t)[...]).astype(BF)

    def ffn_end(t):
        T = ROWS[t]
        scatter_finish(t, S_F1B, S_F2)
        db = prow(R_DB + t)
        g0, g1, s0, s1 = (prow(base + 2 * t + k) for base in (R_GN, R_SF) for k in (0, 1))

        @pl.loop(0, T // CH)
        def _(i):
            r = pl.ds(mo(i * CH, CH), CH)
            second = g(B_N1, t)[r, :] * g0 + s0 + summed(t, r) + db
            n, inv, res = lnfwd(second, g1, s1)
            g(B_N2, t)[r, :] = n
            g(B_R2, t)[r, :] = jnp.broadcast_to(inv, (CH, 128))
            g(B_Y, t)[r, :] = res.astype(BF)

        local(g(B_Y, t), (o_y0, o_y1)[t], S_FIN, 0, t)

    def forward_qkv(t, k):
        forward_cols(t, g(B_WQ, t), k, S_QKV, S_QKVZ)

    def forward_up(t):
        for k in (0, 1):
            forward_cols(t, g(B_WU, t), k, S_UP, S_UPZ)

    for k in range(3):
        forward_qkv(1, k)
    forward_out(1)
    for k in range(3):
        project(1, k)
        forward_qkv(0, k)
    send_up(0)
    send_dn(0)
    attention(1)
    forward_out(0)
    forward_up(1)
    for k in range(3):
        project(0, k)
    attention(0)
    forward_up(0)
    def fold(a):
        return jnp.sum(a.reshape(CH // 8, 8, D), axis=0)

    def put_bias(k, row):
        g(B_BG, 0)[k:k + 1, :] = row

    def ln_back(t, din, nrm, inv, gain):
        gg = din * gain
        m1 = jnp.mean(gg, axis=-1, keepdims=True)
        m2 = jnp.mean(gg * nrm, axis=-1, keepdims=True)
        return inv * (gg - m1 - nrm * m2)

    steps = (32, 64)

    def out_back(t):
        T = ROWS[t]
        wait(g(B_COT, t), S_COT, 0, t)
        for i in range(4):
            row = slice(i * steps[t], i * steps[t] + 1)
            g(B_CLN, t)[i:i + 1, :] = g(B_N2, t)[row, :]
            g(B_CLR, t)[i:i + 1, :] = g(B_R2, t)[row, :]
            g(B_CLC, t)[i:i + 1, :] = g(B_COT, t)[row, :].astype(F32)
        gain = prow(R_GN + 2 * t + 1)
        me4 = (2 * y + c) * T
        zero = jnp.zeros((8, D), F32)

        def body(i, acc):
            r = pl.ds(mo(i * CH, CH), CH)
            dout = g(B_COT, t)[r, :].astype(F32)
            nrm = g(B_N2, t)[r, :]
            dsec = ln_back(t, dout, nrm, g(B_R2, t)[r, 0:1], gain)
            g(B_N2, t)[r, :] = dsec
            g(B_DF, t)[pl.ds(mo(me4 + i * CH, CH), CH), :] = dsec.astype(BF)
            return (acc[0] + fold(dout * nrm), acc[1] + fold(dout))

        acc = lax.fori_loop(0, T // CH, body, (zero, zero))
        for k, a in zip((R_GN + 2 * t + 1, R_SF + 2 * t + 1), acc):
            put_bias(k, jnp.sum(a, axis=0, keepdims=True))

    def cls_back(t):
        dcls = g(B_CG, 0)[t, 0:4, :]
        nrm = g(B_CLN, t)[0:4, :]
        dsec = ln_back(t, g(B_CLC, t)[0:4, :] + dcls, nrm, g(B_CLR, t)[0:4, 0:1], prow(R_GN + 2 * t + 1))
        for i in range(4):
            g(B_N2, t)[i * steps[t]:i * steps[t] + 1, :] = dsec[i:i + 1, :]
        g(B_CFW, 0)[4 * t:4 * t + 4, :] = dsec
        for k, a in ((R_GN + 2 * t + 1, dcls * nrm), (R_SF + 2 * t + 1, dcls)):
            put_bias(k, g(B_BG, 0)[k:k + 1, :] + jnp.sum(a, axis=0, keepdims=True))

    def cls_place(t):
        r = lax.broadcasted_iota(jnp.int32, (16, 64), 0)
        j = lax.broadcasted_iota(jnp.int32, (16, 64), 1)
        which = (j == (r >> 2) * 16 + 4 * t + (r & 3)).astype(F32).astype(BF)
        rows = nn(which, g(B_CF, 0)[...].reshape(64, D))
        g(B_CLD, t)[...] = rows
        da = nt(rows.astype(BF), g(B_WD, t)[...])
        g(B_CLP, t)[...] = da * g(B_CLS, t)[...].astype(F32)
        cls_rows(t, g(B_DF, t), g(B_CLD, t))

    def cls_rows(t, buf, new):
        top = lax.broadcasted_iota(jnp.int32, (16, 1), 0) == 0
        for k in range(16):
            tile = pl.ds(k // 4 * ROWS[t] + k % 4 * steps[t], 16)
            buf[tile, :] = jnp.where(top, new[k:k + 1, :], buf[tile, :].astype(F32)).astype(BF)

    def down_pair(t, yy):
        T = ROWS[t]
        rows = pl.ds(mo(2 * yy * T, 128), 2 * T)

        @pl.loop(0, 3)
        def _(j):
            cols = pl.ds(mo(j * 256, 128), 256)
            da = nt(g(B_DF, t)[rows, :], g(B_WD, t)[cols, :])
            g(B_SL, t)[rows, cols] = (da * g(B_SL, t)[rows, cols].astype(F32)).astype(BF)

    def pre_back(t, between=lambda: None):
        gather_near(t, B_DF, S_DC)
        down_pair(t, y)
        between()
        gather_forward(t, B_DF, S_DY, S_DF)
        gather_far(t, B_DF, S_DF)
        down_pair(t, 1 - y)

    def ffn_back(t, point=lambda: None):
        gather_sent(t, B_DF, S_DY, S_DC, S_DF)
        cls_place(t)
        ACT, DF, WD, WU = g(B_ACT, t), g(B_DF, t), g(B_WD, t), g(B_WU, t)
        for k in range(3):
            cols = pl.ds(mo((1 - x) * HALF + 128 * k, 128), 128)
            WD[cols, :] = tn(ACT[:, cols], DF[...]).astype(BF)
            send(WD.at[cols], g(B_GD, t).at[pl.ds(128 * k, 128)], S_GD + k, t, xpeer)
        cls_rows(t, g(B_SL, t), g(B_CLP, t))
        point()

        scatter_partial(t, lambda rows: nt(g(B_SL, t)[rows, :], g(B_WU, t)[...]), S_D1A, S_D1B, S_D2)
        point()
        own_sum = nn(jnp.ones((8, ROWS[t]), F32).astype(BF), g(B_DF, t)[slot_rows(t, y, c), :])
        put_bias(R_DB + t, own_sum[0:1, :])
        ones = jnp.ones((8, 4 * ROWS[t]), F32).astype(BF)
        sums = nn(ones, g(B_SL, t)[...])[0:1, :]
        for xx in (0, 1):
            part = sums[:, xx * HALF:(xx + 1) * HALF]
            at = R_UB + 4 * t + xx

            @pl.when(y == 0)
            def _():
                g(B_BG, 0)[at:at + 1, lane_half] = part

            @pl.when(y == 1)
            def _():
                g(B_BG, 0)[at + 2:at + 3, lane_half] = part

        cols = pl.ds(mo(x * HALF, 128), HALF)
        WD[cols, :] = tn(ACT[:, cols], DF[...]).astype(BF)
        for dy in (1, 0):
            far, near = (pl.ds(mo(flip(y, dy) * HALF + xx * 192, 64), 192) for xx in (1 - x, x))

            @pl.loop(0, 3)
            def _(j):
                cols = pl.ds(mo(flip(y, dy) * HALF + j * 128, 128), 128)
                WU[cols, :] = tn(g(B_MID, t)[:, cols], g(B_SL, t)[...]).astype(BF)

            send(WU.at[far], g(B_XU, t).at[pl.ds((1 - dy) * 192, 192)], S_XU1 - dy, t, xpeer)
            point()

    def relay_up(t, dy):
        WU, GU, mine = g(B_WU, t), g(B_GU, t), 2 * y + c
        got = g(B_XU, t).at[pl.ds((1 - dy) * 192, 192)]
        wait(got, S_XU1 - dy, t)
        yy = flip(y, dy)
        for r0 in (0, 96):
            r = pl.ds(mo(yy * HALF + x * 192 + r0, 32), 96)
            WU[r, :] = (WU[r, :].astype(F32) + got[pl.ds(r0, 96), :].astype(F32)).astype(BF)
        for dc in (1, 0):
            owner = sh(yy, x, flip(c, dc))
            rows = WU.at[pl.ds(mo(96 * owner, 32), 96)]
            if dy + dc:
                send(rows, GU.at[mine], S_GU1 - dy, t, (rep, owner))
            else:
                local(rows, GU.at[mine], S_GU1, t)

    g(B_BG, 0)[...] = jnp.zeros((32, D), F32)
    g(B_CFW, 0)[...] = jnp.zeros((16, D), F32)
    ffn(1)
    ffn(0)
    ffn_end(1)
    out_back(1)
    gather_rows(1, B_DF, S_DY, S_DC, S_DF)
    ffn_end(0)

    def pick(T, lo, step):
        ri = lax.broadcasted_iota(jnp.int32, (16, T), 0) & 7
        ci = lax.broadcasted_iota(jnp.int32, (16, T), 1)
        return (((ri & 4) == lo) & (ci == (ri & 3) * step)).astype(F32).astype(BF)

    both = nn(pick(128, 0, 32), g(B_Y, 0)[...]) + nn(pick(256, 4, 64), g(B_Y, 1)[...])
    top = lax.broadcasted_iota(jnp.int32, (16, HALF), 0) < 8
    g(B_CM, 0)[:, :HALF] = jnp.where(top, both[:, :HALF], both[:, HALF:]).astype(BF)
    ri = lax.broadcasted_iota(jnp.int32, (16, 128), 0)
    pos = jnp.zeros((16, 128), jnp.int32)
    for i in range(4):
        pos = jnp.where(ri == i, i_pos[i], pos)
    g(B_CM, 0)[:, HALF:] = pos.astype(F32).astype(BF)
    mine = g(B_GA, 0).at[s * 4 + rep]
    for k in (1, 2, 3):
        send(g(B_CM, 0), mine, S_CZ, 0, ((rep + k) % 4, s))
    g(B_GA, 0)[s * 4 + rep] = g(B_CM, 0)[...]
    out_back(0)
    wait(g(B_GA, 0).at[pl.ds(0, 3)], S_CZ, 0)
    four = g(B_GA, 0).at[pl.ds(s * 4, 4)]
    send(four, four, S_CPC, 0, sib)
    for d in NEIGH:
        if not d[2]:
            send(four, four, S_CP, 0, (rep, sh(*peer(d))))
    gather_rows(0, B_DF, S_DY, S_DC, S_DF)

    for t in (0, 1):
        own = g(B_X, t).at[pl.ds(mo(c * ROWS[t], 128), ROWS[t])]
        wait(own, S_X, t, 1)
        for buf, n, far, near, pair in ((g(B_WQ, t), 3, S_QKV, S_QKVC, S_QKVZ), (g(B_WU, t), 2, S_UP, S_UPC, S_UPZ)):
            wait(buf.at[pl.ds(0, 96)], near, t, 1)
            for k in range(n):
                wait(part_of(buf, 288, k), far + k, t, 1)
                wait(part_of(buf, 288, k), pair + k, t, 1)
        wait(g(B_WO, t).at[pl.ds(0, 144)], S_OUT, t, 1)

        @pl.when(c == y)
        def _():
            wait(g(B_WO, t).at[pl.ds(0, 96)], S_OUTZ, t, 1)

        @pl.when(c != y)
        def _():
            wait(g(B_WO, t).at[pl.ds(0, 96)], S_OUTC, t, 1)
            wait(g(B_WO, t).at[pl.ds(0, 192)], S_OUTZ, t, 1)

        wait(g(B_WD, t).at[pl.ds(0, HALF)], S_DN, t, 1)
        wait(g(B_OS, t), S_OP, t, 1)
        gather_sent(t, B_MID, S_MY, S_MC, S_MF)
        scatter_sent(t, S_F1A, S_F1B, S_F2)
    wait(g(B_SP, 0).at[pl.ds(0, 7)], S_SMALL, 0, 1)
    wait(g(B_GA, 0).at[pl.ds(0, 3)], S_CZ, 0, 1)
    def pass_cls():
        twelve = g(B_GA, 0).at[pl.ds(0, 12)]
        wait(twelve, S_CP, 0)
        for d in NEIGH:
            if not d[2]:
                got = g(B_GA, 0).at[pl.ds(sh(*peer(d)) * 4, 4)]
                send(got, got, S_CPF, 0, sib)

    pre_back(1, pass_cls)

    wait(g(B_GA, 0).at[pl.ds(0, 4)], S_CPC, 0)
    wait(g(B_GA, 0).at[pl.ds(0, 12)], S_CPF, 0)
    wait(g(B_GA, 0).at[pl.ds(0, 4)], S_CPC, 0, 1)
    for name in (S_CP, S_CPF):
        wait(g(B_GA, 0).at[pl.ds(0, 12)], name, 0, 1)

    def pick_all(base):
        ri = lax.broadcasted_iota(jnp.int32, (128, 512), 0)
        ci = lax.broadcasted_iota(jnp.int32, (128, 512), 1)
        blk = ci >> 4
        within = (ci & 15) - base
        row = ((blk & 3) * 8 + (blk >> 2)) * 4 + within
        return ((within >= 0) & (within < 4) & (ri == row)).astype(F32).astype(BF)

    ga = g(B_GA, 0)[...].reshape(512, 512)
    qa_f = nn(pick_all(0), ga)
    qa = qa_f[:, :HALF].astype(BF)
    pa = nn(pick_all(4), ga)[:, :HALF].astype(BF)
    qb = nn(pick_all(8), ga)[:, :HALF].astype(BF)
    pb = nn(pick_all(12), ga)[:, :HALF].astype(BF)
    scale = 2.0 / math.sqrt(D)
    logits = (nt(qa, pa) + nt(qb, pb)) * scale
    lane = lax.broadcasted_iota(jnp.int32, (1, 128), 1)
    cnt = jnp.zeros((1, 128), jnp.int32)
    for k in range(32):
        cnt = jnp.where(lane >> 2 == k, i_cnt[k], cnt)
    masked = jnp.where((cnt <= 0) | (lane & 3 == 0), logits, NEG_FILL)
    mx = jnp.max(masked, axis=1, keepdims=True)
    ex = jnp.exp(masked - mx)
    sm = jnp.sum(ex, axis=1, keepdims=True)
    hit = lax.broadcasted_iota(jnp.int32, (128, 128), 1).astype(F32) == qa_f[:, HALF:]
    ce = mx + jnp.log(sm) - jnp.sum(jnp.where(hit, masked, 0.0), axis=1, keepdims=True)
    o_loss[...] = jnp.broadcast_to(jnp.sum(ce, axis=0, keepdims=True) * (1.0 / 128.0), (8, 128))
    dl = (ex / sm - hit.astype(F32)).astype(BF)
    ri = lax.broadcasted_iota(jnp.int32, (16, 128), 0)
    ci = lax.broadcasted_iota(jnp.int32, (16, 128), 1)
    sel = ((ri < 4) & (ci == ri + 4 * (rep * 8 + s))).astype(F32).astype(BF)
    dlq = nn(sel, dl).astype(BF)
    dlp = nt(sel, dl.T).astype(BF) if False else lax.dot_general(
        sel, dl, (((1,), (1,)), ((), ())), preferred_element_type=F32).astype(BF)
    g(B_CG, 0)[0, :, :HALF] = nn(dlq, pa) * scale
    g(B_CG, 0)[0, :, HALF:] = nn(dlq, pb) * scale
    g(B_CG, 0)[1, :, :HALF] = nn(dlp, qa) * scale
    g(B_CG, 0)[1, :, HALF:] = nn(dlp, qb) * scale

    def mid_back(t):
        T = ROWS[t]
        scatter_finish(t, S_D1B, S_D2)
        gain = prow(R_GN + 2 * t)
        zero = jnp.zeros((8, D), F32)

        def body(i, acc):
            r = pl.ds(mo(i * CH, CH), CH)
            dmid = g(B_N2, t)[r, :] + summed(t, r)
            nrm = g(B_N1, t)[r, :]
            dfirst = ln_back(t, dmid, nrm, g(B_R1, t)[r, 0:1], gain)
            low = dfirst.astype(BF)
            g(B_N1, t)[r, :] = dfirst
            g(B_DA, t)[pl.ds(mo(c * T + i * CH, CH), CH), :] = low
            return (acc[0] + fold(dmid * nrm), acc[1] + fold(dmid), acc[2] + fold(low.astype(F32)))

        acc = lax.fori_loop(0, T // CH, body, (zero, zero, zero))
        own = g(B_DA, t).at[pl.ds(mo(c * T, 128), T)]
        send(own, own, S_DA, t, sib)
        for k, a in zip((R_GN + 2 * t, R_SF + 2 * t, R_OB + t), acc):
            put_bias(k, jnp.sum(a, axis=0, keepdims=True))

    def attention_back(t, point):
        T = ROWS[t]
        QKV, P, ATT, DA, WO, WQ = g(B_QKV, t), g(B_P, t), g(B_ATT, t), g(B_DA, t), g(B_WO, t), g(B_WQ, t)
        wait(DA.at[pl.ds(mo((1 - c) * T, 128), T)], S_DA, t)

        DAT = g(B_DAT, t)
        DAT[...] = nt(DA[...], WO[...]).astype(BF)

        @pl.loop(0, 3)
        def _(j):
            cols = pl.ds(mo(j * 128, 128), 128)
            WO[cols, :] = tn(ATT[:, cols], DA[...]).astype(BF)

        dst = g(B_GO, t).at[y * 2 + x]
        for xx in (0, 1):
            for cc in (0, 1):
                src = WO.at[pl.ds((2 * xx + cc) * 96, 96)]
                dev = sh(c, xx, cc)

                @pl.when(dev == s)
                def _():
                    local(src, dst, S_GO, t)

                @pl.when(dev != s)
                def _():
                    send(src, dst, S_GO, t, (rep, dev))

        point()
        for grp in (0, 1):
            rows = pl.ds(grp * T, T)

            @pl.loop(0, 3)
            def _(hp):
                lanes = pl.ds(mo(hp * 128, 128), 128)
                dat = DAT[rows, lanes]
                qs, ks = lanes, pl.ds(mo(HALF + hp * 128, 128), 128)
                vs = pl.ds(mo(2 * HALF + hp * 128, 128), 128)
                q, k, val = QKV[rows, qs], QKV[rows, ks], QKV[rows, vs]
                dq, dk, dv = [], [], []
                for h, msk in ((0, mask_a), (1, mask_b)):
                    p = P[grp * 6 + hp * 2 + h]
                    dp = nt(dat * msk, val)
                    ds = (p * (dp - jnp.sum(dp * p, axis=-1, keepdims=True))).astype(BF)
                    dv.append(tn(p.astype(BF), dat))
                    dq.append(nn(ds, k))
                    dk.append(tn(ds, q))
                root = 1.0 / math.sqrt(HD)
                QKV[rows, qs] = (jnp.where(lane_lo, dq[0], dq[1]) * root).astype(BF)
                QKV[rows, ks] = (jnp.where(lane_lo, dk[0], dk[1]) * root).astype(BF)
                QKV[rows, vs] = jnp.where(lane_lo, dv[0], dv[1]).astype(BF)

            point()

        g(B_OS, t)[...] = nt(QKV[pl.ds(mo((1 - c) * T, 128), T), :], WQ[...]).astype(BF)
        send(g(B_OS, t), g(B_OR, t), S_DX, t, sib)
        g(B_KP, t)[0] = nt(QKV[pl.ds(mo(c * T, 128), T), :], WQ[...])

        ones = jnp.ones((8, 2 * T), F32).astype(BF)
        sums = nn(ones, QKV[...])[0:1, :]
        g(B_BG, 0)[R_QB + t:R_QB + t + 1, lane_half] = sums[:, :HALF]
        g(B_BG, 0)[R_VB + t:R_VB + t + 1, lane_half] = sums[:, 2 * HALF:]

        if t == 0:
            send_small()
        far_rows = pl.ds(mo((1 - y) * HALF, 128), HALF)
        for k in range(3):
            lanes = slice(k * HALF, (k + 1) * HALF)

            @pl.loop(0, 3)
            def _(j):
                cols = pl.ds(mo(j * 256, 128), 256)
                WQ[cols, lanes] = tn(g(B_X, t)[:, cols], QKV[:, lanes]).astype(BF)

            send(WQ.at[far_rows, pl.ds(k * HALF, HALF)], g(B_YQ, t).at[:, pl.ds(k * HALF, HALF)], S_YQ + k, t, ypeer)
            point()

    def send_small():
        BG, BGC, BGR = (g(b, 0) for b in (B_BG, B_BGC, B_BGR))
        low = BG[...].astype(BF)
        for k in range(8):
            T96[...] = jnp.zeros((16, HALF), F32)
            T96[:, 0:128] = nt(low[0:16, :], place(128, 96, 96 * k))
            at = 12 + 2 * (k // 4)
            T96[0:2, 128:384] = nt(low[0:16, :], place(256, 192, 192 * (k % 4)))[at:at + 2, :]
            for t in (0, 1):
                row = 16 + 4 * t + k // 2
                T96[12 + t:13 + t, :] = BG[row:row + 1, k % 2 * HALF:(k % 2 + 1) * HALF]
            BGC[k] = T96[...].astype(BF)
        for d in NEIGH:
            dest = sh(*peer(d))
            send(BGC.at[dest], BGR.at[s], S_BG, 0, (rep, dest))
        local(BGC.at[s], BGR.at[s], S_BG, 0)

    def relay_qkv(t, k):
        WQ, YQ, lanes = g(B_WQ, t), g(B_YQ, t), pl.ds(k * HALF, HALF)
        wait(YQ.at[:, lanes], S_YQ + k, t)
        for r0 in range(0, HALF, 128):
            r = pl.ds(mo(y * HALF + r0, 128), 128)
            WQ[r, lanes] = (WQ[r, lanes].astype(F32) + YQ[pl.ds(r0, 128), lanes].astype(F32)).astype(BF)
        dst = g(B_GQ, t).at[2 * x + c, :, lanes]
        for dx, dc in ((1, 0), (1, 1), (0, 1), (0, 0)):
            owner = sh(y, flip(x, dx), flip(c, dc))
            src = WQ.at[pl.ds(mo(96 * owner, 32), 96), lanes]
            if dx + dc:
                send(src, dst, S_GQ + k, t, (rep, owner))
            else:
                local(src, dst, S_GQ + k, t)

    def input_back(t):
        T = ROWS[t]
        wait(g(B_OR, t), S_DX, t)

        @pl.loop(0, T // CH)
        def _(i):
            r = pl.ds(mo(i * CH, CH), CH)
            g(B_Y, t)[r, :] = (g(B_N1, t)[r, :] + g(B_KP, t)[0, r, :] + g(B_OR, t)[r, :].astype(F32)).astype(BF)

        local(g(B_Y, t), (o_gx0, o_gx1)[t], S_FIN2, 0, t)

    def make_dn(t, k):
        def each(use):
            wait(g(B_GD, t).at[pl.ds(128 * k, 128)], S_GD + k, t)
            for r0 in (128 * k, 128 * k + 64):
                own = g(B_WD, t)[pl.ds(mo(x * HALF + r0, 64), 64), :].astype(F32)
                use(pl.ds(r0, 64), pl.ds(0, D), own + g(B_GD, t)[pl.ds(r0, 64), :].astype(F32))
        return each

    def make_up(t, dy, xx):
        GU = g(B_GU, t)
        yy = flip(y, dy)

        def each(use):
            if xx == 0:
                wait(GU.at[pl.ds(0, 2)], S_GU1 - dy, t)
            cols = slice(xx * HALF, (xx + 1) * HALF)
            for cc in (0, 1):
                use(pl.ds(0, 96), pl.ds(mo((4 * yy + 2 * xx + cc) * HALF, 128), HALF), GU[2 * yy + cc, :, cols].astype(F32))
        return each

    def make_out(t):
        GO = g(B_GO, t)

        def each(use):
            wait(GO, S_GO, t)
            tot = GO[0].astype(F32)
            for k in range(1, 4):
                tot = tot + GO[k].astype(F32)
            use(pl.ds(0, 96), pl.ds(0, D), tot)
        return each

    def make_qkv(t, part):
        GQ = g(B_GQ, t)

        def each(use):
            cols = slice(part * HALF, (part + 1) * HALF)
            wait(GQ.at[:, :, pl.ds(part * HALF, HALF)], S_GQ + part, t)
            for cc in (0, 1):
                tot = GQ[cc, :, cols].astype(F32) + GQ[2 + cc, :, cols].astype(F32)
                use(pl.ds(0, 96), pl.ds(part * D + cc * HALF, HALF), tot)
        return each

    def each_small(use):
        BGR = g(B_BGR, 0)
        wait(BGR, S_BG, 0)
        tot = BGR[0].astype(F32)
        for k in range(1, 8):
            tot = tot + BGR[k].astype(F32)
        use(pl.ds(0, 16), pl.ds(0, HALF), tot)

    is_end = (rep == 0) | (rep == 3)
    units = []

    def unit(kind, t, each, out, rows, cols):
        if kind == 4:
            bufs = (B_BGS, B_BGA, B_BGB)
        else:
            bufs = (B_ZSD + kind, B_ZAD + kind, B_ZBD + kind)
        units.append((len(units), tuple(g(b, t) for b in bufs), each, out, rows, cols))

    def add_dn(t):
        for k in range(3):
            unit(0, t, make_dn(t, k), o_od.at[t], (128 * k, 128), (0, D))
    def add_up(t):
        for dy in (1, 0):
            for xx in (0, 1):
                at = mo((2 * flip(y, dy) + xx) * D, 128)
                unit(1, t, make_up(t, dy, xx), o_ou.at[t], (0, 96), (at, D))

    def add_qkv(t):
        for part in range(3):
            unit(3, t, make_qkv(t, part), o_oq.at[t], (0, 96), (part * D, D))

    add_dn(1)
    add_up(1)
    add_dn(0)
    unit(2, 1, make_out(1), o_oo.at[1], (0, 96), (0, D))
    add_up(0)
    unit(2, 0, make_out(0), o_oo.at[0], (0, 96), (0, D))
    add_qkv(1)
    unit(4, 0, each_small, o_obg, (0, 16), (0, HALF))
    add_qkv(0)
    assert len(units) == N_UNITS

    def hop(which, u):
        at = which * N_UNITS + u[0]
        return S_Z + at // 2, at % 2

    def view(ref, u):
        return ref.at[pl.ds(*u[4]), pl.ds(*u[5])]

    def ends(u):
        ZS, ZA, ZB = u[1]

        def put(r, cl, val):
            ZS[r, cl] = val.astype(ZS.dtype)

        for end, mid in ((0, 1), (3, 2)):
            @pl.when(rep == end)
            def _():
                u[2](put)
                send(view(ZS, u), view(ZA, u), *hop(0, u), (mid, s))

    def stage_a(u):
        ZS, ZA, ZB = u[1]

        def put_add(r, cl, val):
            ZS[r, cl] = (val + ZA[r, cl].astype(F32)).astype(ZS.dtype)

        for end, mid in ((0, 1), (3, 2)):
            @pl.when(rep == mid)
            def _():
                wait(view(ZA, u), *hop(0, u))
                u[2](put_add)
                send(view(ZS, u), view(ZB, u), *hop(1, u), (3 - mid, s))

    def stage_b(u):
        ZS, ZA, ZB = u[1]
        for end, mid in ((0, 1), (3, 2)):
            @pl.when(rep == mid)
            def _():
                wait(view(ZB, u), *hop(1, u))
                wait(view(ZB, u), *hop(1, u), 1)
                for r0 in range(u[4][0], u[4][0] + u[4][1], 16):
                    r, cl = pl.ds(r0, 16), pl.ds(*u[5])
                    ZS[r, cl] = (ZS[r, cl].astype(F32) + ZB[r, cl].astype(F32)).astype(ZS.dtype)
                send(view(ZS, u), view(u[3], u), *hop(2, u), (end, s))
                local(view(ZS, u), view(u[3], u), *hop(2, u))

    done = [0, 0, 0]

    def advance(n0, n1, n2):
        while done[0] < n0 or done[1] < n1 or done[2] < n2:
            for k, (step, n) in enumerate(((ends, n0), (stage_a, n1), (stage_b, n2))):
                if done[k] < n:
                    step(units[done[k]])
                    done[k] += 1

    relays = [functools.partial(relay_up, t, dy) for t in (1, 0) for dy in (1, 0)]
    relays += [functools.partial(relay_qkv, t, k) for t in (1, 0) for k in range(3)]

    def point():
        *steps, through = plan.pop(0)
        while len(relays) > 10 - through:
            relays.pop(0)()
        advance(*steps)

    plan = PLAN[:]
    cls_back(1)
    cls_back(0)
    mine = g(B_CF, 0).at[2 * y + c]
    g(B_CF, 0)[2 * y + c] = g(B_CFW, 0)[...].astype(BF)
    fixers = (ypeer, sib, (rep, sh(1 - y, x, 1 - c)))
    for dev in fixers:
        send(mine, mine, S_CF, 0, dev)
    pre_back(0)
    wait(g(B_CF, 0).at[pl.ds(0, 3)], S_CF, 0)
    for t in (0, 1):
        wait(g(B_Y, t), S_FIN, 0, t)
    ffn_back(1)
    ffn_back(0, point)
    mid_back(1)
    attention_back(1, point)
    mid_back(0)
    attention_back(0, point)
    input_back(1)
    input_back(0)
    while plan:
        point()
    for k in range(done[0], N_UNITS + 1):
        advance(min(k + 1, N_UNITS), k, k - 2)
    advance(N_UNITS, N_UNITS, N_UNITS)

    for u in units:
        ZS = view(u[1][0], u)
        wait(ZS, *hop(2, u))

        @pl.when(is_end)
        def _():
            wait(ZS, *hop(0, u), 1)

        @pl.when(jnp.logical_not(is_end))
        def _():
            wait(ZS, *hop(2, u), 1)

    for t in (0, 1):
        scatter_sent(t, S_D1A, S_D1B, S_D2)
        wait(g(B_OS, t), S_DA, t, 1)
        wait(g(B_OS, t), S_DX, t, 1)
        for k in range(3):
            wait(g(B_GD, t).at[pl.ds(0, 128)], S_GD + k, t, 1)
        wait(g(B_GU, t).at[pl.ds(0, 2)], S_GU, t, 1)
        wait(g(B_GU, t).at[pl.ds(0, 1)], S_GU1, t, 1)
        for dy in (0, 1):
            wait(g(B_XU, t).at[pl.ds(0, 192)], S_XU1 - dy, t, 1)

        @pl.when(c == y)
        def _():
            wait(g(B_GO, t).at[pl.ds(0, 3)], S_GO, t, 1)

        @pl.when(c != y)
        def _():
            wait(g(B_GO, t), S_GO, t, 1)

        for k in range(3):
            wait(g(B_YQ, t).at[:, pl.ds(k * HALF, HALF)], S_YQ + k, t, 1)
            wait(g(B_GQ, t).at[pl.ds(0, 3), :, pl.ds(k * HALF, HALF)], S_GQ + k, t, 1)
        wait(g(B_Y, t), S_FIN2, 0, t)
    wait(g(B_BGR, 0).at[pl.ds(0, 7)], S_BG, 0, 1)
    wait(g(B_CF, 0).at[pl.ds(0, 3)], S_CF, 0, 1)


def fused_call(*args):
    hbm = pl.BlockSpec(memory_space=pl.ANY)
    vm = pl.BlockSpec(memory_space=pltpu.VMEM)
    sm = pl.BlockSpec(memory_space=pltpu.SMEM)
    out_shape = [
        jax.ShapeDtypeStruct((8, 128), F32),
        jax.ShapeDtypeStruct((128, D), BF),
        jax.ShapeDtypeStruct((256, D), BF),
        jax.ShapeDtypeStruct((128, D), BF),
        jax.ShapeDtypeStruct((256, D), BF),
        jax.ShapeDtypeStruct((2, 96, 3 * D), BF),
        jax.ShapeDtypeStruct((2, 96, D), BF),
        jax.ShapeDtypeStruct((2, 96, 4 * D), BF),
        jax.ShapeDtypeStruct((2, HALF, D), BF),
        jax.ShapeDtypeStruct((16, HALF), F32),
    ]
    return pl.pallas_call(
        fused_kernel,
        out_shape=out_shape,
        in_specs=[hbm] * 8 + [vm] * 6 + [sm] * 2,
        out_specs=[vm] + [hbm] * 9,
        scratch_shapes=[shape for _, shape in scratch_list()] + [pltpu.SemaphoreType.DMA((N_SEMS,))],
        compiler_params=pltpu.CompilerParams(collective_id=0, has_side_effects=True, vmem_limit_bytes=VMEM_LIMIT),
        cost_estimate=pl.CostEstimate(flops=18 * 10**9, bytes_accessed=40 * 10**6, transcendentals=4 * 10**6),
    )(*args)


def widen_kernel(*refs):
    loss, y0, y1, gx0, gx1, oq, oo, ou, od, bg = refs[:10]
    r_loss, r_y0, r_y1, r_gx0, r_gx1, r_q, r_qb, r_o, r_ob, r_u, r_ub, r_d, r_db, r_gn, r_sf = refs[10:25]
    low = refs[25:29]
    wide = refs[29:33]
    through = refs[33:37]
    sem_in, sem_out, sem_move, sem_move_out = refs[37:]
    groups = list(zip((oq, ou, od, oo), low, wide, (r_q, r_u, r_d, r_o)))
    reads, writes, moves = [], [], []
    for k, (src, lo, hi, dst) in enumerate(groups):
        for t in (0, 1):
            reads.append(pltpu.make_async_copy(src.at[t], lo.at[t], sem_in.at[2 * k + t]))
            reads[-1].start()
    for k, (src, dst) in enumerate(((y0, r_y0), (y1, r_y1), (gx0, r_gx0), (gx1, r_gx1))):
        moves.append((pltpu.make_async_copy(src, through[k], sem_move.at[k]),
                      pltpu.make_async_copy(through[k], dst, sem_move_out.at[k])))
        moves[-1][0].start()
    r_loss[...] = loss[0:1, 0:1]
    r_ob[...] = bg[0:2, 0:96]
    r_db[...] = bg[2:4, 0:96]
    for t in (0, 1):
        r_gn[t] = bg[4 + 2 * t:6 + 2 * t, 0:96]
        r_sf[t] = bg[8 + 2 * t:10 + 2 * t, 0:96]
    r_qb[...] = bg[0:2, 128:320]
    r_ub[...] = bg[12:14, :]
    for k, (src, lo, hi, dst) in enumerate(groups):
        for t in (0, 1):
            reads[2 * k + t].wait()
            hi[t] = lo[t].astype(F32)
            writes.append(pltpu.make_async_copy(hi.at[t], dst.at[t], sem_out.at[2 * k + t]))
            writes[-1].start()
    for there, onward in moves:
        there.wait()
        onward.start()
    for copy in writes + [onward for there, onward in moves]:
        copy.wait()


def widen_call(*args):
    hbm = pl.BlockSpec(memory_space=pl.ANY)
    vm = pl.BlockSpec(memory_space=pltpu.VMEM)

    def out(dtype, *shape):
        return jax.ShapeDtypeStruct(shape, dtype)

    shapes = [(2, 96, 3 * D), (2, 96, 4 * D), (2, HALF, D), (2, 96, D)]
    return pl.pallas_call(
        widen_kernel,
        out_shape=[out(F32, 1, 1), out(BF, 128, D), out(BF, 256, D), out(BF, 128, D), out(BF, 256, D),
                   out(F32, *shapes[0]), out(F32, 2, 192), out(F32, *shapes[3]), out(F32, 2, 96),
                   out(F32, *shapes[1]), out(F32, 2, HALF), out(F32, *shapes[2]), out(F32, 2, 96),
                   out(F32, 2, 2, 96), out(F32, 2, 2, 96)],
        in_specs=[vm] + [hbm] * 8 + [vm],
        out_specs=[vm, hbm, hbm, hbm, hbm, hbm, vm, hbm, vm, hbm, vm, hbm, vm, vm, vm],
        scratch_shapes=[pltpu.VMEM(shape, BF) for shape in shapes] + [pltpu.VMEM(shape, F32) for shape in shapes]
        + [pltpu.VMEM((rows, D), BF) for rows in ROWS * 2]
        + [pltpu.SemaphoreType.DMA((8,)), pltpu.SemaphoreType.DMA((8,)), pltpu.SemaphoreType.DMA((4,)),
           pltpu.SemaphoreType.DMA((4,))],
        compiler_params=pltpu.CompilerParams(vmem_limit_bytes=VMEM_LIMIT),
    )(*args)


def local_fast(query_tokens, passage_tokens, query_cot, passage_cot, bucket_counts, positives, qkv_weight, qv_bias,
               out_weight, out_bias, up_weight, up_bias, down_weight, down_bias, norm_gains, norm_shifts):
    results = widen_call(*fused_call(
        query_tokens.reshape(128, D), passage_tokens.reshape(256, D),
        query_cot.reshape(128, D), passage_cot.reshape(256, D),
        qkv_weight, out_weight, up_weight, down_weight,
        qv_bias, out_bias, up_bias, down_bias, norm_gains, norm_shifts, bucket_counts, positives))
    loss, y0, y1, gx0, gx1 = results[:5]
    return (loss.reshape(()), y0.reshape(query_tokens.shape), y1.reshape(passage_tokens.shape),
            gx0.reshape(query_tokens.shape), gx1.reshape(passage_tokens.shape), *results[5:])


def solution(mesh):
    in_specs = (
        P(("rep", "shard"), None, None),
        P(("rep", "shard"), None, None),
        P(("rep", "shard"), None, None),
        P(("rep", "shard"), None, None),
        P(),
        P(("rep", "shard")),
        P(None, "shard", None),
        P(None, "shard"),
        P(None, "shard", None),
        P(None, "shard"),
        P(None, "shard", None),
        P(None, "shard"),
        P(None, "shard", None),
        P(None, "shard"),
        P(None, None, "shard"),
        P(None, None, "shard"),
    )
    out_specs = (
        P(),
        P(("rep", "shard"), None, None),
        P(("rep", "shard"), None, None),
        P(("rep", "shard"), None, None),
        P(("rep", "shard"), None, None),
        P(None, "shard", None),
        P(None, "shard"),
        P(None, "shard", None),
        P(None, "shard"),
        P(None, "shard", None),
        P(None, "shard"),
        P(None, "shard", None),
        P(None, "shard"),
        P(None, None, "shard"),
        P(None, None, "shard"),
    )
    small_mesh = (mesh.shape["rep"], mesh.shape["shard"]) == (4, 8)
    step = local_fast if small_mesh else local
    return jax.shard_map(step, mesh=mesh, in_specs=in_specs, out_specs=out_specs, check_vma=False)
```

```python
import functools
import math

import jax
import jax.numpy as jnp
from jax import lax
from jax.experimental import pallas as pl
from jax.experimental.pallas import tpu as pltpu
from jax.sharding import PartitionSpec as P

HD = 64
SHORT = 64


LN_EPS = 1e-05
NEG_FILL = -1e30
INV_ROOT_TWO = 0.7071067811865476
INV_ROOT_TWO_PI = 0.3989422804014327
VMEM_LIMIT = 66 * 1000 * 1000


def for_sending(array):
    return jax.tree.map(lambda a: a.astype(jnp.bfloat16) if a.dtype == jnp.float32 else a, array)


def pick_tower(stacks, tower_index):
    qkv_w, qv_b, out_w, out_b, up_w, up_b, down_w, down_b, gains, shifts = stacks
    return (
        qkv_w[tower_index],
        qv_b[tower_index],
        out_w[tower_index],
        out_b[tower_index],
        up_w[tower_index],
        up_b[tower_index],
        down_w[tower_index],
        down_b[tower_index],
        gains[tower_index].T,
        shifts[tower_index].T,
    )


def fetch_layer(stacks, tower_index):
    return lax.all_gather(for_sending(pick_tower(stacks, tower_index)), "shard", axis=0, tiled=True)


def fetch_again(stacks, tower_index):
    return lax.all_gather(for_sending(pick_tower(stacks, tower_index)), "shard", axis=0, tiled=True)


def normalize(hidden):
    row_mean = jnp.mean(hidden, axis=-1, keepdims=True)
    centred = hidden - row_mean
    inv_std = lax.rsqrt(jnp.mean(centred * centred, axis=-1, keepdims=True) + LN_EPS)
    return (centred * inv_std, inv_std)


def norm_back(grad_in, normed, inv_std):
    return inv_std * (
        grad_in
        - jnp.mean(grad_in, axis=-1, keepdims=True)
        - normed * jnp.mean(grad_in * normed, axis=-1, keepdims=True)
    )


def block_mask(long_flags, length, short_len):
    row_part = lax.broadcasted_iota(jnp.int32, (length, length), 0) // short_len
    col_part = lax.broadcasted_iota(jnp.int32, (length, length), 1) // short_len
    return long_flags[:, None, None] | (row_part == col_part)[None]


def head_scores(head_query, head_key, attn_mask):
    raw_scores = jnp.einsum(
        "slhd,smhd->shlm", head_query, head_key, preferred_element_type=jnp.float32
    ) * (1.0 / math.sqrt(HD))
    return jnp.where(attn_mask[:, None], raw_scores, NEG_FILL)


def layer_forward(tokens, weights, attn_mask):
    qkv_w, qv_b, out_w, out_b, up_w, up_b, down_w, down_b, gains, shifts = weights
    seq_count, length, model_width = tokens.shape
    head_count = model_width // HD
    token_rows = tokens.reshape(seq_count * length, model_width)
    qv_float = qv_b.astype(jnp.float32)
    qkv_bias = jnp.concatenate(
        [qv_float[:model_width], jnp.zeros((model_width,), jnp.float32), qv_float[model_width:]]
    )
    qkv_low = (jnp.dot(token_rows, qkv_w, preferred_element_type=jnp.float32) + qkv_bias).astype(
        jnp.bfloat16
    )
    head_split = qkv_low.reshape(seq_count, length, 3, head_count, HD)
    scores = head_scores(head_split[:, :, 0], head_split[:, :, 1], attn_mask)
    row_max = jnp.max(scores, axis=-1, keepdims=True)
    exp_scores = jnp.exp(scores - row_max)
    row_total = jnp.sum(exp_scores, axis=-1, keepdims=True)
    attn_probs = (exp_scores / row_total).astype(jnp.bfloat16)
    log_total = row_max + jnp.log(row_total)
    attn_mixed = jnp.einsum(
        "shlm,smhd->slhd", attn_probs, head_split[:, :, 2], preferred_element_type=jnp.float32
    )
    attn_low = attn_mixed.reshape(seq_count * length, model_width).astype(jnp.bfloat16)
    first_sum = (
        token_rows.astype(jnp.float32)
        + jnp.dot(attn_low, out_w, preferred_element_type=jnp.float32)
        + out_b.astype(jnp.float32)
    )
    normed_one, inv_one = normalize(first_sum)
    gain_float = gains.astype(jnp.float32)
    shift_float = shifts.astype(jnp.float32)
    middle = normed_one * gain_float[:, 0] + shift_float[:, 0]
    middle_low = middle.astype(jnp.bfloat16)
    pre_act = jnp.dot(middle_low, up_w, preferred_element_type=jnp.float32) + up_b.astype(
        jnp.float32
    )
    act_low = jax.nn.gelu(pre_act, approximate=False).astype(jnp.bfloat16)
    second = (
        middle
        + jnp.dot(act_low, down_w, preferred_element_type=jnp.float32)
        + down_b.astype(jnp.float32)
    )
    normed_two, inv_two = normalize(second)
    result = normed_two * gain_float[:, 1] + shift_float[:, 1]
    kept = (
        token_rows,
        qkv_low,
        log_total,
        attn_low,
        normed_one,
        inv_one,
        middle_low,
        pre_act,
        act_low,
        normed_two,
        inv_two,
    )
    return (result, kept)


def layer_backward(grad_out, weights, kept, attn_mask):
    qkv_w, qv_b, out_w, out_b, up_w, up_b, down_w, down_b, gains, shifts = weights
    (
        token_rows,
        qkv_low,
        log_total,
        attn_low,
        normed_one,
        inv_one,
        middle_low,
        pre_act,
        act_low,
        normed_two,
        inv_two,
    ) = kept
    seq_count = attn_mask.shape[0]
    model_width = token_rows.shape[1]
    length = token_rows.shape[0] // seq_count
    head_count = model_width // HD
    gain_float = gains.astype(jnp.float32)
    gain_two = jnp.sum(grad_out * normed_two, axis=0)
    shift_two = jnp.sum(grad_out, axis=0)
    d_second = norm_back(grad_out * gain_float[:, 1], normed_two, inv_two)
    d_ffn = d_second.astype(jnp.bfloat16)
    d_down_w = jnp.dot(act_low.T, d_ffn, preferred_element_type=jnp.float32)
    d_down_b = jnp.sum(d_ffn.astype(jnp.float32), axis=0)
    d_act = jnp.dot(d_ffn, down_w.T, preferred_element_type=jnp.float32)
    gelu_slope = (
        0.5 * (1.0 + lax.erf(pre_act * INV_ROOT_TWO))
        + pre_act * jnp.exp(-0.5 * pre_act * pre_act) * INV_ROOT_TWO_PI
    )
    d_pre = (d_act * gelu_slope).astype(jnp.bfloat16)
    d_up_w = jnp.dot(middle_low.T, d_pre, preferred_element_type=jnp.float32)
    d_up_b = jnp.sum(d_pre.astype(jnp.float32), axis=0)
    d_middle = d_second + jnp.dot(d_pre, up_w.T, preferred_element_type=jnp.float32)
    gain_one = jnp.sum(d_middle * normed_one, axis=0)
    shift_one = jnp.sum(d_middle, axis=0)
    d_first = norm_back(d_middle * gain_float[:, 0], normed_one, inv_one)
    d_attn_out = d_first.astype(jnp.bfloat16)
    d_out_w = jnp.dot(attn_low.T, d_attn_out, preferred_element_type=jnp.float32)
    d_out_b = jnp.sum(d_attn_out.astype(jnp.float32), axis=0)
    d_mixed = (
        jnp.dot(d_attn_out, out_w.T, preferred_element_type=jnp.float32)
        .astype(jnp.bfloat16)
        .reshape(seq_count, length, head_count, HD)
    )
    head_split = qkv_low.reshape(seq_count, length, 3, head_count, HD)
    head_query = head_split[:, :, 0]
    head_key = head_split[:, :, 1]
    head_value = head_split[:, :, 2]
    attn_probs = jnp.exp(head_scores(head_query, head_key, attn_mask) - log_total)
    d_probs = jnp.einsum("slhd,smhd->shlm", d_mixed, head_value, preferred_element_type=jnp.float32)
    d_value = jnp.einsum(
        "shlm,slhd->smhd",
        attn_probs.astype(jnp.bfloat16),
        d_mixed,
        preferred_element_type=jnp.float32,
    )
    d_scores = (
        attn_probs * (d_probs - jnp.sum(d_probs * attn_probs, axis=-1, keepdims=True))
    ).astype(jnp.bfloat16)
    d_query = jnp.einsum(
        "shlm,smhd->slhd", d_scores, head_key, preferred_element_type=jnp.float32
    ) * (1.0 / math.sqrt(HD))
    d_key = jnp.einsum(
        "shlm,slhd->smhd", d_scores, head_query, preferred_element_type=jnp.float32
    ) * (1.0 / math.sqrt(HD))
    d_qkv = (
        jnp.stack([d_query, d_key, d_value], axis=2)
        .reshape(seq_count * length, 3 * model_width)
        .astype(jnp.bfloat16)
    )
    d_qkv_w = jnp.dot(token_rows.T, d_qkv, preferred_element_type=jnp.float32)
    column_sums = jnp.sum(d_qkv.astype(jnp.float32), axis=0)
    d_qv_b = jnp.concatenate([column_sums[:model_width], column_sums[2 * model_width :]])
    d_tokens = d_first + jnp.dot(d_qkv, qkv_w.T, preferred_element_type=jnp.float32)
    layer_grads = (
        d_qkv_w,
        d_qv_b,
        d_out_w,
        d_out_b,
        d_up_w,
        d_up_b,
        d_down_w,
        d_down_b,
        jnp.stack([gain_one, gain_two], axis=1),
        jnp.stack([shift_one, shift_two], axis=1),
    )
    return (d_tokens, layer_grads)


def reduce_layer(layer_grads):
    owned_grads = (
        lax.psum_scatter(layer_grads[0], "shard", scatter_dimension=0, tiled=True),
        lax.psum_scatter(layer_grads[1], "shard", scatter_dimension=0, tiled=True),
        lax.psum_scatter(layer_grads[2], "shard", scatter_dimension=0, tiled=True),
        lax.psum_scatter(layer_grads[3], "shard", scatter_dimension=0, tiled=True),
        lax.psum_scatter(layer_grads[4], "shard", scatter_dimension=0, tiled=True),
        lax.psum_scatter(layer_grads[5], "shard", scatter_dimension=0, tiled=True),
        lax.psum_scatter(layer_grads[6], "shard", scatter_dimension=0, tiled=True),
        lax.psum_scatter(layer_grads[7], "shard", scatter_dimension=0, tiled=True),
        lax.psum_scatter(layer_grads[8], "shard", scatter_dimension=0, tiled=True),
        lax.psum_scatter(layer_grads[9], "shard", scatter_dimension=0, tiled=True),
    )
    quarter = (
        lax.psum_scatter(
            owned_grads[0].astype(jnp.bfloat16), "rep", scatter_dimension=0, tiled=True
        ).astype(jnp.float32),
        lax.psum_scatter(
            owned_grads[1].astype(jnp.bfloat16), "rep", scatter_dimension=0, tiled=True
        ).astype(jnp.float32),
        lax.psum_scatter(
            owned_grads[2].astype(jnp.bfloat16), "rep", scatter_dimension=0, tiled=True
        ).astype(jnp.float32),
        lax.psum_scatter(
            owned_grads[3].astype(jnp.bfloat16), "rep", scatter_dimension=0, tiled=True
        ).astype(jnp.float32),
        lax.psum_scatter(
            owned_grads[4].astype(jnp.bfloat16), "rep", scatter_dimension=0, tiled=True
        ).astype(jnp.float32),
        lax.psum_scatter(
            owned_grads[5].astype(jnp.bfloat16), "rep", scatter_dimension=0, tiled=True
        ).astype(jnp.float32),
        lax.psum_scatter(
            owned_grads[6].astype(jnp.bfloat16), "rep", scatter_dimension=0, tiled=True
        ).astype(jnp.float32),
        lax.psum_scatter(
            owned_grads[7].astype(jnp.bfloat16), "rep", scatter_dimension=0, tiled=True
        ).astype(jnp.float32),
        lax.psum_scatter(
            owned_grads[8].astype(jnp.bfloat16), "rep", scatter_dimension=0, tiled=True
        ).astype(jnp.float32),
        lax.psum_scatter(
            owned_grads[9].astype(jnp.bfloat16), "rep", scatter_dimension=0, tiled=True
        ).astype(jnp.float32),
    )
    return (
        lax.all_gather(quarter[0].astype(jnp.bfloat16), "rep", axis=0, tiled=True).astype(
            jnp.float32
        ),
        lax.all_gather(quarter[1].astype(jnp.bfloat16), "rep", axis=0, tiled=True).astype(
            jnp.float32
        ),
        lax.all_gather(quarter[2].astype(jnp.bfloat16), "rep", axis=0, tiled=True).astype(
            jnp.float32
        ),
        lax.all_gather(quarter[3].astype(jnp.bfloat16), "rep", axis=0, tiled=True).astype(
            jnp.float32
        ),
        lax.all_gather(quarter[4].astype(jnp.bfloat16), "rep", axis=0, tiled=True).astype(
            jnp.float32
        ),
        lax.all_gather(quarter[5].astype(jnp.bfloat16), "rep", axis=0, tiled=True).astype(
            jnp.float32
        ),
        lax.all_gather(quarter[6].astype(jnp.bfloat16), "rep", axis=0, tiled=True).astype(
            jnp.float32
        ),
        lax.all_gather(quarter[7].astype(jnp.bfloat16), "rep", axis=0, tiled=True).astype(
            jnp.float32
        ),
        lax.all_gather(quarter[8].astype(jnp.bfloat16), "rep", axis=0, tiled=True).astype(
            jnp.float32
        ),
        lax.all_gather(quarter[9].astype(jnp.bfloat16), "rep", axis=0, tiled=True).astype(
            jnp.float32
        ),
    )


def local(
    query_tokens,
    passage_tokens,
    query_cot,
    passage_cot,
    bucket_counts,
    positives,
    qkv_weight,
    qv_bias,
    out_weight,
    out_bias,
    up_weight,
    up_bias,
    down_weight,
    down_bias,
    norm_gains,
    norm_shifts,
):
    stacks = (
        qkv_weight,
        qv_bias,
        out_weight,
        out_bias,
        up_weight,
        up_bias,
        down_weight,
        down_bias,
        norm_gains,
        norm_shifts,
    )
    blocks, long_len, model_width = passage_tokens.shape
    query_count, query_len, unused_width = query_tokens.shape
    subs_count = long_len // SHORT
    slot_count = blocks * subs_count
    my_index = lax.axis_index(("rep", "shard"))
    own_count = lax.dynamic_index_in_dim(bucket_counts, my_index, 0, keepdims=False)
    passage_mask = block_mask(lax.iota(jnp.int32, blocks) < own_count, long_len, SHORT)
    query_mask = block_mask(jnp.ones((query_count,), dtype=bool), query_len, query_len)
    query_weights = fetch_layer(stacks, 0)
    query_result, query_kept = layer_forward(query_tokens, query_weights, query_mask)
    passage_weights = fetch_layer(stacks, 1)
    passage_result, passage_kept = layer_forward(passage_tokens, passage_weights, passage_mask)
    query_cls = query_result.reshape(query_count, query_len, model_width)[:, 0].astype(jnp.bfloat16)
    passage_cls = (
        passage_result.reshape(blocks, subs_count, SHORT, model_width)[:, :, 0]
        .reshape(slot_count, model_width)
        .astype(jnp.bfloat16)
    )
    every_cls = lax.all_gather(passage_cls, ("rep", "shard"), axis=0, tiled=True)
    cand_count = every_cls.shape[0]
    device_count = bucket_counts.shape[0]
    score_scale = 2.0 / math.sqrt(model_width)
    logits = jnp.dot(query_cls, every_cls.T, preferred_element_type=jnp.float32) * score_scale
    slot_ids = lax.iota(jnp.int32, cand_count)
    owner_index = slot_ids // slot_count
    owner_counts = jnp.sum(
        jnp.where(
            owner_index[:, None] == lax.iota(jnp.int32, device_count)[None], bucket_counts[None], 0
        ),
        axis=1,
    )
    slot_valid = (slot_ids % slot_count // subs_count >= owner_counts) | (
        slot_ids % subs_count == 0
    )
    masked = jnp.where(slot_valid[None], logits, NEG_FILL)
    row_max = jnp.max(masked, axis=1, keepdims=True)
    exp_scores = jnp.exp(masked - row_max)
    row_total = jnp.sum(exp_scores, axis=1, keepdims=True)
    log_total = row_max[:, 0] + jnp.log(row_total[:, 0])
    hit_mask = slot_ids[None] == positives[:, None]
    picked = jnp.sum(jnp.where(hit_mask, masked, 0.0), axis=1)
    local_loss = jnp.sum(log_total - picked)
    d_logits = (exp_scores / row_total - hit_mask.astype(jnp.float32)).astype(jnp.bfloat16)
    d_query_cls = jnp.dot(d_logits, every_cls, preferred_element_type=jnp.float32) * score_scale
    d_cands = (
        lax.dot_general(
            d_logits, query_cls, (((0,), (0,)), ((), ())), preferred_element_type=jnp.float32
        )
        * score_scale
    )
    d_passage_cls = lax.psum_scatter(d_cands, ("rep", "shard"), scatter_dimension=0, tiled=True)
    loss_sum = lax.psum(local_loss, ("rep", "shard"))
    loss = loss_sum / (query_count * lax.axis_size(("rep", "shard")))
    query_dout = (
        query_cot.astype(jnp.float32)
        .at[:, 0]
        .add(d_query_cls)
        .reshape(query_count * query_len, model_width)
    )
    passage_dout = (
        passage_cot.astype(jnp.float32)
        .reshape(blocks, subs_count, SHORT, model_width)
        .at[:, :, 0]
        .add(d_passage_cls.reshape(blocks, subs_count, model_width))
        .reshape(blocks * long_len, model_width)
    )
    passage_back = fetch_again(stacks, 1)
    passage_dx, passage_grads = layer_backward(
        passage_dout, passage_back, passage_kept, passage_mask
    )
    passage_owned = reduce_layer(passage_grads)
    query_back = fetch_again(stacks, 0)
    query_dx, query_grads = layer_backward(query_dout, query_back, query_kept, query_mask)
    query_owned = reduce_layer(query_grads)
    stacked = [
        jnp.stack([first_g, second_g]) for first_g, second_g in zip(query_owned, passage_owned)
    ]
    gains_grad = jnp.swapaxes(stacked[8], 1, 2)
    shifts_grad = jnp.swapaxes(stacked[9], 1, 2)
    return (
        loss,
        query_result.reshape(query_count, query_len, model_width).astype(jnp.bfloat16),
        passage_result.reshape(blocks, long_len, model_width).astype(jnp.bfloat16),
        query_dx.reshape(query_count, query_len, model_width).astype(jnp.bfloat16),
        passage_dx.reshape(blocks, long_len, model_width).astype(jnp.bfloat16),
        stacked[0],
        stacked[1],
        stacked[2],
        stacked[3],
        stacked[4],
        stacked[5],
        stacked[6],
        stacked[7],
        gains_grad,
        shifts_grad,
    )


BF = jnp.bfloat16
F32 = jnp.float32
MESH = pl.DeviceIdType.MESH
ROWS = (128, 256)
D = 768
HALF = 384
FFN = 768
PLAN = [(2, 2, 0, 0), (2, 2, 1, 0), (2, 2, 1, 0), (3, 3, 2, 1), (4, 3, 2, 2), (6, 4, 2, 2), (6, 5, 3, 2), (10, 8, 5, 2), (10, 8, 7, 3), (10, 10, 9, 3), (13, 10, 10, 5), (14, 11, 10, 5), (15, 12, 10, 6), (15, 15, 13, 6), (18, 17, 15, 7), (20, 18, 16, 7), (21, 21, 18, 9), (21, 21, 18, 9), (22, 21, 18, 10), (23, 21, 18, 10), (23, 21, 20, 10)]
NEIGH = tuple((dy, dx, dc) for dy in (1, 0) for dx in (1, 0) for dc in (1, 0) if dy + dx + dc)

(S_X, S_QKV, S_QKV1, S_QKV2, S_QKVC, S_QKVZ, S_QKVZ1, S_QKVZ2, S_OUT, S_OUTC, S_OUTZ, S_UP, S_UP1, S_UPC, S_UPZ, S_UPZ1,
 S_DN, S_OP, S_MY, S_MC, S_MF, S_F1A, S_F1B, S_F2, S_DY, S_DC, S_DF, S_D1A, S_D1B, S_D2,
 S_DA, S_DX, S_GD, S_GD1, S_GD2, S_GU, S_GU1, S_XU, S_XU1, S_GO, S_GQ, S_GQ1, S_GQ2, S_YQ, S_YQ1, S_YQ2, S_SMALL, S_CZ, S_CP, S_CPC, S_CPF, S_BG, S_COT, S_FIN, S_FIN2, S_CF, S_Z) = range(57)
N_UNITS = 23
N_SEMS = 4 * S_Z + 6 * N_UNITS + 2


def nn(a, b):
    return jnp.dot(a, b, preferred_element_type=F32)


def nt(a, b):
    return lax.dot_general(a, b, (((1,), (1,)), ((), ())), preferred_element_type=F32)


def tn(a, b):
    return lax.dot_general(a, b, (((0,), (0,)), ((), ())), preferred_element_type=F32)


def flip(v, d):
    return 1 - v if d else v


def mo(v, m):
    return pl.multiple_of(v, m)


(B_X, B_COT, B_WQ, B_WO, B_WU, B_WD, B_QB, B_UB, B_QKV, B_P, B_ATT, B_OS,
 B_OR, B_N1, B_N2, B_R1, B_R2, B_MID, B_ACT, B_SL, B_S1, B_V1, B_S2, B_V2,
 B_KP, B_Y, B_DF, B_DA, B_GD, B_GU, B_GO, B_GQ, B_ZSD, B_ZSU, B_ZSO, B_ZSQ,
 B_ZAD, B_ZAU, B_ZAO, B_ZAQ, B_ZBD, B_ZBU, B_ZBO, B_ZBQ, B_CLN, B_CLR, B_CLC, B_CLS,
 B_CLD, B_CLP, B_CFW, B_CF, B_YQ, B_T96, B_SP, B_BGC, B_PV, B_BG, B_BGS, B_BGR,
 B_BGA, B_BGB, B_CM, B_GA, B_CG, B_DAT, B_XU) = range(67)


def scratch_list():
    s = []

    def add(name, t, shape, dtype):
        s.append(((name, t), pltpu.VMEM(shape, dtype)))

    for t, T in enumerate(ROWS):
        add(B_X, t, (2 * T, D), BF)
        add(B_COT, t, (T, D), BF)
        add(B_WQ, t, (D, 3 * HALF), BF)
        add(B_WO, t, (HALF, D), BF)
        add(B_WU, t, (D, FFN), BF)
        add(B_WD, t, (FFN, D), BF)
        add(B_QB, t, (8, 3 * HALF), F32)
        add(B_UB, t, (8, FFN), F32)
        add(B_QKV, t, (2 * T, 3 * HALF), BF)
        add(B_P, t, (12, T, T), F32)
        add(B_ATT, t, (2 * T, HALF), BF)
        add(B_OS, t, (T, D), BF)
        add(B_OR, t, (T, D), BF)
        add(B_N1, t, (T, D), F32)
        add(B_N2, t, (T, D), F32)
        add(B_R1, t, (T, 128), F32)
        add(B_R2, t, (T, 128), F32)
        add(B_MID, t, (4 * T, D), BF)
        add(B_ACT, t, (4 * T, FFN), BF)
        add(B_SL, t, (4 * T, FFN), BF)
        add(B_S1, t, (2, T, D), BF)
        add(B_V1, t, (2, T, D), BF)
        add(B_S2, t, (T, D), BF)
        add(B_V2, t, (T, D), BF)
        add(B_KP, t, (2, T, D), F32)
        add(B_Y, t, (T, D), BF)
        add(B_DF, t, (4 * T, D), BF)
        add(B_DA, t, (2 * T, D), BF)
        add(B_DAT, t, (2 * T, HALF), BF)
        add(B_GD, t, (HALF, D), BF)
        add(B_GU, t, (4, 96, FFN), BF)
        add(B_XU, t, (HALF, FFN), BF)
        add(B_GO, t, (4, 96, D), BF)
        add(B_GQ, t, (4, 96, 3 * HALF), BF)
        add(B_YQ, t, (HALF, 3 * HALF), BF)
        for first in (B_ZSD, B_ZAD, B_ZBD):
            add(first, t, (HALF, D), BF)
            add(first + 1, t, (96, 4 * D), BF)
            add(first + 2, t, (96, D), BF)
            add(first + 3, t, (96, 3 * D), BF)
    for t in (0, 1):
        add(B_CLN, t, (8, D), F32)
        add(B_CLR, t, (8, 128), F32)
        add(B_CLC, t, (8, D), F32)
        add(B_CLS, t, (16, FFN), BF)
        add(B_CLD, t, (16, D), F32)
        add(B_CLP, t, (16, FFN), F32)
    add(B_CFW, 0, (16, D), F32)
    add(B_CF, 0, (4, 16, D), BF)
    add(B_T96, 0, (16, HALF), F32)
    add(B_SP, 0, (8, 16, HALF), BF)
    add(B_PV, 0, (32, D), F32)
    add(B_BG, 0, (32, D), F32)
    add(B_BGC, 0, (8, 16, HALF), BF)
    add(B_BGR, 0, (8, 16, HALF), BF)
    add(B_BGS, 0, (16, HALF), F32)
    add(B_BGA, 0, (16, HALF), F32)
    add(B_BGB, 0, (16, HALF), F32)
    add(B_CM, 0, (16, 512), BF)
    add(B_GA, 0, (32, 16, 512), BF)
    add(B_CG, 0, (2, 16, D), F32)
    return s


def fused_kernel(*refs):
    (i_x0, i_x1, i_cot0, i_cot1, i_qkvw, i_outw, i_upw, i_dnw, i_qvb, i_ob, i_ub, i_db, i_gn, i_sf, i_cnt, i_pos,
     o_loss, o_y0, o_y1, o_gx0, o_gx1, o_oq, o_oo, o_ou, o_od, o_obg) = refs[:26]
    held = {key: ref for (key, _), ref in zip(scratch_list(), refs[26:])}
    sems = refs[-1]

    def g(name, t):
        return held[(name, t)]

    rep = lax.axis_index("rep")
    s = lax.axis_index("shard")
    y = s // 4
    x = (s // 2) % 2
    c = s % 2
    x_in = (i_x0, i_x1)
    cot_in = (i_cot0, i_cot1)

    def sem(name, t, side):
        return sems.at[4 * name + 2 * t + side]

    def sh(yy, xx, cc):
        return yy * 4 + xx * 2 + cc

    def send(src, dst, name, t, dev):
        pltpu.make_async_remote_copy(src, dst, send_sem=sem(name, t, 1), recv_sem=sem(name, t, 0),
                                     device_id=dev, device_id_type=MESH).start()

    def local(src, dst, name, t, side=0):
        pltpu.make_async_copy(src, dst, sem(name, t, side)).start()

    def wait(ref, name, t, side=0):
        pltpu.make_async_copy(ref, ref, sem(name, t, side)).wait()

    def peer(d):
        return flip(y, d[0]), flip(x, d[1]), flip(c, d[2])

    sib = (rep, sh(y, x, 1 - c))
    ypeer = (rep, sh(1 - y, x, c))
    xpeer = (rep, sh(y, 1 - x, c))

    bar = pltpu.get_barrier_semaphore()
    for d in NEIGH:
        pl.semaphore_signal(bar, 1, device_id=(rep, sh(*peer(d))), device_id_type=MESH)
    for k in (1, 2, 3):
        pl.semaphore_signal(bar, 1, device_id=((rep + k) % 4, s), device_id_type=MESH)

    T96, SP, PV = (g(b, 0) for b in (B_T96, B_SP, B_PV))
    T96[...] = jnp.zeros((16, HALF), F32)
    T96[0:2, 0:96] = i_ob[...].astype(F32)
    T96[2:4, 0:96] = i_db[...].astype(F32)
    for t in (0, 1):
        for k in (0, 1):
            T96[4 + 2 * t + k:5 + 2 * t + k, 0:96] = i_gn[t, k:k + 1, :].astype(F32)
            T96[8 + 2 * t + k:9 + 2 * t + k, 0:96] = i_sf[t, k:k + 1, :].astype(F32)
    T96[0:2, 128:320] = i_qvb[...].astype(F32)
    T96[12:14, :] = i_ub[...].astype(F32)
    SP[s] = T96[...].astype(BF)

    def place(n, w, at):
        i = lax.broadcasted_iota(jnp.int32, (n, D), 0)
        j = lax.broadcasted_iota(jnp.int32, (n, D), 1)
        return ((j == i + at) & (i < w)).astype(F32).astype(BF)

    pl.semaphore_wait(bar, 10)

    half = rep % 2
    zpair = (rep + 1 - 2 * half, s)
    for d in NEIGH:
        send(SP.at[s], SP.at[s], S_SMALL, 0, (rep, sh(*peer(d))))
    rows96 = pl.ds(mo(s * 96, 32), 96)
    half48 = pl.ds(mo(half * 48, 16), 48)

    def send_x(t):
        T = ROWS[t]
        own = g(B_X, t).at[pl.ds(mo(c * T, 128), T)]
        send(x_in[t], own, S_X, t, sib)
        local(x_in[t], own, S_X, t)

    def rows48(owner):
        return pl.ds(mo(owner * 96 + half * 48, 16), 48)

    def send_cols(t, src, dst, pieces, far, near):
        for k in range(len(pieces((y, x, c)))):
            for d in NEIGH + ((0, 0, 0),):
                p = peer(d)
                cols, to = pl.ds(mo(pieces(p)[k], 128), HALF), pl.ds(k * HALF, HALF)
                if d[0] + d[1]:
                    send(src.at[t, half48, cols], dst.at[rows48(s), to], far + k, t, (rep, sh(*p)))
                elif d[2]:
                    send(src.at[t, :, cols], dst.at[rows96, to], near, t, sib)
                else:
                    local(src.at[t, :, cols], dst.at[rows96, to], near, t)

    def send_qkv(t):
        send_cols(t, i_qkvw, g(B_WQ, t), lambda p: [part * D + p[2] * HALF for part in range(3)], S_QKV, S_QKVC)

    def send_up(t):
        send_cols(t, i_upw, g(B_WU, t), lambda p: [HALF * (4 * p[0] + 2 * xx + p[2]) for xx in (0, 1)], S_UP, S_UPC)

    def part_of(buf, rows, k):
        return buf.at[pl.ds(0, rows), pl.ds(k * HALF, HALF)]

    def forward_cols(t, buf, k, far, pair):
        wait(part_of(buf, 288, k), far + k, t)
        for d in NEIGH:
            if d[0] + d[1]:
                piece = buf.at[rows48(sh(*peer(d))), pl.ds(k * HALF, HALF)]
                send(piece, piece, pair + k, t, zpair)

    def send_out(t):
        WO = g(B_WO, t)
        for dy in (0, 1):
            for dx in (0, 1):
                dev = (rep, sh(flip(y, dy), flip(x, dx), y))
                if dy + dx:
                    send(i_outw.at[t, half48], WO.at[rows48(x * 2 + c)], S_OUT, t, dev)
                else:
                    dst = WO.at[pl.ds(mo((x * 2 + c) * 96, 32), 96)]

                    @pl.when(c == y)
                    def _():
                        local(i_outw.at[t], dst, S_OUTC, t)

                    @pl.when(c != y)
                    def _():
                        send(i_outw.at[t], dst, S_OUTC, t, dev)

    def forward_out(t):
        WO = g(B_WO, t)

        def go(xs):
            for xx in xs:
                for cc in (0, 1):
                    piece = WO.at[rows48(xx * 2 + cc)]
                    send(piece, piece, S_OUTZ, t, zpair)

        @pl.when(c == y)
        def _():
            wait(WO.at[pl.ds(0, 96)], S_OUT, t)
            go((1 - x,))

        @pl.when(c != y)
        def _():
            wait(WO.at[pl.ds(0, 192)], S_OUT, t)
            go((0, 1))

    def whole_out(t):
        WO = g(B_WO, t)

        @pl.when(c == y)
        def _():
            wait(WO.at[pl.ds(0, 192)], S_OUTC, t)
            wait(WO.at[pl.ds(0, 96)], S_OUTZ, t)

        @pl.when(c != y)
        def _():
            wait(WO.at[pl.ds(0, 192)], S_OUTZ, t)

    def send_dn(t):
        dst = g(B_WD, t).at[pl.ds(mo(x * HALF, 128), HALF)]
        send(i_dnw.at[t], dst, S_DN, t, xpeer)
        local(i_dnw.at[t], dst, S_DN, t)

    for t in (1, 0):
        send_x(t)
        send_qkv(t)
        send_out(t)
    send_up(1)
    send_dn(1)
    for t in (0, 1):
        local(cot_in[t], g(B_COT, t), S_COT, 0, t)

    wait(SP.at[pl.ds(0, 7)], S_SMALL, 0)
    low96 = jnp.zeros((16, D), F32)
    low192 = [jnp.zeros((16, D), F32) for _ in (0, 1)]
    for k in range(8):
        low96 = low96 + nn(SP[k, :, 0:128], place(128, 96, 96 * k))
        low192[k // 4] = low192[k // 4] + nn(SP[k, :, 128:384], place(256, 192, 192 * (k % 4)))
    PV[0:16, :] = low96
    PV[12:14, :] = low192[0][0:2, :]
    PV[14:16, :] = low192[1][0:2, :]
    for k in range(8):
        for t in (0, 1):
            at, lanes = 16 + 4 * t + k // 2, slice(k % 2 * HALF, (k % 2 + 1) * HALF)
            PV[at:at + 1, lanes] = SP[k].astype(F32)[12 + t:13 + t, :]
    R_OB, R_DB, R_GN, R_SF, R_QB, R_VB, R_UB = 0, 2, 4, 8, 12, 14, 16

    def prow(k):
        return PV[k:k + 1, :]

    lane_half = pl.ds(mo(c * HALF, 128), HALF)
    for t in (0, 1):
        g(B_QB, t)[...] = jnp.zeros((8, 3 * HALF), F32)
        g(B_QB, t)[0:1, 0:HALF] = PV[R_QB + t:R_QB + t + 1, lane_half]
        g(B_QB, t)[0:1, 2 * HALF:] = PV[R_VB + t:R_VB + t + 1, lane_half]
        for xx in (0, 1):
            at = R_UB + 4 * t + xx
            lo, hi = PV[at:at + 1, lane_half], PV[at + 2:at + 3, lane_half]
            g(B_UB, t)[0:1, xx * HALF:(xx + 1) * HALF] = jnp.where(jnp.full((1, HALF), y) == 0, lo, hi)

    def same_part(t, grp):
        T = ROWS[t]
        shift = 5 if t == 0 else 6
        ri = lax.broadcasted_iota(jnp.int32, (T, T), 0) >> shift
        ci = lax.broadcasted_iota(jnp.int32, (T, T), 1) >> shift
        m = ri == ci
        if t == 1:
            m = m | (jnp.full((T, T), i_cnt[rep * 8 + (s // 2) * 2 + grp]) > 0)
        return m

    lane_lo = lax.broadcasted_iota(jnp.int32, (1, 128), 1) < 64
    mask_a = lane_lo.astype(F32).astype(BF)
    mask_b = (1.0 - lane_lo.astype(F32)).astype(BF)

    def lnfwd(first, gain, shift):
        mean = jnp.mean(first, axis=-1, keepdims=True)
        cen = first - mean
        inv = lax.rsqrt(jnp.mean(cen * cen, axis=-1, keepdims=True) + LN_EPS)
        n = cen * inv
        return n, inv, n * gain + shift

    CH = 64

    def project(t, k):
        X, WQ = g(B_X, t), g(B_WQ, t)
        if k == 0:
            wait(X, S_X, t)
            wait(WQ.at[pl.ds(0, 192)], S_QKVC, t)
        wait(part_of(WQ, 288, k), S_QKVZ + k, t)
        cols = slice(k * HALF, (k + 1) * HALF)
        g(B_QKV, t)[:, cols] = (nn(X[...], WQ[:, cols]) + g(B_QB, t)[0:1, cols]).astype(BF)

    def attention(t):
        T = ROWS[t]
        X, WQ, QKV, P, ATT = g(B_X, t), g(B_WQ, t), g(B_QKV, t), g(B_P, t), g(B_ATT, t)
        @pl.loop(0, 2)
        def _(grp):
            rows = pl.ds(mo(grp * T, 128), T)
            m = same_part(t, grp)

            @pl.loop(0, 3)
            def _(hp):
                q = QKV[rows, pl.ds(mo(hp * 128, 128), 128)]
                k = QKV[rows, pl.ds(mo(HALF + hp * 128, 128), 128)]
                val = QKV[rows, pl.ds(mo(2 * HALF + hp * 128, 128), 128)]
                outs = []
                for h, msk in ((0, mask_a), (1, mask_b)):
                    sc = jnp.where(m, nt(q * msk, k) * (1.0 / math.sqrt(HD)), NEG_FILL)
                    mx = jnp.max(sc, axis=-1, keepdims=True)
                    e = jnp.exp(sc - mx)
                    p = e * (1.0 / jnp.sum(e, axis=-1, keepdims=True))
                    P[grp * 6 + hp * 2 + h] = p
                    outs.append(nn(p.astype(BF), val))
                ATT[rows, pl.ds(mo(hp * 128, 128), 128)] = jnp.where(lane_lo, outs[0], outs[1]).astype(BF)

        whole_out(t)
        g(B_OS, t)[...] = nn(ATT[pl.ds(mo((1 - c) * T, 128), T), :], g(B_WO, t)[...]).astype(BF)
        send(g(B_OS, t), g(B_OR, t), S_OP, t, sib)
        g(B_KP, t)[0] = nn(ATT[pl.ds(mo(c * T, 128), T), :], g(B_WO, t)[...])
        wait(g(B_OR, t), S_OP, t)
        me4 = (2 * y + c) * T
        ob, gain, shift = prow(R_OB + t), prow(R_GN + 2 * t), prow(R_SF + 2 * t)

        @pl.loop(0, T // CH)
        def _(i):
            r = pl.ds(mo(i * CH, CH), CH)
            first = (X[pl.ds(mo(c * T + i * CH, CH), CH), :].astype(F32) + g(B_KP, t)[0, r, :]
                     + g(B_OR, t)[r, :].astype(F32) + ob)
            n, inv, mid = lnfwd(first, gain, shift)
            g(B_N1, t)[r, :] = n
            g(B_R1, t)[r, :] = jnp.broadcast_to(inv, (CH, 128))
            g(B_MID, t)[pl.ds(mo(me4 + i * CH, CH), CH), :] = mid.astype(BF)

        gather_rows(t, B_MID, S_MY, S_MC, S_MF)

    def slot_rows(t, yy, cc):
        T = ROWS[t]
        return pl.ds(mo((2 * yy + cc) * T, 128), T)

    def gather_rows(t, buf, ny, nc, nf):
        own = g(buf, t).at[slot_rows(t, y, c)]
        send(own, own, ny, t, ypeer)
        send(own, own, nc, t, sib)

    def gather_near(t, buf, nc):
        wait(g(buf, t).at[slot_rows(t, y, 1 - c)], nc, t)

    def gather_forward(t, buf, ny, nf):
        got = g(buf, t).at[slot_rows(t, 1 - y, c)]
        wait(got, ny, t)
        send(got, got, nf, t, sib)

    def gather_far(t, buf, nf):
        wait(g(buf, t).at[slot_rows(t, 1 - y, 1 - c)], nf, t)

    def gather_sent(t, buf, ny, nc, nf):
        own = g(buf, t).at[slot_rows(t, y, c)]
        wait(own, ny, t, 1)
        wait(own, nc, t, 1)
        wait(own, nf, t, 1)

    def up_pair(t, yy):
        T = ROWS[t]
        rows = pl.ds(mo(2 * yy * T, 128), 2 * T)

        @pl.loop(0, 3)
        def _(j):
            cols = pl.ds(mo(j * 256, 128), 256)
            pre = nn(g(B_MID, t)[rows, :], g(B_WU, t)[:, cols]) + g(B_UB, t)[0:1, cols]
            cdf = 0.5 * (1.0 + lax.erf(pre * INV_ROOT_TWO))
            g(B_ACT, t)[rows, cols] = (pre * cdf).astype(BF)
            g(B_SL, t)[rows, cols] = (cdf + pre * jnp.exp(-0.5 * pre * pre) * INV_ROOT_TWO_PI).astype(BF)

    def scatter_partial(t, part, n1a, n1b, n2):
        S1, V1, S2, V2, KP = g(B_S1, t), g(B_V1, t), g(B_S2, t), g(B_V2, t), g(B_KP, t)
        S1[0] = part(slot_rows(t, 1 - y, 1 - c)).astype(BF)
        send(S1.at[0], V1.at[0], n1a, t, sib)
        KP[0] = part(slot_rows(t, 1 - y, c))
        S1[1] = part(slot_rows(t, y, 1 - c)).astype(BF)
        send(S1.at[1], V1.at[1], n1b, t, sib)
        wait(V1.at[0], n1a, t)
        S2[...] = (KP[0] + V1[0].astype(F32)).astype(BF)
        send(S2, V2, n2, t, ypeer)
        KP[1] = part(slot_rows(t, y, c))

    def scatter_finish(t, n1b, n2):
        wait(g(B_V1, t).at[1], n1b, t)
        wait(g(B_V2, t), n2, t)

    def scatter_sent(t, n1a, n1b, n2):
        wait(g(B_S1, t).at[0], n1a, t, 1)
        wait(g(B_S1, t).at[1], n1b, t, 1)
        wait(g(B_S2, t), n2, t, 1)

    def summed(t, r):
        return g(B_KP, t)[1, r, :] + g(B_V1, t)[1, r, :].astype(F32) + g(B_V2, t)[r, :].astype(F32)

    def ffn(t):
        gather_near(t, B_MID, S_MC)
        gather_forward(t, B_MID, S_MY, S_MF)
        wait(g(B_WU, t).at[pl.ds(0, 192)], S_UPC, t)
        for k in (0, 1):
            wait(part_of(g(B_WU, t), 288, k), S_UPZ + k, t)
        up_pair(t, y)
        gather_far(t, B_MID, S_MF)
        up_pair(t, 1 - y)
        wait(g(B_WD, t), S_DN, t)
        scatter_partial(t, lambda rows: nn(g(B_ACT, t)[rows, :], g(B_WD, t)[...]), S_F1A, S_F1B, S_F2)
        T = ROWS[t]
        r = lax.broadcasted_iota(jnp.int32, (16, 4 * T), 0)
        j = lax.broadcasted_iota(jnp.int32, (16, 4 * T), 1)
        at_cls = (j == (r >> 2) * T + (r & 3) * (32, 64)[t]).astype(F32).astype(BF)
        g(B_CLS, t)[...] = nn(at_cls, g(B_SL, t)[...]).astype(BF)

    def ffn_end(t):
        T = ROWS[t]
        scatter_finish(t, S_F1B, S_F2)
        db = prow(R_DB + t)
        g0, g1, s0, s1 = (prow(base + 2 * t + k) for base in (R_GN, R_SF) for k in (0, 1))

        @pl.loop(0, T // CH)
        def _(i):
            r = pl.ds(mo(i * CH, CH), CH)
            second = g(B_N1, t)[r, :] * g0 + s0 + summed(t, r) + db
            n, inv, res = lnfwd(second, g1, s1)
            g(B_N2, t)[r, :] = n
            g(B_R2, t)[r, :] = jnp.broadcast_to(inv, (CH, 128))
            g(B_Y, t)[r, :] = res.astype(BF)

        local(g(B_Y, t), (o_y0, o_y1)[t], S_FIN, 0, t)

    def forward_qkv(t, k):
        forward_cols(t, g(B_WQ, t), k, S_QKV, S_QKVZ)

    def forward_up(t):
        for k in (0, 1):
            forward_cols(t, g(B_WU, t), k, S_UP, S_UPZ)

    for k in range(3):
        forward_qkv(1, k)
    forward_out(1)
    for k in range(3):
        project(1, k)
        forward_qkv(0, k)
    send_up(0)
    send_dn(0)
    attention(1)
    forward_out(0)
    forward_up(1)
    for k in range(3):
        project(0, k)
    attention(0)
    forward_up(0)
    def fold(a):
        return jnp.sum(a.reshape(CH // 8, 8, D), axis=0)

    def put_bias(k, row):
        g(B_BG, 0)[k:k + 1, :] = row

    def ln_back(t, din, nrm, inv, gain):
        gg = din * gain
        m1 = jnp.mean(gg, axis=-1, keepdims=True)
        m2 = jnp.mean(gg * nrm, axis=-1, keepdims=True)
        return inv * (gg - m1 - nrm * m2)

    steps = (32, 64)

    def out_back(t):
        T = ROWS[t]
        wait(g(B_COT, t), S_COT, 0, t)
        for i in range(4):
            row = slice(i * steps[t], i * steps[t] + 1)
            g(B_CLN, t)[i:i + 1, :] = g(B_N2, t)[row, :]
            g(B_CLR, t)[i:i + 1, :] = g(B_R2, t)[row, :]
            g(B_CLC, t)[i:i + 1, :] = g(B_COT, t)[row, :].astype(F32)
        gain = prow(R_GN + 2 * t + 1)
        me4 = (2 * y + c) * T
        zero = jnp.zeros((8, D), F32)

        def body(i, acc):
            r = pl.ds(mo(i * CH, CH), CH)
            dout = g(B_COT, t)[r, :].astype(F32)
            nrm = g(B_N2, t)[r, :]
            dsec = ln_back(t, dout, nrm, g(B_R2, t)[r, 0:1], gain)
            g(B_N2, t)[r, :] = dsec
            g(B_DF, t)[pl.ds(mo(me4 + i * CH, CH), CH), :] = dsec.astype(BF)
            return (acc[0] + fold(dout * nrm), acc[1] + fold(dout))

        acc = lax.fori_loop(0, T // CH, body, (zero, zero))
        for k, a in zip((R_GN + 2 * t + 1, R_SF + 2 * t + 1), acc):
            put_bias(k, jnp.sum(a, axis=0, keepdims=True))

    def cls_back(t):
        dcls = g(B_CG, 0)[t, 0:4, :]
        nrm = g(B_CLN, t)[0:4, :]
        dsec = ln_back(t, g(B_CLC, t)[0:4, :] + dcls, nrm, g(B_CLR, t)[0:4, 0:1], prow(R_GN + 2 * t + 1))
        for i in range(4):
            g(B_N2, t)[i * steps[t]:i * steps[t] + 1, :] = dsec[i:i + 1, :]
        g(B_CFW, 0)[4 * t:4 * t + 4, :] = dsec
        for k, a in ((R_GN + 2 * t + 1, dcls * nrm), (R_SF + 2 * t + 1, dcls)):
            put_bias(k, g(B_BG, 0)[k:k + 1, :] + jnp.sum(a, axis=0, keepdims=True))

    def cls_place(t):
        r = lax.broadcasted_iota(jnp.int32, (16, 64), 0)
        j = lax.broadcasted_iota(jnp.int32, (16, 64), 1)
        which = (j == (r >> 2) * 16 + 4 * t + (r & 3)).astype(F32).astype(BF)
        rows = nn(which, g(B_CF, 0)[...].reshape(64, D))
        g(B_CLD, t)[...] = rows
        da = nt(rows.astype(BF), g(B_WD, t)[...])
        g(B_CLP, t)[...] = da * g(B_CLS, t)[...].astype(F32)
        cls_rows(t, g(B_DF, t), g(B_CLD, t))

    def cls_rows(t, buf, new):
        top = lax.broadcasted_iota(jnp.int32, (16, 1), 0) == 0
        for k in range(16):
            tile = pl.ds(k // 4 * ROWS[t] + k % 4 * steps[t], 16)
            buf[tile, :] = jnp.where(top, new[k:k + 1, :], buf[tile, :].astype(F32)).astype(BF)

    def down_pair(t, yy):
        T = ROWS[t]
        rows = pl.ds(mo(2 * yy * T, 128), 2 * T)

        @pl.loop(0, 3)
        def _(j):
            cols = pl.ds(mo(j * 256, 128), 256)
            da = nt(g(B_DF, t)[rows, :], g(B_WD, t)[cols, :])
            g(B_SL, t)[rows, cols] = (da * g(B_SL, t)[rows, cols].astype(F32)).astype(BF)

    def pre_back(t, between=lambda: None):
        gather_near(t, B_DF, S_DC)
        down_pair(t, y)
        between()
        gather_forward(t, B_DF, S_DY, S_DF)
        gather_far(t, B_DF, S_DF)
        down_pair(t, 1 - y)

    def ffn_back(t, point=lambda: None):
        gather_sent(t, B_DF, S_DY, S_DC, S_DF)
        cls_place(t)
        ACT, DF, WD, WU = g(B_ACT, t), g(B_DF, t), g(B_WD, t), g(B_WU, t)
        for k in range(3):
            cols = pl.ds(mo((1 - x) * HALF + 128 * k, 128), 128)
            WD[cols, :] = tn(ACT[:, cols], DF[...]).astype(BF)
            send(WD.at[cols], g(B_GD, t).at[pl.ds(128 * k, 128)], S_GD + k, t, xpeer)
        cls_rows(t, g(B_SL, t), g(B_CLP, t))
        point()

        scatter_partial(t, lambda rows: nt(g(B_SL, t)[rows, :], g(B_WU, t)[...]), S_D1A, S_D1B, S_D2)
        point()
        own_sum = nn(jnp.ones((8, ROWS[t]), F32).astype(BF), g(B_DF, t)[slot_rows(t, y, c), :])
        put_bias(R_DB + t, own_sum[0:1, :])
        ones = jnp.ones((8, 4 * ROWS[t]), F32).astype(BF)
        sums = nn(ones, g(B_SL, t)[...])[0:1, :]
        for xx in (0, 1):
            part = sums[:, xx * HALF:(xx + 1) * HALF]
            at = R_UB + 4 * t + xx

            @pl.when(y == 0)
            def _():
                g(B_BG, 0)[at:at + 1, lane_half] = part

            @pl.when(y == 1)
            def _():
                g(B_BG, 0)[at + 2:at + 3, lane_half] = part

        cols = pl.ds(mo(x * HALF, 128), HALF)
        WD[cols, :] = tn(ACT[:, cols], DF[...]).astype(BF)
        for dy in (1, 0):
            far, near = (pl.ds(mo(flip(y, dy) * HALF + xx * 192, 64), 192) for xx in (1 - x, x))

            @pl.loop(0, 3)
            def _(j):
                cols = pl.ds(mo(flip(y, dy) * HALF + j * 128, 128), 128)
                WU[cols, :] = tn(g(B_MID, t)[:, cols], g(B_SL, t)[...]).astype(BF)

            send(WU.at[far], g(B_XU, t).at[pl.ds((1 - dy) * 192, 192)], S_XU1 - dy, t, xpeer)
            point()

    def relay_up(t, dy):
        WU, GU, mine = g(B_WU, t), g(B_GU, t), 2 * y + c
        got = g(B_XU, t).at[pl.ds((1 - dy) * 192, 192)]
        wait(got, S_XU1 - dy, t)
        yy = flip(y, dy)
        for r0 in (0, 96):
            r = pl.ds(mo(yy * HALF + x * 192 + r0, 32), 96)
            WU[r, :] = (WU[r, :].astype(F32) + got[pl.ds(r0, 96), :].astype(F32)).astype(BF)
        for dc in (1, 0):
            owner = sh(yy, x, flip(c, dc))
            rows = WU.at[pl.ds(mo(96 * owner, 32), 96)]
            if dy + dc:
                send(rows, GU.at[mine], S_GU1 - dy, t, (rep, owner))
            else:
                local(rows, GU.at[mine], S_GU1, t)

    g(B_BG, 0)[...] = jnp.zeros((32, D), F32)
    g(B_CFW, 0)[...] = jnp.zeros((16, D), F32)
    ffn(1)
    ffn(0)
    ffn_end(1)
    out_back(1)
    gather_rows(1, B_DF, S_DY, S_DC, S_DF)
    ffn_end(0)

    def pick(T, lo, step):
        ri = lax.broadcasted_iota(jnp.int32, (16, T), 0) & 7
        ci = lax.broadcasted_iota(jnp.int32, (16, T), 1)
        return (((ri & 4) == lo) & (ci == (ri & 3) * step)).astype(F32).astype(BF)

    both = nn(pick(128, 0, 32), g(B_Y, 0)[...]) + nn(pick(256, 4, 64), g(B_Y, 1)[...])
    top = lax.broadcasted_iota(jnp.int32, (16, HALF), 0) < 8
    g(B_CM, 0)[:, :HALF] = jnp.where(top, both[:, :HALF], both[:, HALF:]).astype(BF)
    ri = lax.broadcasted_iota(jnp.int32, (16, 128), 0)
    pos = jnp.zeros((16, 128), jnp.int32)
    for i in range(4):
        pos = jnp.where(ri == i, i_pos[i], pos)
    g(B_CM, 0)[:, HALF:] = pos.astype(F32).astype(BF)
    mine = g(B_GA, 0).at[s * 4 + rep]
    for k in (1, 2, 3):
        send(g(B_CM, 0), mine, S_CZ, 0, ((rep + k) % 4, s))
    g(B_GA, 0)[s * 4 + rep] = g(B_CM, 0)[...]
    out_back(0)
    wait(g(B_GA, 0).at[pl.ds(0, 3)], S_CZ, 0)
    four = g(B_GA, 0).at[pl.ds(s * 4, 4)]
    send(four, four, S_CPC, 0, sib)
    for d in NEIGH:
        if not d[2]:
            send(four, four, S_CP, 0, (rep, sh(*peer(d))))
    gather_rows(0, B_DF, S_DY, S_DC, S_DF)

    for t in (0, 1):
        own = g(B_X, t).at[pl.ds(mo(c * ROWS[t], 128), ROWS[t])]
        wait(own, S_X, t, 1)
        for buf, n, far, near, pair in ((g(B_WQ, t), 3, S_QKV, S_QKVC, S_QKVZ), (g(B_WU, t), 2, S_UP, S_UPC, S_UPZ)):
            wait(buf.at[pl.ds(0, 96)], near, t, 1)
            for k in range(n):
                wait(part_of(buf, 288, k), far + k, t, 1)
                wait(part_of(buf, 288, k), pair + k, t, 1)
        wait(g(B_WO, t).at[pl.ds(0, 144)], S_OUT, t, 1)

        @pl.when(c == y)
        def _():
            wait(g(B_WO, t).at[pl.ds(0, 96)], S_OUTZ, t, 1)

        @pl.when(c != y)
        def _():
            wait(g(B_WO, t).at[pl.ds(0, 96)], S_OUTC, t, 1)
            wait(g(B_WO, t).at[pl.ds(0, 192)], S_OUTZ, t, 1)

        wait(g(B_WD, t).at[pl.ds(0, HALF)], S_DN, t, 1)
        wait(g(B_OS, t), S_OP, t, 1)
        gather_sent(t, B_MID, S_MY, S_MC, S_MF)
        scatter_sent(t, S_F1A, S_F1B, S_F2)
    wait(g(B_SP, 0).at[pl.ds(0, 7)], S_SMALL, 0, 1)
    wait(g(B_GA, 0).at[pl.ds(0, 3)], S_CZ, 0, 1)
    def pass_cls():
        twelve = g(B_GA, 0).at[pl.ds(0, 12)]
        wait(twelve, S_CP, 0)
        for d in NEIGH:
            if not d[2]:
                got = g(B_GA, 0).at[pl.ds(sh(*peer(d)) * 4, 4)]
                send(got, got, S_CPF, 0, sib)

    pre_back(1, pass_cls)

    wait(g(B_GA, 0).at[pl.ds(0, 4)], S_CPC, 0)
    wait(g(B_GA, 0).at[pl.ds(0, 12)], S_CPF, 0)
    wait(g(B_GA, 0).at[pl.ds(0, 4)], S_CPC, 0, 1)
    for name in (S_CP, S_CPF):
        wait(g(B_GA, 0).at[pl.ds(0, 12)], name, 0, 1)

    def pick_all(base):
        ri = lax.broadcasted_iota(jnp.int32, (128, 512), 0)
        ci = lax.broadcasted_iota(jnp.int32, (128, 512), 1)
        blk = ci >> 4
        within = (ci & 15) - base
        row = ((blk & 3) * 8 + (blk >> 2)) * 4 + within
        return ((within >= 0) & (within < 4) & (ri == row)).astype(F32).astype(BF)

    ga = g(B_GA, 0)[...].reshape(512, 512)
    qa_f = nn(pick_all(0), ga)
    qa = qa_f[:, :HALF].astype(BF)
    pa = nn(pick_all(4), ga)[:, :HALF].astype(BF)
    qb = nn(pick_all(8), ga)[:, :HALF].astype(BF)
    pb = nn(pick_all(12), ga)[:, :HALF].astype(BF)
    scale = 2.0 / math.sqrt(D)
    logits = (nt(qa, pa) + nt(qb, pb)) * scale
    lane = lax.broadcasted_iota(jnp.int32, (1, 128), 1)
    cnt = jnp.zeros((1, 128), jnp.int32)
    for k in range(32):
        cnt = jnp.where(lane >> 2 == k, i_cnt[k], cnt)
    masked = jnp.where((cnt <= 0) | (lane & 3 == 0), logits, NEG_FILL)
    mx = jnp.max(masked, axis=1, keepdims=True)
    ex = jnp.exp(masked - mx)
    sm = jnp.sum(ex, axis=1, keepdims=True)
    hit = lax.broadcasted_iota(jnp.int32, (128, 128), 1).astype(F32) == qa_f[:, HALF:]
    ce = mx + jnp.log(sm) - jnp.sum(jnp.where(hit, masked, 0.0), axis=1, keepdims=True)
    o_loss[...] = jnp.broadcast_to(jnp.sum(ce, axis=0, keepdims=True) * (1.0 / 128.0), (8, 128))
    dl = (ex / sm - hit.astype(F32)).astype(BF)
    ri = lax.broadcasted_iota(jnp.int32, (16, 128), 0)
    ci = lax.broadcasted_iota(jnp.int32, (16, 128), 1)
    sel = ((ri < 4) & (ci == ri + 4 * (rep * 8 + s))).astype(F32).astype(BF)
    dlq = nn(sel, dl).astype(BF)
    dlp = nt(sel, dl.T).astype(BF) if False else lax.dot_general(
        sel, dl, (((1,), (1,)), ((), ())), preferred_element_type=F32).astype(BF)
    g(B_CG, 0)[0, :, :HALF] = nn(dlq, pa) * scale
    g(B_CG, 0)[0, :, HALF:] = nn(dlq, pb) * scale
    g(B_CG, 0)[1, :, :HALF] = nn(dlp, qa) * scale
    g(B_CG, 0)[1, :, HALF:] = nn(dlp, qb) * scale

    def mid_back(t):
        T = ROWS[t]
        scatter_finish(t, S_D1B, S_D2)
        gain = prow(R_GN + 2 * t)
        zero = jnp.zeros((8, D), F32)

        def body(i, acc):
            r = pl.ds(mo(i * CH, CH), CH)
            dmid = g(B_N2, t)[r, :] + summed(t, r)
            nrm = g(B_N1, t)[r, :]
            dfirst = ln_back(t, dmid, nrm, g(B_R1, t)[r, 0:1], gain)
            low = dfirst.astype(BF)
            g(B_N1, t)[r, :] = dfirst
            g(B_DA, t)[pl.ds(mo(c * T + i * CH, CH), CH), :] = low
            return (acc[0] + fold(dmid * nrm), acc[1] + fold(dmid), acc[2] + fold(low.astype(F32)))

        acc = lax.fori_loop(0, T // CH, body, (zero, zero, zero))
        own = g(B_DA, t).at[pl.ds(mo(c * T, 128), T)]
        send(own, own, S_DA, t, sib)
        for k, a in zip((R_GN + 2 * t, R_SF + 2 * t, R_OB + t), acc):
            put_bias(k, jnp.sum(a, axis=0, keepdims=True))

    def attention_back(t, point):
        T = ROWS[t]
        QKV, P, ATT, DA, WO, WQ = g(B_QKV, t), g(B_P, t), g(B_ATT, t), g(B_DA, t), g(B_WO, t), g(B_WQ, t)
        wait(DA.at[pl.ds(mo((1 - c) * T, 128), T)], S_DA, t)

        DAT = g(B_DAT, t)
        DAT[...] = nt(DA[...], WO[...]).astype(BF)

        @pl.loop(0, 3)
        def _(j):
            cols = pl.ds(mo(j * 128, 128), 128)
            WO[cols, :] = tn(ATT[:, cols], DA[...]).astype(BF)

        dst = g(B_GO, t).at[y * 2 + x]
        for xx in (0, 1):
            for cc in (0, 1):
                src = WO.at[pl.ds((2 * xx + cc) * 96, 96)]
                dev = sh(c, xx, cc)

                @pl.when(dev == s)
                def _():
                    local(src, dst, S_GO, t)

                @pl.when(dev != s)
                def _():
                    send(src, dst, S_GO, t, (rep, dev))

        point()
        for grp in (0, 1):
            rows = pl.ds(grp * T, T)

            @pl.loop(0, 3)
            def _(hp):
                lanes = pl.ds(mo(hp * 128, 128), 128)
                dat = DAT[rows, lanes]
                qs, ks = lanes, pl.ds(mo(HALF + hp * 128, 128), 128)
                vs = pl.ds(mo(2 * HALF + hp * 128, 128), 128)
                q, k, val = QKV[rows, qs], QKV[rows, ks], QKV[rows, vs]
                dq, dk, dv = [], [], []
                for h, msk in ((0, mask_a), (1, mask_b)):
                    p = P[grp * 6 + hp * 2 + h]
                    dp = nt(dat * msk, val)
                    ds = (p * (dp - jnp.sum(dp * p, axis=-1, keepdims=True))).astype(BF)
                    dv.append(tn(p.astype(BF), dat))
                    dq.append(nn(ds, k))
                    dk.append(tn(ds, q))
                root = 1.0 / math.sqrt(HD)
                QKV[rows, qs] = (jnp.where(lane_lo, dq[0], dq[1]) * root).astype(BF)
                QKV[rows, ks] = (jnp.where(lane_lo, dk[0], dk[1]) * root).astype(BF)
                QKV[rows, vs] = jnp.where(lane_lo, dv[0], dv[1]).astype(BF)

            point()

        g(B_OS, t)[...] = nt(QKV[pl.ds(mo((1 - c) * T, 128), T), :], WQ[...]).astype(BF)
        send(g(B_OS, t), g(B_OR, t), S_DX, t, sib)
        g(B_KP, t)[0] = nt(QKV[pl.ds(mo(c * T, 128), T), :], WQ[...])

        ones = jnp.ones((8, 2 * T), F32).astype(BF)
        sums = nn(ones, QKV[...])[0:1, :]
        g(B_BG, 0)[R_QB + t:R_QB + t + 1, lane_half] = sums[:, :HALF]
        g(B_BG, 0)[R_VB + t:R_VB + t + 1, lane_half] = sums[:, 2 * HALF:]

        if t == 0:
            send_small()
        far_rows = pl.ds(mo((1 - y) * HALF, 128), HALF)
        for k in range(3):
            lanes = slice(k * HALF, (k + 1) * HALF)

            @pl.loop(0, 3)
            def _(j):
                cols = pl.ds(mo(j * 256, 128), 256)
                WQ[cols, lanes] = tn(g(B_X, t)[:, cols], QKV[:, lanes]).astype(BF)

            send(WQ.at[far_rows, pl.ds(k * HALF, HALF)], g(B_YQ, t).at[:, pl.ds(k * HALF, HALF)], S_YQ + k, t, ypeer)
            point()

    def send_small():
        BG, BGC, BGR = (g(b, 0) for b in (B_BG, B_BGC, B_BGR))
        low = BG[...].astype(BF)
        for k in range(8):
            T96[...] = jnp.zeros((16, HALF), F32)
            T96[:, 0:128] = nt(low[0:16, :], place(128, 96, 96 * k))
            at = 12 + 2 * (k // 4)
            T96[0:2, 128:384] = nt(low[0:16, :], place(256, 192, 192 * (k % 4)))[at:at + 2, :]
            for t in (0, 1):
                row = 16 + 4 * t + k // 2
                T96[12 + t:13 + t, :] = BG[row:row + 1, k % 2 * HALF:(k % 2 + 1) * HALF]
            BGC[k] = T96[...].astype(BF)
        for d in NEIGH:
            dest = sh(*peer(d))
            send(BGC.at[dest], BGR.at[s], S_BG, 0, (rep, dest))
        local(BGC.at[s], BGR.at[s], S_BG, 0)

    def relay_qkv(t, k):
        WQ, YQ, lanes = g(B_WQ, t), g(B_YQ, t), pl.ds(k * HALF, HALF)
        wait(YQ.at[:, lanes], S_YQ + k, t)
        for r0 in range(0, HALF, 128):
            r = pl.ds(mo(y * HALF + r0, 128), 128)
            WQ[r, lanes] = (WQ[r, lanes].astype(F32) + YQ[pl.ds(r0, 128), lanes].astype(F32)).astype(BF)
        dst = g(B_GQ, t).at[2 * x + c, :, lanes]
        for dx, dc in ((1, 0), (1, 1), (0, 1), (0, 0)):
            owner = sh(y, flip(x, dx), flip(c, dc))
            src = WQ.at[pl.ds(mo(96 * owner, 32), 96), lanes]
            if dx + dc:
                send(src, dst, S_GQ + k, t, (rep, owner))
            else:
                local(src, dst, S_GQ + k, t)

    def input_back(t):
        T = ROWS[t]
        wait(g(B_OR, t), S_DX, t)

        @pl.loop(0, T // CH)
        def _(i):
            r = pl.ds(mo(i * CH, CH), CH)
            g(B_Y, t)[r, :] = (g(B_N1, t)[r, :] + g(B_KP, t)[0, r, :] + g(B_OR, t)[r, :].astype(F32)).astype(BF)

        local(g(B_Y, t), (o_gx0, o_gx1)[t], S_FIN2, 0, t)

    def make_dn(t, k):
        def each(use):
            wait(g(B_GD, t).at[pl.ds(128 * k, 128)], S_GD + k, t)
            for r0 in (128 * k, 128 * k + 64):
                own = g(B_WD, t)[pl.ds(mo(x * HALF + r0, 64), 64), :].astype(F32)
                use(pl.ds(r0, 64), pl.ds(0, D), own + g(B_GD, t)[pl.ds(r0, 64), :].astype(F32))
        return each

    def make_up(t, dy, xx):
        GU = g(B_GU, t)
        yy = flip(y, dy)

        def each(use):
            if xx == 0:
                wait(GU.at[pl.ds(0, 2)], S_GU1 - dy, t)
            cols = slice(xx * HALF, (xx + 1) * HALF)
            for cc in (0, 1):
                use(pl.ds(0, 96), pl.ds(mo((4 * yy + 2 * xx + cc) * HALF, 128), HALF), GU[2 * yy + cc, :, cols].astype(F32))
        return each

    def make_out(t):
        GO = g(B_GO, t)

        def each(use):
            wait(GO, S_GO, t)
            tot = GO[0].astype(F32)
            for k in range(1, 4):
                tot = tot + GO[k].astype(F32)
            use(pl.ds(0, 96), pl.ds(0, D), tot)
        return each

    def make_qkv(t, part):
        GQ = g(B_GQ, t)

        def each(use):
            cols = slice(part * HALF, (part + 1) * HALF)
            wait(GQ.at[:, :, pl.ds(part * HALF, HALF)], S_GQ + part, t)
            for cc in (0, 1):
                tot = GQ[cc, :, cols].astype(F32) + GQ[2 + cc, :, cols].astype(F32)
                use(pl.ds(0, 96), pl.ds(part * D + cc * HALF, HALF), tot)
        return each

    def each_small(use):
        BGR = g(B_BGR, 0)
        wait(BGR, S_BG, 0)
        tot = BGR[0].astype(F32)
        for k in range(1, 8):
            tot = tot + BGR[k].astype(F32)
        use(pl.ds(0, 16), pl.ds(0, HALF), tot)

    is_end = (rep == 0) | (rep == 3)
    units = []

    def unit(kind, t, each, out, rows, cols):
        if kind == 4:
            bufs = (B_BGS, B_BGA, B_BGB)
        else:
            bufs = (B_ZSD + kind, B_ZAD + kind, B_ZBD + kind)
        units.append((len(units), tuple(g(b, t) for b in bufs), each, out, rows, cols))

    def add_dn(t):
        for k in range(3):
            unit(0, t, make_dn(t, k), o_od.at[t], (128 * k, 128), (0, D))
    def add_up(t):
        for dy in (1, 0):
            for xx in (0, 1):
                at = mo((2 * flip(y, dy) + xx) * D, 128)
                unit(1, t, make_up(t, dy, xx), o_ou.at[t], (0, 96), (at, D))

    def add_qkv(t):
        for part in range(3):
            unit(3, t, make_qkv(t, part), o_oq.at[t], (0, 96), (part * D, D))

    add_dn(1)
    add_up(1)
    add_dn(0)
    unit(2, 1, make_out(1), o_oo.at[1], (0, 96), (0, D))
    add_up(0)
    unit(2, 0, make_out(0), o_oo.at[0], (0, 96), (0, D))
    add_qkv(1)
    unit(4, 0, each_small, o_obg, (0, 16), (0, HALF))
    add_qkv(0)
    assert len(units) == N_UNITS

    def hop(which, u):
        at = which * N_UNITS + u[0]
        return S_Z + at // 2, at % 2

    def view(ref, u):
        return ref.at[pl.ds(*u[4]), pl.ds(*u[5])]

    def ends(u):
        ZS, ZA, ZB = u[1]

        def put(r, cl, val):
            ZS[r, cl] = val.astype(ZS.dtype)

        for end, mid in ((0, 1), (3, 2)):
            @pl.when(rep == end)
            def _():
                u[2](put)
                send(view(ZS, u), view(ZA, u), *hop(0, u), (mid, s))

    def stage_a(u):
        ZS, ZA, ZB = u[1]

        def put_add(r, cl, val):
            ZS[r, cl] = (val + ZA[r, cl].astype(F32)).astype(ZS.dtype)

        for end, mid in ((0, 1), (3, 2)):
            @pl.when(rep == mid)
            def _():
                wait(view(ZA, u), *hop(0, u))
                u[2](put_add)
                send(view(ZS, u), view(ZB, u), *hop(1, u), (3 - mid, s))

    def stage_b(u):
        ZS, ZA, ZB = u[1]
        for end, mid in ((0, 1), (3, 2)):
            @pl.when(rep == mid)
            def _():
                wait(view(ZB, u), *hop(1, u))
                wait(view(ZB, u), *hop(1, u), 1)
                for r0 in range(u[4][0], u[4][0] + u[4][1], 16):
                    r, cl = pl.ds(r0, 16), pl.ds(*u[5])
                    ZS[r, cl] = (ZS[r, cl].astype(F32) + ZB[r, cl].astype(F32)).astype(ZS.dtype)
                send(view(ZS, u), view(u[3], u), *hop(2, u), (end, s))
                local(view(ZS, u), view(u[3], u), *hop(2, u))

    done = [0, 0, 0]

    def advance(n0, n1, n2):
        while done[0] < n0 or done[1] < n1 or done[2] < n2:
            for k, (step, n) in enumerate(((ends, n0), (stage_a, n1), (stage_b, n2))):
                if done[k] < n:
                    step(units[done[k]])
                    done[k] += 1

    relays = [functools.partial(relay_up, t, dy) for t in (1, 0) for dy in (1, 0)]
    relays += [functools.partial(relay_qkv, t, k) for t in (1, 0) for k in range(3)]

    def point():
        *steps, through = plan.pop(0)
        while len(relays) > 10 - through:
            relays.pop(0)()
        advance(*steps)

    plan = PLAN[:]
    cls_back(1)
    cls_back(0)
    mine = g(B_CF, 0).at[2 * y + c]
    g(B_CF, 0)[2 * y + c] = g(B_CFW, 0)[...].astype(BF)
    fixers = (ypeer, sib, (rep, sh(1 - y, x, 1 - c)))
    for dev in fixers:
        send(mine, mine, S_CF, 0, dev)
    pre_back(0)
    wait(g(B_CF, 0).at[pl.ds(0, 3)], S_CF, 0)
    for t in (0, 1):
        wait(g(B_Y, t), S_FIN, 0, t)
    ffn_back(1)
    ffn_back(0, point)
    mid_back(1)
    attention_back(1, point)
    mid_back(0)
    attention_back(0, point)
    input_back(1)
    input_back(0)
    while plan:
        point()
    for k in range(done[0], N_UNITS + 1):
        advance(min(k + 1, N_UNITS), k, k - 2)
    advance(N_UNITS, N_UNITS, N_UNITS)

    for u in units:
        ZS = view(u[1][0], u)
        wait(ZS, *hop(2, u))

        @pl.when(is_end)
        def _():
            wait(ZS, *hop(0, u), 1)

        @pl.when(jnp.logical_not(is_end))
        def _():
            wait(ZS, *hop(2, u), 1)

    for t in (0, 1):
        scatter_sent(t, S_D1A, S_D1B, S_D2)
        wait(g(B_OS, t), S_DA, t, 1)
        wait(g(B_OS, t), S_DX, t, 1)
        for k in range(3):
            wait(g(B_GD, t).at[pl.ds(0, 128)], S_GD + k, t, 1)
        wait(g(B_GU, t).at[pl.ds(0, 2)], S_GU, t, 1)
        wait(g(B_GU, t).at[pl.ds(0, 1)], S_GU1, t, 1)
        for dy in (0, 1):
            wait(g(B_XU, t).at[pl.ds(0, 192)], S_XU1 - dy, t, 1)

        @pl.when(c == y)
        def _():
            wait(g(B_GO, t).at[pl.ds(0, 3)], S_GO, t, 1)

        @pl.when(c != y)
        def _():
            wait(g(B_GO, t), S_GO, t, 1)

        for k in range(3):
            wait(g(B_YQ, t).at[:, pl.ds(k * HALF, HALF)], S_YQ + k, t, 1)
            wait(g(B_GQ, t).at[pl.ds(0, 3), :, pl.ds(k * HALF, HALF)], S_GQ + k, t, 1)
        wait(g(B_Y, t), S_FIN2, 0, t)
    wait(g(B_BGR, 0).at[pl.ds(0, 7)], S_BG, 0, 1)
    wait(g(B_CF, 0).at[pl.ds(0, 3)], S_CF, 0, 1)


def fused_call(*args):
    hbm = pl.BlockSpec(memory_space=pl.ANY)
    vm = pl.BlockSpec(memory_space=pltpu.VMEM)
    sm = pl.BlockSpec(memory_space=pltpu.SMEM)
    out_shape = [
        jax.ShapeDtypeStruct((8, 128), F32),
        jax.ShapeDtypeStruct((128, D), BF),
        jax.ShapeDtypeStruct((256, D), BF),
        jax.ShapeDtypeStruct((128, D), BF),
        jax.ShapeDtypeStruct((256, D), BF),
        jax.ShapeDtypeStruct((2, 96, 3 * D), BF),
        jax.ShapeDtypeStruct((2, 96, D), BF),
        jax.ShapeDtypeStruct((2, 96, 4 * D), BF),
        jax.ShapeDtypeStruct((2, HALF, D), BF),
        jax.ShapeDtypeStruct((16, HALF), F32),
    ]
    return pl.pallas_call(
        fused_kernel,
        out_shape=out_shape,
        in_specs=[hbm] * 8 + [vm] * 6 + [sm] * 2,
        out_specs=[vm] + [hbm] * 9,
        scratch_shapes=[shape for _, shape in scratch_list()] + [pltpu.SemaphoreType.DMA((N_SEMS,))],
        compiler_params=pltpu.CompilerParams(collective_id=0, has_side_effects=True, vmem_limit_bytes=VMEM_LIMIT),
        cost_estimate=pl.CostEstimate(flops=18 * 10**9, bytes_accessed=40 * 10**6, transcendentals=4 * 10**6),
    )(*args)


def widen_kernel(*refs):
    loss, y0, y1, gx0, gx1, oq, oo, ou, od, bg = refs[:10]
    r_loss, r_y0, r_y1, r_gx0, r_gx1, r_q, r_qb, r_o, r_ob, r_u, r_ub, r_d, r_db, r_gn, r_sf = refs[10:25]
    low = refs[25:29]
    wide = refs[29:33]
    through = refs[33:37]
    sem_in, sem_out, sem_move, sem_move_out = refs[37:]
    groups = list(zip((oq, ou, od, oo), low, wide, (r_q, r_u, r_d, r_o)))
    reads, writes, moves = [], [], []
    for k, (src, lo, hi, dst) in enumerate(groups):
        for t in (0, 1):
            reads.append(pltpu.make_async_copy(src.at[t], lo.at[t], sem_in.at[2 * k + t]))
            reads[-1].start()
    for k, (src, dst) in enumerate(((y0, r_y0), (y1, r_y1), (gx0, r_gx0), (gx1, r_gx1))):
        moves.append((pltpu.make_async_copy(src, through[k], sem_move.at[k]),
                      pltpu.make_async_copy(through[k], dst, sem_move_out.at[k])))
        moves[-1][0].start()
    r_loss[...] = loss[0:1, 0:1]
    r_ob[...] = bg[0:2, 0:96]
    r_db[...] = bg[2:4, 0:96]
    for t in (0, 1):
        r_gn[t] = bg[4 + 2 * t:6 + 2 * t, 0:96]
        r_sf[t] = bg[8 + 2 * t:10 + 2 * t, 0:96]
    r_qb[...] = bg[0:2, 128:320]
    r_ub[...] = bg[12:14, :]
    for k, (src, lo, hi, dst) in enumerate(groups):
        for t in (0, 1):
            reads[2 * k + t].wait()
            hi[t] = lo[t].astype(F32)
            writes.append(pltpu.make_async_copy(hi.at[t], dst.at[t], sem_out.at[2 * k + t]))
            writes[-1].start()
    for there, onward in moves:
        there.wait()
        onward.start()
    for copy in writes + [onward for there, onward in moves]:
        copy.wait()


def widen_call(*args):
    hbm = pl.BlockSpec(memory_space=pl.ANY)
    vm = pl.BlockSpec(memory_space=pltpu.VMEM)

    def out(dtype, *shape):
        return jax.ShapeDtypeStruct(shape, dtype)

    shapes = [(2, 96, 3 * D), (2, 96, 4 * D), (2, HALF, D), (2, 96, D)]
    return pl.pallas_call(
        widen_kernel,
        out_shape=[out(F32, 1, 1), out(BF, 128, D), out(BF, 256, D), out(BF, 128, D), out(BF, 256, D),
                   out(F32, *shapes[0]), out(F32, 2, 192), out(F32, *shapes[3]), out(F32, 2, 96),
                   out(F32, *shapes[1]), out(F32, 2, HALF), out(F32, *shapes[2]), out(F32, 2, 96),
                   out(F32, 2, 2, 96), out(F32, 2, 2, 96)],
        in_specs=[vm] + [hbm] * 8 + [vm],
        out_specs=[vm, hbm, hbm, hbm, hbm, hbm, vm, hbm, vm, hbm, vm, hbm, vm, vm, vm],
        scratch_shapes=[pltpu.VMEM(shape, BF) for shape in shapes] + [pltpu.VMEM(shape, F32) for shape in shapes]
        + [pltpu.VMEM((rows, D), BF) for rows in ROWS * 2]
        + [pltpu.SemaphoreType.DMA((8,)), pltpu.SemaphoreType.DMA((8,)), pltpu.SemaphoreType.DMA((4,)),
           pltpu.SemaphoreType.DMA((4,))],
        compiler_params=pltpu.CompilerParams(vmem_limit_bytes=VMEM_LIMIT),
    )(*args)


def local_fast(query_tokens, passage_tokens, query_cot, passage_cot, bucket_counts, positives, qkv_weight, qv_bias,
               out_weight, out_bias, up_weight, up_bias, down_weight, down_bias, norm_gains, norm_shifts):
    results = widen_call(*fused_call(
        query_tokens.reshape(128, D), passage_tokens.reshape(256, D),
        query_cot.reshape(128, D), passage_cot.reshape(256, D),
        qkv_weight, out_weight, up_weight, down_weight,
        qv_bias, out_bias, up_bias, down_bias, norm_gains, norm_shifts, bucket_counts, positives))
    loss, y0, y1, gx0, gx1 = results[:5]
    return (loss.reshape(()), y0.reshape(query_tokens.shape), y1.reshape(passage_tokens.shape),
            gx0.reshape(query_tokens.shape), gx1.reshape(passage_tokens.shape), *results[5:])


def solution(mesh):
    in_specs = (
        P(("rep", "shard"), None, None),
        P(("rep", "shard"), None, None),
        P(("rep", "shard"), None, None),
        P(("rep", "shard"), None, None),
        P(),
        P(("rep", "shard")),
        P(None, "shard", None),
        P(None, "shard"),
        P(None, "shard", None),
        P(None, "shard"),
        P(None, "shard", None),
        P(None, "shard"),
        P(None, "shard", None),
        P(None, "shard"),
        P(None, None, "shard"),
        P(None, None, "shard"),
    )
    out_specs = (
        P(),
        P(("rep", "shard"), None, None),
        P(("rep", "shard"), None, None),
        P(("rep", "shard"), None, None),
        P(("rep", "shard"), None, None),
        P(None, "shard", None),
        P(None, "shard"),
        P(None, "shard", None),
        P(None, "shard"),
        P(None, "shard", None),
        P(None, "shard"),
        P(None, "shard", None),
        P(None, "shard"),
        P(None, None, "shard"),
        P(None, None, "shard"),
    )
    small_mesh = (mesh.shape["rep"], mesh.shape["shard"]) == (4, 8)
    step = local_fast if small_mesh else local
    return jax.shard_map(step, mesh=mesh, in_specs=in_specs, out_specs=out_specs, check_vma=False)
```
